32 devices in a mesh: grp: 2 (over y), seg: 8 (over z, x), tp: 2 (over core).
Axes of the slice: x: 2, y: 2, z: 4, core: 2. Of those that a mesh axis runs over, the one named last changes fastest.
Arguments:
- queries: bfloat16 [2048, 5120], P(('grp', 'seg'), 'tp'), parts along dimension 0, may hold values from -42 to 42
- key_vectors: bfloat16 [2048, 1024], P(('grp', 'seg'), 'tp'), parts along dimension 0, may hold values from -4.5 to 4.5
- value_vectors: bfloat16 [2048, 1024], P(('grp', 'seg'), 'tp'), parts along dimension 0, may hold values from -5 to 5
- direction: bfloat16 [2048, 5120], P(('grp', 'seg'), 'tp'), parts along dimension 0, may hold values from -5 to 5
- rewards: float32 [2048], P(('grp', 'seg')), parts along dimension 0, may hold values from -4 to 4
- logprobs: float32 [2048], P(('grp', 'seg')), parts along dimension 0, may hold values from -6 to -0.05
- ref_logprobs: float32 [2048], P(('grp', 'seg')), parts along dimension 0, may hold values from -6 to -0.05
- value_est: float32 [2048], P(('grp', 'seg')), parts along dimension 0, may hold values from -4 to 4
- parents: int32 [16], P('grp'), parts along dimension 0, may hold values from -1 to 4, as said below
- seg_lengths: int32 [16], P('grp'), parts along dimension 0, may hold values from 1 to 128, 768 in all
Outputs:
- grad_queries: bfloat16 [2048, 5120], P(('grp', 'seg'), 'tp'), parts along dimension 0
- grad_keys: bfloat16 [2048, 1024], P(('grp', 'seg'), 'tp'), parts along dimension 0
- grad_values: bfloat16 [2048, 1024], P(('grp', 'seg'), 'tp'), parts along dimension 0
- advantages: float32 [2048], P(('grp', 'seg')), parts along dimension 0
The draws below stay inside these ranges and needn't reach their ends.
There are 2 independent parts, one for each index of `grp`. The reference program is written for one: setup_inputs(seed, part) draws one part's arguments, and reference() takes and returns one part's arrays. A program takes and returns all parts, laid end to end along the dimension named above; each array names one. Nothing has to cross between parts.
Inputs may be any that keep to these rules, and one draw needn't show every extreme that they name: `parents`: segment 0 has parent -1 and every other segment's parent is an earlier segment; segment 0 is the root (the shared prompt segment) and an ancestor of every later segment; no segment has more than 4 ancestors, and some have exactly 4.
All inputs are finite; a program needn't handle non-finite values.
Results may differ from the reference program's by a relative error of at most 0.0091.
Values may be sent and summed in bfloat16 or wider, within the bound.
No kernel may reach another device: no remote copies, remote signals or barrier semaphores. Data moves between devices by JAX's collectives and lax.ppermute only.
A program may use at most 64 MiB of HBM per device.

```python
import math
import jax
import jax.numpy as jnp
import numpy as np
from jax import lax

QH = 40
KVH = 8
HD = 128
SEGLEN = 128
DEPTH = 5
PRE = 1
NSEG = 8
TOKENS = 1024


def paired_keys(key):
    raw_normal = jnp.clip(jax.random.normal(jax.random.fold_in(key, 91), (TOKENS, KVH * HD), jnp.float32), -4.5, 4.5)
    base_draw = raw_normal
    return base_draw


def draw_key_vectors(key, part):
    drawn = paired_keys(key)
    return drawn.astype(jnp.bfloat16)


def draw_queries(key, part):
    key = jax.random.fold_in(key, 5)
    raw_normal = jnp.clip(jax.random.normal(key, (TOKENS, QH * HD), jnp.float32), -4.5, 4.5)
    base_draw = raw_normal
    drawn = base_draw
    return drawn.astype(jnp.bfloat16)


def draw_parents(key, part):
    key = jax.random.fold_in(key, 11)
    seg_index = jnp.arange(NSEG, dtype=jnp.int32)
    rest_count = NSEG - PRE
    bound_one = PRE + (rest_count + 14) // 15
    bound_two = PRE + (rest_count * 3 + 14) // 15
    bound_three = PRE + (rest_count * 7 + 14) // 15
    high_bound = jnp.where(seg_index < bound_one, PRE, jnp.where(seg_index < bound_two, bound_one, jnp.where(seg_index < bound_three, bound_two, bound_three)))
    low_bound = PRE - 1
    random_bits = jax.random.randint(key, (NSEG,), 0, 1 << 30, dtype=jnp.int32)
    picked = low_bound + random_bits % (high_bound - low_bound)
    picked = jnp.where(seg_index == bound_two - 1, bound_one - 1, picked)
    picked = jnp.where(seg_index == bound_three - 1, bound_two - 1, picked)
    picked = jnp.where(seg_index == NSEG - 1, bound_three - 1, picked)
    return jnp.where(seg_index < PRE, seg_index - 1, picked).astype(jnp.int32)


def levels(stream_key, shape, split, smallest, top_value):
    gain = 1.0
    for dim, parts in split:
        steps = jax.random.uniform(jax.random.fold_in(jax.random.fold_in(stream_key, 6), dim), (parts,), jnp.float32, smallest / len(split), top_value / len(split))
        gain = gain * jnp.repeat(jnp.exp(steps), shape[dim] // parts).reshape((-1,) + (1,) * (len(shape) - 1 - dim))
    return gain


def split_up(amount, total, reach, slope):
    loads = [(1 << 20) // math.isqrt(standing ** slope) + 1 for standing in range(2, amount + 1)]
    spare, given = total - reach - (amount - 1), [1] * (amount - 1)
    while spare > 0:
        movable = [i for i in range(amount - 1) if given[i] < reach]
        whole, budget = sum([loads[i] for i in movable]), spare
        for i in movable:
            addition = min(reach - given[i], max(1, budget * loads[i] // whole), spare)
            given[i] = given[i] + addition
            spare = spare - addition
    return np.array([reach] + given)


def ragged_sizes(stream_key, number_of, total, most, slope):
    if number_of == 2:
        one = jax.random.randint(stream_key, (), max(1, total - most), min(most, total - 1) + 1)
        return jnp.stack([one, total - one])
    sizes = jnp.asarray(split_up(number_of, total, most, slope), jnp.int32)
    couples = (number_of - 1) // 2
    source_of, sink = sizes[1:1 + 2 * couples:2], sizes[2:2 + 2 * couples:2]
    room = jnp.minimum(source_of - 1, most - sink)
    shifted = jax.random.randint(jax.random.fold_in(stream_key, 1), (couples,), 0, 1 << 20) % (room + 1)
    sizes = sizes.at[1:1 + 2 * couples:2].set(source_of - shifted).at[2:2 + 2 * couples:2].set(sink + shifted)
    return sizes[jax.random.permutation(jax.random.fold_in(stream_key, 2), number_of)]


def normal_values(rng, extent, scale, limit, cuts=(), kind=jnp.bfloat16):
    factor_of = levels(rng, extent, cuts, -0.22, 0.18) if cuts else 1.0
    values = jax.random.normal(rng, extent, jnp.float32) * scale * factor_of
    return jnp.minimum(jnp.maximum(values, -limit), limit).astype(kind)


def setup_inputs(seed: int = 0, part: int = 0) -> dict:
    keys = jax.random.split(jax.random.key(seed), 11)
    own_keys = jax.random.split(jax.random.fold_in(keys[10], part), 11)
    queries = draw_queries(jax.random.fold_in(jax.random.fold_in(keys[10], part), 71), part)
    key_vectors = draw_key_vectors(jax.random.fold_in(jax.random.fold_in(keys[10], part), 71), part)
    value_vectors = normal_values(own_keys[2], (TOKENS, KVH * HD), 1.0, 5.0, ((0, 8), (1, 2)))
    direction = normal_values(own_keys[3], (TOKENS, QH * HD), 1.0, 5.0, ((0, 8), (1, 2)))
    rewards = normal_values(own_keys[4], (TOKENS,), 0.5, 4.0, ((0, 8),), jnp.float32)
    logprobs = jnp.clip(-6.0 + 5.95 * jax.random.uniform(own_keys[5], (TOKENS,), jnp.float32) ** levels(own_keys[5], (TOKENS,), ((0, 8),), -0.2, 0.2), -6.0, -0.05)
    ref_logprobs = jnp.clip(-6.0 + 5.95 * jax.random.uniform(own_keys[6], (TOKENS,), jnp.float32) ** levels(own_keys[6], (TOKENS,), ((0, 8),), -0.2, 0.2), -6.0, -0.05)
    value_est = normal_values(own_keys[7], (TOKENS,), 0.5, 4.0, ((0, 8),), jnp.float32)
    parents = draw_parents(jax.random.fold_in(jax.random.fold_in(keys[10], part), 71), part)
    seg_lengths = ragged_sizes(own_keys[9], NSEG, NSEG * SEGLEN * 3 // 4, SEGLEN, 1).astype(jnp.int32)
    return dict(queries=queries, key_vectors=key_vectors, value_vectors=value_vectors, direction=direction, rewards=rewards, logprobs=logprobs, ref_logprobs=ref_logprobs, value_est=value_est, parents=parents, seg_lengths=seg_lengths)


BETA = 0.1
LAMBDA_SEG = 0.7


def lookup(table_values, lookup_ids):
    matches = lookup_ids[..., None] == jnp.arange(table_values.shape[0], dtype=jnp.int32)
    return jnp.sum(jnp.where(matches, table_values, 0), axis=-1).astype(jnp.int32)


def ancestors(parents, count):
    current = jnp.arange(parents.shape[0], dtype=jnp.int32)
    chain_list = []
    for depth_step in range(count):
        parent_ids = lookup(parents, current)
        current = jnp.where(current >= 0, parent_ids, -1).astype(jnp.int32)
        chain_list.append(current)
    return jnp.stack(chain_list, axis=1)


def local_terms(rewards, logprobs, ref_logprobs, value_est, seg_lengths, log_rate):
    length = rewards.shape[1]
    positions = jnp.arange(length, dtype=jnp.int32)
    is_valid = positions[None, :] < seg_lengths[:, None]
    next_value = jnp.concatenate([value_est[:, 1:], jnp.zeros_like(value_est[:, :1])], axis=1)
    next_value = jnp.where(positions[None, :] + 1 < seg_lengths[:, None], next_value, 0.0)
    deltas = jnp.where(is_valid, rewards - BETA * (logprobs - ref_logprobs) + next_value - value_est, 0.0)
    offset = (positions[None, :] - positions[:, None]).astype(jnp.float32)
    discount = jnp.where(offset >= 0, jnp.exp(offset * log_rate), 0.0)
    local_sum = jnp.dot(deltas, discount.T, precision=lax.Precision.HIGHEST)
    return local_sum, is_valid


def tree_solve(first_local, first_value, parents, seg_lengths, log_rate, sweeps):
    children = (parents[None, :] == jnp.arange(parents.shape[0], dtype=jnp.int32)[:, None]).astype(jnp.float32)
    child_count = jnp.sum(children, axis=1)
    tree_weights = children / jnp.maximum(child_count, 1.0)[:, None]
    later_value = jnp.dot(tree_weights, first_value, precision=lax.Precision.HIGHEST)
    lengths_f = seg_lengths.astype(jnp.float32)
    base_term = first_local + jnp.exp((lengths_f - 1.0) * log_rate) * later_value
    factor = jnp.exp(lengths_f * log_rate)
    head_adv = base_term
    for depth_step in range(sweeps):
        head_adv = base_term + factor * jnp.dot(tree_weights, head_adv, precision=lax.Precision.HIGHEST)
    later_head = jnp.dot(tree_weights, head_adv, precision=lax.Precision.HIGHEST)
    return later_value, later_head


def advantage_rows(local_sum, is_valid, seg_lengths, later_value, later_head, log_rate):
    positions = jnp.arange(local_sum.shape[1], dtype=jnp.float32)
    lengths_f = seg_lengths.astype(jnp.float32)[:, None]
    value_part = jnp.exp((lengths_f - 1.0 - positions[None, :]) * log_rate) * later_value[:, None]
    head_part = jnp.exp((lengths_f - positions[None, :]) * log_rate) * later_head[:, None]
    return jnp.where(is_valid, local_sum + value_part + head_part, 0.0)


def build_mask(slot_ids, seg_lengths, length):
    slot_lengths = lookup(seg_lengths, slot_ids)
    positions = jnp.arange(length, dtype=jnp.int32)
    key_valid = (slot_ids >= 0)[:, :, None] & (positions[None, None, :] < slot_lengths[:, :, None])
    self_slot = (jnp.arange(slot_ids.shape[1]) == 0)[None, None, :, None]
    causal = positions[None, None, None, :] <= positions[None, :, None, None]
    keymask = key_valid[:, None, :, :] & (jnp.logical_not(self_slot) | causal)
    return keymask.reshape(slot_ids.shape[0], length, -1)


def attend_group(q_group, do_group, k_group, v_group, keymask):
    score_scale = q_group.shape[-1] ** -0.5
    q_wide = q_group.astype(jnp.float32)
    do_wide = do_group.astype(jnp.float32)
    k_wide = k_group.astype(jnp.float32)
    v_wide = v_group.astype(jnp.float32)
    scores = jnp.einsum('tjd,kd->jtk', q_wide, k_wide) * score_scale
    scores = jnp.where(keymask[None], scores, -1e30)
    row_max = jnp.max(scores, axis=-1, keepdims=True)
    weights = jnp.exp(scores - row_max)
    attn_prob = weights / jnp.sum(weights, axis=-1, keepdims=True)
    prob_low = attn_prob.astype(jnp.bfloat16)
    attn_out = jnp.einsum('jtk,kd->tjd', prob_low.astype(jnp.float32), v_wide)
    row_dot = jnp.sum(do_wide * attn_out, axis=-1)
    dprob = jnp.einsum('tjd,kd->jtk', do_wide, v_wide)
    dscore = (attn_prob * (dprob - jnp.transpose(row_dot)[:, :, None])).astype(jnp.bfloat16)
    grad_q = (jnp.einsum('jtk,kd->tjd', dscore.astype(jnp.float32), k_wide) * score_scale).astype(jnp.bfloat16)
    grad_k = jnp.einsum('jtk,tjd->kd', dscore.astype(jnp.float32), q_wide) * score_scale
    grad_v = jnp.einsum('jtk,tjd->kd', prob_low.astype(jnp.float32), do_wide)
    return grad_q, grad_k, grad_v


def segment_backward(q_one, do_one, kv_one, mask_one):
    length, kv_heads, group_size, head_dim = q_one.shape
    flat_kv = kv_one.reshape(-1, 2, kv_heads, head_dim)

    def per_group(inputs):
        return attend_group(inputs[0], inputs[1], inputs[2], inputs[3], mask_one)

    grad_q, grad_k, grad_v = lax.map(per_group, (jnp.moveaxis(q_one, 1, 0), jnp.moveaxis(do_one, 1, 0), jnp.moveaxis(flat_kv[:, 0], 1, 0), jnp.moveaxis(flat_kv[:, 1], 1, 0)))
    grad_q = jnp.moveaxis(grad_q, 0, 1).reshape(length, -1)
    grad_kv = jnp.stack([jnp.moveaxis(grad_k, 0, 1), jnp.moveaxis(grad_v, 0, 1)], axis=1)
    return grad_q, grad_kv.reshape(kv_one.shape[0], length, -1)


def reference(queries, key_vectors, value_vectors, direction, rewards, logprobs, ref_logprobs, value_est, parents, seg_lengths):
    log_rate = math.log(LAMBDA_SEG) / SEGLEN
    grid = (NSEG, SEGLEN)
    local_sum, is_valid = local_terms(rewards.reshape(grid), logprobs.reshape(grid), ref_logprobs.reshape(grid), value_est.reshape(grid), seg_lengths, log_rate)
    later_value, later_head = tree_solve(local_sum[:, 0], value_est.reshape(grid)[:, 0], parents, seg_lengths, log_rate, DEPTH)
    advantage = advantage_rows(local_sum, is_valid, seg_lengths, later_value, later_head, log_rate)
    grad_out = (advantage[:, :, None] * direction.reshape(NSEG, SEGLEN, -1).astype(jnp.float32)).astype(jnp.bfloat16)
    chains = ancestors(parents, DEPTH - 1)
    slot_ids = jnp.concatenate([jnp.arange(NSEG, dtype=jnp.int32)[:, None], chains], axis=1)
    keymask = build_mask(slot_ids, seg_lengths, SEGLEN)
    kv_width = KVH * HD
    kv_all = jnp.concatenate([key_vectors, value_vectors], axis=1).reshape(NSEG, SEGLEN, 2 * kv_width)
    head_shape = (NSEG, SEGLEN, KVH, QH // KVH, HD)

    def per_segment(inputs):
        slot_kv = jnp.take(kv_all, jnp.maximum(inputs[2], 0).astype(jnp.int32), axis=0)
        return segment_backward(inputs[0], inputs[1], slot_kv, inputs[3])

    grad_q, grad_kv = lax.map(per_segment, (queries.reshape(head_shape), grad_out.reshape(head_shape), slot_ids, keymask))
    targets = jnp.where(slot_ids >= 0, slot_ids, NSEG).astype(jnp.int32).reshape(-1)
    kv_grads = jax.ops.segment_sum(grad_kv.reshape(NSEG * DEPTH, -1), targets, num_segments=NSEG + 1)[:NSEG]
    kv_grads = kv_grads.reshape(TOKENS, 2 * kv_width)
    grad_keys = kv_grads[:, :kv_width].astype(jnp.bfloat16)
    grad_values = kv_grads[:, kv_width:].astype(jnp.bfloat16)
    return grad_q.reshape(TOKENS, QH * HD), grad_keys, grad_values, advantage.reshape(TOKENS)
```

```python
import functools
import math

import jax
import jax.numpy as jnp
from jax import lax
from jax.experimental import pallas as pl
from jax.experimental.pallas import tpu as pltpu
from jax.sharding import PartitionSpec as P

HD = 128
DEPTH = 5
BETA = 0.1
LAMBDA_SEG = 0.7
GATHER_LIMIT = 16
LOG2E = math.log2(math.e)


def lookup(table_values, lookup_ids):
    matches = lookup_ids[..., None] == jnp.arange(table_values.shape[0], dtype=jnp.int32)
    return jnp.sum(jnp.where(matches, table_values, 0), axis=-1)


def ancestors(parents, count):
    current = jnp.arange(parents.shape[0], dtype=jnp.int32)
    chain_list = []
    for depth_step in range(count):
        parent_ids = lookup(parents, current)
        current = jnp.where(current >= 0, parent_ids, -1)
        chain_list.append(current)
    return jnp.stack(chain_list, axis=1)


def delta_rows(rewards, logprobs, ref_logprobs, value_est, next_value, own_len):
    positions = lax.broadcasted_iota(jnp.int32, rewards.shape, 1)
    next_value = jnp.where(positions + 1 < own_len, next_value, 0.0)
    return jnp.where(
        positions < own_len,
        rewards - BETA * (logprobs - ref_logprobs) + next_value - value_est,
        0.0,
    )


def attend_kernel(
    log_rate,
    group_size,
    depth,
    own_ref,
    src_ref,
    dst_ref,
    slot_len_ref,
    parents_ref,
    lengths_ref,
    first_ref,
    deltas_ref,
    q_ref,
    dir_ref,
    k_ref,
    v_ref,
    dq_ref,
    dk_ref,
    dv_ref,
    adv_ref,
    do_scr,
    bias_scr,
    p_scr,
    ds_scr,
):
    length = q_ref.shape[0]
    slots = src_ref.shape[0]
    kv_heads = k_ref.shape[2] // HD
    own = own_ref[0]
    own_len = slot_len_ref[0]
    count = parents_ref.shape[1]

    row_id = lax.broadcasted_iota(jnp.int32, (count, count), 0)
    col_id = lax.broadcasted_iota(jnp.int32, (count, count), 1)
    eye = row_id == col_id

    def to_row(col):
        return jnp.sum(jnp.where(eye, col, 0.0), axis=0, keepdims=True)

    children = (parents_ref[...] == row_id).astype(jnp.float32)
    weights = children / jnp.maximum(jnp.sum(children, axis=1, keepdims=True), 1.0)
    lens_col = jnp.sum(jnp.where(eye, lengths_ref[...].astype(jnp.float32), 0.0), axis=1, keepdims=True)
    first_local = first_ref[:, 0:1]
    first_value = first_ref[:, 1:2]
    later_value = jnp.sum(weights * to_row(first_value), axis=1, keepdims=True)
    base_term = first_local + jnp.exp((lens_col - 1.0) * log_rate) * later_value
    factor = jnp.exp(lens_col * log_rate)
    head = base_term
    for _ in range(depth):
        head = base_term + factor * jnp.sum(weights * to_row(head), axis=1, keepdims=True)
    later_head = jnp.sum(weights * to_row(head), axis=1, keepdims=True)
    mine = lax.broadcasted_iota(jnp.int32, (count, 1), 0) == own
    my_value = jnp.sum(jnp.where(mine, later_value, 0.0), axis=0, keepdims=True)
    my_head = jnp.sum(jnp.where(mine, later_head, 0.0), axis=0, keepdims=True)

    t_id = lax.broadcasted_iota(jnp.int32, (length, length), 0)
    j_id = lax.broadcasted_iota(jnp.int32, (length, length), 1)
    offset = (j_id - t_id).astype(jnp.float32)
    discount = jnp.where(offset >= 0, jnp.exp(offset * log_rate), 0.0)
    local_sum = jnp.sum(discount * deltas_ref[...], axis=1, keepdims=True)
    t_col = lax.broadcasted_iota(jnp.int32, (length, 1), 0)
    left = (own_len - t_col).astype(jnp.float32)
    advantage = jnp.where(
        t_col < own_len,
        local_sum
        + jnp.exp((left - 1.0) * log_rate) * my_value
        + jnp.exp(left * log_rate) * my_head,
        0.0,
    )
    adv_ref[...] = jnp.sum(jnp.where(t_id == j_id, advantage, 0.0), axis=0, keepdims=True)
    do_scr[...] = (advantage * dir_ref[...].astype(jnp.float32)).astype(jnp.bfloat16)

    for slot in range(slots):
        seen = t_id < slot_len_ref[slot]
        if slot == 0:
            seen = jnp.logical_and(seen, t_id <= j_id)
        bias_scr[slot * length : (slot + 1) * length, :] = jnp.where(seen, 0.0, -1e30)

    dk_ref[...] = jnp.zeros_like(dk_ref)
    dv_ref[...] = jnp.zeros_like(dv_ref)
    scale = HD**-0.5
    contract_last = (((1,), (1,)), ((), ()))
    contract_first = (((0,), (0,)), ((), ()))

    for g in range(kv_heads):
        kv_cols = slice(g * HD, (g + 1) * HD)
        k_all = jnp.concatenate([k_ref[src_ref[s], :, kv_cols] for s in range(slots)], axis=0)
        v_all = jnp.concatenate([v_ref[src_ref[s], :, kv_cols] for s in range(slots)], axis=0)
        heads = [
            slice((g * group_size + j) * HD, (g * group_size + j + 1) * HD)
            for j in range(group_size)
        ]
        q_all = jnp.concatenate([q_ref[:, c] for c in heads], axis=0)
        do_all = jnp.concatenate([do_scr[:, c] for c in heads], axis=0)
        for j in range(group_size):
            rows = slice(j * length, (j + 1) * length)
            scores = lax.dot_general(
                k_all, q_all[rows], contract_last, preferred_element_type=jnp.float32
            )
            scores = scores * (scale * LOG2E) + bias_scr[...]
            top = jnp.max(scores, axis=0, keepdims=True)
            unnorm = jnp.exp2(scores - top)
            prob = unnorm * (1.0 / jnp.sum(unnorm, axis=0, keepdims=True))
            prob_low = prob.astype(jnp.bfloat16)
            dprob = lax.dot_general(
                v_all, do_all[rows], contract_last, preferred_element_type=jnp.float32
            )
            row_dot = jnp.sum(prob_low.astype(jnp.float32) * dprob, axis=0, keepdims=True)
            dscore = (prob * (dprob - row_dot)).astype(jnp.bfloat16)
            p_scr[:, rows] = prob_low
            ds_scr[:, rows] = dscore
        dscore_all = ds_scr[...]
        dq_t = lax.dot_general(
            k_all, dscore_all, contract_first, preferred_element_type=jnp.float32
        )
        for j in range(group_size):
            dq_ref[:, heads[j]] = (
                jnp.transpose(dq_t[:, j * length : (j + 1) * length]) * scale
            ).astype(dq_ref.dtype)
        dk_all = jnp.dot(dscore_all, q_all, preferred_element_type=jnp.float32) * scale
        dv_all = jnp.dot(p_scr[...], do_all, preferred_element_type=jnp.float32)
        for s in range(slots):
            rows = slice(s * length, (s + 1) * length)

            @pl.when(slot_len_ref[s] > 0)
            def _():
                dk_ref[dst_ref[s], :, kv_cols] = dk_all[rows].astype(dk_ref.dtype)
                dv_ref[dst_ref[s], :, kv_cols] = dv_all[rows].astype(dv_ref.dtype)


def attend(
    own, src, dst, slot_lens, parents, lengths, first, deltas, q, direction, k, v, out_slots, log_rate
):
    length, kv_width = k.shape[1:]
    slots = src.shape[0]
    keys = slots * length
    group_size = q.shape[1] // kv_width
    smem = pl.BlockSpec(memory_space=pltpu.SMEM)
    vmem = pl.BlockSpec(memory_space=pltpu.VMEM)
    products = 5 * 2 * keys * length * q.shape[1]
    return pl.pallas_call(
        functools.partial(attend_kernel, log_rate, group_size, DEPTH),
        out_shape=(
            jax.ShapeDtypeStruct(q.shape, jnp.bfloat16),
            jax.ShapeDtypeStruct((out_slots, length, kv_width), jnp.bfloat16),
            jax.ShapeDtypeStruct((out_slots, length, kv_width), jnp.bfloat16),
            jax.ShapeDtypeStruct((1, length), jnp.float32),
        ),
        in_specs=[smem] * 4 + [vmem] * 8,
        out_specs=(vmem,) * 4,
        scratch_shapes=[
            pltpu.VMEM(q.shape, jnp.bfloat16),
            pltpu.VMEM((keys, length), jnp.float32),
            pltpu.VMEM((keys, group_size * length), jnp.bfloat16),
            pltpu.VMEM((keys, group_size * length), jnp.bfloat16),
        ],
        compiler_params=pltpu.CompilerParams(vmem_limit_bytes=40 * 1024 * 1024),
        cost_estimate=pl.CostEstimate(
            flops=products, bytes_accessed=8 * 1024 * 1024, transcendentals=keys * q.shape[1]
        ),
        name="tree_attention_backward",
    )(own, src, dst, slot_lens, parents, lengths, first, deltas, q, direction, k, v)


def fetch_rows(spread, wanted):
    routed = jnp.take(spread, jnp.maximum(wanted, 0), axis=0)
    return lax.all_to_all(routed, "seg", split_axis=0, concat_axis=2, tiled=True)


def return_rows(grad_rows, wanted, total_segs):
    returned = lax.all_to_all(grad_rows, "seg", split_axis=2, concat_axis=0, tiled=True)
    piece_len = returned.shape[2]
    feature_len = returned.shape[3]
    routed_ids = wanted.reshape(-1)
    targets = jnp.where(routed_ids >= 0, routed_ids, total_segs)
    summed = jax.ops.segment_sum(
        returned.reshape(-1, piece_len * feature_len).astype(jnp.float32),
        targets,
        num_segments=total_segs + 1,
    )[:total_segs]
    return lax.all_to_all(
        summed.reshape(total_segs, piece_len, feature_len),
        "seg",
        split_axis=0,
        concat_axis=1,
        tiled=True,
    )


def body(
    queries,
    key_vectors,
    value_vectors,
    direction,
    rewards,
    logprobs,
    ref_logprobs,
    value_est,
    parents,
    seg_lengths,
):
    total_segs = parents.shape[0]
    groups = lax.axis_size("seg")
    held_segs = total_segs // groups
    assert held_segs == 1
    length = rewards.shape[0]
    own = lax.axis_index("seg")
    log_rate = math.log(LAMBDA_SEG) / length
    kv_width = key_vectors.shape[1]
    own_len = lax.dynamic_slice_in_dim(seg_lengths, own, 1)

    next_value = jnp.concatenate([value_est[1:], jnp.zeros_like(value_est[:1])])
    deltas = delta_rows(
        rewards[None], logprobs[None], ref_logprobs[None], value_est[None], next_value[None], own_len[0]
    )
    powers = jnp.exp(jnp.arange(length, dtype=jnp.float32) * log_rate)
    first_pair = jnp.stack([jnp.sum(deltas[0] * powers), value_est[0]])[None]
    first = lax.all_gather(first_pair, "seg", axis=0, tiled=True)

    chains = ancestors(parents, DEPTH - 1)
    held_wanted = lax.dynamic_slice_in_dim(chains, own, 1)
    slot_ids = jnp.concatenate([jnp.reshape(own, (1, 1)), held_wanted], axis=1)[0]
    slot_lens = lookup(seg_lengths, slot_ids)
    args = (jnp.reshape(own, (1,)),)
    tail = (parents[None], seg_lengths[None], first, deltas, queries, direction)
    if groups <= GATHER_LIMIT:
        keys = lax.all_gather(key_vectors[None], "seg", axis=0, tiled=True)
        values = lax.all_gather(value_vectors[None], "seg", axis=0, tiled=True)
        src = jnp.maximum(slot_ids, 0)
        grad_q, grad_k, grad_v, advantage = attend(
            *args, src, src, slot_lens, *tail, keys, values, total_segs, log_rate
        )
        grad_keys = lax.psum_scatter(grad_k, "seg", scatter_dimension=0, tiled=True)[0]
        grad_values = lax.psum_scatter(grad_v, "seg", scatter_dimension=0, tiled=True)[0]
    else:
        kv_local = jnp.concatenate([key_vectors, value_vectors], axis=1)[None]
        spread = lax.all_to_all(kv_local, "seg", split_axis=1, concat_axis=0, tiled=True)
        arrived = fetch_rows(spread, chains)[0]
        slot_kv = jnp.concatenate([kv_local, arrived], axis=0)
        src = jnp.arange(DEPTH, dtype=jnp.int32)
        grad_q, grad_k, grad_v, advantage = attend(
            *args,
            src,
            src,
            slot_lens,
            *tail,
            slot_kv[:, :, :kv_width],
            slot_kv[:, :, kv_width:],
            DEPTH,
            log_rate,
        )
        grad_kv = jnp.concatenate([grad_k, grad_v], axis=2)
        summed = return_rows(grad_kv[None, 1:], chains, total_segs)[0]
        summed = summed + grad_kv[0].astype(jnp.float32)
        grad_keys = summed[:, :kv_width].astype(jnp.bfloat16)
        grad_values = summed[:, kv_width:].astype(jnp.bfloat16)
    return (grad_q, grad_keys, grad_values, advantage[0])


def solution(mesh):
    in_specs = (
        P(("grp", "seg"), "tp"),
        P(("grp", "seg"), "tp"),
        P(("grp", "seg"), "tp"),
        P(("grp", "seg"), "tp"),
        P(("grp", "seg")),
        P(("grp", "seg")),
        P(("grp", "seg")),
        P(("grp", "seg")),
        P("grp"),
        P("grp"),
    )
    out_specs = (
        P(("grp", "seg"), "tp"),
        P(("grp", "seg"), "tp"),
        P(("grp", "seg"), "tp"),
        P(("grp", "seg")),
    )
    return jax.shard_map(body, mesh=mesh, in_specs=in_specs, out_specs=out_specs, check_vma=False)
```

```python
import functools
import math

import jax
import jax.numpy as jnp
from jax import lax
from jax.experimental import pallas as pl
from jax.experimental.pallas import tpu as pltpu
from jax.sharding import PartitionSpec as P

HD = 128
DEPTH = 5
BETA = 0.1
LAMBDA_SEG = 0.7
PAIRED_GROUPS = 8
LOG2E = math.log2(math.e)


def lookup(table_values, lookup_ids):
    matches = lookup_ids[..., None] == jnp.arange(table_values.shape[0], dtype=jnp.int32)
    return jnp.sum(jnp.where(matches, table_values, 0), axis=-1)


def ancestors(parents, count):
    current = jnp.arange(parents.shape[0], dtype=jnp.int32)
    chain_list = []
    for depth_step in range(count):
        parent_ids = lookup(parents, current)
        current = jnp.where(current >= 0, parent_ids, -1)
        chain_list.append(current)
    return jnp.stack(chain_list, axis=1)


def token_terms(log_rate, own_len, rewards, logprobs, ref_logprobs, values):
    positions = lax.broadcasted_iota(jnp.int32, rewards.shape, 1)
    later = jnp.concatenate([values[:, 1:], values[:, :1]], axis=1)
    later = jnp.where(positions + 1 < own_len, later, 0.0)
    deltas = jnp.where(
        positions < own_len, rewards - BETA * (logprobs - ref_logprobs) + later - values, 0.0
    )
    powers = jnp.exp(positions.astype(jnp.float32) * log_rate)
    first_local = jnp.sum(deltas * powers, axis=1, keepdims=True)
    firsts = jnp.where(positions == 0, first_local, jnp.where(positions == 1, values[:, :1], 0.0))
    return deltas, firsts


def pack_kernel(
    log_rate,
    parts,
    own_ref,
    lengths_ref,
    k_ref,
    v_ref,
    rewards_ref,
    logprobs_ref,
    ref_logprobs_ref,
    values_ref,
    *out_refs,
):
    terms_ref = out_refs[-1]
    own = own_ref[0]
    heads = k_ref.shape[1] // HD // parts
    for step, out_ref in enumerate(out_refs[:-1]):
        part = lax.rem(own + step, parts)
        for h in range(heads):
            columns = pl.ds(pl.multiple_of((part * heads + h) * HD, HD), HD)
            out_ref[h] = k_ref[:, columns]
            out_ref[heads + h] = v_ref[:, columns]
    length = k_ref.shape[0]
    deltas, firsts = token_terms(
        log_rate,
        lengths_ref[own],
        rewards_ref[...],
        logprobs_ref[...],
        ref_logprobs_ref[...],
        values_ref[...],
    )
    mine = lax.broadcasted_iota(jnp.int32, (terms_ref.shape[0], length), 0) == own
    terms_ref[:, :length] = jnp.where(mine, deltas, 0.0)
    terms_ref[:, length:] = jnp.where(mine, firsts, 0.0)


def pack(own, lengths, k, v, token_rows, parts, log_rate):
    length, width = k.shape
    smem = pl.BlockSpec(memory_space=pltpu.SMEM)
    vmem = pl.BlockSpec(memory_space=pltpu.VMEM)
    heads = width // HD // parts
    block = jax.ShapeDtypeStruct((2 * heads, length, HD), k.dtype)
    terms = jax.ShapeDtypeStruct((lengths.shape[0], 2 * length), jnp.float32)
    return pl.pallas_call(
        functools.partial(pack_kernel, log_rate, parts),
        out_shape=(block,) * parts + (terms,),
        in_specs=[smem] * 2 + [vmem] * 6,
        out_specs=(vmem,) * (parts + 1),
        cost_estimate=pl.CostEstimate(
            flops=length * 100, bytes_accessed=8 * length * width, transcendentals=length
        ),
        name="pack_keys_values",
    )(own, lengths, k, v, *token_rows)


def attend_kernel(log_rate, group_size, depth, segs, sources, *refs):
    own_ref, parents_s, lengths_s, parents_ref, lengths_ref, terms_ref = refs[:6]
    refs = refs[6:]
    q_refs, dir_refs, kv_refs = refs[:segs], refs[segs : 2 * segs], refs[2 * segs : 2 * segs + sources]
    refs = refs[2 * segs + sources :]
    adv_ref, dq_refs, dkv_refs = refs[0], refs[1 : 1 + segs], refs[1 + segs : 1 + segs + sources // segs]
    q_scr, do_scr, kv_scr, bias_scr, p_scr, ds_scr, acc_scr = refs[1 + segs + sources // segs :]

    length = q_refs[0].shape[0]
    kv_heads = kv_scr.shape[1] // 2
    count = parents_s.shape[0]
    own = own_ref[0]
    part = lax.rem(own, segs)

    row_id = lax.broadcasted_iota(jnp.int32, (count, count), 0)
    col_id = lax.broadcasted_iota(jnp.int32, (count, count), 1)
    eye = row_id == col_id

    def to_row(col):
        return jnp.sum(jnp.where(eye, col, 0.0), axis=0, keepdims=True)

    children = (parents_ref[...] == row_id).astype(jnp.float32)
    weights = children / jnp.maximum(jnp.sum(children, axis=1, keepdims=True), 1.0)
    lens_col = jnp.sum(
        jnp.where(eye, lengths_ref[...].astype(jnp.float32), 0.0), axis=1, keepdims=True
    )
    first_local = terms_ref[:, length : length + 1]
    first_value = terms_ref[:, length + 1 : length + 2]
    later_value = jnp.sum(weights * to_row(first_value), axis=1, keepdims=True)
    base_term = first_local + jnp.exp((lens_col - 1.0) * log_rate) * later_value
    factor = jnp.exp(lens_col * log_rate)
    head = base_term
    for _ in range(depth):
        head = base_term + factor * jnp.sum(weights * to_row(head), axis=1, keepdims=True)
    later_head = jnp.sum(weights * to_row(head), axis=1, keepdims=True)

    t_id = lax.broadcasted_iota(jnp.int32, (length, length), 0)
    j_id = lax.broadcasted_iota(jnp.int32, (length, length), 1)
    offset = (j_id - t_id).astype(jnp.float32)
    discount = jnp.where(offset >= 0, jnp.exp(offset * log_rate), 0.0)
    t_col = lax.broadcasted_iota(jnp.int32, (length, 1), 0)
    seg_col = lax.broadcasted_iota(jnp.int32, (count, 1), 0)

    for source in range(sources):
        kv_scr[source] = kv_refs[source][...]
    acc_scr[...] = jnp.zeros_like(acc_scr)

    slot_sources = []
    for i in range(segs):
        seg = own - part + lax.rem(part + i, segs)
        seg_len = lengths_s[seg]
        mine = seg_col == seg
        my_value = jnp.sum(jnp.where(mine, later_value, 0.0), axis=0, keepdims=True)
        my_head = jnp.sum(jnp.where(mine, later_head, 0.0), axis=0, keepdims=True)
        deltas = jnp.sum(jnp.where(mine, terms_ref[:, :length], 0.0), axis=0, keepdims=True)
        local_sum = jnp.sum(discount * deltas, axis=1, keepdims=True)
        left = (seg_len - t_col).astype(jnp.float32)
        advantage = jnp.where(
            t_col < seg_len,
            local_sum
            + jnp.exp((left - 1.0) * log_rate) * my_value
            + jnp.exp(left * log_rate) * my_head,
            0.0,
        )
        if i == 0:
            adv_ref[...] = jnp.sum(jnp.where(t_id == j_id, advantage, 0.0), axis=0, keepdims=True)
        heads = kv_heads * group_size
        first_col = part * heads * HD if q_refs[i].shape[1] > heads * HD else 0
        for h in range(heads):
            columns = pl.ds(pl.multiple_of(first_col + h * HD, HD), HD)
            q_scr[i, h] = q_refs[i][:, columns]
            grad_out = advantage * dir_refs[i][:, columns].astype(jnp.float32)
            do_scr[i, h] = grad_out.astype(jnp.bfloat16)

        ancestor = seg
        chosen = []
        for slot in range(depth):
            if slot > 0:
                ancestor = jnp.where(
                    ancestor >= 0, parents_s[jnp.maximum(ancestor, 0)], -1
                ).astype(jnp.int32)
            slot_len = jnp.where(ancestor >= 0, lengths_s[jnp.maximum(ancestor, 0)], 0)
            if segs == 1:
                chosen.append(slot)
            else:
                known = jnp.maximum(ancestor, 0)
                steps = (own - part) // segs - known // segs
                turn = lax.rem(lax.rem(known, segs) - part + segs, segs)
                chosen.append(jnp.where(ancestor >= 0, steps * segs + turn, 0))
            seen = t_id < slot_len
            if slot == 0:
                seen = jnp.logical_and(seen, t_id <= j_id)
            bias_scr[i, slot * length : (slot + 1) * length, :] = jnp.where(seen, 0.0, -1e30)
        slot_sources.append(chosen)

    scale = HD**-0.5
    contract_last = (((1,), (1,)), ((), ()))
    contract_first = (((0,), (0,)), ((), ()))
    for i in range(segs):
        chosen = slot_sources[i]
        for g in range(kv_heads):
            k_all = jnp.concatenate([kv_scr[s, g] for s in chosen], axis=0)
            v_all = jnp.concatenate([kv_scr[s, kv_heads + g] for s in chosen], axis=0)
            mine = slice(g * group_size, (g + 1) * group_size)
            q_all = q_scr[i, mine].reshape(group_size * length, HD)
            do_all = do_scr[i, mine].reshape(group_size * length, HD)
            for j in range(group_size):
                rows = slice(j * length, (j + 1) * length)
                scores = lax.dot_general(
                    k_all, q_all[rows], contract_last, preferred_element_type=jnp.float32
                )
                scores = scores * (scale * LOG2E) + bias_scr[i]
                top = jnp.max(scores, axis=0, keepdims=True)
                unnorm = jnp.exp2(scores - top)
                prob = unnorm * (1.0 / jnp.sum(unnorm, axis=0, keepdims=True))
                prob_low = prob.astype(jnp.bfloat16)
                dprob = lax.dot_general(
                    v_all, do_all[rows], contract_last, preferred_element_type=jnp.float32
                )
                row_dot = jnp.sum(prob_low.astype(jnp.float32) * dprob, axis=0, keepdims=True)
                dscore = (prob * (dprob - row_dot)).astype(jnp.bfloat16)
                p_scr[:, rows] = prob_low
                ds_scr[:, rows] = dscore
            dscore_all = ds_scr[...]
            dq_t = lax.dot_general(
                k_all, dscore_all, contract_first, preferred_element_type=jnp.float32
            )
            for j in range(group_size):
                head = g * group_size + j
                dq_refs[i][:, head * HD : (head + 1) * HD] = (
                    jnp.transpose(dq_t[:, j * length : (j + 1) * length]) * scale
                ).astype(jnp.bfloat16)
            dk_all = jnp.dot(dscore_all, q_all, preferred_element_type=jnp.float32) * scale
            dv_all = jnp.dot(p_scr[...], do_all, preferred_element_type=jnp.float32)
            for slot, s in enumerate(chosen):
                rows = slice(slot * length, (slot + 1) * length)
                acc_scr[s, g] += dk_all[rows]
                acc_scr[s, kv_heads + g] += dv_all[rows]
    for step in range(sources // segs):
        for i in range(segs):
            dkv_refs[step][i] = acc_scr[step * segs + i].astype(jnp.bfloat16)


def attend(own, parents, lengths, terms, q_list, dir_list, kv_list, log_rate):
    segs, sources = len(q_list), len(kv_list)
    planes, length, _ = kv_list[0].shape
    kv_heads = planes // 2
    width = q_list[-1].shape[1]
    group_size = width // HD // kv_heads
    keys = DEPTH * length
    smem = pl.BlockSpec(memory_space=pltpu.SMEM)
    vmem = pl.BlockSpec(memory_space=pltpu.VMEM)
    out_shape = (
        (jax.ShapeDtypeStruct((1, length), jnp.float32),)
        + (jax.ShapeDtypeStruct((length, width), jnp.bfloat16),) * segs
        + (jax.ShapeDtypeStruct((segs, planes, length, HD), jnp.bfloat16),) * (sources // segs)
    )
    outs = pl.pallas_call(
        functools.partial(attend_kernel, log_rate, group_size, DEPTH, segs, sources),
        out_shape=out_shape,
        in_specs=[smem] * 3 + [vmem] * (3 + 2 * segs + sources),
        out_specs=(vmem,) * len(out_shape),
        scratch_shapes=[
            pltpu.VMEM((segs, width // HD, length, HD), jnp.bfloat16),
            pltpu.VMEM((segs, width // HD, length, HD), jnp.bfloat16),
            pltpu.VMEM((sources, planes, length, HD), jnp.bfloat16),
            pltpu.VMEM((segs, keys, length), jnp.float32),
            pltpu.VMEM((keys, group_size * length), jnp.bfloat16),
            pltpu.VMEM((keys, group_size * length), jnp.bfloat16),
            pltpu.VMEM((sources, planes, length, HD), jnp.float32),
        ],
        compiler_params=pltpu.CompilerParams(vmem_limit_bytes=40 * 1024 * 1024),
        cost_estimate=pl.CostEstimate(
            flops=5 * 2 * keys * length * width * segs,
            bytes_accessed=8 * 1024 * 1024,
            transcendentals=keys * width * segs,
        ),
        name="tree_attention_backward",
    )(own, parents, lengths, parents[None], lengths[None], terms, *q_list, *dir_list, *kv_list)
    return outs[0], outs[1 : 1 + segs], outs[1 + segs :]


def permute(array, pairs):
    return lax.ppermute(array, "seg", pairs)


def climb(block, groups):
    two = permute(block, [(i, i + 4) for i in range(groups - 4)])
    one = permute(block, [(i, i + 2) for i in range(groups - 2)])
    three = permute(two, [(i, i + 2) for i in range(4, groups - 2)])
    return one, two, three


def descend(one, two, three, groups):
    passed = permute(three, [(i, i - 2) for i in range(6, groups)])
    from_one = permute(one, [(i, i - 2) for i in range(2, groups)])
    two = (two.astype(jnp.float32) + passed.astype(jnp.float32)).astype(two.dtype)
    from_two = permute(two, [(i, i - 4) for i in range(4, groups)])
    return from_one.astype(jnp.float32) + from_two.astype(jnp.float32)


def paired_body(own, queries, direction, key_vectors, value_vectors, token_rows, parents, lengths, log_rate):
    groups = lax.axis_size("seg")
    part = own[0] % 2
    swap = [(i, i ^ 1) for i in range(groups)]
    kept, given, terms = pack(own, lengths, key_vectors, value_vectors, token_rows, 2, log_rate)
    taken = permute(given, swap)
    kept_far = climb(kept, groups)
    half = queries.shape[1] // 2
    q_taken = permute(lax.dynamic_slice_in_dim(queries, (1 - part) * half, half, 1), swap)
    dir_taken = permute(lax.dynamic_slice_in_dim(direction, (1 - part) * half, half, 1), swap)
    taken_far = climb(taken, groups)
    for bit in (1, 2, 4):
        terms = terms + permute(terms, [(i, i ^ bit) for i in range(groups)])
    kv_list = [kept, taken]
    for pair in zip(kept_far, taken_far):
        kv_list += pair
    advantage, dq, dkv = attend(
        own, parents, lengths, terms, [queries, q_taken], [direction, dir_taken], kv_list, log_rate
    )
    dq_back = permute(dq[1], swap)
    total = dkv[0].astype(jnp.float32) + descend(dkv[1], dkv[2], dkv[3], groups)
    total = total.astype(jnp.bfloat16)
    dkv_back = permute(total[1], swap)
    first = part == 0

    def join(mine, other):
        return jnp.concatenate([jnp.where(first, mine, other), jnp.where(first, other, mine)], axis=1)

    def flat(block):
        return jnp.moveaxis(block, 0, 1).reshape(block.shape[1], -1)

    heads = total.shape[1] // 2
    grad_keys = join(flat(total[0, :heads]), flat(dkv_back[:heads]))
    grad_values = join(flat(total[0, heads:]), flat(dkv_back[heads:]))
    return join(dq[0], dq_back), grad_keys, grad_values, advantage[0]


def fetch_rows(spread, wanted):
    routed = jnp.take(spread, jnp.maximum(wanted, 0), axis=0)
    return lax.all_to_all(routed, "seg", split_axis=0, concat_axis=2, tiled=True)


def return_rows(grad_rows, wanted, total_segs):
    returned = lax.all_to_all(grad_rows, "seg", split_axis=2, concat_axis=0, tiled=True)
    piece_len = returned.shape[2]
    feature_len = returned.shape[3]
    routed_ids = wanted.reshape(-1)
    targets = jnp.where(routed_ids >= 0, routed_ids, total_segs)
    summed = jax.ops.segment_sum(
        returned.reshape(-1, piece_len * feature_len).astype(jnp.float32),
        targets,
        num_segments=total_segs + 1,
    )[:total_segs]
    return lax.all_to_all(
        summed.reshape(total_segs, piece_len, feature_len),
        "seg",
        split_axis=0,
        concat_axis=1,
        tiled=True,
    )


def routed_body(own, queries, direction, key_vectors, value_vectors, token_rows, parents, lengths, log_rate):
    total_segs = parents.shape[0]
    length = queries.shape[0]
    block, terms = pack(own, lengths, key_vectors, value_vectors, token_rows, 1, log_rate)
    planes = block.shape[0]
    mine = lax.dynamic_slice_in_dim(terms, own[0], 1)
    terms = lax.all_gather(mine, "seg", axis=0, tiled=True)
    flat = jnp.moveaxis(block, 0, 1).reshape(1, length, planes * HD)
    spread = lax.all_to_all(flat, "seg", split_axis=1, concat_axis=0, tiled=True)
    chains = ancestors(parents, DEPTH - 1)
    arrived = fetch_rows(spread, chains)[0].reshape(DEPTH - 1, length, planes, HD)
    arrived = jnp.moveaxis(arrived, 2, 1)
    kv_list = [block] + [arrived[slot] for slot in range(DEPTH - 1)]
    advantage, dq, dkv = attend(
        own, parents, lengths, terms, [queries], [direction], kv_list, log_rate
    )
    rows = jnp.moveaxis(jnp.concatenate(dkv[1:]), 1, 2).reshape(1, DEPTH - 1, length, planes * HD)
    summed = return_rows(rows, chains, total_segs)[0]
    summed = summed + jnp.moveaxis(dkv[0][0], 0, 1).reshape(length, planes * HD).astype(jnp.float32)
    width = key_vectors.shape[1]
    grad_keys = summed[:, :width].astype(jnp.bfloat16)
    grad_values = summed[:, width:].astype(jnp.bfloat16)
    return dq[0], grad_keys, grad_values, advantage[0]


def body(
    queries,
    key_vectors,
    value_vectors,
    direction,
    rewards,
    logprobs,
    ref_logprobs,
    value_est,
    parents,
    seg_lengths,
):
    groups = lax.axis_size("seg")
    assert parents.shape[0] == groups
    own = jnp.reshape(lax.axis_index("seg"), (1,))
    log_rate = math.log(LAMBDA_SEG) / rewards.shape[0]
    token_rows = [rewards[None], logprobs[None], ref_logprobs[None], value_est[None]]
    plan = paired_body if groups == PAIRED_GROUPS else routed_body
    return plan(
        own, queries, direction, key_vectors, value_vectors, token_rows, parents, seg_lengths, log_rate
    )


def solution(mesh):
    in_specs = (
        P(("grp", "seg"), "tp"),
        P(("grp", "seg"), "tp"),
        P(("grp", "seg"), "tp"),
        P(("grp", "seg"), "tp"),
        P(("grp", "seg")),
        P(("grp", "seg")),
        P(("grp", "seg")),
        P(("grp", "seg")),
        P("grp"),
        P("grp"),
    )
    out_specs = (
        P(("grp", "seg"), "tp"),
        P(("grp", "seg"), "tp"),
        P(("grp", "seg"), "tp"),
        P(("grp", "seg")),
    )
    return jax.shard_map(body, mesh=mesh, in_specs=in_specs, out_specs=out_specs, check_vma=False)
```

```python
import functools
import math

import jax
import jax.numpy as jnp
from jax import lax
from jax.experimental import pallas as pl
from jax.experimental.pallas import tpu as pltpu
from jax.sharding import PartitionSpec as P

HD = 128
DEPTH = 5
BETA = 0.1
LAMBDA_SEG = 0.7
PAIRED_GROUPS = 8
LOG2E = math.log2(math.e)


def lookup(table_values, lookup_ids):
    matches = lookup_ids[..., None] == jnp.arange(table_values.shape[0], dtype=jnp.int32)
    return jnp.sum(jnp.where(matches, table_values, 0), axis=-1)


def ancestors(parents, count):
    current = jnp.arange(parents.shape[0], dtype=jnp.int32)
    chain_list = []
    for depth_step in range(count):
        parent_ids = lookup(parents, current)
        current = jnp.where(current >= 0, parent_ids, -1)
        chain_list.append(current)
    return jnp.stack(chain_list, axis=1)


def token_terms(log_rate, own_len, rewards, logprobs, ref_logprobs, values):
    positions = lax.broadcasted_iota(jnp.int32, rewards.shape, 1)
    later = jnp.concatenate([values[:, 1:], values[:, :1]], axis=1)
    later = jnp.where(positions + 1 < own_len, later, 0.0)
    deltas = jnp.where(
        positions < own_len, rewards - BETA * (logprobs - ref_logprobs) + later - values, 0.0
    )
    powers = jnp.exp(positions.astype(jnp.float32) * log_rate)
    first_local = jnp.sum(deltas * powers, axis=1, keepdims=True)
    firsts = jnp.where(positions == 0, first_local, jnp.where(positions == 1, values[:, :1], 0.0))
    return deltas, firsts


def pack_kernel(
    log_rate,
    parts,
    own_ref,
    lengths_ref,
    k_ref,
    v_ref,
    rewards_ref,
    logprobs_ref,
    ref_logprobs_ref,
    values_ref,
    *out_refs,
):
    terms_ref = out_refs[-1]
    own = own_ref[0]
    heads = k_ref.shape[1] // HD // parts
    for step, out_ref in enumerate(out_refs[:-1]):
        part = lax.rem(own + step, parts)
        for h in range(heads):
            columns = pl.ds(pl.multiple_of((part * heads + h) * HD, HD), HD)
            out_ref[h, 0] = k_ref[:, columns]
            out_ref[h, 1] = v_ref[:, columns]
    length = k_ref.shape[0]
    deltas, firsts = token_terms(
        log_rate,
        lengths_ref[own],
        rewards_ref[...],
        logprobs_ref[...],
        ref_logprobs_ref[...],
        values_ref[...],
    )
    mine = lax.broadcasted_iota(jnp.int32, (terms_ref.shape[0], length), 0) == own
    terms_ref[:, :length] = jnp.where(mine, deltas, 0.0)
    terms_ref[:, length:] = jnp.where(mine, firsts, 0.0)


def pack(own, lengths, k, v, token_rows, parts, log_rate):
    length, width = k.shape
    smem = pl.BlockSpec(memory_space=pltpu.SMEM)
    vmem = pl.BlockSpec(memory_space=pltpu.VMEM)
    heads = width // HD // parts
    block = jax.ShapeDtypeStruct((heads, 2, length, HD), k.dtype)
    terms = jax.ShapeDtypeStruct((lengths.shape[0], 2 * length), jnp.float32)
    return pl.pallas_call(
        functools.partial(pack_kernel, log_rate, parts),
        out_shape=(block,) * parts + (terms,),
        in_specs=[smem] * 2 + [vmem] * 6,
        out_specs=(vmem,) * (parts + 1),
        cost_estimate=pl.CostEstimate(
            flops=length * 100, bytes_accessed=8 * length * width, transcendentals=length
        ),
        name="pack_keys_values",
    )(own, lengths, k, v, *token_rows)


def pack_queries_kernel(own_ref, q_ref, dir_ref, out_ref):
    other = 1 - lax.rem(own_ref[0], 2)
    heads = out_ref.shape[1]
    for h in range(heads):
        columns = pl.ds(pl.multiple_of((other * heads + h) * HD, HD), HD)
        out_ref[0, h] = q_ref[:, columns]
        out_ref[1, h] = dir_ref[:, columns]


def pack_queries(own, q, direction):
    length, width = q.shape
    smem = pl.BlockSpec(memory_space=pltpu.SMEM)
    vmem = pl.BlockSpec(memory_space=pltpu.VMEM)
    return pl.pallas_call(
        pack_queries_kernel,
        out_shape=jax.ShapeDtypeStruct((2, width // HD // 2, length, HD), q.dtype),
        in_specs=[smem, vmem, vmem],
        out_specs=vmem,
        cost_estimate=pl.CostEstimate(flops=0, bytes_accessed=6 * length * width, transcendentals=0),
        name="pack_queries",
    )(own, q, direction)


def prepare_kernel(
    log_rate,
    depth,
    segs,
    own_ref,
    parents_s,
    lengths_s,
    parents_ref,
    lengths_ref,
    terms_ref,
    row_ref,
    adv_ref,
    bias_ref,
):
    length = row_ref.shape[1]
    count = parents_s.shape[0]
    own = own_ref[0]
    part = lax.rem(own, segs)

    row_id = lax.broadcasted_iota(jnp.int32, (count, count), 0)
    col_id = lax.broadcasted_iota(jnp.int32, (count, count), 1)
    eye = row_id == col_id

    def to_row(col):
        return jnp.sum(jnp.where(eye, col, 0.0), axis=0, keepdims=True)

    children = (parents_ref[...] == row_id).astype(jnp.float32)
    weights = children / jnp.maximum(jnp.sum(children, axis=1, keepdims=True), 1.0)
    lens_col = jnp.sum(
        jnp.where(eye, lengths_ref[...].astype(jnp.float32), 0.0), axis=1, keepdims=True
    )
    first_local = terms_ref[:, length : length + 1]
    first_value = terms_ref[:, length + 1 : length + 2]
    later_value = jnp.sum(weights * to_row(first_value), axis=1, keepdims=True)
    base_term = first_local + jnp.exp((lens_col - 1.0) * log_rate) * later_value
    factor = jnp.exp(lens_col * log_rate)
    head = base_term
    for _ in range(depth):
        head = base_term + factor * jnp.sum(weights * to_row(head), axis=1, keepdims=True)
    later_head = jnp.sum(weights * to_row(head), axis=1, keepdims=True)

    t_id = lax.broadcasted_iota(jnp.int32, (length, length), 0)
    j_id = lax.broadcasted_iota(jnp.int32, (length, length), 1)
    offset = (j_id - t_id).astype(jnp.float32)
    discount = jnp.where(offset >= 0, jnp.exp(offset * log_rate), 0.0)
    t_col = lax.broadcasted_iota(jnp.int32, (length, 1), 0)
    seg_col = lax.broadcasted_iota(jnp.int32, (count, 1), 0)
    for i in range(segs):
        seg = own - part + lax.rem(part + i, segs)
        seg_len = lengths_s[seg]
        mine = seg_col == seg
        my_value = jnp.sum(jnp.where(mine, later_value, 0.0), axis=0, keepdims=True)
        my_head = jnp.sum(jnp.where(mine, later_head, 0.0), axis=0, keepdims=True)
        deltas = jnp.sum(jnp.where(mine, terms_ref[:, :length], 0.0), axis=0, keepdims=True)
        local_sum = jnp.sum(discount * deltas, axis=1, keepdims=True)
        left = (seg_len - t_col).astype(jnp.float32)
        advantage = jnp.where(
            t_col < seg_len,
            local_sum
            + jnp.exp((left - 1.0) * log_rate) * my_value
            + jnp.exp(left * log_rate) * my_head,
            0.0,
        )
        if i == 0:
            row_ref[...] = jnp.sum(jnp.where(t_id == j_id, advantage, 0.0), axis=0, keepdims=True)
        adv_ref[i] = jnp.broadcast_to(advantage, (length, HD))

        ancestor = seg
        for slot in range(depth):
            if slot > 0:
                ancestor = parent_of(ancestor, parents_s)
            slot_len = jnp.where(ancestor >= 0, lengths_s[jnp.maximum(ancestor, 0)], 0)
            seen = t_id < slot_len
            if slot == 0:
                seen = jnp.logical_and(seen, t_id <= j_id)
            bias_ref[i, slot * length : (slot + 1) * length, :] = jnp.where(seen, 0.0, -1e30)


def parent_of(segment, parents_s):
    known = parents_s[jnp.maximum(segment, 0)]
    return jnp.where(segment >= 0, known, -1).astype(jnp.int32)


def prepare(own, parents, lengths, terms, segs, log_rate):
    length = terms.shape[1] // 2
    smem = pl.BlockSpec(memory_space=pltpu.SMEM)
    vmem = pl.BlockSpec(memory_space=pltpu.VMEM)
    return pl.pallas_call(
        functools.partial(prepare_kernel, log_rate, DEPTH, segs),
        out_shape=(
            jax.ShapeDtypeStruct((1, length), jnp.float32),
            jax.ShapeDtypeStruct((segs, length, HD), jnp.float32),
            jax.ShapeDtypeStruct((segs, DEPTH * length, length), jnp.float32),
        ),
        in_specs=[smem] * 3 + [vmem] * 3,
        out_specs=(vmem,) * 3,
        cost_estimate=pl.CostEstimate(
            flops=200 * length * length,
            bytes_accessed=4 * (DEPTH + 1) * segs * length * length,
            transcendentals=length * length,
        ),
        name="prepare_advantages",
    )(own, parents, lengths, parents[None], lengths[None], terms)


def attend_kernel(group_size, depth, chunk, chunks, segs, *refs):
    own_ref, parents_s, adv_ref, bias_ref, q_ref, dir_ref = refs[:6]
    shared_refs = refs[6 : 5 + segs]
    refs = refs[5 + segs :]
    steps = (len(refs) - segs - 4) // 2
    kv_refs, dq_refs, dkv_refs = refs[:steps], refs[steps : steps + segs], refs[steps + segs : -4]
    kv_scr, p_scr, ds_scr, acc_scr = refs[-4:]

    length = q_ref.shape[0]
    own = own_ref[0]
    part = lax.rem(own, segs)
    for step in range(steps):
        for i in range(segs):
            kv_scr[step * segs + i] = kv_refs[step][i * chunks + chunk]
    acc_scr[...] = jnp.zeros_like(acc_scr)

    scale = HD**-0.5
    contract_last = (((1,), (1,)), ((), ()))
    contract_first = (((0,), (0,)), ((), ()))
    for i in range(segs):
        ancestor = own - part + lax.rem(part + i, segs)
        chosen = []
        for slot in range(depth):
            if slot > 0:
                ancestor = parent_of(ancestor, parents_s)
            if segs == 1:
                chosen.append(slot)
            else:
                known = jnp.maximum(ancestor, 0)
                step = (own - part) // segs - known // segs
                turn = lax.rem(lax.rem(known, segs) - part + segs, segs)
                chosen.append(jnp.where(ancestor >= 0, step * segs + turn, 0))
        if i == 0:
            first = (part * chunks + chunk) * group_size
            columns = [
                pl.ds(pl.multiple_of((first + j) * HD, HD), HD) for j in range(group_size)
            ]
            q_list = [q_ref[:, c] for c in columns]
            dir_list = [dir_ref[:, c] for c in columns]
        else:
            first = chunk * group_size
            q_list = [shared_refs[i - 1][0, first + j] for j in range(group_size)]
            dir_list = [shared_refs[i - 1][1, first + j] for j in range(group_size)]
        do_list = [(adv_ref[i] * d.astype(jnp.float32)).astype(jnp.bfloat16) for d in dir_list]
        k_all = jnp.concatenate([kv_scr[s, 0] for s in chosen], axis=0)
        v_all = jnp.concatenate([kv_scr[s, 1] for s in chosen], axis=0)
        for j in range(group_size):
            columns = slice(j * length, (j + 1) * length)
            scores = lax.dot_general(
                k_all, q_list[j], contract_last, preferred_element_type=jnp.float32
            )
            scores = scores * (scale * LOG2E) + bias_ref[i]
            top = jnp.max(scores, axis=0, keepdims=True)
            unnorm = jnp.exp2(scores - top)
            prob = unnorm * (1.0 / jnp.sum(unnorm, axis=0, keepdims=True))
            prob_low = prob.astype(jnp.bfloat16)
            dprob = lax.dot_general(
                v_all, do_list[j], contract_last, preferred_element_type=jnp.float32
            )
            row_dot = jnp.sum(prob_low.astype(jnp.float32) * dprob, axis=0, keepdims=True)
            dscore = (prob * (dprob - row_dot)).astype(jnp.bfloat16)
            p_scr[:, columns] = prob_low
            ds_scr[:, columns] = dscore
        dscore_all = ds_scr[...]
        dq_t = lax.dot_general(
            k_all, dscore_all, contract_first, preferred_element_type=jnp.float32
        )
        for j in range(group_size):
            dq_refs[i][:, j * HD : (j + 1) * HD] = (
                jnp.transpose(dq_t[:, j * length : (j + 1) * length]) * scale
            ).astype(jnp.bfloat16)
        q_all = jnp.concatenate(q_list, axis=0)
        do_all = jnp.concatenate(do_list, axis=0)
        dk_all = jnp.dot(dscore_all, q_all, preferred_element_type=jnp.float32) * scale
        dv_all = jnp.dot(p_scr[...], do_all, preferred_element_type=jnp.float32)
        for slot, s in enumerate(chosen):
            rows = slice(slot * length, (slot + 1) * length)
            acc_scr[s, 0] += dk_all[rows]
            acc_scr[s, 1] += dv_all[rows]
    for step in range(steps):
        for i in range(segs):
            dkv_refs[step][i] = acc_scr[step * segs + i].astype(jnp.bfloat16)


def attend(own, parents, advantages, bias, q, direction, shared, kv_list, chunk, chunks):
    segs, length = advantages.shape[:2]
    steps = len(kv_list)
    group_size = q.shape[1] // HD // chunks // segs
    width = group_size * HD
    keys = DEPTH * length
    smem = pl.BlockSpec(memory_space=pltpu.SMEM)
    vmem = pl.BlockSpec(memory_space=pltpu.VMEM)
    out_shape = (jax.ShapeDtypeStruct((length, width), jnp.bfloat16),) * segs + (
        jax.ShapeDtypeStruct((segs, 2, length, HD), jnp.bfloat16),
    ) * steps
    outs = pl.pallas_call(
        functools.partial(attend_kernel, group_size, DEPTH, chunk, chunks, segs),
        out_shape=out_shape,
        in_specs=[smem] * 2 + [vmem] * (4 + len(shared) + len(kv_list)),
        out_specs=(vmem,) * len(out_shape),
        scratch_shapes=[
            pltpu.VMEM((steps * segs, 2, length, HD), jnp.bfloat16),
            pltpu.VMEM((keys, width), jnp.bfloat16),
            pltpu.VMEM((keys, width), jnp.bfloat16),
            pltpu.VMEM((steps * segs, 2, length, HD), jnp.float32),
        ],
        compiler_params=pltpu.CompilerParams(vmem_limit_bytes=40 * 1024 * 1024),
        cost_estimate=pl.CostEstimate(
            flops=5 * 2 * keys * length * width * segs,
            bytes_accessed=8 * 1024 * 1024,
            transcendentals=keys * width * segs,
        ),
        name="tree_attention_backward",
    )(own, parents, advantages, bias, q, direction, *shared, *kv_list)
    return outs[:segs], outs[segs:]


def finish_kernel(chunks, own_ref, *refs):
    part = lax.rem(own_ref[0], 2)
    dq_refs, kv_refs = refs[: 2 * chunks], refs[2 * chunks : -3]
    dq_ref, dk_ref, dv_ref = refs[-3:]
    for side in range(2):
        where = part if side == 0 else 1 - part
        for chunk in range(chunks):
            block = dq_refs[side * chunks + chunk]
            width = block.shape[1]
            column = pl.multiple_of((where * chunks + chunk) * width, HD)
            dq_ref[:, pl.ds(column, width)] = block[...]
            columns = pl.ds(pl.multiple_of((where * chunks + chunk) * HD, HD), HD)
            block = kv_refs[side * chunks + chunk]
            dk_ref[:, columns] = block[0]
            dv_ref[:, columns] = block[1]


def finish(own, dq_list, kv_list):
    chunks = len(kv_list) // 2
    length, width = dq_list[0].shape
    smem = pl.BlockSpec(memory_space=pltpu.SMEM)
    vmem = pl.BlockSpec(memory_space=pltpu.VMEM)
    kv_out = jax.ShapeDtypeStruct((length, 2 * chunks * HD), jnp.bfloat16)
    return pl.pallas_call(
        functools.partial(finish_kernel, chunks),
        out_shape=(
            jax.ShapeDtypeStruct((length, 2 * chunks * width), jnp.bfloat16),
            kv_out,
            kv_out,
        ),
        in_specs=[smem] + [vmem] * (4 * chunks),
        out_specs=(vmem,) * 3,
        cost_estimate=pl.CostEstimate(
            flops=0, bytes_accessed=8 * length * width * chunks, transcendentals=0
        ),
        name="join_heads",
    )(own, *dq_list, *kv_list)


def permute(array, pairs):
    return lax.ppermute(array, "seg", pairs)


def after(array, *earlier):
    return lax.optimization_barrier((array, *earlier))[0]


def paired_body(own, queries, direction, key_vectors, value_vectors, token_rows, parents, lengths, log_rate):
    groups = lax.axis_size("seg")
    chunks = key_vectors.shape[1] // HD // 2
    swap = [(i, i ^ 1) for i in range(groups)]
    up = {d: [(i, i + 2 * d) for i in range(groups - 2 * d)] for d in (1, 2)}
    down = {d: [(i, i - 2 * d) for i in range(2 * d, groups)] for d in (1, 2, 3)}
    forward = [(i, i + 2) for i in range(4, groups - 2)]

    kept, given, terms = pack(own, lengths, key_vectors, value_vectors, token_rows, 2, log_rate)
    terms = terms + permute(terms, swap)
    taken = permute(given, swap)
    shares = pack_queries(own, after(queries, given), direction)
    near = jnp.concatenate([kept, taken])
    two = permute(near, up[2])
    one = permute(near, up[1])
    three = permute(two, forward)
    shared = permute(after(shares, near, terms), swap)
    for d in (1, 2):
        terms = terms + permute(terms, down[d])
    row, advantages, bias = prepare(own, parents, lengths, terms, 2, log_rate)
    blocks = [near, one, two, three]

    results = []
    for chunk in range(chunks):
        results.append(
            attend(
                own, parents, advantages, bias, queries, direction, [shared], blocks, chunk, chunks
            )
        )
    dq_own, dq_back, totals, totals_back = [], [], [], []
    for dq, dkv in results:
        arrived = [permute(dkv[d], down[d]) for d in (3, 2, 1)]
        dq_own.append(dq[0])
        dq_back.append(permute(dq[1], swap))
        near = after(dkv[0], results[-1][0][0])
        total = sum(block.astype(jnp.float32) for block in [near] + arrived).astype(jnp.bfloat16)
        totals.append(total[0])
        totals_back.append(permute(total[1], swap))
    grad_q, grad_k, grad_v = finish(own, dq_own + dq_back, totals + totals_back)
    return grad_q, grad_k, grad_v, row[0]


def fetch_rows(spread, wanted):
    routed = jnp.take(spread, jnp.maximum(wanted, 0), axis=0)
    return lax.all_to_all(routed, "seg", split_axis=0, concat_axis=2, tiled=True)


def return_rows(grad_rows, wanted, total_segs):
    returned = lax.all_to_all(grad_rows, "seg", split_axis=2, concat_axis=0, tiled=True)
    piece_len = returned.shape[2]
    feature_len = returned.shape[3]
    routed_ids = wanted.reshape(-1)
    targets = jnp.where(routed_ids >= 0, routed_ids, total_segs)
    summed = jax.ops.segment_sum(
        returned.reshape(-1, piece_len * feature_len).astype(jnp.float32),
        targets,
        num_segments=total_segs + 1,
    )[:total_segs]
    return lax.all_to_all(
        summed.reshape(total_segs, piece_len, feature_len),
        "seg",
        split_axis=0,
        concat_axis=1,
        tiled=True,
    )


def routed_body(own, queries, direction, key_vectors, value_vectors, token_rows, parents, lengths, log_rate):
    total_segs = parents.shape[0]
    length = queries.shape[0]
    block, terms = pack(own, lengths, key_vectors, value_vectors, token_rows, 1, log_rate)
    heads = block.shape[0]
    mine = lax.dynamic_slice_in_dim(terms, own[0], 1)
    terms = lax.all_gather(mine, "seg", axis=0, tiled=True)
    row, advantages, bias = prepare(own, parents, lengths, terms, 1, log_rate)
    flat = jnp.concatenate([key_vectors, value_vectors], axis=1)[None]
    spread = lax.all_to_all(flat, "seg", split_axis=1, concat_axis=0, tiled=True)
    chains = ancestors(parents, DEPTH - 1)
    arrived = fetch_rows(spread, chains)[0]
    slot_kv = jnp.concatenate([flat, arrived]).reshape(DEPTH, length, 2, heads, HD)
    slot_kv = jnp.transpose(slot_kv, (0, 3, 2, 1, 4))
    kv_list = [slot_kv[slot] for slot in range(DEPTH)]
    dq_list, dkv_list = [], []
    for head in range(heads):
        dq, dkv = attend(
            own, parents, advantages, bias, queries, direction, [], kv_list, head, heads
        )
        dq_list.append(dq[0])
        dkv_list.append(jnp.concatenate(dkv))
    rows = jnp.transpose(jnp.stack(dkv_list), (1, 3, 2, 0, 4)).reshape(1, DEPTH, length, -1)
    summed = return_rows(rows[:, 1:], chains, total_segs)[0] + rows[0, 0].astype(jnp.float32)
    width = key_vectors.shape[1]
    grad_keys = summed[:, :width].astype(jnp.bfloat16)
    grad_values = summed[:, width:].astype(jnp.bfloat16)
    return jnp.concatenate(dq_list, axis=1), grad_keys, grad_values, row[0]


def body(
    queries,
    key_vectors,
    value_vectors,
    direction,
    rewards,
    logprobs,
    ref_logprobs,
    value_est,
    parents,
    seg_lengths,
):
    groups = lax.axis_size("seg")
    assert parents.shape[0] == groups
    own = jnp.reshape(lax.axis_index("seg"), (1,))
    log_rate = math.log(LAMBDA_SEG) / rewards.shape[0]
    token_rows = [rewards[None], logprobs[None], ref_logprobs[None], value_est[None]]
    plan = paired_body if groups == PAIRED_GROUPS else routed_body
    return plan(
        own, queries, direction, key_vectors, value_vectors, token_rows, parents, seg_lengths, log_rate
    )


def solution(mesh):
    in_specs = (
        P(("grp", "seg"), "tp"),
        P(("grp", "seg"), "tp"),
        P(("grp", "seg"), "tp"),
        P(("grp", "seg"), "tp"),
        P(("grp", "seg")),
        P(("grp", "seg")),
        P(("grp", "seg")),
        P(("grp", "seg")),
        P("grp"),
        P("grp"),
    )
    out_specs = (
        P(("grp", "seg"), "tp"),
        P(("grp", "seg"), "tp"),
        P(("grp", "seg"), "tp"),
        P(("grp", "seg")),
    )
    return jax.shard_map(body, mesh=mesh, in_specs=in_specs, out_specs=out_specs, check_vma=False)
```

```python
import functools
import math

import jax
import jax.numpy as jnp
from jax import lax
from jax.experimental import pallas as pl
from jax.experimental.pallas import tpu as pltpu
from jax.sharding import PartitionSpec as P

HD = 128
DEPTH = 5
BETA = 0.1
LAMBDA_SEG = 0.7
PAIRED_GROUPS = 8
LOG2E = math.log2(math.e)


def lookup(table_values, lookup_ids):
    matches = lookup_ids[..., None] == jnp.arange(table_values.shape[0], dtype=jnp.int32)
    return jnp.sum(jnp.where(matches, table_values, 0), axis=-1)


def ancestors(parents, count):
    current = jnp.arange(parents.shape[0], dtype=jnp.int32)
    chain_list = []
    for depth_step in range(count):
        parent_ids = lookup(parents, current)
        current = jnp.where(current >= 0, parent_ids, -1)
        chain_list.append(current)
    return jnp.stack(chain_list, axis=1)


def token_terms(log_rate, own_len, rewards, logprobs, ref_logprobs, values):
    positions = lax.broadcasted_iota(jnp.int32, rewards.shape, 1)
    later = jnp.concatenate([values[:, 1:], values[:, :1]], axis=1)
    later = jnp.where(positions + 1 < own_len, later, 0.0)
    deltas = jnp.where(
        positions < own_len, rewards - BETA * (logprobs - ref_logprobs) + later - values, 0.0
    )
    powers = jnp.exp(positions.astype(jnp.float32) * log_rate)
    first_local = jnp.sum(deltas * powers, axis=1, keepdims=True)
    firsts = jnp.where(positions == 0, first_local, jnp.where(positions == 1, values[:, :1], 0.0))
    return deltas, firsts


def pack_kernel(
    log_rate,
    parts,
    own_ref,
    lengths_ref,
    k_ref,
    v_ref,
    rewards_ref,
    logprobs_ref,
    ref_logprobs_ref,
    values_ref,
    *out_refs,
):
    terms_ref = out_refs[-1]
    own = own_ref[0]
    heads = k_ref.shape[1] // HD // parts
    for step, out_ref in enumerate(out_refs[:-1]):
        part = lax.rem(own + step, parts)
        for h in range(heads):
            columns = pl.ds(pl.multiple_of((part * heads + h) * HD, HD), HD)
            out_ref[h, 0] = k_ref[:, columns]
            out_ref[h, 1] = v_ref[:, columns]
    length = k_ref.shape[0]
    deltas, firsts = token_terms(
        log_rate,
        lengths_ref[own],
        rewards_ref[...],
        logprobs_ref[...],
        ref_logprobs_ref[...],
        values_ref[...],
    )
    mine = lax.broadcasted_iota(jnp.int32, (terms_ref.shape[0], length), 0) == own
    terms_ref[:, :length] = jnp.where(mine, deltas, 0.0)
    terms_ref[:, length:] = jnp.where(mine, firsts, 0.0)


def pack(own, lengths, k, v, token_rows, parts, log_rate):
    length, width = k.shape
    smem = pl.BlockSpec(memory_space=pltpu.SMEM)
    vmem = pl.BlockSpec(memory_space=pltpu.VMEM)
    heads = width // HD // parts
    block = jax.ShapeDtypeStruct((heads, 2, length, HD), k.dtype)
    terms = jax.ShapeDtypeStruct((lengths.shape[0], 2 * length), jnp.float32)
    return pl.pallas_call(
        functools.partial(pack_kernel, log_rate, parts),
        out_shape=(block,) * parts + (terms,),
        in_specs=[smem] * 2 + [vmem] * 6,
        out_specs=(vmem,) * (parts + 1),
        cost_estimate=pl.CostEstimate(
            flops=length * 100, bytes_accessed=8 * length * width, transcendentals=length
        ),
        name="pack_keys_values",
    )(own, lengths, k, v, *token_rows)


def pack_queries_kernel(parts, own_ref, q_ref, dir_ref, *out_refs):
    own = own_ref[0]
    chunks = len(out_refs) // parts
    heads = out_refs[0].shape[1]
    for step in range(parts):
        part = lax.rem(own + step, parts)
        for chunk in range(chunks):
            out_ref = out_refs[step * chunks + chunk]
            for h in range(heads):
                column = (part * chunks + chunk) * heads + h
                columns = pl.ds(pl.multiple_of(column * HD, HD), HD)
                out_ref[0, h] = q_ref[:, columns]
                out_ref[1, h] = dir_ref[:, columns]


def pack_queries(own, q, direction, parts, chunks):
    length, width = q.shape
    smem = pl.BlockSpec(memory_space=pltpu.SMEM)
    vmem = pl.BlockSpec(memory_space=pltpu.VMEM)
    block = jax.ShapeDtypeStruct((2, width // HD // parts // chunks, length, HD), q.dtype)
    outs = pl.pallas_call(
        functools.partial(pack_queries_kernel, parts),
        out_shape=(block,) * (parts * chunks),
        in_specs=[smem, vmem, vmem],
        out_specs=(vmem,) * (parts * chunks),
        cost_estimate=pl.CostEstimate(flops=0, bytes_accessed=8 * length * width, transcendentals=0),
        name="pack_queries",
    )(own, q, direction)
    return [outs[step * chunks : (step + 1) * chunks] for step in range(parts)]


def join_blocks_kernel(mine_ref, other_ref, *out_refs):
    for chunk, out_ref in enumerate(out_refs):
        out_ref[0] = mine_ref[chunk]
        out_ref[1] = other_ref[chunk]


def join_blocks(mine, other):
    chunks = mine.shape[0]
    vmem = pl.BlockSpec(memory_space=pltpu.VMEM)
    return pl.pallas_call(
        join_blocks_kernel,
        out_shape=(jax.ShapeDtypeStruct((2,) + mine.shape[1:], mine.dtype),) * chunks,
        in_specs=[vmem] * 2,
        out_specs=(vmem,) * chunks,
        cost_estimate=pl.CostEstimate(flops=0, bytes_accessed=8 * mine.size, transcendentals=0),
        name="join_blocks",
    )(mine, other)


def prepare_kernel(
    log_rate,
    depth,
    segs,
    own_ref,
    parents_s,
    lengths_s,
    parents_ref,
    lengths_ref,
    near_ref,
    far_ref,
    row_ref,
    adv_ref,
    bias_ref,
):
    length = row_ref.shape[1]
    count = parents_s.shape[0]
    terms = near_ref[...] + far_ref[...]
    own = own_ref[0]
    part = lax.rem(own, segs)

    row_id = lax.broadcasted_iota(jnp.int32, (count, count), 0)
    col_id = lax.broadcasted_iota(jnp.int32, (count, count), 1)
    eye = row_id == col_id

    def to_row(col):
        return jnp.sum(jnp.where(eye, col, 0.0), axis=0, keepdims=True)

    children = (parents_ref[...] == row_id).astype(jnp.float32)
    weights = children / jnp.maximum(jnp.sum(children, axis=1, keepdims=True), 1.0)
    lens_col = jnp.sum(
        jnp.where(eye, lengths_ref[...].astype(jnp.float32), 0.0), axis=1, keepdims=True
    )
    first_local = terms[:, length : length + 1]
    first_value = terms[:, length + 1 : length + 2]
    later_value = jnp.sum(weights * to_row(first_value), axis=1, keepdims=True)
    base_term = first_local + jnp.exp((lens_col - 1.0) * log_rate) * later_value
    factor = jnp.exp(lens_col * log_rate)
    head = base_term
    for _ in range(depth):
        head = base_term + factor * jnp.sum(weights * to_row(head), axis=1, keepdims=True)
    later_head = jnp.sum(weights * to_row(head), axis=1, keepdims=True)

    t_id = lax.broadcasted_iota(jnp.int32, (length, length), 0)
    j_id = lax.broadcasted_iota(jnp.int32, (length, length), 1)
    offset = (j_id - t_id).astype(jnp.float32)
    discount = jnp.where(offset >= 0, jnp.exp(offset * log_rate), 0.0)
    t_col = lax.broadcasted_iota(jnp.int32, (length, 1), 0)
    seg_col = lax.broadcasted_iota(jnp.int32, (count, 1), 0)
    for i in range(segs):
        seg = own - part + lax.rem(part + i, segs)
        seg_len = lengths_s[seg]
        mine = seg_col == seg
        my_value = jnp.sum(jnp.where(mine, later_value, 0.0), axis=0, keepdims=True)
        my_head = jnp.sum(jnp.where(mine, later_head, 0.0), axis=0, keepdims=True)
        deltas = jnp.sum(jnp.where(mine, terms[:, :length], 0.0), axis=0, keepdims=True)
        local_sum = jnp.sum(discount * deltas, axis=1, keepdims=True)
        left = (seg_len - t_col).astype(jnp.float32)
        advantage = jnp.where(
            t_col < seg_len,
            local_sum
            + jnp.exp((left - 1.0) * log_rate) * my_value
            + jnp.exp(left * log_rate) * my_head,
            0.0,
        )
        if i == 0:
            row_ref[...] = jnp.sum(jnp.where(t_id == j_id, advantage, 0.0), axis=0, keepdims=True)
        adv_ref[i] = jnp.broadcast_to(advantage, (length, HD))

        ancestor = seg
        for slot in range(depth):
            if slot > 0:
                ancestor = parent_of(ancestor, parents_s)
            slot_len = jnp.where(ancestor >= 0, lengths_s[jnp.maximum(ancestor, 0)], 0)
            seen = t_id < slot_len
            if slot == 0:
                seen = jnp.logical_and(seen, t_id <= j_id)
            bias_ref[i, slot * length : (slot + 1) * length, :] = jnp.where(seen, 0.0, -1e30)


def parent_of(segment, parents_s):
    known = parents_s[jnp.maximum(segment, 0)]
    return jnp.where(segment >= 0, known, -1).astype(jnp.int32)


def prepare(own, parents, lengths, near, far, segs, log_rate):
    length = near.shape[1] // 2
    smem = pl.BlockSpec(memory_space=pltpu.SMEM)
    vmem = pl.BlockSpec(memory_space=pltpu.VMEM)
    return pl.pallas_call(
        functools.partial(prepare_kernel, log_rate, DEPTH, segs),
        out_shape=(
            jax.ShapeDtypeStruct((1, length), jnp.float32),
            jax.ShapeDtypeStruct((segs, length, HD), jnp.float32),
            jax.ShapeDtypeStruct((segs, DEPTH * length, length), jnp.float32),
        ),
        in_specs=[smem] * 3 + [vmem] * 4,
        out_specs=(vmem,) * 3,
        cost_estimate=pl.CostEstimate(
            flops=200 * length * length,
            bytes_accessed=4 * (DEPTH + 1) * segs * length * length,
            transcendentals=length * length,
        ),
        name="prepare_advantages",
    )(own, parents, lengths, parents[None], lengths[None], near, far)


def attend_kernel(depth, segs, *refs):
    own_ref, parents_s, adv_ref, bias_ref = refs[:4]
    query_refs = refs[4 : 4 + segs]
    refs = refs[4 + segs :]
    steps = (len(refs) - segs - 4) // 2
    kv_refs, dq_refs, dkv_refs = refs[:steps], refs[steps : steps + segs], refs[steps + segs : -4]
    kv_scr, p_scr, ds_scr, acc_scr = refs[-4:]

    group_size, length = query_refs[0].shape[1:3]
    own = own_ref[0]
    part = lax.rem(own, segs)
    for step in range(steps):
        for i in range(segs):
            kv_scr[step * segs + i] = kv_refs[step][i]
    acc_scr[...] = jnp.zeros_like(acc_scr)

    scale = HD**-0.5
    contract_last = (((1,), (1,)), ((), ()))
    contract_first = (((0,), (0,)), ((), ()))
    for i in range(segs):
        ancestor = own - part + lax.rem(part + i, segs)
        chosen = []
        for slot in range(depth):
            if slot > 0:
                ancestor = parent_of(ancestor, parents_s)
            if segs == 1:
                chosen.append(slot)
            else:
                known = jnp.maximum(ancestor, 0)
                step = (own - part) // segs - known // segs
                turn = lax.rem(lax.rem(known, segs) - part + segs, segs)
                chosen.append(jnp.where(ancestor >= 0, step * segs + turn, 0))
        q_list = [query_refs[i][0, j] for j in range(group_size)]
        dir_list = [query_refs[i][1, j] for j in range(group_size)]
        do_list = [(adv_ref[i] * d.astype(jnp.float32)).astype(jnp.bfloat16) for d in dir_list]
        k_all = jnp.concatenate([kv_scr[s, 0] for s in chosen], axis=0)
        v_all = jnp.concatenate([kv_scr[s, 1] for s in chosen], axis=0)
        for j in range(group_size):
            columns = slice(j * length, (j + 1) * length)
            scores = lax.dot_general(
                k_all, q_list[j], contract_last, preferred_element_type=jnp.float32
            )
            scores = scores * (scale * LOG2E) + bias_ref[i]
            top = jnp.max(scores, axis=0, keepdims=True)
            unnorm = jnp.exp2(scores - top)
            prob = unnorm * (1.0 / jnp.sum(unnorm, axis=0, keepdims=True))
            prob_low = prob.astype(jnp.bfloat16)
            dprob = lax.dot_general(
                v_all, do_list[j], contract_last, preferred_element_type=jnp.float32
            )
            row_dot = jnp.sum(prob_low.astype(jnp.float32) * dprob, axis=0, keepdims=True)
            dscore = (prob * (dprob - row_dot)).astype(jnp.bfloat16)
            p_scr[:, columns] = prob_low
            ds_scr[:, columns] = dscore
        dscore_all = ds_scr[...]
        dq_t = lax.dot_general(
            k_all, dscore_all, contract_first, preferred_element_type=jnp.float32
        )
        for j in range(group_size):
            dq_refs[i][:, j * HD : (j + 1) * HD] = (
                jnp.transpose(dq_t[:, j * length : (j + 1) * length]) * scale
            ).astype(jnp.bfloat16)
        q_all = jnp.concatenate(q_list, axis=0)
        do_all = jnp.concatenate(do_list, axis=0)
        dk_all = jnp.dot(dscore_all, q_all, preferred_element_type=jnp.float32) * scale
        dv_all = jnp.dot(p_scr[...], do_all, preferred_element_type=jnp.float32)
        for slot, s in enumerate(chosen):
            rows = slice(slot * length, (slot + 1) * length)
            acc_scr[s, 0] += dk_all[rows]
            acc_scr[s, 1] += dv_all[rows]
    for step in range(steps):
        for i in range(segs):
            dkv_refs[step][i] = acc_scr[step * segs + i].astype(jnp.bfloat16)


def attend(own, parents, advantages, bias, query_list, kv_list):
    segs, length = advantages.shape[:2]
    steps = len(kv_list)
    width = query_list[0].shape[1] * HD
    keys = DEPTH * length
    smem = pl.BlockSpec(memory_space=pltpu.SMEM)
    vmem = pl.BlockSpec(memory_space=pltpu.VMEM)
    out_shape = (jax.ShapeDtypeStruct((length, width), jnp.bfloat16),) * segs + (
        jax.ShapeDtypeStruct((segs, 2, length, HD), jnp.bfloat16),
    ) * steps
    outs = pl.pallas_call(
        functools.partial(attend_kernel, DEPTH, segs),
        out_shape=out_shape,
        in_specs=[smem] * 2 + [vmem] * (2 + segs + steps),
        out_specs=(vmem,) * len(out_shape),
        scratch_shapes=[
            pltpu.VMEM((steps * segs, 2, length, HD), jnp.bfloat16),
            pltpu.VMEM((keys, width), jnp.bfloat16),
            pltpu.VMEM((keys, width), jnp.bfloat16),
            pltpu.VMEM((steps * segs, 2, length, HD), jnp.float32),
        ],
        compiler_params=pltpu.CompilerParams(vmem_limit_bytes=40 * 1024 * 1024),
        cost_estimate=pl.CostEstimate(
            flops=5 * 2 * keys * length * width * segs,
            bytes_accessed=8 * 1024 * 1024,
            transcendentals=keys * width * segs,
        ),
        name="tree_attention_backward",
    )(own, parents, advantages, bias, *query_list, *kv_list)
    return outs[:segs], outs[segs:]


def join_queries_kernel(chunks, own_ref, *refs):
    part = lax.rem(own_ref[0], 2)
    dq_ref = refs[-1]
    for side in range(2):
        where = part if side == 0 else 1 - part
        for chunk in range(chunks):
            block = refs[side * chunks + chunk]
            width = block.shape[1]
            column = pl.multiple_of((where * chunks + chunk) * width, HD)
            dq_ref[:, pl.ds(column, width)] = block[...]


def join_queries(own, dq_list):
    length, width = dq_list[0].shape
    smem = pl.BlockSpec(memory_space=pltpu.SMEM)
    vmem = pl.BlockSpec(memory_space=pltpu.VMEM)
    return pl.pallas_call(
        functools.partial(join_queries_kernel, len(dq_list) // 2),
        out_shape=jax.ShapeDtypeStruct((length, len(dq_list) * width), jnp.bfloat16),
        in_specs=[smem] + [vmem] * len(dq_list),
        out_specs=vmem,
        cost_estimate=pl.CostEstimate(
            flops=0, bytes_accessed=4 * length * width * len(dq_list), transcendentals=0
        ),
        name="join_queries",
    )(own, *dq_list)


def join_keys_kernel(chunks, own_ref, *refs):
    part = lax.rem(own_ref[0], 2)
    other_refs, sum_refs = refs[:chunks], refs[chunks:-2]
    many = len(sum_refs) // chunks
    dk_ref, dv_ref = refs[-2:]
    for chunk in range(chunks):
        here = pl.ds(pl.multiple_of((part * chunks + chunk) * HD, HD), HD)
        there = pl.ds(pl.multiple_of(((1 - part) * chunks + chunk) * HD, HD), HD)
        for plane, out_ref in enumerate((dk_ref, dv_ref)):
            blocks = [ref[0, plane] for ref in sum_refs[chunk * many : (chunk + 1) * many]]
            total = sum(block.astype(jnp.float32) for block in blocks)
            out_ref[:, here] = total.astype(jnp.bfloat16)
            out_ref[:, there] = other_refs[chunk][plane]


def join_keys(own, others, summands):
    chunks = len(others)
    length = others[0].shape[1]
    smem = pl.BlockSpec(memory_space=pltpu.SMEM)
    vmem = pl.BlockSpec(memory_space=pltpu.VMEM)
    flat = [block for blocks in summands for block in blocks]
    out = jax.ShapeDtypeStruct((length, 2 * chunks * HD), jnp.bfloat16)
    return pl.pallas_call(
        functools.partial(join_keys_kernel, chunks),
        out_shape=(out, out),
        in_specs=[smem] + [vmem] * (chunks + len(flat)),
        out_specs=(vmem, vmem),
        cost_estimate=pl.CostEstimate(
            flops=0, bytes_accessed=16 * length * HD * chunks, transcendentals=0
        ),
        name="join_keys",
    )(own, *others, *flat)


def permute(array, pairs):
    return lax.ppermute(array, "seg", pairs)


def after(array, *earlier):
    return lax.optimization_barrier((array, *earlier))[0]


def paired_body(own, queries, direction, key_vectors, value_vectors, token_rows, parents, lengths, log_rate):
    groups = lax.axis_size("seg")
    chunks = key_vectors.shape[1] // HD // 2
    swap = [(i, i ^ 1) for i in range(groups)]
    up = {d: [(i, i + 2 * d) for i in range(groups - 2 * d)] for d in (1, 2, 3)}
    down = {d: [(i, i - 2 * d) for i in range(2 * d, groups)] for d in (1, 2, 3)}
    forward = [(i, i + 2) for i in range(4, groups - 2)]

    kept, given, terms = pack(own, lengths, key_vectors, value_vectors, token_rows, 2, log_rate)
    terms = terms + permute(terms, swap)
    taken = permute(given, swap)
    kept_q, given_q = pack_queries(own, after(queries, given), direction, 2, chunks)
    terms = terms + permute(terms, down[1])
    near = join_blocks(kept, after(taken, terms))
    blocks = [[near[0]] + [permute(near[0], up[d]) for d in (3, 2, 1)][::-1]]
    taken_q = [permute(after(given_q[0], near[0]), swap)]
    row, advantages, bias = prepare(
        own, parents, lengths, terms, permute(terms, down[2]), 2, log_rate
    )
    blocks[0][1:] = lax.optimization_barrier((*blocks[0][1:], bias))[:-1]
    for chunk in range(1, chunks):
        taken_q.append(permute(after(given_q[chunk], taken_q[-1], bias), swap))

    dq_own, dq_back, dkv_list = [], [], []
    for chunk in range(chunks):
        gate = blocks[chunk]
        dq, dkv = attend(own, parents, advantages, bias, [kept_q[chunk], taken_q[chunk]], gate)
        dq_own.append(dq[0])
        dq_back.append(dq[1])
        dkv_list.append(dkv)
        if chunk + 1 < chunks:
            block = near[chunk + 1]
            two = permute(after(block, *gate[1:]), up[2])
            one = permute(after(block, dq[0]), up[1])
            three = permute(after(two, dq[0]), forward)
            blocks.append([block, one, two, three])

    last = dq_own[-1]
    summands = []
    for dkv in dkv_list:
        arrived = [permute(dkv[d], down[d]) for d in (3, 2, 1)]
        summands.append([after(dkv[0], last)] + arrived)
    dq_back = [permute(block, swap) for block in dq_back]
    others = []
    for blocks in summands:
        total = sum(block[1].astype(jnp.float32) for block in blocks)
        others.append(permute(total.astype(jnp.bfloat16), swap))
    grad_q = join_queries(own, dq_own + dq_back)
    grad_k, grad_v = join_keys(own, others, summands)
    return grad_q, grad_k, grad_v, row[0]


def fetch_rows(spread, wanted):
    routed = jnp.take(spread, jnp.maximum(wanted, 0), axis=0)
    return lax.all_to_all(routed, "seg", split_axis=0, concat_axis=2, tiled=True)


def return_rows(grad_rows, wanted, total_segs):
    returned = lax.all_to_all(grad_rows, "seg", split_axis=2, concat_axis=0, tiled=True)
    piece_len = returned.shape[2]
    feature_len = returned.shape[3]
    routed_ids = wanted.reshape(-1)
    targets = jnp.where(routed_ids >= 0, routed_ids, total_segs)
    summed = jax.ops.segment_sum(
        returned.reshape(-1, piece_len * feature_len).astype(jnp.float32),
        targets,
        num_segments=total_segs + 1,
    )[:total_segs]
    return lax.all_to_all(
        summed.reshape(total_segs, piece_len, feature_len),
        "seg",
        split_axis=0,
        concat_axis=1,
        tiled=True,
    )


def routed_body(own, queries, direction, key_vectors, value_vectors, token_rows, parents, lengths, log_rate):
    total_segs = parents.shape[0]
    length = queries.shape[0]
    block, terms = pack(own, lengths, key_vectors, value_vectors, token_rows, 1, log_rate)
    heads = block.shape[0]
    mine = lax.dynamic_slice_in_dim(terms, own[0], 1)
    terms = lax.all_gather(mine, "seg", axis=0, tiled=True)
    row, advantages, bias = prepare(
        own, parents, lengths, terms, jnp.zeros_like(terms), 1, log_rate
    )
    flat = jnp.concatenate([key_vectors, value_vectors], axis=1)[None]
    spread = lax.all_to_all(flat, "seg", split_axis=1, concat_axis=0, tiled=True)
    chains = ancestors(parents, DEPTH - 1)
    arrived = fetch_rows(spread, chains)[0]
    slot_kv = jnp.concatenate([flat, arrived]).reshape(DEPTH, length, 2, heads, HD)
    slot_kv = jnp.transpose(slot_kv, (0, 3, 2, 1, 4))
    (kept_q,) = pack_queries(own, queries, direction, 1, heads)
    dq_list, dkv_list = [], []
    for head in range(heads):
        kv_list = [slot_kv[slot : slot + 1, head] for slot in range(DEPTH)]
        dq, dkv = attend(own, parents, advantages, bias, [kept_q[head]], kv_list)
        dq_list.append(dq[0])
        dkv_list.append(jnp.concatenate(dkv))
    rows = jnp.transpose(jnp.stack(dkv_list), (1, 3, 2, 0, 4)).reshape(1, DEPTH, length, -1)
    summed = return_rows(rows[:, 1:], chains, total_segs)[0] + rows[0, 0].astype(jnp.float32)
    width = key_vectors.shape[1]
    grad_keys = summed[:, :width].astype(jnp.bfloat16)
    grad_values = summed[:, width:].astype(jnp.bfloat16)
    return jnp.concatenate(dq_list, axis=1), grad_keys, grad_values, row[0]


def body(
    queries,
    key_vectors,
    value_vectors,
    direction,
    rewards,
    logprobs,
    ref_logprobs,
    value_est,
    parents,
    seg_lengths,
):
    groups = lax.axis_size("seg")
    assert parents.shape[0] == groups
    own = jnp.reshape(lax.axis_index("seg"), (1,))
    log_rate = math.log(LAMBDA_SEG) / rewards.shape[0]
    token_rows = [rewards[None], logprobs[None], ref_logprobs[None], value_est[None]]
    plan = paired_body if groups == PAIRED_GROUPS else routed_body
    return plan(
        own, queries, direction, key_vectors, value_vectors, token_rows, parents, seg_lengths, log_rate
    )


def solution(mesh):
    in_specs = (
        P(("grp", "seg"), "tp"),
        P(("grp", "seg"), "tp"),
        P(("grp", "seg"), "tp"),
        P(("grp", "seg"), "tp"),
        P(("grp", "seg")),
        P(("grp", "seg")),
        P(("grp", "seg")),
        P(("grp", "seg")),
        P("grp"),
        P("grp"),
    )
    out_specs = (
        P(("grp", "seg"), "tp"),
        P(("grp", "seg"), "tp"),
        P(("grp", "seg"), "tp"),
        P(("grp", "seg")),
    )
    return jax.shard_map(body, mesh=mesh, in_specs=in_specs, out_specs=out_specs, check_vma=False)
```

```python
import functools
import math

import jax
import jax.numpy as jnp
from jax import lax
from jax.experimental import pallas as pl
from jax.experimental.pallas import tpu as pltpu
from jax.sharding import PartitionSpec as P

HD = 128
DEPTH = 5
BETA = 0.1
LAMBDA_SEG = 0.7
PAIRED_GROUPS = 8
TERM_ROWS = 16
LOG2E = math.log2(math.e)
SMALL = pltpu.CompilerParams(vmem_limit_bytes=8 * 1024 * 1024)


def lookup(table_values, lookup_ids):
    matches = lookup_ids[..., None] == jnp.arange(table_values.shape[0], dtype=jnp.int32)
    return jnp.sum(jnp.where(matches, table_values, 0), axis=-1)


def ancestors(parents, count):
    current = jnp.arange(parents.shape[0], dtype=jnp.int32)
    chain_list = []
    for depth_step in range(count):
        parent_ids = lookup(parents, current)
        current = jnp.where(current >= 0, parent_ids, -1)
        chain_list.append(current)
    return jnp.stack(chain_list, axis=1)


def token_terms(log_rate, own_len, rewards, logprobs, ref_logprobs, values):
    positions = lax.broadcasted_iota(jnp.int32, rewards.shape, 1)
    later = jnp.concatenate([values[:, 1:], values[:, :1]], axis=1)
    later = jnp.where(positions + 1 < own_len, later, 0.0)
    deltas = jnp.where(
        positions < own_len, rewards - BETA * (logprobs - ref_logprobs) + later - values, 0.0
    )
    powers = jnp.exp(positions.astype(jnp.float32) * log_rate)
    first_local = jnp.sum(deltas * powers, axis=1, keepdims=True)
    firsts = jnp.where(positions == 0, first_local, jnp.where(positions == 1, values[:, :1], 0.0))
    return deltas, firsts


def split_float(value):
    parts = []
    for _ in range(3):
        part = value.astype(jnp.bfloat16)
        parts.append(part)
        value = value - part.astype(jnp.float32)
    return parts


def pack_kernel(
    log_rate,
    own_ref,
    lengths_ref,
    k_ref,
    v_ref,
    rewards_ref,
    logprobs_ref,
    ref_logprobs_ref,
    values_ref,
    kept_ref,
    terms_ref,
    given_ref=None,
):
    own = own_ref[0]
    length = k_ref.shape[0]
    heads = kept_ref.shape[0]
    parts = k_ref.shape[1] // HD // heads
    deltas, firsts = token_terms(
        log_rate,
        lengths_ref[own],
        rewards_ref[...],
        logprobs_ref[...],
        ref_logprobs_ref[...],
        values_ref[...],
    )
    mine = lax.broadcasted_iota(jnp.int32, (terms_ref.shape[0], length), 0) == own
    terms_ref[:, :length] = jnp.where(mine, deltas, 0.0)
    terms_ref[:, length:] = jnp.where(mine, firsts, 0.0)
    for step in range(parts):
        part = lax.rem(own + step, parts)
        for h in range(heads):
            columns = pl.ds(pl.multiple_of((part * heads + h) * HD, HD), HD)
            for plane, ref in enumerate((k_ref, v_ref)):
                if step == 0:
                    kept_ref[h, plane] = ref[:, columns]
                else:
                    first = (h * 2 + plane) * length
                    given_ref[first : first + length, :] = ref[:, columns]
    if parts == 2:
        first = 2 * heads * length
        rows = [part.astype(jnp.float32) for x in (deltas, firsts) for part in split_float(x)]
        rows.append(jnp.zeros((TERM_ROWS - len(rows), HD), jnp.float32))
        given_ref[first : first + TERM_ROWS, :] = jnp.concatenate(rows).astype(jnp.bfloat16)


def pack(own, lengths, k, v, token_rows, parts, log_rate):
    length, width = k.shape
    smem = pl.BlockSpec(memory_space=pltpu.SMEM)
    vmem = pl.BlockSpec(memory_space=pltpu.VMEM)
    heads = width // HD // parts
    out_shape = [
        jax.ShapeDtypeStruct((heads, 2, length, HD), k.dtype),
        jax.ShapeDtypeStruct((lengths.shape[0], 2 * length), jnp.float32),
    ]
    if parts == 2:
        assert length == HD
        out_shape.append(jax.ShapeDtypeStruct((2 * heads * length + TERM_ROWS, HD), k.dtype))
    return pl.pallas_call(
        functools.partial(pack_kernel, log_rate),
        out_shape=out_shape,
        in_specs=[smem] * 2 + [vmem] * 6,
        out_specs=[vmem] * len(out_shape),
        cost_estimate=pl.CostEstimate(
            flops=length * 100, bytes_accessed=8 * length * width, transcendentals=length
        ),
        compiler_params=SMALL,
        name="pack_keys_values",
    )(own, lengths, k, v, *token_rows)


def pack_queries_kernel(parts, own_ref, q_ref, dir_ref, *out_refs):
    own = own_ref[0]
    chunks = len(out_refs) // parts
    heads = out_refs[0].shape[1]
    for step in range(parts):
        part = lax.rem(own + step, parts)
        for chunk in range(chunks):
            out_ref = out_refs[step * chunks + chunk]
            for h in range(heads):
                column = (part * chunks + chunk) * heads + h
                columns = pl.ds(pl.multiple_of(column * HD, HD), HD)
                out_ref[0, h] = q_ref[:, columns]
                out_ref[1, h] = dir_ref[:, columns]


def pack_queries(own, q, direction, parts, chunks):
    length, width = q.shape
    smem = pl.BlockSpec(memory_space=pltpu.SMEM)
    vmem = pl.BlockSpec(memory_space=pltpu.VMEM)
    block = jax.ShapeDtypeStruct((2, width // HD // parts // chunks, length, HD), q.dtype)
    outs = pl.pallas_call(
        functools.partial(pack_queries_kernel, parts),
        out_shape=(block,) * (parts * chunks),
        in_specs=[smem, vmem, vmem],
        out_specs=(vmem,) * (parts * chunks),
        cost_estimate=pl.CostEstimate(flops=0, bytes_accessed=8 * length * width, transcendentals=0),
        compiler_params=SMALL,
        name="pack_queries",
    )(own, q, direction)
    return [outs[step * chunks : (step + 1) * chunks] for step in range(parts)]


def join_blocks_kernel(own_ref, terms_ref, mine_ref, other_ref, all_terms_ref, *out_refs):
    heads, _, length, _ = mine_ref.shape
    for h, out_ref in enumerate(out_refs):
        out_ref[0] = mine_ref[h]
        for plane in range(2):
            first = (h * 2 + plane) * length
            out_ref[1, plane] = other_ref[first : first + length, :]
    tail = other_ref[2 * heads * length :, :].astype(jnp.float32)
    own = own_ref[0]
    other = own + 1 - 2 * lax.rem(own, 2)
    mine = lax.broadcasted_iota(jnp.int32, (terms_ref.shape[0], length), 0) == other
    for i in range(2):
        columns = slice(i * length, (i + 1) * length)
        row = tail[3 * i : 3 * i + 1] + tail[3 * i + 1 : 3 * i + 2] + tail[3 * i + 2 : 3 * i + 3]
        all_terms_ref[:, columns] = terms_ref[:, columns] + jnp.where(mine, row, 0.0)


def join_blocks(own, terms, mine, other):
    chunks = mine.shape[0]
    smem = pl.BlockSpec(memory_space=pltpu.SMEM)
    vmem = pl.BlockSpec(memory_space=pltpu.VMEM)
    block = jax.ShapeDtypeStruct((2,) + mine.shape[1:], mine.dtype)
    outs = pl.pallas_call(
        join_blocks_kernel,
        out_shape=(jax.ShapeDtypeStruct(terms.shape, terms.dtype),) + (block,) * chunks,
        in_specs=[smem] + [vmem] * 3,
        out_specs=(vmem,) * (chunks + 1),
        cost_estimate=pl.CostEstimate(flops=0, bytes_accessed=8 * mine.size, transcendentals=0),
        compiler_params=SMALL,
        name="join_blocks",
    )(own, terms, mine, other)
    return outs[0], outs[1:]


def prepare_kernel(
    log_rate,
    depth,
    segs,
    own_ref,
    parents_s,
    lengths_s,
    parents_ref,
    lengths_ref,
    near_ref,
    far_ref,
    row_ref,
    adv_ref,
    bias_ref,
):
    length = row_ref.shape[1]
    count = parents_s.shape[0]
    terms = near_ref[...] + far_ref[...]
    own = own_ref[0]
    part = lax.rem(own, segs)

    row_id = lax.broadcasted_iota(jnp.int32, (count, count), 0)
    col_id = lax.broadcasted_iota(jnp.int32, (count, count), 1)
    eye = row_id == col_id

    def to_row(col):
        return jnp.sum(jnp.where(eye, col, 0.0), axis=0, keepdims=True)

    children = (parents_ref[...] == row_id).astype(jnp.float32)
    weights = children / jnp.maximum(jnp.sum(children, axis=1, keepdims=True), 1.0)
    lens_col = jnp.sum(
        jnp.where(eye, lengths_ref[...].astype(jnp.float32), 0.0), axis=1, keepdims=True
    )
    first_local = terms[:, length : length + 1]
    first_value = terms[:, length + 1 : length + 2]
    later_value = jnp.sum(weights * to_row(first_value), axis=1, keepdims=True)
    base_term = first_local + jnp.exp((lens_col - 1.0) * log_rate) * later_value
    factor = jnp.exp(lens_col * log_rate)
    head = base_term
    for _ in range(depth):
        head = base_term + factor * jnp.sum(weights * to_row(head), axis=1, keepdims=True)
    later_head = jnp.sum(weights * to_row(head), axis=1, keepdims=True)

    t_id = lax.broadcasted_iota(jnp.int32, (length, length), 0)
    j_id = lax.broadcasted_iota(jnp.int32, (length, length), 1)
    offset = (j_id - t_id).astype(jnp.float32)
    discount = jnp.where(offset >= 0, jnp.exp(offset * log_rate), 0.0)
    t_col = lax.broadcasted_iota(jnp.int32, (length, 1), 0)
    seg_col = lax.broadcasted_iota(jnp.int32, (count, 1), 0)
    for i in range(segs):
        seg = own - part + lax.rem(part + i, segs)
        seg_len = lengths_s[seg]
        mine = seg_col == seg
        my_value = jnp.sum(jnp.where(mine, later_value, 0.0), axis=0, keepdims=True)
        my_head = jnp.sum(jnp.where(mine, later_head, 0.0), axis=0, keepdims=True)
        deltas = jnp.sum(jnp.where(mine, terms[:, :length], 0.0), axis=0, keepdims=True)
        local_sum = jnp.sum(discount * deltas, axis=1, keepdims=True)
        left = (seg_len - t_col).astype(jnp.float32)
        advantage = jnp.where(
            t_col < seg_len,
            local_sum
            + jnp.exp((left - 1.0) * log_rate) * my_value
            + jnp.exp(left * log_rate) * my_head,
            0.0,
        )
        if i == 0:
            row_ref[...] = jnp.sum(jnp.where(t_id == j_id, advantage, 0.0), axis=0, keepdims=True)
        adv_ref[i] = jnp.broadcast_to(advantage, (length, HD))

        ancestor = seg
        for slot in range(depth):
            if slot > 0:
                ancestor = parent_of(ancestor, parents_s)
            slot_len = jnp.where(ancestor >= 0, lengths_s[jnp.maximum(ancestor, 0)], 0)
            seen = t_id < slot_len
            if slot == 0:
                seen = jnp.logical_and(seen, t_id <= j_id)
            bias_ref[i, slot * length : (slot + 1) * length, :] = jnp.where(seen, 0.0, -1e30)


def parent_of(segment, parents_s):
    known = parents_s[jnp.maximum(segment, 0)]
    return jnp.where(segment >= 0, known, -1).astype(jnp.int32)


def prepare(own, parents, lengths, near, far, segs, log_rate):
    length = near.shape[1] // 2
    smem = pl.BlockSpec(memory_space=pltpu.SMEM)
    vmem = pl.BlockSpec(memory_space=pltpu.VMEM)
    return pl.pallas_call(
        functools.partial(prepare_kernel, log_rate, DEPTH, segs),
        out_shape=(
            jax.ShapeDtypeStruct((1, length), jnp.float32),
            jax.ShapeDtypeStruct((segs, length, HD), jnp.float32),
            jax.ShapeDtypeStruct((segs, DEPTH * length, length), jnp.float32),
        ),
        in_specs=[smem] * 3 + [vmem] * 4,
        out_specs=(vmem,) * 3,
        cost_estimate=pl.CostEstimate(
            flops=200 * length * length,
            bytes_accessed=4 * (DEPTH + 1) * segs * length * length,
            transcendentals=length * length,
        ),
        compiler_params=SMALL,
        name="prepare_advantages",
    )(own, parents, lengths, parents[None], lengths[None], near, far)


def attend_kernel(depth, segs, *refs):
    own_ref, parents_s, adv_ref, bias_ref = refs[:4]
    query_refs = refs[4 : 4 + segs]
    refs = refs[4 + segs :]
    steps = (len(refs) - segs - 4) // 2
    kv_refs, dq_refs, dkv_refs = refs[:steps], refs[steps : steps + segs], refs[steps + segs : -4]
    kv_scr, p_scr, ds_scr, acc_scr = refs[-4:]

    group_size, length = query_refs[0].shape[1:3]
    own = own_ref[0]
    part = lax.rem(own, segs)
    for step in range(steps):
        for i in range(segs):
            kv_scr[step * segs + i] = kv_refs[step][i]
    acc_scr[...] = jnp.zeros_like(acc_scr)

    scale = HD**-0.5
    contract_last = (((1,), (1,)), ((), ()))
    contract_first = (((0,), (0,)), ((), ()))
    for i in range(segs):
        ancestor = own - part + lax.rem(part + i, segs)
        chosen = []
        for slot in range(depth):
            if slot > 0:
                ancestor = parent_of(ancestor, parents_s)
            if segs == 1:
                chosen.append(slot)
            else:
                known = jnp.maximum(ancestor, 0)
                step = (own - part) // segs - known // segs
                turn = lax.rem(lax.rem(known, segs) - part + segs, segs)
                chosen.append(jnp.where(ancestor >= 0, step * segs + turn, 0))
        q_list = [query_refs[i][0, j] for j in range(group_size)]
        dir_list = [query_refs[i][1, j] for j in range(group_size)]
        do_list = [(adv_ref[i] * d.astype(jnp.float32)).astype(jnp.bfloat16) for d in dir_list]
        k_all = jnp.concatenate([kv_scr[s, 0] for s in chosen], axis=0)
        v_all = jnp.concatenate([kv_scr[s, 1] for s in chosen], axis=0)
        for j in range(group_size):
            columns = slice(j * length, (j + 1) * length)
            scores = lax.dot_general(
                k_all, q_list[j], contract_last, preferred_element_type=jnp.float32
            )
            scores = scores * (scale * LOG2E) + bias_ref[i]
            top = jnp.max(scores, axis=0, keepdims=True)
            unnorm = jnp.exp2(scores - top)
            prob = unnorm * (1.0 / jnp.sum(unnorm, axis=0, keepdims=True))
            prob_low = prob.astype(jnp.bfloat16)
            dprob = lax.dot_general(
                v_all, do_list[j], contract_last, preferred_element_type=jnp.float32
            )
            row_dot = jnp.sum(prob_low.astype(jnp.float32) * dprob, axis=0, keepdims=True)
            dscore = (prob * (dprob - row_dot)).astype(jnp.bfloat16)
            p_scr[:, columns] = prob_low
            ds_scr[:, columns] = dscore
        dscore_all = ds_scr[...]
        dq_t = lax.dot_general(
            k_all, dscore_all, contract_first, preferred_element_type=jnp.float32
        )
        for j in range(group_size):
            dq_refs[i][:, j * HD : (j + 1) * HD] = (
                jnp.transpose(dq_t[:, j * length : (j + 1) * length]) * scale
            ).astype(jnp.bfloat16)
        q_all = jnp.concatenate(q_list, axis=0)
        do_all = jnp.concatenate(do_list, axis=0)
        dk_all = jnp.dot(dscore_all, q_all, preferred_element_type=jnp.float32) * scale
        dv_all = jnp.dot(p_scr[...], do_all, preferred_element_type=jnp.float32)
        for slot, s in enumerate(chosen):
            rows = slice(slot * length, (slot + 1) * length)
            acc_scr[s, 0] += dk_all[rows]
            acc_scr[s, 1] += dv_all[rows]
    for step in range(steps):
        for i in range(segs):
            dkv_refs[step][i] = acc_scr[step * segs + i].astype(jnp.bfloat16)


def attend(own, parents, advantages, bias, query_list, kv_list):
    segs, length = advantages.shape[:2]
    steps = len(kv_list)
    width = query_list[0].shape[1] * HD
    keys = DEPTH * length
    smem = pl.BlockSpec(memory_space=pltpu.SMEM)
    vmem = pl.BlockSpec(memory_space=pltpu.VMEM)
    out_shape = (jax.ShapeDtypeStruct((length, width), jnp.bfloat16),) * segs + (
        jax.ShapeDtypeStruct((segs, 2, length, HD), jnp.bfloat16),
    ) * steps
    outs = pl.pallas_call(
        functools.partial(attend_kernel, DEPTH, segs),
        out_shape=out_shape,
        in_specs=[smem] * 2 + [vmem] * (2 + segs + steps),
        out_specs=(vmem,) * len(out_shape),
        scratch_shapes=[
            pltpu.VMEM((steps * segs, 2, length, HD), jnp.bfloat16),
            pltpu.VMEM((keys, width), jnp.bfloat16),
            pltpu.VMEM((keys, width), jnp.bfloat16),
            pltpu.VMEM((steps * segs, 2, length, HD), jnp.float32),
        ],
        compiler_params=pltpu.CompilerParams(vmem_limit_bytes=16 * 1024 * 1024),
        cost_estimate=pl.CostEstimate(
            flops=5 * 2 * keys * length * width * segs,
            bytes_accessed=8 * 1024 * 1024,
            transcendentals=keys * width * segs,
        ),
        name="tree_attention_backward",
    )(own, parents, advantages, bias, *query_list, *kv_list)
    return outs[:segs], outs[segs:]


def join_queries_kernel(chunks, own_ref, *refs):
    part = lax.rem(own_ref[0], 2)
    dq_ref = refs[-1]
    for side in range(2):
        where = part if side == 0 else 1 - part
        for chunk in range(chunks):
            block = refs[side * chunks + chunk]
            width = block.shape[1]
            column = pl.multiple_of((where * chunks + chunk) * width, HD)
            dq_ref[:, pl.ds(column, width)] = block[...]


def join_queries(own, dq_list):
    length, width = dq_list[0].shape
    smem = pl.BlockSpec(memory_space=pltpu.SMEM)
    vmem = pl.BlockSpec(memory_space=pltpu.VMEM)
    return pl.pallas_call(
        functools.partial(join_queries_kernel, len(dq_list) // 2),
        out_shape=jax.ShapeDtypeStruct((length, len(dq_list) * width), jnp.bfloat16),
        in_specs=[smem] + [vmem] * len(dq_list),
        out_specs=vmem,
        cost_estimate=pl.CostEstimate(
            flops=0, bytes_accessed=4 * length * width * len(dq_list), transcendentals=0
        ),
        compiler_params=SMALL,
        name="join_queries",
    )(own, *dq_list)


def join_keys_kernel(chunks, own_ref, *refs):
    part = lax.rem(own_ref[0], 2)
    other_refs, sum_refs = refs[:chunks], refs[chunks:-2]
    many = len(sum_refs) // chunks
    dk_ref, dv_ref = refs[-2:]
    for chunk in range(chunks):
        here = pl.ds(pl.multiple_of((part * chunks + chunk) * HD, HD), HD)
        there = pl.ds(pl.multiple_of(((1 - part) * chunks + chunk) * HD, HD), HD)
        for plane, out_ref in enumerate((dk_ref, dv_ref)):
            blocks = [ref[0, plane] for ref in sum_refs[chunk * many : (chunk + 1) * many]]
            total = sum(block.astype(jnp.float32) for block in blocks)
            out_ref[:, here] = total.astype(jnp.bfloat16)
            out_ref[:, there] = other_refs[chunk][plane]


def join_keys(own, others, summands):
    chunks = len(others)
    length = others[0].shape[1]
    smem = pl.BlockSpec(memory_space=pltpu.SMEM)
    vmem = pl.BlockSpec(memory_space=pltpu.VMEM)
    flat = [block for blocks in summands for block in blocks]
    out = jax.ShapeDtypeStruct((length, 2 * chunks * HD), jnp.bfloat16)
    return pl.pallas_call(
        functools.partial(join_keys_kernel, chunks),
        out_shape=(out, out),
        in_specs=[smem] + [vmem] * (chunks + len(flat)),
        out_specs=(vmem, vmem),
        cost_estimate=pl.CostEstimate(
            flops=0, bytes_accessed=16 * length * HD * chunks, transcendentals=0
        ),
        compiler_params=SMALL,
        name="join_keys",
    )(own, *others, *flat)


def permute(array, pairs):
    return lax.ppermute(array, "seg", pairs)


def after(array, *earlier):
    return lax.optimization_barrier((array, *earlier))[0]


def paired_body(own, queries, direction, key_vectors, value_vectors, token_rows, parents, lengths, log_rate):
    groups = lax.axis_size("seg")
    chunks = key_vectors.shape[1] // HD // 2
    swap = [(i, i ^ 1) for i in range(groups)]
    up = {d: [(i, i + 2 * d) for i in range(groups - 2 * d)] for d in (1, 2, 3)}
    down = {d: [(i, i - 2 * d) for i in range(2 * d, groups)] for d in (1, 2, 3)}
    forward = [(i, i + 2) for i in range(4, groups - 2)]

    kept, terms, given = pack(own, lengths, key_vectors, value_vectors, token_rows, 2, log_rate)
    taken = permute(given, swap)
    kept_q, given_q = pack_queries(own, after(queries, given), direction, 2, chunks)
    terms, near = join_blocks(own, terms, kept, taken)
    blocks = [[near[0]] + [permute(near[0], up[d]) for d in (3, 2, 1)][::-1]]
    taken_q = [permute(after(given_q[0], near[0]), swap)]
    terms = terms + permute(terms, down[1])
    row, advantages, bias = prepare(
        own, parents, lengths, terms, permute(terms, down[2]), 2, log_rate
    )
    blocks[0][1:] = lax.optimization_barrier((*blocks[0][1:], bias))[:-1]
    for chunk in range(1, chunks):
        taken_q.append(permute(after(given_q[chunk], taken_q[-1], bias), swap))

    dq_own, dq_back, dkv_list = [], [], []
    for chunk in range(chunks):
        gate = blocks[chunk]
        dq, dkv = attend(own, parents, advantages, bias, [kept_q[chunk], taken_q[chunk]], gate)
        dq_own.append(dq[0])
        dq_back.append(dq[1])
        dkv_list.append(dkv)
        if chunk + 1 < chunks:
            block = near[chunk + 1]
            two = permute(after(block, *gate[1:]), up[2])
            one = permute(after(block, dq[0]), up[1])
            three = permute(after(two, dq[0]), forward)
            blocks.append([block, one, two, three])

    last = dq_own[-1]
    summands = []
    for dkv in dkv_list:
        arrived = [permute(dkv[d], down[d]) for d in (3, 2, 1)]
        summands.append([after(dkv[0], last)] + arrived)
    dq_back = [permute(block, swap) for block in dq_back]
    others = []
    for blocks in summands:
        total = sum(block[1].astype(jnp.float32) for block in blocks)
        others.append(permute(total.astype(jnp.bfloat16), swap))
    grad_q = join_queries(own, dq_own + dq_back)
    grad_k, grad_v = join_keys(own, others, summands)
    return grad_q, grad_k, grad_v, row[0]


def fetch_rows(spread, wanted):
    routed = jnp.take(spread, jnp.maximum(wanted, 0), axis=0)
    return lax.all_to_all(routed, "seg", split_axis=0, concat_axis=2, tiled=True)


def return_rows(grad_rows, wanted, total_segs):
    returned = lax.all_to_all(grad_rows, "seg", split_axis=2, concat_axis=0, tiled=True)
    piece_len = returned.shape[2]
    feature_len = returned.shape[3]
    routed_ids = wanted.reshape(-1)
    targets = jnp.where(routed_ids >= 0, routed_ids, total_segs)
    summed = jax.ops.segment_sum(
        returned.reshape(-1, piece_len * feature_len).astype(jnp.float32),
        targets,
        num_segments=total_segs + 1,
    )[:total_segs]
    return lax.all_to_all(
        summed.reshape(total_segs, piece_len, feature_len),
        "seg",
        split_axis=0,
        concat_axis=1,
        tiled=True,
    )


def routed_body(own, queries, direction, key_vectors, value_vectors, token_rows, parents, lengths, log_rate):
    total_segs = parents.shape[0]
    length = queries.shape[0]
    block, terms = pack(own, lengths, key_vectors, value_vectors, token_rows, 1, log_rate)
    heads = block.shape[0]
    mine = lax.dynamic_slice_in_dim(terms, own[0], 1)
    terms = lax.all_gather(mine, "seg", axis=0, tiled=True)
    row, advantages, bias = prepare(
        own, parents, lengths, terms, jnp.zeros_like(terms), 1, log_rate
    )
    flat = jnp.concatenate([key_vectors, value_vectors], axis=1)[None]
    spread = lax.all_to_all(flat, "seg", split_axis=1, concat_axis=0, tiled=True)
    chains = ancestors(parents, DEPTH - 1)
    arrived = fetch_rows(spread, chains)[0]
    slot_kv = jnp.concatenate([flat, arrived]).reshape(DEPTH, length, 2, heads, HD)
    slot_kv = jnp.transpose(slot_kv, (0, 3, 2, 1, 4))
    (kept_q,) = pack_queries(own, queries, direction, 1, heads)
    dq_list, dkv_list = [], []
    for head in range(heads):
        kv_list = [slot_kv[slot : slot + 1, head] for slot in range(DEPTH)]
        dq, dkv = attend(own, parents, advantages, bias, [kept_q[head]], kv_list)
        dq_list.append(dq[0])
        dkv_list.append(jnp.concatenate(dkv))
    rows = jnp.transpose(jnp.stack(dkv_list), (1, 3, 2, 0, 4)).reshape(1, DEPTH, length, -1)
    summed = return_rows(rows[:, 1:], chains, total_segs)[0] + rows[0, 0].astype(jnp.float32)
    width = key_vectors.shape[1]
    grad_keys = summed[:, :width].astype(jnp.bfloat16)
    grad_values = summed[:, width:].astype(jnp.bfloat16)
    return jnp.concatenate(dq_list, axis=1), grad_keys, grad_values, row[0]


def body(
    queries,
    key_vectors,
    value_vectors,
    direction,
    rewards,
    logprobs,
    ref_logprobs,
    value_est,
    parents,
    seg_lengths,
):
    groups = lax.axis_size("seg")
    assert parents.shape[0] == groups
    own = jnp.reshape(lax.axis_index("seg"), (1,))
    log_rate = math.log(LAMBDA_SEG) / rewards.shape[0]
    token_rows = [rewards[None], logprobs[None], ref_logprobs[None], value_est[None]]
    plan = paired_body if groups == PAIRED_GROUPS else routed_body
    return plan(
        own, queries, direction, key_vectors, value_vectors, token_rows, parents, seg_lengths, log_rate
    )


def solution(mesh):
    in_specs = (
        P(("grp", "seg"), "tp"),
        P(("grp", "seg"), "tp"),
        P(("grp", "seg"), "tp"),
        P(("grp", "seg"), "tp"),
        P(("grp", "seg")),
        P(("grp", "seg")),
        P(("grp", "seg")),
        P(("grp", "seg")),
        P("grp"),
        P("grp"),
    )
    out_specs = (
        P(("grp", "seg"), "tp"),
        P(("grp", "seg"), "tp"),
        P(("grp", "seg"), "tp"),
        P(("grp", "seg")),
    )
    return jax.shard_map(body, mesh=mesh, in_specs=in_specs, out_specs=out_specs, check_vma=False)
```

```python
import functools
import math

import jax
import jax.numpy as jnp
from jax import lax
from jax.experimental import pallas as pl
from jax.experimental.pallas import tpu as pltpu
from jax.sharding import PartitionSpec as P

HD = 128
DEPTH = 5
BETA = 0.1
LAMBDA_SEG = 0.7
PAIRED_GROUPS = 8
TERM_ROWS = 16
LOG2E = math.log2(math.e)
SMALL = pltpu.CompilerParams(vmem_limit_bytes=8 * 1024 * 1024)


def lookup(table_values, lookup_ids):
    matches = lookup_ids[..., None] == jnp.arange(table_values.shape[0], dtype=jnp.int32)
    return jnp.sum(jnp.where(matches, table_values, 0), axis=-1)


def ancestors(parents, count):
    current = jnp.arange(parents.shape[0], dtype=jnp.int32)
    chain_list = []
    for depth_step in range(count):
        parent_ids = lookup(parents, current)
        current = jnp.where(current >= 0, parent_ids, -1)
        chain_list.append(current)
    return jnp.stack(chain_list, axis=1)


def token_terms(log_rate, own_len, rewards, logprobs, ref_logprobs, values):
    positions = lax.broadcasted_iota(jnp.int32, rewards.shape, 1)
    later = jnp.concatenate([values[:, 1:], values[:, :1]], axis=1)
    later = jnp.where(positions + 1 < own_len, later, 0.0)
    deltas = jnp.where(
        positions < own_len, rewards - BETA * (logprobs - ref_logprobs) + later - values, 0.0
    )
    powers = jnp.exp(positions.astype(jnp.float32) * log_rate)
    first_local = jnp.sum(deltas * powers, axis=1, keepdims=True)
    firsts = jnp.where(positions == 0, first_local, jnp.where(positions == 1, values[:, :1], 0.0))
    return deltas, firsts


def split_float(value):
    parts = []
    for _ in range(3):
        part = value.astype(jnp.bfloat16)
        parts.append(part)
        value = value - part.astype(jnp.float32)
    return parts


def pack_kernel(
    log_rate,
    lengths_ref,
    k_ref,
    v_ref,
    rewards_ref,
    logprobs_ref,
    ref_logprobs_ref,
    values_ref,
    *refs,
):
    out_refs, sems = refs[:-1], refs[-1]
    own = lax.axis_index("seg")
    length = k_ref.shape[0]
    parts = len(out_refs)
    heads = k_ref.shape[1] // HD // parts
    copies = []
    for step in range(parts):
        part = lax.rem(own + step, parts)
        for h in range(heads):
            columns = pl.ds(pl.multiple_of((part * heads + h) * HD, HD), HD)
            for plane, ref in enumerate((k_ref, v_ref)):
                rows = pl.ds((h * 2 + plane) * length, length)
                copies.append(
                    pltpu.make_async_copy(
                        ref.at[:, columns], out_refs[step].at[rows, :], sems.at[len(copies)]
                    )
                )
    for copy in copies:
        copy.start()
    terms = token_terms(
        log_rate,
        lengths_ref[own],
        rewards_ref[...],
        logprobs_ref[...],
        ref_logprobs_ref[...],
        values_ref[...],
    )
    rows = [part.astype(jnp.float32) for x in terms for part in split_float(x)]
    rows.append(jnp.zeros((TERM_ROWS - len(rows), HD), jnp.float32))
    rows = jnp.concatenate(rows).astype(jnp.bfloat16)
    for out_ref in out_refs:
        out_ref[2 * heads * length :, :] = rows
    for copy in copies:
        copy.wait()


def pack(lengths, k, v, token_rows, parts, log_rate):
    length, width = k.shape
    smem = pl.BlockSpec(memory_space=pltpu.SMEM)
    vmem = pl.BlockSpec(memory_space=pltpu.VMEM)
    hbm = pl.BlockSpec(memory_space=pltpu.HBM)
    heads = width // HD // parts
    assert length == HD
    block = jax.ShapeDtypeStruct((2 * heads * length + TERM_ROWS, HD), k.dtype)
    return pl.pallas_call(
        functools.partial(pack_kernel, log_rate),
        out_shape=(block,) * parts,
        in_specs=[smem, hbm, hbm] + [vmem] * 4,
        out_specs=(vmem,) * parts,
        scratch_shapes=[pltpu.SemaphoreType.DMA((2 * heads * parts,))],
        cost_estimate=pl.CostEstimate(
            flops=length * 100, bytes_accessed=8 * length * width, transcendentals=length
        ),
        name="pack_keys_values",
    )(lengths, k, v, *token_rows)


def pack_queries_kernel(parts, q_ref, dir_ref, *out_refs):
    own = lax.axis_index("seg")
    chunks = len(out_refs) // parts
    heads = out_refs[0].shape[1]
    for index, out_ref in enumerate(out_refs):
        step, chunk = divmod(index, chunks)
        part = lax.rem(own + step, parts)
        for h in range(heads):
            column = (part * chunks + chunk) * heads + h
            columns = pl.ds(pl.multiple_of(column * HD, HD), HD)
            out_ref[0, h] = q_ref[:, columns]
            out_ref[1, h] = dir_ref[:, columns]


def pack_queries(q, direction, parts, chunks):
    length, width = q.shape
    vmem = pl.BlockSpec(memory_space=pltpu.VMEM)
    block = jax.ShapeDtypeStruct((2, width // HD // parts // chunks, length, HD), q.dtype)
    outs = pl.pallas_call(
        functools.partial(pack_queries_kernel, parts),
        out_shape=(block,) * (parts * chunks),
        in_specs=[vmem, vmem],
        out_specs=(vmem,) * (parts * chunks),
        cost_estimate=pl.CostEstimate(flops=0, bytes_accessed=8 * length * width, transcendentals=0),
        compiler_params=SMALL,
        name="pack_queries",
    )(q, direction)
    return [outs[step * chunks : (step + 1) * chunks] for step in range(parts)]


def parent_of(segment, parents_s):
    known = parents_s[jnp.maximum(segment, 0)]
    return jnp.where(segment >= 0, known, -1).astype(jnp.int32)


def segment_of(own, segs, i):
    part = lax.rem(own, segs)
    return own - part + lax.rem(part + i, segs)


def mask_kernel(depth, parents_s, lengths_s, bias_ref):
    segs, _, length = bias_ref.shape
    own = lax.axis_index("seg")
    u_id = lax.broadcasted_iota(jnp.int32, (length, length), 0)
    t_id = lax.broadcasted_iota(jnp.int32, (length, length), 1)
    for i in range(segs):
        ancestor = segment_of(own, segs, i)
        for slot in range(depth):
            if slot > 0:
                ancestor = parent_of(ancestor, parents_s)
            slot_len = jnp.where(ancestor >= 0, lengths_s[jnp.maximum(ancestor, 0)], 0)
            seen = u_id < slot_len
            if slot == 0:
                seen = jnp.logical_and(seen, u_id <= t_id)
            bias_ref[i, slot * length : (slot + 1) * length, :] = jnp.where(seen, 0.0, -1e30)


def masks(parents, lengths, length, segs):
    smem = pl.BlockSpec(memory_space=pltpu.SMEM)
    return pl.pallas_call(
        functools.partial(mask_kernel, DEPTH),
        out_shape=jax.ShapeDtypeStruct((segs, DEPTH * length, length), jnp.float32),
        in_specs=[smem] * 2,
        out_specs=pl.BlockSpec(memory_space=pltpu.VMEM),
        cost_estimate=pl.CostEstimate(
            flops=8 * DEPTH * segs * length * length,
            bytes_accessed=4 * DEPTH * segs * length * length,
            transcendentals=0,
        ),
        compiler_params=SMALL,
        name="masks",
    )(parents, lengths)


def advantage_kernel(log_rate, depth, segs, parents_s, lengths_s, *refs):
    term_refs, (row_ref, adv_ref) = refs[:-2], refs[-2:]
    length = row_ref.shape[1]
    count = parents_s.shape[0]
    own = lax.axis_index("seg")

    seg_col = lax.broadcasted_iota(jnp.int32, (count, 1), 0)
    if len(term_refs) == 1:
        deltas, firsts = term_refs[0][:, :length], term_refs[0][:, length:]
    else:
        part, pair, pairs = lax.rem(own, segs), own // segs, count // segs
        deltas = firsts = jnp.zeros((count, length), jnp.float32)
        for index, ref in enumerate(term_refs):
            step, side = divmod(index, segs)
            seg = lax.rem(pair - step + pairs, pairs) * segs + lax.rem(part + side, segs)
            tail = ref[ref.shape[0] - TERM_ROWS :, :].astype(jnp.float32)
            deltas = deltas + jnp.where(seg_col == seg, tail[0:1] + tail[1:2] + tail[2:3], 0.0)
            firsts = firsts + jnp.where(seg_col == seg, tail[3:4] + tail[4:5] + tail[5:6], 0.0)

    row_id = lax.broadcasted_iota(jnp.int32, (count, count), 0)
    col_id = lax.broadcasted_iota(jnp.int32, (count, count), 1)
    eye = row_id == col_id

    def to_row(col):
        return jnp.sum(jnp.where(eye, col, 0.0), axis=0, keepdims=True)

    parent_row = jnp.full((1, count), -1, jnp.int32)
    lens_col = jnp.zeros((count, 1), jnp.int32)
    for seg in range(count):
        parent_row = jnp.where(col_id[:1] == seg, parents_s[seg], parent_row)
        lens_col = jnp.where(seg_col == seg, lengths_s[seg], lens_col)
    lens_col = lens_col.astype(jnp.float32)
    children = (parent_row == row_id).astype(jnp.float32)
    weights = children / jnp.maximum(jnp.sum(children, axis=1, keepdims=True), 1.0)
    first_local, first_value = firsts[:, 0:1], firsts[:, 1:2]
    later_value = jnp.sum(weights * to_row(first_value), axis=1, keepdims=True)
    base_term = first_local + jnp.exp((lens_col - 1.0) * log_rate) * later_value
    factor = jnp.exp(lens_col * log_rate)
    head = base_term
    for _ in range(depth):
        head = base_term + factor * jnp.sum(weights * to_row(head), axis=1, keepdims=True)
    later_head = jnp.sum(weights * to_row(head), axis=1, keepdims=True)

    t_id = lax.broadcasted_iota(jnp.int32, (length, length), 0)
    j_id = lax.broadcasted_iota(jnp.int32, (length, length), 1)
    offset = (j_id - t_id).astype(jnp.float32)
    discount = jnp.where(offset >= 0, jnp.exp(offset * log_rate), 0.0)
    t_col = lax.broadcasted_iota(jnp.int32, (length, 1), 0)
    for i in range(segs):
        seg = segment_of(own, segs, i)
        seg_len = lengths_s[seg]
        mine = seg_col == seg
        my_value = jnp.sum(jnp.where(mine, later_value, 0.0), axis=0, keepdims=True)
        my_head = jnp.sum(jnp.where(mine, later_head, 0.0), axis=0, keepdims=True)
        my_deltas = jnp.sum(jnp.where(mine, deltas, 0.0), axis=0, keepdims=True)
        local_sum = jnp.sum(discount * my_deltas, axis=1, keepdims=True)
        left = (seg_len - t_col).astype(jnp.float32)
        advantage = jnp.where(
            t_col < seg_len,
            local_sum
            + jnp.exp((left - 1.0) * log_rate) * my_value
            + jnp.exp(left * log_rate) * my_head,
            0.0,
        )
        if i == 0:
            row_ref[...] = jnp.sum(jnp.where(t_id == j_id, advantage, 0.0), axis=0, keepdims=True)
        adv_ref[i] = jnp.broadcast_to(advantage, (length, HD))


def advantages_of(parents, lengths, terms, length, segs, log_rate):
    smem = pl.BlockSpec(memory_space=pltpu.SMEM)
    vmem = pl.BlockSpec(memory_space=pltpu.VMEM)
    return pl.pallas_call(
        functools.partial(advantage_kernel, log_rate, DEPTH, segs),
        out_shape=(
            jax.ShapeDtypeStruct((1, length), jnp.float32),
            jax.ShapeDtypeStruct((segs, length, HD), jnp.float32),
        ),
        in_specs=[smem] * 2 + [vmem] * len(terms),
        out_specs=(vmem,) * 2,
        cost_estimate=pl.CostEstimate(
            flops=200 * length * length,
            bytes_accessed=8 * segs * length * length,
            transcendentals=length * length,
        ),
        compiler_params=SMALL,
        name="advantages",
    )(parents, lengths, *terms)


def attend_kernel(depth, chunk, segs, sources, group_size, *refs):
    parents_s, adv_ref, bias_ref = refs[:3]
    query_refs, kv_refs = refs[3 : 3 + segs], refs[3 + segs : 3 + segs + sources]
    kv_scr, p_scr, ds_scr, acc_scr = refs[-4:]
    refs = refs[3 + segs + sources : -4]
    steps = sources // segs
    dkv_refs, dq_refs = refs[-steps:], refs[-steps - segs : -steps]

    length = query_refs[0].shape[2]
    own = lax.axis_index("seg")
    for source in range(sources):
        for plane in range(2):
            rows = slice((2 * chunk + plane) * length, (2 * chunk + plane + 1) * length)
            kv_scr[source, plane] = kv_refs[source][rows, :]
    acc_scr[...] = jnp.zeros_like(acc_scr)

    scale = HD**-0.5
    contract_last = (((1,), (1,)), ((), ()))
    contract_first = (((0,), (0,)), ((), ()))
    for i in range(segs):
        ancestor = segment_of(own, segs, i)
        part = lax.rem(own, segs)
        chosen = []
        for slot in range(depth):
            if slot > 0:
                ancestor = parent_of(ancestor, parents_s)
            if segs == 1:
                chosen.append(slot)
            else:
                known = jnp.maximum(ancestor, 0)
                step = (own - part) // segs - known // segs
                turn = lax.rem(lax.rem(known, segs) - part + segs, segs)
                chosen.append(jnp.where(ancestor >= 0, step * segs + turn, 0))
        q_list = [query_refs[i][0, j] for j in range(group_size)]
        dir_list = [query_refs[i][1, j] for j in range(group_size)]
        do_list = [(adv_ref[i] * d.astype(jnp.float32)).astype(jnp.bfloat16) for d in dir_list]
        k_all = jnp.concatenate([kv_scr[s, 0] for s in chosen], axis=0)
        v_all = jnp.concatenate([kv_scr[s, 1] for s in chosen], axis=0)
        for j in range(group_size):
            columns = slice(j * length, (j + 1) * length)
            scores = lax.dot_general(
                k_all, q_list[j], contract_last, preferred_element_type=jnp.float32
            )
            scores = scores * (scale * LOG2E) + bias_ref[i]
            top = jnp.max(scores, axis=0, keepdims=True)
            unnorm = jnp.exp2(scores - top)
            prob = unnorm * (1.0 / jnp.sum(unnorm, axis=0, keepdims=True))
            prob_low = prob.astype(jnp.bfloat16)
            dprob = lax.dot_general(
                v_all, do_list[j], contract_last, preferred_element_type=jnp.float32
            )
            row_dot = jnp.sum(prob_low.astype(jnp.float32) * dprob, axis=0, keepdims=True)
            dscore = (prob * (dprob - row_dot)).astype(jnp.bfloat16)
            p_scr[:, columns] = prob_low
            ds_scr[:, columns] = dscore
        dscore_all = ds_scr[...]
        dq_t = lax.dot_general(
            k_all, dscore_all, contract_first, preferred_element_type=jnp.float32
        )
        for j in range(group_size):
            dq = jnp.transpose(dq_t[:, j * length : (j + 1) * length]) * scale
            dq_refs[i][:, j * HD : (j + 1) * HD] = dq.astype(jnp.bfloat16)
        q_all = jnp.concatenate(q_list, axis=0)
        do_all = jnp.concatenate(do_list, axis=0)
        dk_all = jnp.dot(dscore_all, q_all, preferred_element_type=jnp.float32) * scale
        dv_all = jnp.dot(p_scr[...], do_all, preferred_element_type=jnp.float32)
        for slot, s in enumerate(chosen):
            rows = slice(slot * length, (slot + 1) * length)
            acc_scr[s, 0] += dk_all[rows]
            acc_scr[s, 1] += dv_all[rows]
    for step in range(steps):
        for i in range(segs):
            dkv_refs[step][i] = acc_scr[step * segs + i].astype(jnp.bfloat16)


def attend(parents, advantages, bias, query_list, kv_list, chunk):
    segs, length = advantages.shape[:2]
    sources = len(kv_list)
    steps = sources // segs
    group_size = query_list[0].shape[1]
    width = group_size * HD
    keys = DEPTH * length
    smem = pl.BlockSpec(memory_space=pltpu.SMEM)
    vmem = pl.BlockSpec(memory_space=pltpu.VMEM)
    out_shape = [jax.ShapeDtypeStruct((length, width), jnp.bfloat16)] * segs
    out_shape += [jax.ShapeDtypeStruct((segs, 2, length, HD), jnp.bfloat16)] * steps
    outs = pl.pallas_call(
        functools.partial(attend_kernel, DEPTH, chunk, segs, sources, group_size),
        out_shape=out_shape,
        in_specs=[smem] + [vmem] * (2 + segs + sources),
        out_specs=[vmem] * len(out_shape),
        scratch_shapes=[
            pltpu.VMEM((sources, 2, length, HD), jnp.bfloat16),
            pltpu.VMEM((keys, width), jnp.bfloat16),
            pltpu.VMEM((keys, width), jnp.bfloat16),
            pltpu.VMEM((sources, 2, length, HD), jnp.float32),
        ],
        compiler_params=pltpu.CompilerParams(vmem_limit_bytes=16 * 1024 * 1024),
        cost_estimate=pl.CostEstimate(
            flops=5 * 2 * keys * length * width * segs,
            bytes_accessed=8 * 1024 * 1024,
            transcendentals=keys * width * segs,
        ),
        name="tree_attention_backward",
    )(parents, advantages, bias, *query_list, *kv_list)
    return outs[:segs], outs[segs:]


def join_queries_kernel(*refs):
    part = lax.rem(lax.axis_index("seg"), 2)
    refs, dq_ref = refs[:-1], refs[-1]
    chunks = len(refs) // 2
    width = refs[0].shape[1]
    for index, ref in enumerate(refs):
        side, chunk = divmod(index, chunks)
        where = part if side == 0 else 1 - part
        column = pl.multiple_of((where * chunks + chunk) * width, HD)
        dq_ref[:, pl.ds(column, width)] = ref[...]


def join_queries(own_list, other_list):
    chunks = len(own_list)
    length, width = own_list[0].shape
    vmem = pl.BlockSpec(memory_space=pltpu.VMEM)
    return pl.pallas_call(
        join_queries_kernel,
        out_shape=jax.ShapeDtypeStruct((length, 2 * chunks * width), jnp.bfloat16),
        in_specs=[vmem] * (2 * chunks),
        out_specs=vmem,
        cost_estimate=pl.CostEstimate(
            flops=0, bytes_accessed=8 * length * width * chunks, transcendentals=0
        ),
        compiler_params=SMALL,
        name="join_queries",
    )(*own_list, *other_list)


def join_keys_kernel(chunks, *refs):
    part = lax.rem(lax.axis_index("seg"), 2)
    other_refs, sum_refs = refs[:chunks], refs[chunks:-2]
    many = len(sum_refs) // chunks
    dk_ref, dv_ref = refs[-2:]
    for chunk in range(chunks):
        here = pl.ds(pl.multiple_of((part * chunks + chunk) * HD, HD), HD)
        there = pl.ds(pl.multiple_of(((1 - part) * chunks + chunk) * HD, HD), HD)
        for plane, out_ref in enumerate((dk_ref, dv_ref)):
            blocks = [ref[0, plane] for ref in sum_refs[chunk * many : (chunk + 1) * many]]
            total = sum(block.astype(jnp.float32) for block in blocks)
            out_ref[:, here] = total.astype(jnp.bfloat16)
            out_ref[:, there] = other_refs[chunk][plane]


def join_keys(others, summands):
    chunks = len(others)
    length = others[0].shape[1]
    vmem = pl.BlockSpec(memory_space=pltpu.VMEM)
    flat = [block for blocks in summands for block in blocks]
    out = jax.ShapeDtypeStruct((length, 2 * chunks * HD), jnp.bfloat16)
    return pl.pallas_call(
        functools.partial(join_keys_kernel, chunks),
        out_shape=(out, out),
        in_specs=[vmem] * (chunks + len(flat)),
        out_specs=(vmem, vmem),
        cost_estimate=pl.CostEstimate(
            flops=0, bytes_accessed=16 * length * HD * chunks, transcendentals=0
        ),
        compiler_params=SMALL,
        name="join_keys",
    )(*others, *flat)


def permute(array, pairs):
    return lax.ppermute(array, "seg", pairs)


def after(array, *earlier):
    return lax.optimization_barrier((array, *earlier))[0]


def paired_body(queries, direction, key_vectors, value_vectors, token_rows, parents, lengths, log_rate):
    groups = lax.axis_size("seg")
    length = queries.shape[0]
    chunks = key_vectors.shape[1] // HD // 2
    swap = [(i, i ^ 1) for i in range(groups)]
    steps = range(1, groups // 2)
    up = {d: [(i, (i + 2 * d) % groups) for i in range(groups)] for d in steps}
    down = {d: [(i, (i - 2 * d) % groups) for i in range(groups)] for d in steps}

    kept, given = pack(lengths, key_vectors, value_vectors, token_rows, 2, log_rate)
    taken = permute(given, swap)
    kept_far = [permute(kept, up[d]) for d in steps]
    kept_q, given_q = pack_queries(after(queries, kept), direction, 2, chunks)
    bias = masks(parents, lengths, length, 2)
    gated, *given_q = lax.optimization_barrier((taken, *given_q, *kept_far, bias))[: 1 + chunks]
    taken_q = [permute(block, swap) for block in given_q]
    taken_far = [permute(gated, up[d]) for d in steps]
    blocks = [kept, taken]
    for pair in zip(kept_far, taken_far):
        blocks += pair
    row, advantages = advantages_of(parents, lengths, blocks, length, 2, log_rate)

    dq_own, dq_back, dkv_list = [], [], []
    for chunk in range(chunks):
        query_list = [kept_q[chunk], taken_q[chunk]]
        dq, dkv = attend(parents, advantages, bias, query_list, blocks, chunk)
        dq_own.append(dq[0])
        dq_back.append(dq[1])
        dkv_list.append(dkv)

    summands = []
    for dkv in dkv_list:
        arrived = [permute(dkv[d], down[d]) for d in steps[::-1]]
        summands.append([after(dkv[0], dq_own[-1])] + arrived)
    dq_back = [permute(block, swap) for block in dq_back]
    others = []
    for blocks in summands:
        total = sum(block[1].astype(jnp.float32) for block in blocks)
        others.append(permute(total.astype(jnp.bfloat16), swap))
    grad_q = join_queries(dq_own, dq_back)
    grad_k, grad_v = join_keys(others, summands)
    return grad_q, grad_k, grad_v, row[0]


def fetch_rows(spread, wanted):
    routed = jnp.take(spread, jnp.maximum(wanted, 0), axis=0)
    return lax.all_to_all(routed, "seg", split_axis=0, concat_axis=2, tiled=True)


def return_rows(grad_rows, wanted, total_segs):
    returned = lax.all_to_all(grad_rows, "seg", split_axis=2, concat_axis=0, tiled=True)
    piece_len = returned.shape[2]
    feature_len = returned.shape[3]
    routed_ids = wanted.reshape(-1)
    targets = jnp.where(routed_ids >= 0, routed_ids, total_segs)
    summed = jax.ops.segment_sum(
        returned.reshape(-1, piece_len * feature_len).astype(jnp.float32),
        targets,
        num_segments=total_segs + 1,
    )[:total_segs]
    return lax.all_to_all(
        summed.reshape(total_segs, piece_len, feature_len),
        "seg",
        split_axis=0,
        concat_axis=1,
        tiled=True,
    )


def routed_body(queries, direction, key_vectors, value_vectors, token_rows, parents, lengths, log_rate):
    total_segs = parents.shape[0]
    length, width = key_vectors.shape
    heads = width // HD
    own = lax.axis_index("seg")
    own_len = lax.dynamic_slice_in_dim(lengths, own, 1)[0]
    terms = jnp.concatenate(token_terms(log_rate, own_len, *token_rows), axis=1)
    terms = lax.all_gather(terms, "seg", axis=0, tiled=True)
    row, advantages = advantages_of(parents, lengths, [terms], length, 1, log_rate)
    bias = masks(parents, lengths, length, 1)
    flat = jnp.concatenate([key_vectors, value_vectors], axis=1)[None]
    spread = lax.all_to_all(flat, "seg", split_axis=1, concat_axis=0, tiled=True)
    chains = ancestors(parents, DEPTH - 1)
    arrived = fetch_rows(spread, chains)[0]
    slot_kv = jnp.concatenate([flat, arrived]).reshape(DEPTH, length, 2, heads, HD)
    slot_kv = jnp.transpose(slot_kv, (0, 3, 2, 1, 4)).reshape(DEPTH, -1, HD)
    kv_list = [slot_kv[slot] for slot in range(DEPTH)]
    (kept_q,) = pack_queries(queries, direction, 1, heads)
    dq_list, dkv_list = [], []
    for head in range(heads):
        dq, dkv = attend(parents, advantages, bias, [kept_q[head]], kv_list, head)
        dq_list.append(dq[0])
        dkv_list.append(jnp.concatenate(dkv))
    rows = jnp.transpose(jnp.stack(dkv_list), (1, 3, 2, 0, 4)).reshape(1, DEPTH, length, -1)
    summed = return_rows(rows[:, 1:], chains, total_segs)[0] + rows[0, 0].astype(jnp.float32)
    grad_keys = summed[:, :width].astype(jnp.bfloat16)
    grad_values = summed[:, width:].astype(jnp.bfloat16)
    return jnp.concatenate(dq_list, axis=1), grad_keys, grad_values, row[0]


def body(
    queries,
    key_vectors,
    value_vectors,
    direction,
    rewards,
    logprobs,
    ref_logprobs,
    value_est,
    parents,
    seg_lengths,
):
    groups = lax.axis_size("seg")
    assert parents.shape[0] == groups
    log_rate = math.log(LAMBDA_SEG) / rewards.shape[0]
    token_rows = [rewards[None], logprobs[None], ref_logprobs[None], value_est[None]]
    plan = paired_body if groups == PAIRED_GROUPS else routed_body
    return plan(
        queries, direction, key_vectors, value_vectors, token_rows, parents, seg_lengths, log_rate
    )


def solution(mesh):
    in_specs = (
        P(("grp", "seg"), "tp"),
        P(("grp", "seg"), "tp"),
        P(("grp", "seg"), "tp"),
        P(("grp", "seg"), "tp"),
        P(("grp", "seg")),
        P(("grp", "seg")),
        P(("grp", "seg")),
        P(("grp", "seg")),
        P("grp"),
        P("grp"),
    )
    out_specs = (
        P(("grp", "seg"), "tp"),
        P(("grp", "seg"), "tp"),
        P(("grp", "seg"), "tp"),
        P(("grp", "seg")),
    )
    return jax.shard_map(body, mesh=mesh, in_specs=in_specs, out_specs=out_specs, check_vma=False)
```

```python
import functools
import math

import jax
import jax.numpy as jnp
from jax import lax
from jax.experimental import pallas as pl
from jax.experimental.pallas import tpu as pltpu
from jax.sharding import PartitionSpec as P

HD = 128
DEPTH = 5
BETA = 0.1
LAMBDA_SEG = 0.7
PAIRED_GROUPS = 8
TERM_ROWS = 16
LOG2E = math.log2(math.e)
SMALL = pltpu.CompilerParams(vmem_limit_bytes=8 * 1024 * 1024)


def lookup(table_values, lookup_ids):
    matches = lookup_ids[..., None] == jnp.arange(table_values.shape[0], dtype=jnp.int32)
    return jnp.sum(jnp.where(matches, table_values, 0), axis=-1)


def ancestors(parents, count):
    current = jnp.arange(parents.shape[0], dtype=jnp.int32)
    chain_list = []
    for depth_step in range(count):
        parent_ids = lookup(parents, current)
        current = jnp.where(current >= 0, parent_ids, -1)
        chain_list.append(current)
    return jnp.stack(chain_list, axis=1)


def token_terms(log_rate, own_len, rewards, logprobs, ref_logprobs, values):
    positions = lax.broadcasted_iota(jnp.int32, rewards.shape, 1)
    later = jnp.concatenate([values[:, 1:], values[:, :1]], axis=1)
    later = jnp.where(positions + 1 < own_len, later, 0.0)
    deltas = jnp.where(
        positions < own_len, rewards - BETA * (logprobs - ref_logprobs) + later - values, 0.0
    )
    powers = jnp.exp(positions.astype(jnp.float32) * log_rate)
    first_local = jnp.sum(deltas * powers, axis=1, keepdims=True)
    firsts = jnp.where(positions == 0, first_local, jnp.where(positions == 1, values[:, :1], 0.0))
    return deltas, firsts


def split_float(value):
    parts = []
    for _ in range(3):
        part = value.astype(jnp.bfloat16)
        parts.append(part)
        value = value - part.astype(jnp.float32)
    return parts


def pack_kernel(
    log_rate,
    lengths_ref,
    k_ref,
    v_ref,
    rewards_ref,
    logprobs_ref,
    ref_logprobs_ref,
    values_ref,
    *out_refs,
):
    own = lax.axis_index("seg")
    length = k_ref.shape[0]
    parts = len(out_refs)
    heads = k_ref.shape[1] // HD // parts
    terms = token_terms(
        log_rate,
        lengths_ref[own],
        rewards_ref[...],
        logprobs_ref[...],
        ref_logprobs_ref[...],
        values_ref[...],
    )
    tail = [part.astype(jnp.float32) for x in terms for part in split_float(x)]
    tail.append(jnp.zeros((TERM_ROWS - len(tail), HD), jnp.float32))
    tail = jnp.concatenate(tail).astype(jnp.bfloat16)
    for step, out_ref in enumerate(out_refs):
        part = lax.rem(own + step, parts)
        for h in range(heads):
            columns = pl.ds(pl.multiple_of((part * heads + h) * HD, HD), HD)
            for plane, ref in enumerate((k_ref, v_ref)):
                first = (h * 2 + plane) * length
                out_ref[first : first + length, :] = ref[:, columns]
        out_ref[2 * heads * length :, :] = tail


def pack(lengths, k, v, token_rows, parts, log_rate):
    length, width = k.shape
    smem = pl.BlockSpec(memory_space=pltpu.SMEM)
    vmem = pl.BlockSpec(memory_space=pltpu.VMEM)
    heads = width // HD // parts
    assert length == HD
    block = jax.ShapeDtypeStruct((2 * heads * length + TERM_ROWS, HD), k.dtype)
    return pl.pallas_call(
        functools.partial(pack_kernel, log_rate),
        out_shape=(block,) * parts,
        in_specs=[smem] + [vmem] * 6,
        out_specs=(vmem,) * parts,
        cost_estimate=pl.CostEstimate(
            flops=length * 100, bytes_accessed=8 * length * width, transcendentals=length
        ),
        name="pack_keys_values",
    )(lengths, k, v, *token_rows)


def pack_queries_kernel(parts, q_ref, dir_ref, *out_refs):
    own = lax.axis_index("seg")
    chunks = len(out_refs) // parts
    heads = out_refs[0].shape[1]
    for index, out_ref in enumerate(out_refs):
        step, chunk = divmod(index, chunks)
        part = lax.rem(own + step, parts)
        for h in range(heads):
            column = (part * chunks + chunk) * heads + h
            columns = pl.ds(pl.multiple_of(column * HD, HD), HD)
            out_ref[0, h] = q_ref[:, columns]
            out_ref[1, h] = dir_ref[:, columns]


def pack_queries(q, direction, parts, chunks):
    length, width = q.shape
    vmem = pl.BlockSpec(memory_space=pltpu.VMEM)
    block = jax.ShapeDtypeStruct((2, width // HD // parts // chunks, length, HD), q.dtype)
    outs = pl.pallas_call(
        functools.partial(pack_queries_kernel, parts),
        out_shape=(block,) * (parts * chunks),
        in_specs=[vmem, vmem],
        out_specs=(vmem,) * (parts * chunks),
        cost_estimate=pl.CostEstimate(flops=0, bytes_accessed=8 * length * width, transcendentals=0),
        compiler_params=SMALL,
        name="pack_queries",
    )(q, direction)
    return [outs[step * chunks : (step + 1) * chunks] for step in range(parts)]


def parent_of(segment, parents_s):
    known = parents_s[jnp.maximum(segment, 0)]
    return jnp.where(segment >= 0, known, -1).astype(jnp.int32)


def segment_of(own, segs, i):
    part = lax.rem(own, segs)
    return own - part + lax.rem(part + i, segs)


def read_terms(ref):
    if ref.dtype == jnp.float32:
        length = ref.shape[1] // 2
        return ref[:, :length], ref[:, length:]
    tail = ref[ref.shape[0] - TERM_ROWS :, :].astype(jnp.float32)
    return tail[0:1] + tail[1:2] + tail[2:3], tail[3:4] + tail[4:5] + tail[5:6]


def prepare_kernel(log_rate, depth, parents_s, lengths_s, *refs):
    term_refs, (bias_ref, columns_ref, weights_ref) = refs[:-3], refs[-3:]
    segs, _, length = bias_ref.shape
    count = parents_s.shape[0]
    own = lax.axis_index("seg")

    row_id = lax.broadcasted_iota(jnp.int32, (count, count), 0)
    col_id = lax.broadcasted_iota(jnp.int32, (count, count), 1)
    seg_col = lax.broadcasted_iota(jnp.int32, (count, 1), 0)

    def to_col(row):
        return jnp.sum(jnp.where(row_id == col_id, row, 0.0), axis=1, keepdims=True)

    parent_row = jnp.full((1, count), -1, jnp.int32)
    lens_col = jnp.zeros((count, 1), jnp.int32)
    for seg in range(count):
        parent_row = jnp.where(col_id[:1] == seg, parents_s[seg], parent_row)
        lens_col = jnp.where(seg_col == seg, lengths_s[seg], lens_col)
    lens_col = lens_col.astype(jnp.float32)
    children = (parent_row == row_id).astype(jnp.float32)
    tree = children / jnp.maximum(jnp.sum(children, axis=1, keepdims=True), 1.0)
    factor = jnp.exp(lens_col * log_rate)
    last_factor = jnp.exp((lens_col - 1.0) * log_rate)

    u_id = lax.broadcasted_iota(jnp.int32, (length, length), 0)
    t_id = lax.broadcasted_iota(jnp.int32, (length, length), 1)
    offset = (t_id - u_id).astype(jnp.float32)
    discount = jnp.where(offset >= 0, jnp.exp(offset * log_rate), 0.0)
    t_col = lax.broadcasted_iota(jnp.int32, (length, 1), 0)
    lane = lax.broadcasted_iota(jnp.int32, (count, HD), 1)
    for i in range(segs):
        seg = segment_of(own, segs, i)
        seg_len = lengths_s[seg]
        deltas, _ = read_terms(term_refs[i])
        live = t_col < seg_len
        left = (seg_len - t_col).astype(jnp.float32)
        columns = (
            jnp.sum(discount * deltas, axis=1, keepdims=True),
            jnp.exp((left - 1.0) * log_rate),
            jnp.exp(left * log_rate),
        )
        for index, column in enumerate(columns):
            column = jnp.where(live, column, 0.0)
            columns_ref[i, index] = jnp.broadcast_to(column, (length, HD))

        row = jnp.sum(jnp.where(row_id == seg, tree, 0.0), axis=0, keepdims=True)
        value_col = col = total = to_col(row)
        for _ in range(depth):
            col = to_col(jnp.sum(col * factor * tree, axis=0, keepdims=True))
            total = total + col
        through = to_col(jnp.sum(total * last_factor * tree, axis=0, keepdims=True))
        weights_ref[i, 0] = jnp.where(lane == 1, value_col, 0.0)
        weights_ref[i, 1] = jnp.where(lane == 0, total, jnp.where(lane == 1, through, 0.0))

        ancestor = seg
        for slot in range(depth):
            if slot > 0:
                ancestor = parent_of(ancestor, parents_s)
            slot_len = jnp.where(ancestor >= 0, lengths_s[jnp.maximum(ancestor, 0)], 0)
            seen = u_id < slot_len
            if slot == 0:
                seen = jnp.logical_and(seen, u_id <= t_id)
            bias_ref[i, slot * length : (slot + 1) * length, :] = jnp.where(seen, 0.0, -1e30)


def prepare(parents, lengths, terms, length, log_rate):
    smem = pl.BlockSpec(memory_space=pltpu.SMEM)
    vmem = pl.BlockSpec(memory_space=pltpu.VMEM)
    segs, count = len(terms), parents.shape[0]
    return pl.pallas_call(
        functools.partial(prepare_kernel, log_rate, DEPTH),
        out_shape=(
            jax.ShapeDtypeStruct((segs, DEPTH * length, length), jnp.float32),
            jax.ShapeDtypeStruct((segs, 3, length, HD), jnp.float32),
            jax.ShapeDtypeStruct((segs, 2, count, HD), jnp.float32),
        ),
        in_specs=[smem] * 2 + [vmem] * len(terms),
        out_specs=(vmem,) * 3,
        cost_estimate=pl.CostEstimate(
            flops=20 * DEPTH * segs * length * length,
            bytes_accessed=4 * DEPTH * segs * length * length,
            transcendentals=length * length,
        ),
        compiler_params=SMALL,
        name="prepare",
    )(parents, lengths, *terms)


def advantage_kernel(columns_ref, weights_ref, *refs):
    term_refs, (row_ref, adv_ref) = refs[:-2], refs[-2:]
    segs, _, length, _ = columns_ref.shape
    count = weights_ref.shape[2]
    if len(term_refs) == 1:
        firsts = read_terms(term_refs[0])[1]
    else:
        own = lax.axis_index("seg")
        part, pair, pairs = lax.rem(own, segs), own // segs, count // segs
        seg_id = lax.broadcasted_iota(jnp.int32, (count, length), 0)
        firsts = jnp.zeros((count, length), jnp.float32)
        for index, ref in enumerate(term_refs):
            step, side = divmod(index, segs)
            seg = lax.rem(pair - step + pairs, pairs) * segs + lax.rem(part + side, segs)
            firsts = jnp.where(seg_id == seg, read_terms(ref)[1], firsts)
    for i in range(segs):
        later_value = jnp.sum(weights_ref[i, 0] * firsts, axis=(0, 1), keepdims=True)
        later_head = jnp.sum(weights_ref[i, 1] * firsts, axis=(0, 1), keepdims=True)
        advantage = (
            columns_ref[i, 0] + columns_ref[i, 1] * later_value + columns_ref[i, 2] * later_head
        )
        adv_ref[i] = advantage
        if i == 0:
            row_id = lax.broadcasted_iota(jnp.int32, advantage.shape, 0)
            col_id = lax.broadcasted_iota(jnp.int32, advantage.shape, 1)
            row_ref[...] = jnp.sum(
                jnp.where(row_id == col_id, advantage, 0.0), axis=0, keepdims=True
            )


def advantages_of(columns, weights, terms):
    vmem = pl.BlockSpec(memory_space=pltpu.VMEM)
    segs, _, length, _ = columns.shape
    return pl.pallas_call(
        advantage_kernel,
        out_shape=(
            jax.ShapeDtypeStruct((1, length), jnp.float32),
            jax.ShapeDtypeStruct((segs, length, HD), jnp.float32),
        ),
        in_specs=[vmem] * (2 + len(terms)),
        out_specs=(vmem,) * 2,
        cost_estimate=pl.CostEstimate(
            flops=10 * segs * length * HD, bytes_accessed=16 * segs * length * HD, transcendentals=0
        ),
        compiler_params=SMALL,
        name="advantages",
    )(columns, weights, *terms)


def attend_kernel(depth, chunk, segs, sources, group_size, *refs):
    parents_s, adv_ref, bias_ref = refs[:3]
    query_refs, kv_refs = refs[3 : 3 + segs], refs[3 + segs : 3 + segs + sources]
    kv_scr, p_scr, ds_scr, acc_scr = refs[-4:]
    refs = refs[3 + segs + sources : -4]
    steps = sources // segs
    dkv_refs, dq_refs = refs[-steps:], refs[-steps - segs : -steps]

    length = query_refs[0].shape[2]
    own = lax.axis_index("seg")
    for source in range(sources):
        for plane in range(2):
            rows = slice((2 * chunk + plane) * length, (2 * chunk + plane + 1) * length)
            kv_scr[source, plane] = kv_refs[source][rows, :]
    acc_scr[...] = jnp.zeros_like(acc_scr)

    scale = HD**-0.5
    contract_last = (((1,), (1,)), ((), ()))
    contract_first = (((0,), (0,)), ((), ()))
    for i in range(segs):
        ancestor = segment_of(own, segs, i)
        part = lax.rem(own, segs)
        chosen = []
        for slot in range(depth):
            if slot > 0:
                ancestor = parent_of(ancestor, parents_s)
            if segs == 1:
                chosen.append(slot)
            else:
                known = jnp.maximum(ancestor, 0)
                step = (own - part) // segs - known // segs
                turn = lax.rem(lax.rem(known, segs) - part + segs, segs)
                chosen.append(jnp.where(ancestor >= 0, step * segs + turn, 0))
        q_list = [query_refs[i][0, j] for j in range(group_size)]
        dir_list = [query_refs[i][1, j] for j in range(group_size)]
        do_list = [(adv_ref[i] * d.astype(jnp.float32)).astype(jnp.bfloat16) for d in dir_list]
        k_all = jnp.concatenate([kv_scr[s, 0] for s in chosen], axis=0)
        v_all = jnp.concatenate([kv_scr[s, 1] for s in chosen], axis=0)
        for j in range(group_size):
            columns = slice(j * length, (j + 1) * length)
            scores = lax.dot_general(
                k_all, q_list[j], contract_last, preferred_element_type=jnp.float32
            )
            scores = scores * (scale * LOG2E) + bias_ref[i]
            top = jnp.max(scores, axis=0, keepdims=True)
            unnorm = jnp.exp2(scores - top)
            prob = unnorm * (1.0 / jnp.sum(unnorm, axis=0, keepdims=True))
            prob_low = prob.astype(jnp.bfloat16)
            dprob = lax.dot_general(
                v_all, do_list[j], contract_last, preferred_element_type=jnp.float32
            )
            row_dot = jnp.sum(prob_low.astype(jnp.float32) * dprob, axis=0, keepdims=True)
            dscore = (prob * (dprob - row_dot)).astype(jnp.bfloat16)
            p_scr[:, columns] = prob_low
            ds_scr[:, columns] = dscore
        dscore_all = ds_scr[...]
        dq_t = lax.dot_general(
            k_all, dscore_all, contract_first, preferred_element_type=jnp.float32
        )
        for j in range(group_size):
            dq = jnp.transpose(dq_t[:, j * length : (j + 1) * length]) * scale
            dq_refs[i][:, j * HD : (j + 1) * HD] = dq.astype(jnp.bfloat16)
        q_all = jnp.concatenate(q_list, axis=0)
        do_all = jnp.concatenate(do_list, axis=0)
        dk_all = jnp.dot(dscore_all, q_all, preferred_element_type=jnp.float32) * scale
        dv_all = jnp.dot(p_scr[...], do_all, preferred_element_type=jnp.float32)
        for slot, s in enumerate(chosen):
            rows = slice(slot * length, (slot + 1) * length)
            acc_scr[s, 0] += dk_all[rows]
            acc_scr[s, 1] += dv_all[rows]
    for step in range(steps):
        for i in range(segs):
            dkv_refs[step][i] = acc_scr[step * segs + i].astype(jnp.bfloat16)


def attend(parents, advantages, bias, query_list, kv_list, chunk):
    segs, length = advantages.shape[:2]
    sources = len(kv_list)
    steps = sources // segs
    group_size = query_list[0].shape[1]
    width = group_size * HD
    keys = DEPTH * length
    smem = pl.BlockSpec(memory_space=pltpu.SMEM)
    vmem = pl.BlockSpec(memory_space=pltpu.VMEM)
    out_shape = [jax.ShapeDtypeStruct((length, width), jnp.bfloat16)] * segs
    out_shape += [jax.ShapeDtypeStruct((segs, 2, length, HD), jnp.bfloat16)] * steps
    outs = pl.pallas_call(
        functools.partial(attend_kernel, DEPTH, chunk, segs, sources, group_size),
        out_shape=out_shape,
        in_specs=[smem] + [vmem] * (2 + segs + sources),
        out_specs=[vmem] * len(out_shape),
        scratch_shapes=[
            pltpu.VMEM((sources, 2, length, HD), jnp.bfloat16),
            pltpu.VMEM((keys, width), jnp.bfloat16),
            pltpu.VMEM((keys, width), jnp.bfloat16),
            pltpu.VMEM((sources, 2, length, HD), jnp.float32),
        ],
        compiler_params=pltpu.CompilerParams(vmem_limit_bytes=16 * 1024 * 1024),
        cost_estimate=pl.CostEstimate(
            flops=5 * 2 * keys * length * width * segs,
            bytes_accessed=8 * 1024 * 1024,
            transcendentals=keys * width * segs,
        ),
        name="tree_attention_backward",
    )(parents, advantages, bias, *query_list, *kv_list)
    return outs[:segs], outs[segs:]


def join_queries_kernel(*refs):
    part = lax.rem(lax.axis_index("seg"), 2)
    refs, dq_ref = refs[:-1], refs[-1]
    chunks = len(refs) // 2
    width = refs[0].shape[1]
    for index, ref in enumerate(refs):
        side, chunk = divmod(index, chunks)
        where = part if side == 0 else 1 - part
        column = pl.multiple_of((where * chunks + chunk) * width, HD)
        dq_ref[:, pl.ds(column, width)] = ref[...]


def join_queries(own_list, other_list):
    chunks = len(own_list)
    length, width = own_list[0].shape
    vmem = pl.BlockSpec(memory_space=pltpu.VMEM)
    return pl.pallas_call(
        join_queries_kernel,
        out_shape=jax.ShapeDtypeStruct((length, 2 * chunks * width), jnp.bfloat16),
        in_specs=[vmem] * (2 * chunks),
        out_specs=vmem,
        cost_estimate=pl.CostEstimate(
            flops=0, bytes_accessed=8 * length * width * chunks, transcendentals=0
        ),
        compiler_params=SMALL,
        name="join_queries",
    )(*own_list, *other_list)


def join_keys_kernel(chunks, *refs):
    part = lax.rem(lax.axis_index("seg"), 2)
    other_refs, sum_refs = refs[:chunks], refs[chunks:-2]
    many = len(sum_refs) // chunks
    dk_ref, dv_ref = refs[-2:]
    for chunk in range(chunks):
        here = pl.ds(pl.multiple_of((part * chunks + chunk) * HD, HD), HD)
        there = pl.ds(pl.multiple_of(((1 - part) * chunks + chunk) * HD, HD), HD)
        for plane, out_ref in enumerate((dk_ref, dv_ref)):
            blocks = [ref[0, plane] for ref in sum_refs[chunk * many : (chunk + 1) * many]]
            total = sum(block.astype(jnp.float32) for block in blocks)
            out_ref[:, here] = total.astype(jnp.bfloat16)
            out_ref[:, there] = other_refs[chunk][plane]


def join_keys(others, summands):
    chunks = len(others)
    length = others[0].shape[1]
    vmem = pl.BlockSpec(memory_space=pltpu.VMEM)
    flat = [block for blocks in summands for block in blocks]
    out = jax.ShapeDtypeStruct((length, 2 * chunks * HD), jnp.bfloat16)
    return pl.pallas_call(
        functools.partial(join_keys_kernel, chunks),
        out_shape=(out, out),
        in_specs=[vmem] * (chunks + len(flat)),
        out_specs=(vmem, vmem),
        cost_estimate=pl.CostEstimate(
            flops=0, bytes_accessed=16 * length * HD * chunks, transcendentals=0
        ),
        compiler_params=SMALL,
        name="join_keys",
    )(*others, *flat)


def permute(array, pairs):
    return lax.ppermute(array, "seg", pairs)


def after(array, *earlier):
    return lax.optimization_barrier((array, *earlier))[0]


def paired_body(queries, direction, key_vectors, value_vectors, token_rows, parents, lengths, log_rate):
    groups = lax.axis_size("seg")
    length = queries.shape[0]
    chunks = key_vectors.shape[1] // HD // 2
    swap = [(i, i ^ 1) for i in range(groups)]
    climb = [(i, (i + 2) % groups) for i in range(groups)]
    steps = range(1, groups // 2)
    down = {d: [(i, (i - 2 * d) % groups) for i in range(groups)] for d in steps}

    kept, given = pack(lengths, key_vectors, value_vectors, token_rows, 2, log_rate)
    taken = permute(given, swap)
    chain = [kept, permute(kept, climb)]
    other = [after(taken, chain[1])]
    kept_q, given_q = pack_queries(after(queries, kept), direction, 2, chunks)
    taken_q = [permute(after(given_q[0], *other), swap)]
    bias, columns, weights = prepare(parents, lengths, [kept, other[0]], length, log_rate)
    for step in steps:
        if step + 1 in steps:
            chain.append(permute(chain[-1], climb))
        gate = [bias, taken_q[0]] if step == 1 else []
        other.append(after(permute(other[-1], climb), chain[-1], *gate))
    for block in given_q[1:]:
        taken_q.append(permute(after(block, taken_q[-1]), swap))
    blocks = [block for pair in zip(chain, other) for block in pair]
    row, advantages = advantages_of(columns, weights, blocks)

    dq_own, dq_back, dkv_list = [], [], []
    for chunk in range(chunks):
        query_list = [kept_q[chunk], taken_q[chunk]]
        dq, dkv = attend(parents, advantages, bias, query_list, blocks, chunk)
        dq_own.append(dq[0])
        dq_back.append(dq[1])
        dkv_list.append(dkv)

    summands = []
    for dkv in dkv_list:
        arrived = [permute(dkv[d], down[d]) for d in steps[::-1]]
        summands.append([after(dkv[0], dq_own[-1])] + arrived)
    dq_back = [permute(block, swap) for block in dq_back]
    others = []
    for blocks in summands:
        total = sum(block[1].astype(jnp.float32) for block in blocks)
        others.append(permute(total.astype(jnp.bfloat16), swap))
    grad_q = join_queries(dq_own, dq_back)
    grad_k, grad_v = join_keys(others, summands)
    return grad_q, grad_k, grad_v, row[0]


def fetch_rows(spread, wanted):
    routed = jnp.take(spread, jnp.maximum(wanted, 0), axis=0)
    return lax.all_to_all(routed, "seg", split_axis=0, concat_axis=2, tiled=True)


def return_rows(grad_rows, wanted, total_segs):
    returned = lax.all_to_all(grad_rows, "seg", split_axis=2, concat_axis=0, tiled=True)
    piece_len = returned.shape[2]
    feature_len = returned.shape[3]
    routed_ids = wanted.reshape(-1)
    targets = jnp.where(routed_ids >= 0, routed_ids, total_segs)
    summed = jax.ops.segment_sum(
        returned.reshape(-1, piece_len * feature_len).astype(jnp.float32),
        targets,
        num_segments=total_segs + 1,
    )[:total_segs]
    return lax.all_to_all(
        summed.reshape(total_segs, piece_len, feature_len),
        "seg",
        split_axis=0,
        concat_axis=1,
        tiled=True,
    )


def routed_body(queries, direction, key_vectors, value_vectors, token_rows, parents, lengths, log_rate):
    total_segs = parents.shape[0]
    length, width = key_vectors.shape
    heads = width // HD
    own = lax.axis_index("seg")
    own_len = lax.dynamic_slice_in_dim(lengths, own, 1)[0]
    terms = jnp.concatenate(token_terms(log_rate, own_len, *token_rows), axis=1)
    bias, columns, weights = prepare(parents, lengths, [terms], length, log_rate)
    terms = lax.all_gather(terms, "seg", axis=0, tiled=True)
    row, advantages = advantages_of(columns, weights, [terms])
    flat = jnp.concatenate([key_vectors, value_vectors], axis=1)[None]
    spread = lax.all_to_all(flat, "seg", split_axis=1, concat_axis=0, tiled=True)
    chains = ancestors(parents, DEPTH - 1)
    arrived = fetch_rows(spread, chains)[0]
    slot_kv = jnp.concatenate([flat, arrived]).reshape(DEPTH, length, 2, heads, HD)
    slot_kv = jnp.transpose(slot_kv, (0, 3, 2, 1, 4)).reshape(DEPTH, -1, HD)
    kv_list = [slot_kv[slot] for slot in range(DEPTH)]
    (kept_q,) = pack_queries(queries, direction, 1, heads)
    dq_list, dkv_list = [], []
    for head in range(heads):
        dq, dkv = attend(parents, advantages, bias, [kept_q[head]], kv_list, head)
        dq_list.append(dq[0])
        dkv_list.append(jnp.concatenate(dkv))
    rows = jnp.transpose(jnp.stack(dkv_list), (1, 3, 2, 0, 4)).reshape(1, DEPTH, length, -1)
    summed = return_rows(rows[:, 1:], chains, total_segs)[0] + rows[0, 0].astype(jnp.float32)
    grad_keys = summed[:, :width].astype(jnp.bfloat16)
    grad_values = summed[:, width:].astype(jnp.bfloat16)
    return jnp.concatenate(dq_list, axis=1), grad_keys, grad_values, row[0]


def body(
    queries,
    key_vectors,
    value_vectors,
    direction,
    rewards,
    logprobs,
    ref_logprobs,
    value_est,
    parents,
    seg_lengths,
):
    groups = lax.axis_size("seg")
    assert parents.shape[0] == groups
    log_rate = math.log(LAMBDA_SEG) / rewards.shape[0]
    token_rows = [rewards[None], logprobs[None], ref_logprobs[None], value_est[None]]
    plan = paired_body if groups == PAIRED_GROUPS else routed_body
    return plan(
        queries, direction, key_vectors, value_vectors, token_rows, parents, seg_lengths, log_rate
    )


def solution(mesh):
    in_specs = (
        P(("grp", "seg"), "tp"),
        P(("grp", "seg"), "tp"),
        P(("grp", "seg"), "tp"),
        P(("grp", "seg"), "tp"),
        P(("grp", "seg")),
        P(("grp", "seg")),
        P(("grp", "seg")),
        P(("grp", "seg")),
        P("grp"),
        P("grp"),
    )
    out_specs = (
        P(("grp", "seg"), "tp"),
        P(("grp", "seg"), "tp"),
        P(("grp", "seg"), "tp"),
        P(("grp", "seg")),
    )
    return jax.shard_map(body, mesh=mesh, in_specs=in_specs, out_specs=out_specs, check_vma=False)
```

```python
import functools
import math

import jax
import jax.numpy as jnp
from jax import lax
from jax.experimental import pallas as pl
from jax.experimental.pallas import tpu as pltpu
from jax.sharding import PartitionSpec as P

HD = 128
DEPTH = 5
BETA = 0.1
LAMBDA_SEG = 0.7
PAIRED_GROUPS = 8
TERM_ROWS = 16
LOG2E = math.log2(math.e)
SMALL = pltpu.CompilerParams(vmem_limit_bytes=8 * 1024 * 1024)


def lookup(table_values, lookup_ids):
    matches = lookup_ids[..., None] == jnp.arange(table_values.shape[0], dtype=jnp.int32)
    return jnp.sum(jnp.where(matches, table_values, 0), axis=-1)


def ancestors(parents, count):
    current = jnp.arange(parents.shape[0], dtype=jnp.int32)
    chain_list = []
    for depth_step in range(count):
        parent_ids = lookup(parents, current)
        current = jnp.where(current >= 0, parent_ids, -1)
        chain_list.append(current)
    return jnp.stack(chain_list, axis=1)


def token_terms(log_rate, own_len, rewards, logprobs, ref_logprobs, values):
    positions = lax.broadcasted_iota(jnp.int32, rewards.shape, 1)
    later = jnp.concatenate([values[:, 1:], values[:, :1]], axis=1)
    later = jnp.where(positions + 1 < own_len, later, 0.0)
    deltas = jnp.where(
        positions < own_len, rewards - BETA * (logprobs - ref_logprobs) + later - values, 0.0
    )
    powers = jnp.exp(positions.astype(jnp.float32) * log_rate)
    first_local = jnp.sum(deltas * powers, axis=1, keepdims=True)
    firsts = jnp.where(positions == 0, first_local, jnp.where(positions == 1, values[:, :1], 0.0))
    return deltas, firsts


def split_float(value):
    parts = []
    for _ in range(3):
        part = value.astype(jnp.bfloat16)
        parts.append(part)
        value = value - part.astype(jnp.float32)
    return parts


def pack_kernel(
    log_rate,
    lengths_ref,
    k_ref,
    v_ref,
    rewards_ref,
    logprobs_ref,
    ref_logprobs_ref,
    values_ref,
    *out_refs,
):
    own = lax.axis_index("seg")
    length = k_ref.shape[0]
    parts = len(out_refs)
    heads = k_ref.shape[1] // HD // parts
    terms = token_terms(
        log_rate,
        lengths_ref[own],
        rewards_ref[...],
        logprobs_ref[...],
        ref_logprobs_ref[...],
        values_ref[...],
    )
    tail = [part.astype(jnp.float32) for x in terms for part in split_float(x)]
    tail.append(jnp.zeros((TERM_ROWS - len(tail), HD), jnp.float32))
    tail = jnp.concatenate(tail).astype(jnp.bfloat16)
    for step, out_ref in enumerate(out_refs):
        part = lax.rem(own + step, parts)
        for h in range(heads):
            columns = pl.ds(pl.multiple_of((part * heads + h) * HD, HD), HD)
            for plane, ref in enumerate((k_ref, v_ref)):
                first = (h * 2 + plane) * length
                out_ref[first : first + length, :] = ref[:, columns]
        out_ref[2 * heads * length :, :] = tail


def pack(lengths, k, v, token_rows, parts, log_rate):
    length, width = k.shape
    smem = pl.BlockSpec(memory_space=pltpu.SMEM)
    vmem = pl.BlockSpec(memory_space=pltpu.VMEM)
    heads = width // HD // parts
    assert length == HD
    block = jax.ShapeDtypeStruct((2 * heads * length + TERM_ROWS, HD), k.dtype)
    return pl.pallas_call(
        functools.partial(pack_kernel, log_rate),
        out_shape=(block,) * parts,
        in_specs=[smem] + [vmem] * 6,
        out_specs=(vmem,) * parts,
        cost_estimate=pl.CostEstimate(
            flops=length * 100, bytes_accessed=8 * length * width, transcendentals=length
        ),
        name="pack_keys_values",
    )(lengths, k, v, *token_rows)


def pack_queries_kernel(parts, q_ref, dir_ref, *out_refs):
    own = lax.axis_index("seg")
    chunks = len(out_refs) // parts
    heads = out_refs[0].shape[1]
    for index, out_ref in enumerate(out_refs):
        step, chunk = divmod(index, chunks)
        part = lax.rem(own + step, parts)
        for h in range(heads):
            column = (part * chunks + chunk) * heads + h
            columns = pl.ds(pl.multiple_of(column * HD, HD), HD)
            out_ref[0, h] = q_ref[:, columns]
            out_ref[1, h] = dir_ref[:, columns]


def pack_queries(q, direction, parts, chunks):
    length, width = q.shape
    vmem = pl.BlockSpec(memory_space=pltpu.VMEM)
    block = jax.ShapeDtypeStruct((2, width // HD // parts // chunks, length, HD), q.dtype)
    outs = pl.pallas_call(
        functools.partial(pack_queries_kernel, parts),
        out_shape=(block,) * (parts * chunks),
        in_specs=[vmem, vmem],
        out_specs=(vmem,) * (parts * chunks),
        cost_estimate=pl.CostEstimate(flops=0, bytes_accessed=8 * length * width, transcendentals=0),
        compiler_params=SMALL,
        name="pack_queries",
    )(q, direction)
    return [outs[step * chunks : (step + 1) * chunks] for step in range(parts)]


def parent_of(segment, parents_s):
    known = parents_s[jnp.maximum(segment, 0)]
    return jnp.where(segment >= 0, known, -1).astype(jnp.int32)


def segment_of(own, segs, i):
    part = lax.rem(own, segs)
    return own - part + lax.rem(part + i, segs)


def read_terms(ref):
    if ref.dtype == jnp.float32:
        length = ref.shape[1] // 2
        return ref[:, :length], ref[:, length:]
    tail = ref[ref.shape[0] - TERM_ROWS :, :].astype(jnp.float32)
    return tail[0:1] + tail[1:2] + tail[2:3], tail[3:4] + tail[4:5] + tail[5:6]


def prepare_kernel(log_rate, depth, parents_s, lengths_s, *refs):
    term_refs, (bias_ref, columns_ref, weights_ref, firsts_ref) = refs[:-4], refs[-4:]
    segs, _, length = bias_ref.shape
    count = parents_s.shape[0]
    own = lax.axis_index("seg")
    firsts_ref[...] = jnp.zeros_like(firsts_ref)

    row_id = lax.broadcasted_iota(jnp.int32, (count, count), 0)
    col_id = lax.broadcasted_iota(jnp.int32, (count, count), 1)
    seg_col = lax.broadcasted_iota(jnp.int32, (count, 1), 0)

    def to_col(row):
        return jnp.sum(jnp.where(row_id == col_id, row, 0.0), axis=1, keepdims=True)

    parent_row = jnp.full((1, count), -1, jnp.int32)
    lens_col = jnp.zeros((count, 1), jnp.int32)
    for seg in range(count):
        parent_row = jnp.where(col_id[:1] == seg, parents_s[seg], parent_row)
        lens_col = jnp.where(seg_col == seg, lengths_s[seg], lens_col)
    lens_col = lens_col.astype(jnp.float32)
    children = (parent_row == row_id).astype(jnp.float32)
    tree = children / jnp.maximum(jnp.sum(children, axis=1, keepdims=True), 1.0)
    factor = jnp.exp(lens_col * log_rate)
    last_factor = jnp.exp((lens_col - 1.0) * log_rate)

    u_id = lax.broadcasted_iota(jnp.int32, (length, length), 0)
    t_id = lax.broadcasted_iota(jnp.int32, (length, length), 1)
    offset = (t_id - u_id).astype(jnp.float32)
    discount = jnp.where(offset >= 0, jnp.exp(offset * log_rate), 0.0)
    t_col = lax.broadcasted_iota(jnp.int32, (length, 1), 0)
    lane = lax.broadcasted_iota(jnp.int32, (count, HD), 1)
    for i in range(segs):
        seg = segment_of(own, segs, i)
        seg_len = lengths_s[seg]
        deltas, firsts = read_terms(term_refs[i])
        firsts_ref[...] += jnp.where(seg_col == seg, firsts, 0.0)
        live = t_col < seg_len
        left = (seg_len - t_col).astype(jnp.float32)
        columns = (
            jnp.sum(discount * deltas, axis=1, keepdims=True),
            jnp.exp((left - 1.0) * log_rate),
            jnp.exp(left * log_rate),
        )
        for index, column in enumerate(columns):
            column = jnp.where(live, column, 0.0)
            columns_ref[i, index] = jnp.broadcast_to(column, (length, HD))

        row = jnp.sum(jnp.where(row_id == seg, tree, 0.0), axis=0, keepdims=True)
        value_col = col = total = to_col(row)
        for _ in range(depth):
            col = to_col(jnp.sum(col * factor * tree, axis=0, keepdims=True))
            total = total + col
        through = to_col(jnp.sum(total * last_factor * tree, axis=0, keepdims=True))
        weights_ref[i, 0] = jnp.where(lane == 1, value_col, 0.0)
        weights_ref[i, 1] = jnp.where(lane == 0, total, jnp.where(lane == 1, through, 0.0))

        ancestor = seg
        for slot in range(depth):
            if slot > 0:
                ancestor = parent_of(ancestor, parents_s)
            slot_len = jnp.where(ancestor >= 0, lengths_s[jnp.maximum(ancestor, 0)], 0)
            seen = u_id < slot_len
            if slot == 0:
                seen = jnp.logical_and(seen, u_id <= t_id)
            bias_ref[i, slot * length : (slot + 1) * length, :] = jnp.where(seen, 0.0, -1e30)


def prepare(parents, lengths, terms, length, log_rate):
    smem = pl.BlockSpec(memory_space=pltpu.SMEM)
    vmem = pl.BlockSpec(memory_space=pltpu.VMEM)
    segs, count = len(terms), parents.shape[0]
    return pl.pallas_call(
        functools.partial(prepare_kernel, log_rate, DEPTH),
        out_shape=(
            jax.ShapeDtypeStruct((segs, DEPTH * length, length), jnp.float32),
            jax.ShapeDtypeStruct((segs, 3, length, HD), jnp.float32),
            jax.ShapeDtypeStruct((segs, 2, count, HD), jnp.float32),
            jax.ShapeDtypeStruct((count, length), jnp.float32),
        ),
        in_specs=[smem] * 2 + [vmem] * len(terms),
        out_specs=(vmem,) * 4,
        cost_estimate=pl.CostEstimate(
            flops=20 * DEPTH * segs * length * length,
            bytes_accessed=4 * DEPTH * segs * length * length,
            transcendentals=length * length,
        ),
        compiler_params=SMALL,
        name="prepare",
    )(parents, lengths, *terms)


def advantage_kernel(columns_ref, weights_ref, near_ref, far_ref, row_ref, adv_ref):
    firsts = near_ref[...] + far_ref[...]
    for i in range(columns_ref.shape[0]):
        later_value = jnp.sum(weights_ref[i, 0] * firsts, axis=(0, 1), keepdims=True)
        later_head = jnp.sum(weights_ref[i, 1] * firsts, axis=(0, 1), keepdims=True)
        advantage = (
            columns_ref[i, 0] + columns_ref[i, 1] * later_value + columns_ref[i, 2] * later_head
        )
        adv_ref[i] = advantage
        if i == 0:
            row_id = lax.broadcasted_iota(jnp.int32, advantage.shape, 0)
            col_id = lax.broadcasted_iota(jnp.int32, advantage.shape, 1)
            row_ref[...] = jnp.sum(
                jnp.where(row_id == col_id, advantage, 0.0), axis=0, keepdims=True
            )


def advantages_of(columns, weights, near, far):
    vmem = pl.BlockSpec(memory_space=pltpu.VMEM)
    segs, _, length, _ = columns.shape
    return pl.pallas_call(
        advantage_kernel,
        out_shape=(
            jax.ShapeDtypeStruct((1, length), jnp.float32),
            jax.ShapeDtypeStruct((segs, length, HD), jnp.float32),
        ),
        in_specs=[vmem] * 4,
        out_specs=(vmem,) * 2,
        cost_estimate=pl.CostEstimate(
            flops=10 * segs * length * HD, bytes_accessed=16 * segs * length * HD, transcendentals=0
        ),
        compiler_params=SMALL,
        name="advantages",
    )(columns, weights, near, far)


def attend_kernel(depth, chunk, segs, sources, group_size, *refs):
    parents_s, adv_ref, bias_ref = refs[:3]
    query_refs, kv_refs = refs[3 : 3 + segs], refs[3 + segs : 3 + segs + sources]
    kv_scr, p_scr, ds_scr, acc_scr = refs[-4:]
    refs = refs[3 + segs + sources : -4]
    steps = sources // segs
    dkv_refs, dq_refs = refs[-steps:], refs[-steps - segs : -steps]

    length = query_refs[0].shape[2]
    own = lax.axis_index("seg")
    for source in range(sources):
        for plane in range(2):
            rows = slice((2 * chunk + plane) * length, (2 * chunk + plane + 1) * length)
            kv_scr[source, plane] = kv_refs[source][rows, :]
    acc_scr[...] = jnp.zeros_like(acc_scr)

    scale = HD**-0.5
    contract_last = (((1,), (1,)), ((), ()))
    contract_first = (((0,), (0,)), ((), ()))
    for i in range(segs):
        ancestor = segment_of(own, segs, i)
        part = lax.rem(own, segs)
        chosen = []
        for slot in range(depth):
            if slot > 0:
                ancestor = parent_of(ancestor, parents_s)
            if segs == 1:
                chosen.append(slot)
            else:
                known = jnp.maximum(ancestor, 0)
                step = (own - part) // segs - known // segs
                turn = lax.rem(lax.rem(known, segs) - part + segs, segs)
                chosen.append(jnp.where(ancestor >= 0, step * segs + turn, 0))
        q_list = [query_refs[i][0, j] for j in range(group_size)]
        dir_list = [query_refs[i][1, j] for j in range(group_size)]
        do_list = [(adv_ref[i] * d.astype(jnp.float32)).astype(jnp.bfloat16) for d in dir_list]
        k_all = jnp.concatenate([kv_scr[s, 0] for s in chosen], axis=0)
        v_all = jnp.concatenate([kv_scr[s, 1] for s in chosen], axis=0)
        for j in range(group_size):
            columns = slice(j * length, (j + 1) * length)
            scores = lax.dot_general(
                k_all, q_list[j], contract_last, preferred_element_type=jnp.float32
            )
            scores = scores * (scale * LOG2E) + bias_ref[i]
            top = jnp.max(scores, axis=0, keepdims=True)
            unnorm = jnp.exp2(scores - top)
            prob = unnorm * (1.0 / jnp.sum(unnorm, axis=0, keepdims=True))
            prob_low = prob.astype(jnp.bfloat16)
            dprob = lax.dot_general(
                v_all, do_list[j], contract_last, preferred_element_type=jnp.float32
            )
            row_dot = jnp.sum(prob_low.astype(jnp.float32) * dprob, axis=0, keepdims=True)
            dscore = (prob * (dprob - row_dot)).astype(jnp.bfloat16)
            p_scr[:, columns] = prob_low
            ds_scr[:, columns] = dscore
        dscore_all = ds_scr[...]
        dq_t = lax.dot_general(
            k_all, dscore_all, contract_first, preferred_element_type=jnp.float32
        )
        for j in range(group_size):
            dq = jnp.transpose(dq_t[:, j * length : (j + 1) * length]) * scale
            dq_refs[i][:, j * HD : (j + 1) * HD] = dq.astype(jnp.bfloat16)
        q_all = jnp.concatenate(q_list, axis=0)
        do_all = jnp.concatenate(do_list, axis=0)
        dk_all = jnp.dot(dscore_all, q_all, preferred_element_type=jnp.float32) * scale
        dv_all = jnp.dot(p_scr[...], do_all, preferred_element_type=jnp.float32)
        for slot, s in enumerate(chosen):
            rows = slice(slot * length, (slot + 1) * length)
            acc_scr[s, 0] += dk_all[rows]
            acc_scr[s, 1] += dv_all[rows]
    for step in range(steps):
        for i in range(segs):
            dkv_refs[step][i] = acc_scr[step * segs + i].astype(jnp.bfloat16)


def attend(parents, advantages, bias, query_list, kv_list, chunk):
    segs, length = advantages.shape[:2]
    sources = len(kv_list)
    steps = sources // segs
    group_size = query_list[0].shape[1]
    width = group_size * HD
    keys = DEPTH * length
    smem = pl.BlockSpec(memory_space=pltpu.SMEM)
    vmem = pl.BlockSpec(memory_space=pltpu.VMEM)
    out_shape = [jax.ShapeDtypeStruct((length, width), jnp.bfloat16)] * segs
    out_shape += [jax.ShapeDtypeStruct((segs, 2, length, HD), jnp.bfloat16)] * steps
    outs = pl.pallas_call(
        functools.partial(attend_kernel, DEPTH, chunk, segs, sources, group_size),
        out_shape=out_shape,
        in_specs=[smem] + [vmem] * (2 + segs + sources),
        out_specs=[vmem] * len(out_shape),
        scratch_shapes=[
            pltpu.VMEM((sources, 2, length, HD), jnp.bfloat16),
            pltpu.VMEM((keys, width), jnp.bfloat16),
            pltpu.VMEM((keys, width), jnp.bfloat16),
            pltpu.VMEM((sources, 2, length, HD), jnp.float32),
        ],
        compiler_params=pltpu.CompilerParams(vmem_limit_bytes=16 * 1024 * 1024),
        cost_estimate=pl.CostEstimate(
            flops=5 * 2 * keys * length * width * segs,
            bytes_accessed=8 * 1024 * 1024,
            transcendentals=keys * width * segs,
        ),
        name="tree_attention_backward",
    )(parents, advantages, bias, *query_list, *kv_list)
    return outs[:segs], outs[segs:]


def join_queries_kernel(*refs):
    part = lax.rem(lax.axis_index("seg"), 2)
    refs, dq_ref = refs[:-1], refs[-1]
    chunks = len(refs) // 2
    width = refs[0].shape[1]
    for index, ref in enumerate(refs):
        side, chunk = divmod(index, chunks)
        where = part if side == 0 else 1 - part
        column = pl.multiple_of((where * chunks + chunk) * width, HD)
        dq_ref[:, pl.ds(column, width)] = ref[...]


def join_queries(own_list, other_list):
    chunks = len(own_list)
    length, width = own_list[0].shape
    vmem = pl.BlockSpec(memory_space=pltpu.VMEM)
    return pl.pallas_call(
        join_queries_kernel,
        out_shape=jax.ShapeDtypeStruct((length, 2 * chunks * width), jnp.bfloat16),
        in_specs=[vmem] * (2 * chunks),
        out_specs=vmem,
        cost_estimate=pl.CostEstimate(
            flops=0, bytes_accessed=8 * length * width * chunks, transcendentals=0
        ),
        compiler_params=SMALL,
        name="join_queries",
    )(*own_list, *other_list)


def join_keys_kernel(chunks, *refs):
    part = lax.rem(lax.axis_index("seg"), 2)
    other_refs, sum_refs = refs[:chunks], refs[chunks:-2]
    many = len(sum_refs) // chunks
    dk_ref, dv_ref = refs[-2:]
    for chunk in range(chunks):
        here = pl.ds(pl.multiple_of((part * chunks + chunk) * HD, HD), HD)
        there = pl.ds(pl.multiple_of(((1 - part) * chunks + chunk) * HD, HD), HD)
        for plane, out_ref in enumerate((dk_ref, dv_ref)):
            blocks = [ref[0, plane] for ref in sum_refs[chunk * many : (chunk + 1) * many]]
            total = sum(block.astype(jnp.float32) for block in blocks)
            out_ref[:, here] = total.astype(jnp.bfloat16)
            out_ref[:, there] = other_refs[chunk][plane]


def join_keys(others, summands):
    chunks = len(others)
    length = others[0].shape[1]
    vmem = pl.BlockSpec(memory_space=pltpu.VMEM)
    flat = [block for blocks in summands for block in blocks]
    out = jax.ShapeDtypeStruct((length, 2 * chunks * HD), jnp.bfloat16)
    return pl.pallas_call(
        functools.partial(join_keys_kernel, chunks),
        out_shape=(out, out),
        in_specs=[vmem] * (chunks + len(flat)),
        out_specs=(vmem, vmem),
        cost_estimate=pl.CostEstimate(
            flops=0, bytes_accessed=16 * length * HD * chunks, transcendentals=0
        ),
        compiler_params=SMALL,
        name="join_keys",
    )(*others, *flat)


def permute(array, pairs):
    return lax.ppermute(array, "seg", pairs)


def after(array, *earlier):
    return lax.optimization_barrier((array, *earlier))[0]


def paired_body(queries, direction, key_vectors, value_vectors, token_rows, parents, lengths, log_rate):
    groups = lax.axis_size("seg")
    length = queries.shape[0]
    chunks = key_vectors.shape[1] // HD // 2
    steps = range(1, groups // 2)
    swap = [(i, i ^ 1) for i in range(groups)]
    down = {d: [(i, i - 2 * d) for i in range(2 * d, groups)] for d in steps}

    def climb(block, step):
        return permute(block, [(i, i + 2) for i in range(2 * step - 2, groups - 2)])

    kept, given = pack(lengths, key_vectors, value_vectors, token_rows, 2, log_rate)
    taken = permute(given, swap)
    chain = [kept, climb(kept, 1)]
    other = [after(taken, chain[1])]
    kept_q, given_q = pack_queries(after(queries, kept), direction, 2, chunks)
    bias, columns, weights, firsts = prepare(parents, lengths, [kept, taken], length, log_rate)
    firsts = firsts + permute(firsts, down[1])
    row, advantages = advantages_of(columns, weights, firsts, permute(firsts, down[2]))
    taken_q = [permute(after(given_q[0], *other), swap)]
    for step in steps:
        if step + 1 in steps:
            chain.append(climb(chain[-1], step + 1))
        gate = {1: [firsts, taken_q[0]], 2: [advantages]}.get(step, [])
        other.append(after(climb(other[-1], step), chain[-1], *gate))
    for block in given_q[1:]:
        taken_q.append(permute(after(block, taken_q[-1]), swap))
    blocks = [block for pair in zip(chain, other) for block in pair]

    dq_own, dq_back, dkv_list = [], [], []
    for chunk in range(chunks):
        query_list = [kept_q[chunk], taken_q[chunk]]
        dq, dkv = attend(parents, advantages, bias, query_list, blocks, chunk)
        dq_own.append(dq[0])
        dq_back.append(dq[1])
        dkv_list.append(dkv)

    summands = []
    for dkv in dkv_list:
        arrived = [permute(dkv[d], down[d]) for d in steps[::-1]]
        summands.append([after(dkv[0], dq_own[-1])] + arrived)
    dq_back = [permute(block, swap) for block in dq_back]
    others = []
    for blocks in summands:
        total = sum(block[1].astype(jnp.float32) for block in blocks)
        others.append(permute(total.astype(jnp.bfloat16), swap))
    grad_q = join_queries(dq_own, dq_back)
    grad_k, grad_v = join_keys(others, summands)
    return grad_q, grad_k, grad_v, row[0]


def fetch_rows(spread, wanted):
    routed = jnp.take(spread, jnp.maximum(wanted, 0), axis=0)
    return lax.all_to_all(routed, "seg", split_axis=0, concat_axis=2, tiled=True)


def return_rows(grad_rows, wanted, total_segs):
    returned = lax.all_to_all(grad_rows, "seg", split_axis=2, concat_axis=0, tiled=True)
    piece_len = returned.shape[2]
    feature_len = returned.shape[3]
    routed_ids = wanted.reshape(-1)
    targets = jnp.where(routed_ids >= 0, routed_ids, total_segs)
    summed = jax.ops.segment_sum(
        returned.reshape(-1, piece_len * feature_len).astype(jnp.float32),
        targets,
        num_segments=total_segs + 1,
    )[:total_segs]
    return lax.all_to_all(
        summed.reshape(total_segs, piece_len, feature_len),
        "seg",
        split_axis=0,
        concat_axis=1,
        tiled=True,
    )


def routed_body(queries, direction, key_vectors, value_vectors, token_rows, parents, lengths, log_rate):
    total_segs = parents.shape[0]
    length, width = key_vectors.shape
    heads = width // HD
    own = lax.axis_index("seg")
    own_len = lax.dynamic_slice_in_dim(lengths, own, 1)[0]
    terms = jnp.concatenate(token_terms(log_rate, own_len, *token_rows), axis=1)
    bias, columns, weights, firsts = prepare(parents, lengths, [terms], length, log_rate)
    firsts = lax.all_gather(
        lax.dynamic_slice_in_dim(firsts, own, 1), "seg", axis=0, tiled=True
    )
    row, advantages = advantages_of(columns, weights, firsts, jnp.zeros_like(firsts))
    flat = jnp.concatenate([key_vectors, value_vectors], axis=1)[None]
    spread = lax.all_to_all(flat, "seg", split_axis=1, concat_axis=0, tiled=True)
    chains = ancestors(parents, DEPTH - 1)
    arrived = fetch_rows(spread, chains)[0]
    slot_kv = jnp.concatenate([flat, arrived]).reshape(DEPTH, length, 2, heads, HD)
    slot_kv = jnp.transpose(slot_kv, (0, 3, 2, 1, 4)).reshape(DEPTH, -1, HD)
    kv_list = [slot_kv[slot] for slot in range(DEPTH)]
    (kept_q,) = pack_queries(queries, direction, 1, heads)
    dq_list, dkv_list = [], []
    for head in range(heads):
        dq, dkv = attend(parents, advantages, bias, [kept_q[head]], kv_list, head)
        dq_list.append(dq[0])
        dkv_list.append(jnp.concatenate(dkv))
    rows = jnp.transpose(jnp.stack(dkv_list), (1, 3, 2, 0, 4)).reshape(1, DEPTH, length, -1)
    summed = return_rows(rows[:, 1:], chains, total_segs)[0] + rows[0, 0].astype(jnp.float32)
    grad_keys = summed[:, :width].astype(jnp.bfloat16)
    grad_values = summed[:, width:].astype(jnp.bfloat16)
    return jnp.concatenate(dq_list, axis=1), grad_keys, grad_values, row[0]


def body(
    queries,
    key_vectors,
    value_vectors,
    direction,
    rewards,
    logprobs,
    ref_logprobs,
    value_est,
    parents,
    seg_lengths,
):
    groups = lax.axis_size("seg")
    assert parents.shape[0] == groups
    log_rate = math.log(LAMBDA_SEG) / rewards.shape[0]
    token_rows = [rewards[None], logprobs[None], ref_logprobs[None], value_est[None]]
    plan = paired_body if groups == PAIRED_GROUPS else routed_body
    return plan(
        queries, direction, key_vectors, value_vectors, token_rows, parents, seg_lengths, log_rate
    )


def solution(mesh):
    in_specs = (
        P(("grp", "seg"), "tp"),
        P(("grp", "seg"), "tp"),
        P(("grp", "seg"), "tp"),
        P(("grp", "seg"), "tp"),
        P(("grp", "seg")),
        P(("grp", "seg")),
        P(("grp", "seg")),
        P(("grp", "seg")),
        P("grp"),
        P("grp"),
    )
    out_specs = (
        P(("grp", "seg"), "tp"),
        P(("grp", "seg"), "tp"),
        P(("grp", "seg"), "tp"),
        P(("grp", "seg")),
    )
    return jax.shard_map(body, mesh=mesh, in_specs=in_specs, out_specs=out_specs, check_vma=False)
```

```python
import functools
import math

import jax
import jax.numpy as jnp
from jax import lax
from jax.experimental import pallas as pl
from jax.experimental.pallas import tpu as pltpu
from jax.sharding import PartitionSpec as P

HD = 128
DEPTH = 5
BETA = 0.1
LAMBDA_SEG = 0.7
PAIRED_GROUPS = 8
TERM_ROWS = 16
LOG2E = math.log2(math.e)
SMALL = pltpu.CompilerParams(vmem_limit_bytes=8 * 1024 * 1024)


def lookup(table_values, lookup_ids):
    matches = lookup_ids[..., None] == jnp.arange(table_values.shape[0], dtype=jnp.int32)
    return jnp.sum(jnp.where(matches, table_values, 0), axis=-1)


def ancestors(parents, count):
    current = jnp.arange(parents.shape[0], dtype=jnp.int32)
    chain_list = []
    for depth_step in range(count):
        parent_ids = lookup(parents, current)
        current = jnp.where(current >= 0, parent_ids, -1)
        chain_list.append(current)
    return jnp.stack(chain_list, axis=1)


def token_terms(log_rate, own_len, rewards, logprobs, ref_logprobs, values):
    positions = lax.broadcasted_iota(jnp.int32, rewards.shape, 1)
    later = jnp.concatenate([values[:, 1:], values[:, :1]], axis=1)
    later = jnp.where(positions + 1 < own_len, later, 0.0)
    deltas = jnp.where(
        positions < own_len, rewards - BETA * (logprobs - ref_logprobs) + later - values, 0.0
    )
    powers = jnp.exp(positions.astype(jnp.float32) * log_rate)
    first_local = jnp.sum(deltas * powers, axis=1, keepdims=True)
    firsts = jnp.where(positions == 0, first_local, jnp.where(positions == 1, values[:, :1], 0.0))
    return deltas, firsts


def split_float(value):
    parts = []
    for _ in range(3):
        part = value.astype(jnp.bfloat16)
        parts.append(part)
        value = value - part.astype(jnp.float32)
    return parts


def pack_kernel(
    log_rate,
    lengths_ref,
    k_ref,
    v_ref,
    rewards_ref,
    logprobs_ref,
    ref_logprobs_ref,
    values_ref,
    *out_refs,
):
    own = lax.axis_index("seg")
    length = k_ref.shape[0]
    parts = len(out_refs)
    heads = k_ref.shape[1] // HD // parts
    terms = token_terms(
        log_rate,
        lengths_ref[own],
        rewards_ref[...],
        logprobs_ref[...],
        ref_logprobs_ref[...],
        values_ref[...],
    )
    tail = [part.astype(jnp.float32) for x in terms for part in split_float(x)]
    tail.append(jnp.zeros((TERM_ROWS - len(tail), HD), jnp.float32))
    tail = jnp.concatenate(tail).astype(jnp.bfloat16)
    for step, out_ref in enumerate(out_refs):
        part = lax.rem(own + step, parts)
        for h in range(heads):
            columns = pl.ds(pl.multiple_of((part * heads + h) * HD, HD), HD)
            for plane, ref in enumerate((k_ref, v_ref)):
                first = (h * 2 + plane) * length
                out_ref[first : first + length, :] = ref[:, columns]
        out_ref[2 * heads * length :, :] = tail


def pack(lengths, k, v, token_rows, parts, log_rate):
    length, width = k.shape
    smem = pl.BlockSpec(memory_space=pltpu.SMEM)
    vmem = pl.BlockSpec(memory_space=pltpu.VMEM)
    heads = width // HD // parts
    assert length == HD
    block = jax.ShapeDtypeStruct((2 * heads * length + TERM_ROWS, HD), k.dtype)
    return pl.pallas_call(
        functools.partial(pack_kernel, log_rate),
        out_shape=(block,) * parts,
        in_specs=[smem] + [vmem] * 6,
        out_specs=(vmem,) * parts,
        cost_estimate=pl.CostEstimate(
            flops=length * 100, bytes_accessed=8 * length * width, transcendentals=length
        ),
        name="pack_keys_values",
    )(lengths, k, v, *token_rows)


def pack_queries_kernel(parts, q_ref, dir_ref, *out_refs):
    own = lax.axis_index("seg")
    chunks = len(out_refs) // parts
    heads = out_refs[0].shape[1]
    for index, out_ref in enumerate(out_refs):
        step, chunk = divmod(index, chunks)
        part = lax.rem(own + step, parts)
        for h in range(heads):
            column = (part * chunks + chunk) * heads + h
            columns = pl.ds(pl.multiple_of(column * HD, HD), HD)
            out_ref[0, h] = q_ref[:, columns]
            out_ref[1, h] = dir_ref[:, columns]


def pack_queries(q, direction, parts, chunks):
    length, width = q.shape
    vmem = pl.BlockSpec(memory_space=pltpu.VMEM)
    block = jax.ShapeDtypeStruct((2, width // HD // parts // chunks, length, HD), q.dtype)
    outs = pl.pallas_call(
        functools.partial(pack_queries_kernel, parts),
        out_shape=(block,) * (parts * chunks),
        in_specs=[vmem, vmem],
        out_specs=(vmem,) * (parts * chunks),
        cost_estimate=pl.CostEstimate(flops=0, bytes_accessed=8 * length * width, transcendentals=0),
        compiler_params=SMALL,
        name="pack_queries",
    )(q, direction)
    return [outs[step * chunks : (step + 1) * chunks] for step in range(parts)]


def parent_of(segment, parents_s):
    known = parents_s[jnp.maximum(segment, 0)]
    return jnp.where(segment >= 0, known, -1).astype(jnp.int32)


def ring_place(pair):
    return jnp.where(pair >= 2, 5 - pair, pair)


def segment_of(own, segs, i):
    part = lax.rem(own, segs)
    return own - part + lax.rem(part + i, segs)


def read_terms(ref):
    if ref.dtype == jnp.float32:
        length = ref.shape[1] // 2
        return ref[:, :length], ref[:, length:]
    tail = ref[ref.shape[0] - TERM_ROWS :, :].astype(jnp.float32)
    return tail[0:1] + tail[1:2] + tail[2:3], tail[3:4] + tail[4:5] + tail[5:6]


def prepare_kernel(log_rate, depth, parents_s, lengths_s, *refs):
    term_refs, (bias_ref, columns_ref, weights_ref) = refs[:-3], refs[-3:]
    segs, _, length = bias_ref.shape
    count = parents_s.shape[0]
    own = lax.axis_index("seg")

    row_id = lax.broadcasted_iota(jnp.int32, (count, count), 0)
    col_id = lax.broadcasted_iota(jnp.int32, (count, count), 1)
    seg_col = lax.broadcasted_iota(jnp.int32, (count, 1), 0)

    def to_col(row):
        return jnp.sum(jnp.where(row_id == col_id, row, 0.0), axis=1, keepdims=True)

    parent_row = jnp.full((1, count), -1, jnp.int32)
    lens_col = jnp.zeros((count, 1), jnp.int32)
    for seg in range(count):
        parent_row = jnp.where(col_id[:1] == seg, parents_s[seg], parent_row)
        lens_col = jnp.where(seg_col == seg, lengths_s[seg], lens_col)
    lens_col = lens_col.astype(jnp.float32)
    children = (parent_row == row_id).astype(jnp.float32)
    tree = children / jnp.maximum(jnp.sum(children, axis=1, keepdims=True), 1.0)
    factor = jnp.exp(lens_col * log_rate)
    last_factor = jnp.exp((lens_col - 1.0) * log_rate)

    u_id = lax.broadcasted_iota(jnp.int32, (length, length), 0)
    t_id = lax.broadcasted_iota(jnp.int32, (length, length), 1)
    offset = (t_id - u_id).astype(jnp.float32)
    discount = jnp.where(offset >= 0, jnp.exp(offset * log_rate), 0.0)
    t_col = lax.broadcasted_iota(jnp.int32, (length, 1), 0)
    lane = lax.broadcasted_iota(jnp.int32, (count, HD), 1)
    for i in range(segs):
        seg = segment_of(own, segs, i)
        seg_len = lengths_s[seg]
        deltas, _ = read_terms(term_refs[i])
        live = t_col < seg_len
        left = (seg_len - t_col).astype(jnp.float32)
        columns = (
            jnp.sum(discount * deltas, axis=1, keepdims=True),
            jnp.exp((left - 1.0) * log_rate),
            jnp.exp(left * log_rate),
        )
        for index, column in enumerate(columns):
            column = jnp.where(live, column, 0.0)
            columns_ref[i, index] = jnp.broadcast_to(column, (length, HD))

        row = jnp.sum(jnp.where(row_id == seg, tree, 0.0), axis=0, keepdims=True)
        value_col = col = total = to_col(row)
        for _ in range(depth):
            col = to_col(jnp.sum(col * factor * tree, axis=0, keepdims=True))
            total = total + col
        through = to_col(jnp.sum(total * last_factor * tree, axis=0, keepdims=True))
        weights_ref[i, 0] = jnp.where(lane == 1, value_col, 0.0)
        weights_ref[i, 1] = jnp.where(lane == 0, total, jnp.where(lane == 1, through, 0.0))

        ancestor = seg
        for slot in range(depth):
            if slot > 0:
                ancestor = parent_of(ancestor, parents_s)
            slot_len = jnp.where(ancestor >= 0, lengths_s[jnp.maximum(ancestor, 0)], 0)
            seen = u_id < slot_len
            if slot == 0:
                seen = jnp.logical_and(seen, u_id <= t_id)
            bias_ref[i, slot * length : (slot + 1) * length, :] = jnp.where(seen, 0.0, -1e30)


def prepare(parents, lengths, terms, length, log_rate):
    smem = pl.BlockSpec(memory_space=pltpu.SMEM)
    vmem = pl.BlockSpec(memory_space=pltpu.VMEM)
    segs, count = len(terms), parents.shape[0]
    return pl.pallas_call(
        functools.partial(prepare_kernel, log_rate, DEPTH),
        out_shape=(
            jax.ShapeDtypeStruct((segs, DEPTH * length, length), jnp.float32),
            jax.ShapeDtypeStruct((segs, 3, length, HD), jnp.float32),
            jax.ShapeDtypeStruct((segs, 2, count, HD), jnp.float32),
        ),
        in_specs=[smem] * 2 + [vmem] * len(terms),
        out_specs=(vmem,) * 3,
        cost_estimate=pl.CostEstimate(
            flops=20 * DEPTH * segs * length * length,
            bytes_accessed=4 * DEPTH * segs * length * length,
            transcendentals=length * length,
        ),
        compiler_params=SMALL,
        name="prepare",
    )(parents, lengths, *terms)


def advantage_kernel(columns_ref, weights_ref, *refs):
    term_refs, (row_ref, adv_ref) = refs[:-2], refs[-2:]
    segs, _, length, _ = columns_ref.shape
    count = weights_ref.shape[2]
    if len(term_refs) == 1:
        firsts = read_terms(term_refs[0])[1]
    else:
        own = lax.axis_index("seg")
        part, pair, pairs = lax.rem(own, segs), own // segs, count // segs
        seg_id = lax.broadcasted_iota(jnp.int32, (count, length), 0)
        firsts = jnp.zeros((count, length), jnp.float32)
        for index, ref in enumerate(term_refs):
            step, side = divmod(index, segs)
            place = lax.rem(ring_place(pair) - step + pairs, pairs)
            seg = ring_place(place) * segs + lax.rem(part + side, segs)
            firsts = jnp.where(seg_id == seg, read_terms(ref)[1], firsts)
    for i in range(segs):
        later_value = jnp.sum(weights_ref[i, 0] * firsts, axis=(0, 1), keepdims=True)
        later_head = jnp.sum(weights_ref[i, 1] * firsts, axis=(0, 1), keepdims=True)
        advantage = (
            columns_ref[i, 0] + columns_ref[i, 1] * later_value + columns_ref[i, 2] * later_head
        )
        adv_ref[i] = advantage
        if i == 0:
            row_id = lax.broadcasted_iota(jnp.int32, advantage.shape, 0)
            col_id = lax.broadcasted_iota(jnp.int32, advantage.shape, 1)
            row_ref[...] = jnp.sum(
                jnp.where(row_id == col_id, advantage, 0.0), axis=0, keepdims=True
            )


def advantages_of(columns, weights, terms):
    vmem = pl.BlockSpec(memory_space=pltpu.VMEM)
    segs, _, length, _ = columns.shape
    return pl.pallas_call(
        advantage_kernel,
        out_shape=(
            jax.ShapeDtypeStruct((1, length), jnp.float32),
            jax.ShapeDtypeStruct((segs, length, HD), jnp.float32),
        ),
        in_specs=[vmem] * (2 + len(terms)),
        out_specs=(vmem,) * 2,
        cost_estimate=pl.CostEstimate(
            flops=10 * segs * length * HD, bytes_accessed=16 * segs * length * HD, transcendentals=0
        ),
        compiler_params=SMALL,
        name="advantages",
    )(columns, weights, *terms)


def attend_kernel(depth, chunk, segs, sources, group_size, *refs):
    parents_s, adv_ref, bias_ref = refs[:3]
    query_refs, kv_refs = refs[3 : 3 + segs], refs[3 + segs : 3 + segs + sources]
    kv_scr, p_scr, ds_scr, acc_scr = refs[-4:]
    refs = refs[3 + segs + sources : -4]
    steps = sources // segs
    dkv_refs, dq_refs = refs[-steps:], refs[-steps - segs : -steps]

    length = query_refs[0].shape[2]
    own = lax.axis_index("seg")
    for source in range(sources):
        for plane in range(2):
            rows = slice((2 * chunk + plane) * length, (2 * chunk + plane + 1) * length)
            kv_scr[source, plane] = kv_refs[source][rows, :]
    acc_scr[...] = jnp.zeros_like(acc_scr)

    scale = HD**-0.5
    contract_last = (((1,), (1,)), ((), ()))
    contract_first = (((0,), (0,)), ((), ()))
    for i in range(segs):
        ancestor = segment_of(own, segs, i)
        part = lax.rem(own, segs)
        chosen = []
        for slot in range(depth):
            if slot > 0:
                ancestor = parent_of(ancestor, parents_s)
            if segs == 1:
                chosen.append(slot)
            else:
                known = jnp.maximum(ancestor, 0)
                step = ring_place((own - part) // segs) - ring_place(known // segs)
                step = lax.rem(step + sources // segs, sources // segs)
                turn = lax.rem(lax.rem(known, segs) - part + segs, segs)
                chosen.append(jnp.where(ancestor >= 0, step * segs + turn, 0))
        q_list = [query_refs[i][0, j] for j in range(group_size)]
        dir_list = [query_refs[i][1, j] for j in range(group_size)]
        do_list = [(adv_ref[i] * d.astype(jnp.float32)).astype(jnp.bfloat16) for d in dir_list]
        k_all = jnp.concatenate([kv_scr[s, 0] for s in chosen], axis=0)
        v_all = jnp.concatenate([kv_scr[s, 1] for s in chosen], axis=0)
        q_all = jnp.concatenate(q_list, axis=0)
        do_all = jnp.concatenate(do_list, axis=0)
        all_scores = lax.dot_general(
            k_all, q_all, contract_last, preferred_element_type=jnp.float32
        )
        all_dprob = lax.dot_general(
            v_all, do_all, contract_last, preferred_element_type=jnp.float32
        )
        for j in range(group_size):
            columns = slice(j * length, (j + 1) * length)
            scores = all_scores[:, columns] * (scale * LOG2E) + bias_ref[i]
            top = jnp.max(scores, axis=0, keepdims=True)
            unnorm = jnp.exp2(scores - top)
            prob = unnorm * (1.0 / jnp.sum(unnorm, axis=0, keepdims=True))
            prob_low = prob.astype(jnp.bfloat16)
            dprob = all_dprob[:, columns]
            row_dot = jnp.sum(prob_low.astype(jnp.float32) * dprob, axis=0, keepdims=True)
            dscore = (prob * (dprob - row_dot)).astype(jnp.bfloat16)
            p_scr[:, columns] = prob_low
            ds_scr[:, columns] = dscore
        dscore_all = ds_scr[...]
        dq_t = lax.dot_general(
            k_all, dscore_all, contract_first, preferred_element_type=jnp.float32
        )
        for j in range(group_size):
            dq = jnp.transpose(dq_t[:, j * length : (j + 1) * length]) * scale
            dq_refs[i][:, j * HD : (j + 1) * HD] = dq.astype(jnp.bfloat16)
        dk_all = jnp.dot(dscore_all, q_all, preferred_element_type=jnp.float32) * scale
        dv_all = jnp.dot(p_scr[...], do_all, preferred_element_type=jnp.float32)
        for slot, s in enumerate(chosen):
            rows = slice(slot * length, (slot + 1) * length)
            acc_scr[s, 0] += dk_all[rows]
            acc_scr[s, 1] += dv_all[rows]
    for step in range(steps):
        for i in range(segs):
            dkv_refs[step][i] = acc_scr[step * segs + i].astype(jnp.bfloat16)


def attend(parents, advantages, bias, query_list, kv_list, chunk):
    segs, length = advantages.shape[:2]
    sources = len(kv_list)
    steps = sources // segs
    group_size = query_list[0].shape[1]
    width = group_size * HD
    keys = DEPTH * length
    smem = pl.BlockSpec(memory_space=pltpu.SMEM)
    vmem = pl.BlockSpec(memory_space=pltpu.VMEM)
    out_shape = [jax.ShapeDtypeStruct((length, width), jnp.bfloat16)] * segs
    out_shape += [jax.ShapeDtypeStruct((segs, 2, length, HD), jnp.bfloat16)] * steps
    outs = pl.pallas_call(
        functools.partial(attend_kernel, DEPTH, chunk, segs, sources, group_size),
        out_shape=out_shape,
        in_specs=[smem] + [vmem] * (2 + segs + sources),
        out_specs=[vmem] * len(out_shape),
        scratch_shapes=[
            pltpu.VMEM((sources, 2, length, HD), jnp.bfloat16),
            pltpu.VMEM((keys, width), jnp.bfloat16),
            pltpu.VMEM((keys, width), jnp.bfloat16),
            pltpu.VMEM((sources, 2, length, HD), jnp.float32),
        ],
        compiler_params=pltpu.CompilerParams(vmem_limit_bytes=16 * 1024 * 1024),
        cost_estimate=pl.CostEstimate(
            flops=5 * 2 * keys * length * width * segs,
            bytes_accessed=8 * 1024 * 1024,
            transcendentals=keys * width * segs,
        ),
        name="tree_attention_backward",
    )(parents, advantages, bias, *query_list, *kv_list)
    return outs[:segs], outs[segs:]


def join_queries_kernel(*refs):
    part = lax.rem(lax.axis_index("seg"), 2)
    refs, dq_ref = refs[:-1], refs[-1]
    chunks = len(refs) // 2
    width = refs[0].shape[1]
    for index, ref in enumerate(refs):
        side, chunk = divmod(index, chunks)
        where = part if side == 0 else 1 - part
        column = pl.multiple_of((where * chunks + chunk) * width, HD)
        dq_ref[:, pl.ds(column, width)] = ref[...]


def join_queries(own_list, other_list):
    chunks = len(own_list)
    length, width = own_list[0].shape
    vmem = pl.BlockSpec(memory_space=pltpu.VMEM)
    return pl.pallas_call(
        join_queries_kernel,
        out_shape=jax.ShapeDtypeStruct((length, 2 * chunks * width), jnp.bfloat16),
        in_specs=[vmem] * (2 * chunks),
        out_specs=vmem,
        cost_estimate=pl.CostEstimate(
            flops=0, bytes_accessed=8 * length * width * chunks, transcendentals=0
        ),
        compiler_params=SMALL,
        name="join_queries",
    )(*own_list, *other_list)


def join_keys_kernel(chunks, *refs):
    part = lax.rem(lax.axis_index("seg"), 2)
    other_refs, sum_refs = refs[:chunks], refs[chunks:-2]
    many = len(sum_refs) // chunks
    dk_ref, dv_ref = refs[-2:]
    for chunk in range(chunks):
        here = pl.ds(pl.multiple_of((part * chunks + chunk) * HD, HD), HD)
        there = pl.ds(pl.multiple_of(((1 - part) * chunks + chunk) * HD, HD), HD)
        for plane, out_ref in enumerate((dk_ref, dv_ref)):
            blocks = [ref[0, plane] for ref in sum_refs[chunk * many : (chunk + 1) * many]]
            total = sum(block.astype(jnp.float32) for block in blocks)
            out_ref[:, here] = total.astype(jnp.bfloat16)
            out_ref[:, there] = other_refs[chunk][plane]


def join_keys(others, summands):
    chunks = len(others)
    length = others[0].shape[1]
    vmem = pl.BlockSpec(memory_space=pltpu.VMEM)
    flat = [block for blocks in summands for block in blocks]
    out = jax.ShapeDtypeStruct((length, 2 * chunks * HD), jnp.bfloat16)
    return pl.pallas_call(
        functools.partial(join_keys_kernel, chunks),
        out_shape=(out, out),
        in_specs=[vmem] * (chunks + len(flat)),
        out_specs=(vmem, vmem),
        cost_estimate=pl.CostEstimate(
            flops=0, bytes_accessed=16 * length * HD * chunks, transcendentals=0
        ),
        compiler_params=SMALL,
        name="join_keys",
    )(*others, *flat)


def permute(array, pairs):
    return lax.ppermute(array, "seg", pairs)


def after(array, *earlier):
    return lax.optimization_barrier((array, *earlier))[0]


def paired_body(queries, direction, key_vectors, value_vectors, token_rows, parents, lengths, log_rate):
    groups = lax.axis_size("seg")
    length = queries.shape[0]
    chunks = key_vectors.shape[1] // HD // 2
    swap = [(i, i ^ 1) for i in range(groups)]
    steps = range(1, groups // 2)
    ring = [0, 1, 3, 2]

    def turn(distance):
        pairs = []
        for place, pair in enumerate(ring):
            target = ring[(place + distance) % len(ring)]
            pairs += [(2 * pair + x, 2 * target + x) for x in range(2)]
        return pairs

    climb = turn(1)
    down = {d: turn(-d) for d in steps}

    kept, given = pack(lengths, key_vectors, value_vectors, token_rows, 2, log_rate)
    taken = permute(given, swap)
    chain = [kept, permute(kept, climb)]
    other = [after(taken, chain[1])]
    kept_q, given_q = pack_queries(after(queries, kept), direction, 2, chunks)
    taken_q = [permute(after(given_q[0], *other), swap)]
    bias, columns, weights = prepare(parents, lengths, [kept, other[0]], length, log_rate)
    for step in steps:
        if step + 1 in steps:
            chain.append(permute(chain[-1], climb))
        gate = [bias, taken_q[0]] if step == 1 else []
        other.append(after(permute(other[-1], climb), chain[-1], *gate))
    for block in given_q[1:]:
        taken_q.append(permute(after(block, taken_q[-1]), swap))
    blocks = [block for pair in zip(chain, other) for block in pair]
    row, advantages = advantages_of(columns, weights, blocks)

    dq_own, dq_back, dkv_list = [], [], []
    for chunk in range(chunks):
        query_list = [kept_q[chunk], taken_q[chunk]]
        dq, dkv = attend(parents, advantages, bias, query_list, blocks, chunk)
        dq_own.append(dq[0])
        dq_back.append(dq[1])
        dkv_list.append(dkv)

    summands = []
    for dkv in dkv_list:
        arrived = [permute(dkv[d], down[d]) for d in steps[::-1]]
        summands.append([after(dkv[0], dq_own[-1])] + arrived)
    dq_back = [permute(block, swap) for block in dq_back]
    others = []
    for blocks in summands:
        total = sum(block[1].astype(jnp.float32) for block in blocks)
        others.append(permute(total.astype(jnp.bfloat16), swap))
    grad_q = join_queries(dq_own, dq_back)
    grad_k, grad_v = join_keys(others, summands)
    return grad_q, grad_k, grad_v, row[0]


def fetch_rows(spread, wanted):
    routed = jnp.take(spread, jnp.maximum(wanted, 0), axis=0)
    return lax.all_to_all(routed, "seg", split_axis=0, concat_axis=2, tiled=True)


def return_rows(grad_rows, wanted, total_segs):
    returned = lax.all_to_all(grad_rows, "seg", split_axis=2, concat_axis=0, tiled=True)
    piece_len = returned.shape[2]
    feature_len = returned.shape[3]
    routed_ids = wanted.reshape(-1)
    targets = jnp.where(routed_ids >= 0, routed_ids, total_segs)
    summed = jax.ops.segment_sum(
        returned.reshape(-1, piece_len * feature_len).astype(jnp.float32),
        targets,
        num_segments=total_segs + 1,
    )[:total_segs]
    return lax.all_to_all(
        summed.reshape(total_segs, piece_len, feature_len),
        "seg",
        split_axis=0,
        concat_axis=1,
        tiled=True,
    )


def routed_body(queries, direction, key_vectors, value_vectors, token_rows, parents, lengths, log_rate):
    total_segs = parents.shape[0]
    length, width = key_vectors.shape
    heads = width // HD
    own = lax.axis_index("seg")
    own_len = lax.dynamic_slice_in_dim(lengths, own, 1)[0]
    terms = jnp.concatenate(token_terms(log_rate, own_len, *token_rows), axis=1)
    bias, columns, weights = prepare(parents, lengths, [terms], length, log_rate)
    terms = lax.all_gather(terms, "seg", axis=0, tiled=True)
    row, advantages = advantages_of(columns, weights, [terms])
    flat = jnp.concatenate([key_vectors, value_vectors], axis=1)[None]
    spread = lax.all_to_all(flat, "seg", split_axis=1, concat_axis=0, tiled=True)
    chains = ancestors(parents, DEPTH - 1)
    arrived = fetch_rows(spread, chains)[0]
    slot_kv = jnp.concatenate([flat, arrived]).reshape(DEPTH, length, 2, heads, HD)
    slot_kv = jnp.transpose(slot_kv, (0, 3, 2, 1, 4)).reshape(DEPTH, -1, HD)
    kv_list = [slot_kv[slot] for slot in range(DEPTH)]
    (kept_q,) = pack_queries(queries, direction, 1, heads)
    dq_list, dkv_list = [], []
    for head in range(heads):
        dq, dkv = attend(parents, advantages, bias, [kept_q[head]], kv_list, head)
        dq_list.append(dq[0])
        dkv_list.append(jnp.concatenate(dkv))
    rows = jnp.transpose(jnp.stack(dkv_list), (1, 3, 2, 0, 4)).reshape(1, DEPTH, length, -1)
    summed = return_rows(rows[:, 1:], chains, total_segs)[0] + rows[0, 0].astype(jnp.float32)
    grad_keys = summed[:, :width].astype(jnp.bfloat16)
    grad_values = summed[:, width:].astype(jnp.bfloat16)
    return jnp.concatenate(dq_list, axis=1), grad_keys, grad_values, row[0]


def body(
    queries,
    key_vectors,
    value_vectors,
    direction,
    rewards,
    logprobs,
    ref_logprobs,
    value_est,
    parents,
    seg_lengths,
):
    groups = lax.axis_size("seg")
    assert parents.shape[0] == groups
    log_rate = math.log(LAMBDA_SEG) / rewards.shape[0]
    token_rows = [rewards[None], logprobs[None], ref_logprobs[None], value_est[None]]
    plan = paired_body if groups == PAIRED_GROUPS else routed_body
    return plan(
        queries, direction, key_vectors, value_vectors, token_rows, parents, seg_lengths, log_rate
    )


def solution(mesh):
    in_specs = (
        P(("grp", "seg"), "tp"),
        P(("grp", "seg"), "tp"),
        P(("grp", "seg"), "tp"),
        P(("grp", "seg"), "tp"),
        P(("grp", "seg")),
        P(("grp", "seg")),
        P(("grp", "seg")),
        P(("grp", "seg")),
        P("grp"),
        P("grp"),
    )
    out_specs = (
        P(("grp", "seg"), "tp"),
        P(("grp", "seg"), "tp"),
        P(("grp", "seg"), "tp"),
        P(("grp", "seg")),
    )
    return jax.shard_map(body, mesh=mesh, in_specs=in_specs, out_specs=out_specs, check_vma=False)
```

```python
import functools
import math

import jax
import jax.numpy as jnp
from jax import lax
from jax.experimental import pallas as pl
from jax.experimental.pallas import tpu as pltpu
from jax.sharding import PartitionSpec as P

HD = 128
DEPTH = 5
BETA = 0.1
LAMBDA_SEG = 0.7
PAIRED_GROUPS = 8
TERM_ROWS = 16
LOG2E = math.log2(math.e)
SMALL = pltpu.CompilerParams(vmem_limit_bytes=8 * 1024 * 1024)


def lookup(table_values, lookup_ids):
    matches = lookup_ids[..., None] == jnp.arange(table_values.shape[0], dtype=jnp.int32)
    return jnp.sum(jnp.where(matches, table_values, 0), axis=-1)


def ancestors(parents, count):
    current = jnp.arange(parents.shape[0], dtype=jnp.int32)
    chain_list = []
    for depth_step in range(count):
        parent_ids = lookup(parents, current)
        current = jnp.where(current >= 0, parent_ids, -1)
        chain_list.append(current)
    return jnp.stack(chain_list, axis=1)


def token_terms(log_rate, own_len, rewards, logprobs, ref_logprobs, values):
    positions = lax.broadcasted_iota(jnp.int32, rewards.shape, 1)
    later = jnp.concatenate([values[:, 1:], values[:, :1]], axis=1)
    later = jnp.where(positions + 1 < own_len, later, 0.0)
    deltas = jnp.where(
        positions < own_len, rewards - BETA * (logprobs - ref_logprobs) + later - values, 0.0
    )
    powers = jnp.exp(positions.astype(jnp.float32) * log_rate)
    first_local = jnp.sum(deltas * powers, axis=1, keepdims=True)
    firsts = jnp.where(positions == 0, first_local, jnp.where(positions == 1, values[:, :1], 0.0))
    return deltas, firsts


def split_float(value):
    parts = []
    for _ in range(3):
        part = value.astype(jnp.bfloat16)
        parts.append(part)
        value = value - part.astype(jnp.float32)
    return parts


def pack_kernel(
    log_rate,
    parts,
    lengths_ref,
    k_ref,
    v_ref,
    rewards_ref,
    logprobs_ref,
    ref_logprobs_ref,
    values_ref,
    *out_refs,
):
    own = lax.axis_index("seg")
    length = k_ref.shape[0]
    heads = len(out_refs) // parts
    terms = token_terms(
        log_rate,
        lengths_ref[own],
        rewards_ref[...],
        logprobs_ref[...],
        ref_logprobs_ref[...],
        values_ref[...],
    )
    tail = [part.astype(jnp.float32) for x in terms for part in split_float(x)]
    tail.append(jnp.zeros((TERM_ROWS - len(tail), HD), jnp.float32))
    tail = jnp.concatenate(tail).astype(jnp.bfloat16)
    for index, out_ref in enumerate(out_refs):
        step, h = divmod(index, heads)
        part = lax.rem(own + step, parts)
        columns = pl.ds(pl.multiple_of((part * heads + h) * HD, HD), HD)
        out_ref[:length, :] = k_ref[:, columns]
        out_ref[length : 2 * length, :] = v_ref[:, columns]
        if h == 0:
            out_ref[2 * length :, :] = tail


def pack(lengths, k, v, token_rows, parts, log_rate):
    length, width = k.shape
    smem = pl.BlockSpec(memory_space=pltpu.SMEM)
    vmem = pl.BlockSpec(memory_space=pltpu.VMEM)
    heads = width // HD // parts
    assert length == HD
    blocks = [
        jax.ShapeDtypeStruct((2 * length + (TERM_ROWS if h == 0 else 0), HD), k.dtype)
        for h in range(heads)
    ]
    outs = pl.pallas_call(
        functools.partial(pack_kernel, log_rate, parts),
        out_shape=blocks * parts,
        in_specs=[smem] + [vmem] * 6,
        out_specs=[vmem] * (heads * parts),
        cost_estimate=pl.CostEstimate(
            flops=length * 100, bytes_accessed=8 * length * width, transcendentals=length
        ),
        name="pack_keys_values",
    )(lengths, k, v, *token_rows)
    return [outs[step * heads : (step + 1) * heads] for step in range(parts)]


def join_blocks_kernel(mine_ref, other_ref, out_ref):
    rows = mine_ref.shape[0]
    out_ref[:rows, :] = mine_ref[...]
    out_ref[rows:, :] = other_ref[...]


def join_blocks(mine, other):
    vmem = pl.BlockSpec(memory_space=pltpu.VMEM)
    return pl.pallas_call(
        join_blocks_kernel,
        out_shape=jax.ShapeDtypeStruct((2 * mine.shape[0], HD), mine.dtype),
        in_specs=[vmem] * 2,
        out_specs=vmem,
        cost_estimate=pl.CostEstimate(flops=0, bytes_accessed=8 * mine.size, transcendentals=0),
        compiler_params=SMALL,
        name="join_blocks",
    )(mine, other)


def pack_queries_kernel(parts, q_ref, dir_ref, *out_refs):
    own = lax.axis_index("seg")
    chunks = len(out_refs) // parts
    heads = out_refs[0].shape[1]
    for index, out_ref in enumerate(out_refs):
        step, chunk = divmod(index, chunks)
        part = lax.rem(own + step, parts)
        for h in range(heads):
            column = (part * chunks + chunk) * heads + h
            columns = pl.ds(pl.multiple_of(column * HD, HD), HD)
            out_ref[0, h] = q_ref[:, columns]
            out_ref[1, h] = dir_ref[:, columns]


def pack_queries(q, direction, parts, chunks):
    length, width = q.shape
    vmem = pl.BlockSpec(memory_space=pltpu.VMEM)
    block = jax.ShapeDtypeStruct((2, width // HD // parts // chunks, length, HD), q.dtype)
    outs = pl.pallas_call(
        functools.partial(pack_queries_kernel, parts),
        out_shape=(block,) * (parts * chunks),
        in_specs=[vmem, vmem],
        out_specs=(vmem,) * (parts * chunks),
        cost_estimate=pl.CostEstimate(flops=0, bytes_accessed=8 * length * width, transcendentals=0),
        compiler_params=SMALL,
        name="pack_queries",
    )(q, direction)
    return [outs[step * chunks : (step + 1) * chunks] for step in range(parts)]


def parent_of(segment, parents_s):
    known = parents_s[jnp.maximum(segment, 0)]
    return jnp.where(segment >= 0, known, -1).astype(jnp.int32)


def ring_place(pair):
    return jnp.where(pair >= 2, 5 - pair, pair)


def segment_of(own, segs, i):
    part = lax.rem(own, segs)
    return own - part + lax.rem(part + i, segs)


def read_terms(ref, end=None):
    if ref.dtype == jnp.float32:
        length = ref.shape[1] // 2
        return ref[:, :length], ref[:, length:]
    tail = ref[end - TERM_ROWS : end, :].astype(jnp.float32)
    return tail[0:1] + tail[1:2] + tail[2:3], tail[3:4] + tail[4:5] + tail[5:6]


def prepare_kernel(log_rate, depth, parents_s, lengths_s, *refs):
    term_refs, (bias_ref, columns_ref, weights_ref) = refs[:-3], refs[-3:]
    segs, _, length = bias_ref.shape
    count = parents_s.shape[0]
    own = lax.axis_index("seg")

    row_id = lax.broadcasted_iota(jnp.int32, (count, count), 0)
    col_id = lax.broadcasted_iota(jnp.int32, (count, count), 1)
    seg_col = lax.broadcasted_iota(jnp.int32, (count, 1), 0)

    def to_col(row):
        return jnp.sum(jnp.where(row_id == col_id, row, 0.0), axis=1, keepdims=True)

    parent_row = jnp.full((1, count), -1, jnp.int32)
    lens_col = jnp.zeros((count, 1), jnp.int32)
    for seg in range(count):
        parent_row = jnp.where(col_id[:1] == seg, parents_s[seg], parent_row)
        lens_col = jnp.where(seg_col == seg, lengths_s[seg], lens_col)
    lens_col = lens_col.astype(jnp.float32)
    children = (parent_row == row_id).astype(jnp.float32)
    tree = children / jnp.maximum(jnp.sum(children, axis=1, keepdims=True), 1.0)
    factor = jnp.exp(lens_col * log_rate)
    last_factor = jnp.exp((lens_col - 1.0) * log_rate)

    u_id = lax.broadcasted_iota(jnp.int32, (length, length), 0)
    t_id = lax.broadcasted_iota(jnp.int32, (length, length), 1)
    offset = (t_id - u_id).astype(jnp.float32)
    discount = jnp.where(offset >= 0, jnp.exp(offset * log_rate), 0.0)
    t_col = lax.broadcasted_iota(jnp.int32, (length, 1), 0)
    lane = lax.broadcasted_iota(jnp.int32, (count, HD), 1)
    for i in range(segs):
        seg = segment_of(own, segs, i)
        seg_len = lengths_s[seg]
        deltas, _ = read_terms(term_refs[i], term_refs[i].shape[0])
        live = t_col < seg_len
        left = (seg_len - t_col).astype(jnp.float32)
        columns = (
            jnp.sum(discount * deltas, axis=1, keepdims=True),
            jnp.exp((left - 1.0) * log_rate),
            jnp.exp(left * log_rate),
        )
        for index, column in enumerate(columns):
            column = jnp.where(live, column, 0.0)
            columns_ref[i, index] = jnp.broadcast_to(column, (length, HD))

        row = jnp.sum(jnp.where(row_id == seg, tree, 0.0), axis=0, keepdims=True)
        value_col = col = total = to_col(row)
        for _ in range(depth):
            col = to_col(jnp.sum(col * factor * tree, axis=0, keepdims=True))
            total = total + col
        through = to_col(jnp.sum(total * last_factor * tree, axis=0, keepdims=True))
        weights_ref[i, 0] = jnp.where(lane == 1, value_col, 0.0)
        weights_ref[i, 1] = jnp.where(lane == 0, total, jnp.where(lane == 1, through, 0.0))

        ancestor = seg
        for slot in range(depth):
            if slot > 0:
                ancestor = parent_of(ancestor, parents_s)
            slot_len = jnp.where(ancestor >= 0, lengths_s[jnp.maximum(ancestor, 0)], 0)
            seen = u_id < slot_len
            if slot == 0:
                seen = jnp.logical_and(seen, u_id <= t_id)
            bias_ref[i, slot * length : (slot + 1) * length, :] = jnp.where(seen, 0.0, -1e30)


def prepare(parents, lengths, terms, length, log_rate):
    smem = pl.BlockSpec(memory_space=pltpu.SMEM)
    vmem = pl.BlockSpec(memory_space=pltpu.VMEM)
    segs, count = len(terms), parents.shape[0]
    return pl.pallas_call(
        functools.partial(prepare_kernel, log_rate, DEPTH),
        out_shape=(
            jax.ShapeDtypeStruct((segs, DEPTH * length, length), jnp.float32),
            jax.ShapeDtypeStruct((segs, 3, length, HD), jnp.float32),
            jax.ShapeDtypeStruct((segs, 2, count, HD), jnp.float32),
        ),
        in_specs=[smem] * 2 + [vmem] * len(terms),
        out_specs=(vmem,) * 3,
        cost_estimate=pl.CostEstimate(
            flops=20 * DEPTH * segs * length * length,
            bytes_accessed=4 * DEPTH * segs * length * length,
            transcendentals=length * length,
        ),
        compiler_params=SMALL,
        name="prepare",
    )(parents, lengths, *terms)


def advantage_kernel(columns_ref, weights_ref, *refs):
    term_refs, (row_ref, adv_ref) = refs[:-2], refs[-2:]
    segs, _, length, _ = columns_ref.shape
    count = weights_ref.shape[2]
    if len(term_refs) == 1:
        firsts = read_terms(term_refs[0])[1]
    else:
        own = lax.axis_index("seg")
        part, pair, pairs = lax.rem(own, segs), own // segs, count // segs
        seg_id = lax.broadcasted_iota(jnp.int32, (count, length), 0)
        firsts = jnp.zeros((count, length), jnp.float32)
        for step, ref in enumerate(term_refs):
            place = lax.rem(ring_place(pair) - step + pairs, pairs)
            for side in range(segs):
                seg = ring_place(place) * segs + lax.rem(part + side, segs)
                end = (side + 1) * (ref.shape[0] // segs)
                firsts = jnp.where(seg_id == seg, read_terms(ref, end)[1], firsts)
    for i in range(segs):
        later_value = jnp.sum(weights_ref[i, 0] * firsts, axis=(0, 1), keepdims=True)
        later_head = jnp.sum(weights_ref[i, 1] * firsts, axis=(0, 1), keepdims=True)
        advantage = (
            columns_ref[i, 0] + columns_ref[i, 1] * later_value + columns_ref[i, 2] * later_head
        )
        adv_ref[i] = advantage
        if i == 0:
            row_id = lax.broadcasted_iota(jnp.int32, advantage.shape, 0)
            col_id = lax.broadcasted_iota(jnp.int32, advantage.shape, 1)
            row_ref[...] = jnp.sum(
                jnp.where(row_id == col_id, advantage, 0.0), axis=0, keepdims=True
            )


def advantages_of(columns, weights, terms):
    vmem = pl.BlockSpec(memory_space=pltpu.VMEM)
    segs, _, length, _ = columns.shape
    return pl.pallas_call(
        advantage_kernel,
        out_shape=(
            jax.ShapeDtypeStruct((1, length), jnp.float32),
            jax.ShapeDtypeStruct((segs, length, HD), jnp.float32),
        ),
        in_specs=[vmem] * (2 + len(terms)),
        out_specs=(vmem,) * 2,
        cost_estimate=pl.CostEstimate(
            flops=10 * segs * length * HD, bytes_accessed=16 * segs * length * HD, transcendentals=0
        ),
        compiler_params=SMALL,
        name="advantages",
    )(columns, weights, *terms)


def attend_kernel(depth, segs, steps, group_size, *refs):
    parents_s, adv_ref, bias_ref = refs[:3]
    query_refs, kv_refs = refs[3 : 3 + segs], refs[3 + segs : 3 + segs + steps]
    kv_scr, p_scr, ds_scr, acc_scr = refs[-4:]
    refs = refs[3 + segs + steps : -4]
    dkv_refs, dq_refs = refs[-steps:], refs[-steps - segs : -steps]

    length = query_refs[0].shape[2]
    own = lax.axis_index("seg")
    for source in range(steps * segs):
        step, side = divmod(source, segs)
        for plane in range(2):
            first = side * (kv_refs[step].shape[0] // segs) + plane * length
            kv_scr[source, plane] = kv_refs[step][first : first + length, :]
    acc_scr[...] = jnp.zeros_like(acc_scr)

    scale = HD**-0.5
    contract_last = (((1,), (1,)), ((), ()))
    contract_first = (((0,), (0,)), ((), ()))
    for i in range(segs):
        ancestor = segment_of(own, segs, i)
        part = lax.rem(own, segs)
        chosen = []
        for slot in range(depth):
            if slot > 0:
                ancestor = parent_of(ancestor, parents_s)
            if segs == 1:
                chosen.append(slot)
            else:
                known = jnp.maximum(ancestor, 0)
                step = ring_place((own - part) // segs) - ring_place(known // segs)
                step = lax.rem(step + steps, steps)
                turn = lax.rem(lax.rem(known, segs) - part + segs, segs)
                chosen.append(jnp.where(ancestor >= 0, step * segs + turn, 0))
        q_list = [query_refs[i][0, j] for j in range(group_size)]
        dir_list = [query_refs[i][1, j] for j in range(group_size)]
        do_list = [(adv_ref[i] * d.astype(jnp.float32)).astype(jnp.bfloat16) for d in dir_list]
        k_all = jnp.concatenate([kv_scr[s, 0] for s in chosen], axis=0)
        v_all = jnp.concatenate([kv_scr[s, 1] for s in chosen], axis=0)
        q_all = jnp.concatenate(q_list, axis=0)
        do_all = jnp.concatenate(do_list, axis=0)
        all_scores = lax.dot_general(
            k_all, q_all, contract_last, preferred_element_type=jnp.float32
        )
        all_dprob = lax.dot_general(
            v_all, do_all, contract_last, preferred_element_type=jnp.float32
        )
        for j in range(group_size):
            columns = slice(j * length, (j + 1) * length)
            scores = all_scores[:, columns] * (scale * LOG2E) + bias_ref[i]
            top = jnp.max(scores, axis=0, keepdims=True)
            unnorm = jnp.exp2(scores - top)
            prob = unnorm * (1.0 / jnp.sum(unnorm, axis=0, keepdims=True))
            prob_low = prob.astype(jnp.bfloat16)
            dprob = all_dprob[:, columns]
            row_dot = jnp.sum(prob_low.astype(jnp.float32) * dprob, axis=0, keepdims=True)
            dscore = (prob * (dprob - row_dot)).astype(jnp.bfloat16)
            p_scr[:, columns] = prob_low
            ds_scr[:, columns] = dscore
        dscore_all = ds_scr[...]
        dq_t = lax.dot_general(
            k_all, dscore_all, contract_first, preferred_element_type=jnp.float32
        )
        for j in range(group_size):
            dq = jnp.transpose(dq_t[:, j * length : (j + 1) * length]) * scale
            dq_refs[i][:, j * HD : (j + 1) * HD] = dq.astype(jnp.bfloat16)
        dk_all = jnp.dot(dscore_all, q_all, preferred_element_type=jnp.float32) * scale
        dv_all = jnp.dot(p_scr[...], do_all, preferred_element_type=jnp.float32)
        for slot, s in enumerate(chosen):
            rows = slice(slot * length, (slot + 1) * length)
            acc_scr[s, 0] += dk_all[rows]
            acc_scr[s, 1] += dv_all[rows]
    for step in range(steps):
        for i in range(segs):
            dkv_refs[step][i] = acc_scr[step * segs + i].astype(jnp.bfloat16)


def attend(parents, advantages, bias, query_list, kv_list):
    segs, length = advantages.shape[:2]
    steps = len(kv_list)
    sources = steps * segs
    group_size = query_list[0].shape[1]
    width = group_size * HD
    keys = DEPTH * length
    smem = pl.BlockSpec(memory_space=pltpu.SMEM)
    vmem = pl.BlockSpec(memory_space=pltpu.VMEM)
    out_shape = [jax.ShapeDtypeStruct((length, width), jnp.bfloat16)] * segs
    out_shape += [jax.ShapeDtypeStruct((segs, 2, length, HD), jnp.bfloat16)] * steps
    outs = pl.pallas_call(
        functools.partial(attend_kernel, DEPTH, segs, steps, group_size),
        out_shape=out_shape,
        in_specs=[smem] + [vmem] * (2 + segs + steps),
        out_specs=[vmem] * len(out_shape),
        scratch_shapes=[
            pltpu.VMEM((sources, 2, length, HD), jnp.bfloat16),
            pltpu.VMEM((keys, width), jnp.bfloat16),
            pltpu.VMEM((keys, width), jnp.bfloat16),
            pltpu.VMEM((sources, 2, length, HD), jnp.float32),
        ],
        compiler_params=pltpu.CompilerParams(vmem_limit_bytes=16 * 1024 * 1024),
        cost_estimate=pl.CostEstimate(
            flops=5 * 2 * keys * length * width * segs,
            bytes_accessed=8 * 1024 * 1024,
            transcendentals=keys * width * segs,
        ),
        name="tree_attention_backward",
    )(parents, advantages, bias, *query_list, *kv_list)
    return outs[:segs], outs[segs:]


def join_queries_kernel(*refs):
    part = lax.rem(lax.axis_index("seg"), 2)
    refs, dq_ref = refs[:-1], refs[-1]
    chunks = len(refs) // 2
    width = refs[0].shape[1]
    for index, ref in enumerate(refs):
        side, chunk = divmod(index, chunks)
        where = part if side == 0 else 1 - part
        column = pl.multiple_of((where * chunks + chunk) * width, HD)
        dq_ref[:, pl.ds(column, width)] = ref[...]


def join_queries(own_list, other_list):
    chunks = len(own_list)
    length, width = own_list[0].shape
    vmem = pl.BlockSpec(memory_space=pltpu.VMEM)
    return pl.pallas_call(
        join_queries_kernel,
        out_shape=jax.ShapeDtypeStruct((length, 2 * chunks * width), jnp.bfloat16),
        in_specs=[vmem] * (2 * chunks),
        out_specs=vmem,
        cost_estimate=pl.CostEstimate(
            flops=0, bytes_accessed=8 * length * width * chunks, transcendentals=0
        ),
        compiler_params=SMALL,
        name="join_queries",
    )(*own_list, *other_list)


def join_keys_kernel(chunks, *refs):
    part = lax.rem(lax.axis_index("seg"), 2)
    other_refs, sum_refs = refs[:chunks], refs[chunks:-2]
    many = len(sum_refs) // chunks
    dk_ref, dv_ref = refs[-2:]
    for chunk in range(chunks):
        here = pl.ds(pl.multiple_of((part * chunks + chunk) * HD, HD), HD)
        there = pl.ds(pl.multiple_of(((1 - part) * chunks + chunk) * HD, HD), HD)
        for plane, out_ref in enumerate((dk_ref, dv_ref)):
            blocks = [ref[0, plane] for ref in sum_refs[chunk * many : (chunk + 1) * many]]
            total = sum(block.astype(jnp.float32) for block in blocks)
            out_ref[:, here] = total.astype(jnp.bfloat16)
            out_ref[:, there] = other_refs[chunk][plane]


def join_keys(others, summands):
    chunks = len(others)
    length = others[0].shape[1]
    vmem = pl.BlockSpec(memory_space=pltpu.VMEM)
    flat = [block for blocks in summands for block in blocks]
    out = jax.ShapeDtypeStruct((length, 2 * chunks * HD), jnp.bfloat16)
    return pl.pallas_call(
        functools.partial(join_keys_kernel, chunks),
        out_shape=(out, out),
        in_specs=[vmem] * (chunks + len(flat)),
        out_specs=(vmem, vmem),
        cost_estimate=pl.CostEstimate(
            flops=0, bytes_accessed=16 * length * HD * chunks, transcendentals=0
        ),
        compiler_params=SMALL,
        name="join_keys",
    )(*others, *flat)


def permute(array, pairs):
    return lax.ppermute(array, "seg", pairs)


def after(array, *earlier):
    return lax.optimization_barrier((array, *earlier))[0]


def paired_body(queries, direction, key_vectors, value_vectors, token_rows, parents, lengths, log_rate):
    groups = lax.axis_size("seg")
    length = queries.shape[0]
    chunks = key_vectors.shape[1] // HD // 2
    swap = [(i, i ^ 1) for i in range(groups)]
    steps = range(1, groups // 2)
    ring = [0, 1, 3, 2]

    def turn(distance):
        pairs = []
        for place, pair in enumerate(ring):
            target = ring[(place + distance) % len(ring)]
            pairs += [(2 * pair + x, 2 * target + x) for x in range(2)]
        return pairs

    climb = turn(1)
    down = {d: turn(-d) for d in steps}

    kept, given = pack(lengths, key_vectors, value_vectors, token_rows, 2, log_rate)
    taken = [permute(block, swap) for block in given]
    kept_q, given_q = pack_queries(after(queries, kept[0]), direction, 2, chunks)
    bias, columns, weights = prepare(parents, lengths, [kept[0], taken[0]], length, log_rate)
    near = [
        join_blocks(mine, after(other, *kept_q) if chunk == 0 else other)
        for chunk, (mine, other) in enumerate(zip(kept, taken))
    ]
    chain = [near[0]]
    for gate in ([], near[1:], [bias]):
        chain.append(permute(after(chain[-1], *gate), climb))
    chains = [chain]
    taken_q = [permute(after(given_q[0], chain[1]), swap)]
    for chunk in range(1, chunks):
        block, query_block = lax.optimization_barrier((near[chunk], given_q[chunk], bias, chain[-1]))[:2]
        chains.append([block] + [permute(block, turn(d)) for d in steps])
        taken_q.append(permute(query_block, swap))
    row, advantages = advantages_of(columns, weights, chains[0])

    dq_own, dq_back, dkv_list = [], [], []
    for chunk in range(chunks):
        query_list = [kept_q[chunk], taken_q[chunk]]
        dq, dkv = attend(parents, advantages, bias, query_list, chains[chunk])
        dq_own.append(dq[0])
        dq_back.append(dq[1])
        dkv_list.append(dkv)

    summands = []
    for dkv in dkv_list:
        arrived = [permute(dkv[d], down[d]) for d in steps[::-1]]
        summands.append([after(dkv[0], dq_own[-1])] + arrived)
    dq_back = [permute(block, swap) for block in dq_back]
    others = []
    for blocks in summands:
        total = sum(block[1].astype(jnp.float32) for block in blocks)
        others.append(permute(total.astype(jnp.bfloat16), swap))
    grad_q = join_queries(dq_own, dq_back)
    grad_k, grad_v = join_keys(others, summands)
    return grad_q, grad_k, grad_v, row[0]


def fetch_rows(spread, wanted):
    routed = jnp.take(spread, jnp.maximum(wanted, 0), axis=0)
    return lax.all_to_all(routed, "seg", split_axis=0, concat_axis=2, tiled=True)


def return_rows(grad_rows, wanted, total_segs):
    returned = lax.all_to_all(grad_rows, "seg", split_axis=2, concat_axis=0, tiled=True)
    piece_len = returned.shape[2]
    feature_len = returned.shape[3]
    routed_ids = wanted.reshape(-1)
    targets = jnp.where(routed_ids >= 0, routed_ids, total_segs)
    summed = jax.ops.segment_sum(
        returned.reshape(-1, piece_len * feature_len).astype(jnp.float32),
        targets,
        num_segments=total_segs + 1,
    )[:total_segs]
    return lax.all_to_all(
        summed.reshape(total_segs, piece_len, feature_len),
        "seg",
        split_axis=0,
        concat_axis=1,
        tiled=True,
    )


def routed_body(queries, direction, key_vectors, value_vectors, token_rows, parents, lengths, log_rate):
    total_segs = parents.shape[0]
    length, width = key_vectors.shape
    heads = width // HD
    own = lax.axis_index("seg")
    own_len = lax.dynamic_slice_in_dim(lengths, own, 1)[0]
    terms = jnp.concatenate(token_terms(log_rate, own_len, *token_rows), axis=1)
    bias, columns, weights = prepare(parents, lengths, [terms], length, log_rate)
    terms = lax.all_gather(terms, "seg", axis=0, tiled=True)
    row, advantages = advantages_of(columns, weights, [terms])
    flat = jnp.concatenate([key_vectors, value_vectors], axis=1)[None]
    spread = lax.all_to_all(flat, "seg", split_axis=1, concat_axis=0, tiled=True)
    chains = ancestors(parents, DEPTH - 1)
    arrived = fetch_rows(spread, chains)[0]
    slot_kv = jnp.concatenate([flat, arrived]).reshape(DEPTH, length, 2, heads, HD)
    slot_kv = jnp.transpose(slot_kv, (0, 3, 2, 1, 4)).reshape(DEPTH, heads, 2 * length, HD)
    (kept_q,) = pack_queries(queries, direction, 1, heads)
    dq_list, dkv_list = [], []
    for head in range(heads):
        kv_list = [slot_kv[slot, head] for slot in range(DEPTH)]
        dq, dkv = attend(parents, advantages, bias, [kept_q[head]], kv_list)
        dq_list.append(dq[0])
        dkv_list.append(jnp.concatenate(dkv))
    rows = jnp.transpose(jnp.stack(dkv_list), (1, 3, 2, 0, 4)).reshape(1, DEPTH, length, -1)
    summed = return_rows(rows[:, 1:], chains, total_segs)[0] + rows[0, 0].astype(jnp.float32)
    grad_keys = summed[:, :width].astype(jnp.bfloat16)
    grad_values = summed[:, width:].astype(jnp.bfloat16)
    return jnp.concatenate(dq_list, axis=1), grad_keys, grad_values, row[0]


def body(
    queries,
    key_vectors,
    value_vectors,
    direction,
    rewards,
    logprobs,
    ref_logprobs,
    value_est,
    parents,
    seg_lengths,
):
    groups = lax.axis_size("seg")
    assert parents.shape[0] == groups
    log_rate = math.log(LAMBDA_SEG) / rewards.shape[0]
    token_rows = [rewards[None], logprobs[None], ref_logprobs[None], value_est[None]]
    plan = paired_body if groups == PAIRED_GROUPS else routed_body
    return plan(
        queries, direction, key_vectors, value_vectors, token_rows, parents, seg_lengths, log_rate
    )


def solution(mesh):
    in_specs = (
        P(("grp", "seg"), "tp"),
        P(("grp", "seg"), "tp"),
        P(("grp", "seg"), "tp"),
        P(("grp", "seg"), "tp"),
        P(("grp", "seg")),
        P(("grp", "seg")),
        P(("grp", "seg")),
        P(("grp", "seg")),
        P("grp"),
        P("grp"),
    )
    out_specs = (
        P(("grp", "seg"), "tp"),
        P(("grp", "seg"), "tp"),
        P(("grp", "seg"), "tp"),
        P(("grp", "seg")),
    )
    return jax.shard_map(body, mesh=mesh, in_specs=in_specs, out_specs=out_specs, check_vma=False)
```

```python
import functools
import math

import jax
import jax.numpy as jnp
from jax import lax
from jax.experimental import pallas as pl
from jax.experimental.pallas import tpu as pltpu
from jax.sharding import PartitionSpec as P

HD = 128
DEPTH = 5
BETA = 0.1
LAMBDA_SEG = 0.7
PAIRED_GROUPS = 8
TERM_ROWS = 16
LOG2E = math.log2(math.e)
SMALL = pltpu.CompilerParams(vmem_limit_bytes=8 * 1024 * 1024)


def lookup(table_values, lookup_ids):
    matches = lookup_ids[..., None] == jnp.arange(table_values.shape[0], dtype=jnp.int32)
    return jnp.sum(jnp.where(matches, table_values, 0), axis=-1)


def ancestors(parents, count):
    current = jnp.arange(parents.shape[0], dtype=jnp.int32)
    chain_list = []
    for depth_step in range(count):
        parent_ids = lookup(parents, current)
        current = jnp.where(current >= 0, parent_ids, -1)
        chain_list.append(current)
    return jnp.stack(chain_list, axis=1)


def token_terms(log_rate, own_len, rewards, logprobs, ref_logprobs, values):
    positions = lax.broadcasted_iota(jnp.int32, rewards.shape, 1)
    later = jnp.concatenate([values[:, 1:], values[:, :1]], axis=1)
    later = jnp.where(positions + 1 < own_len, later, 0.0)
    deltas = jnp.where(
        positions < own_len, rewards - BETA * (logprobs - ref_logprobs) + later - values, 0.0
    )
    powers = jnp.exp(positions.astype(jnp.float32) * log_rate)
    first_local = jnp.sum(deltas * powers, axis=1, keepdims=True)
    firsts = jnp.where(positions == 0, first_local, jnp.where(positions == 1, values[:, :1], 0.0))
    return deltas, firsts


def split_float(value):
    parts = []
    for _ in range(3):
        part = value.astype(jnp.bfloat16)
        parts.append(part)
        value = value - part.astype(jnp.float32)
    return parts


def pack_kernel(
    log_rate,
    lengths_ref,
    k_ref,
    v_ref,
    rewards_ref,
    logprobs_ref,
    ref_logprobs_ref,
    values_ref,
    *out_refs,
):
    own = lax.axis_index("seg")
    length = k_ref.shape[0]
    parts = len(out_refs)
    heads = k_ref.shape[1] // HD // parts
    terms = token_terms(
        log_rate,
        lengths_ref[own],
        rewards_ref[...],
        logprobs_ref[...],
        ref_logprobs_ref[...],
        values_ref[...],
    )
    tail = [part.astype(jnp.float32) for x in terms for part in split_float(x)]
    tail.append(jnp.zeros((TERM_ROWS - len(tail), HD), jnp.float32))
    tail = jnp.concatenate(tail).astype(jnp.bfloat16)
    for step, out_ref in enumerate(out_refs):
        part = lax.rem(own + step, parts)
        for h in range(heads):
            columns = pl.ds(pl.multiple_of((part * heads + h) * HD, HD), HD)
            for plane, ref in enumerate((k_ref, v_ref)):
                first = (h * 2 + plane) * length
                out_ref[first : first + length, :] = ref[:, columns]
        out_ref[2 * heads * length :, :] = tail


def pack(lengths, k, v, token_rows, parts, log_rate):
    length, width = k.shape
    smem = pl.BlockSpec(memory_space=pltpu.SMEM)
    vmem = pl.BlockSpec(memory_space=pltpu.VMEM)
    heads = width // HD // parts
    assert length == HD
    block = jax.ShapeDtypeStruct((2 * heads * length + TERM_ROWS, HD), k.dtype)
    return pl.pallas_call(
        functools.partial(pack_kernel, log_rate),
        out_shape=(block,) * parts,
        in_specs=[smem] + [vmem] * 6,
        out_specs=(vmem,) * parts,
        cost_estimate=pl.CostEstimate(
            flops=length * 100, bytes_accessed=8 * length * width, transcendentals=length
        ),
        name="pack_keys_values",
    )(lengths, k, v, *token_rows)


def pack_queries_kernel(parts, q_ref, dir_ref, *out_refs):
    own = lax.axis_index("seg")
    chunks = len(out_refs) // parts
    heads = out_refs[0].shape[1]
    for index, out_ref in enumerate(out_refs):
        step, chunk = divmod(index, chunks)
        part = lax.rem(own + step, parts)
        for h in range(heads):
            column = (part * chunks + chunk) * heads + h
            columns = pl.ds(pl.multiple_of(column * HD, HD), HD)
            out_ref[0, h] = q_ref[:, columns]
            out_ref[1, h] = dir_ref[:, columns]


def pack_queries(q, direction, parts, chunks):
    length, width = q.shape
    vmem = pl.BlockSpec(memory_space=pltpu.VMEM)
    block = jax.ShapeDtypeStruct((2, width // HD // parts // chunks, length, HD), q.dtype)
    outs = pl.pallas_call(
        functools.partial(pack_queries_kernel, parts),
        out_shape=(block,) * (parts * chunks),
        in_specs=[vmem, vmem],
        out_specs=(vmem,) * (parts * chunks),
        cost_estimate=pl.CostEstimate(flops=0, bytes_accessed=8 * length * width, transcendentals=0),
        compiler_params=SMALL,
        name="pack_queries",
    )(q, direction)
    return [outs[step * chunks : (step + 1) * chunks] for step in range(parts)]


def parent_of(segment, parents_s):
    known = parents_s[jnp.maximum(segment, 0)]
    return jnp.where(segment >= 0, known, -1).astype(jnp.int32)


def ring_place(pair):
    return jnp.where(pair >= 2, 5 - pair, pair)


def segment_of(own, segs, i):
    part = lax.rem(own, segs)
    return own - part + lax.rem(part + i, segs)


def read_terms(ref):
    if ref.dtype == jnp.float32:
        length = ref.shape[1] // 2
        return ref[:, :length], ref[:, length:]
    tail = ref[ref.shape[0] - TERM_ROWS :, :].astype(jnp.float32)
    return tail[0:1] + tail[1:2] + tail[2:3], tail[3:4] + tail[4:5] + tail[5:6]


def prepare_kernel(log_rate, depth, parents_s, lengths_s, *refs):
    term_refs, (bias_ref, columns_ref, weights_ref) = refs[:-3], refs[-3:]
    segs, _, length = bias_ref.shape
    count = parents_s.shape[0]
    own = lax.axis_index("seg")

    row_id = lax.broadcasted_iota(jnp.int32, (count, count), 0)
    col_id = lax.broadcasted_iota(jnp.int32, (count, count), 1)
    seg_col = lax.broadcasted_iota(jnp.int32, (count, 1), 0)

    def to_col(row):
        return jnp.sum(jnp.where(row_id == col_id, row, 0.0), axis=1, keepdims=True)

    parent_row = jnp.full((1, count), -1, jnp.int32)
    lens_col = jnp.zeros((count, 1), jnp.int32)
    for seg in range(count):
        parent_row = jnp.where(col_id[:1] == seg, parents_s[seg], parent_row)
        lens_col = jnp.where(seg_col == seg, lengths_s[seg], lens_col)
    lens_col = lens_col.astype(jnp.float32)
    children = (parent_row == row_id).astype(jnp.float32)
    tree = children / jnp.maximum(jnp.sum(children, axis=1, keepdims=True), 1.0)
    factor = jnp.exp(lens_col * log_rate)
    last_factor = jnp.exp((lens_col - 1.0) * log_rate)

    u_id = lax.broadcasted_iota(jnp.int32, (length, length), 0)
    t_id = lax.broadcasted_iota(jnp.int32, (length, length), 1)
    offset = (t_id - u_id).astype(jnp.float32)
    discount = jnp.where(offset >= 0, jnp.exp(offset * log_rate), 0.0)
    t_col = lax.broadcasted_iota(jnp.int32, (length, 1), 0)
    lane = lax.broadcasted_iota(jnp.int32, (count, HD), 1)
    for i in range(segs):
        seg = segment_of(own, segs, i)
        seg_len = lengths_s[seg]
        deltas, _ = read_terms(term_refs[i])
        live = t_col < seg_len
        left = (seg_len - t_col).astype(jnp.float32)
        columns = (
            jnp.sum(discount * deltas, axis=1, keepdims=True),
            jnp.exp((left - 1.0) * log_rate),
            jnp.exp(left * log_rate),
        )
        for index, column in enumerate(columns):
            column = jnp.where(live, column, 0.0)
            columns_ref[i, index] = jnp.broadcast_to(column, (length, HD))

        row = jnp.sum(jnp.where(row_id == seg, tree, 0.0), axis=0, keepdims=True)
        value_col = col = total = to_col(row)
        for _ in range(depth):
            col = to_col(jnp.sum(col * factor * tree, axis=0, keepdims=True))
            total = total + col
        through = to_col(jnp.sum(total * last_factor * tree, axis=0, keepdims=True))
        weights_ref[i, 0] = jnp.where(lane == 1, value_col, 0.0)
        weights_ref[i, 1] = jnp.where(lane == 0, total, jnp.where(lane == 1, through, 0.0))

        ancestor = seg
        for slot in range(depth):
            if slot > 0:
                ancestor = parent_of(ancestor, parents_s)
            slot_len = jnp.where(ancestor >= 0, lengths_s[jnp.maximum(ancestor, 0)], 0)
            seen = u_id < slot_len
            if slot == 0:
                seen = jnp.logical_and(seen, u_id <= t_id)
            bias_ref[i, slot * length : (slot + 1) * length, :] = jnp.where(seen, 0.0, -1e30)


def prepare(parents, lengths, terms, length, log_rate):
    smem = pl.BlockSpec(memory_space=pltpu.SMEM)
    vmem = pl.BlockSpec(memory_space=pltpu.VMEM)
    segs, count = len(terms), parents.shape[0]
    return pl.pallas_call(
        functools.partial(prepare_kernel, log_rate, DEPTH),
        out_shape=(
            jax.ShapeDtypeStruct((segs, DEPTH * length, length), jnp.float32),
            jax.ShapeDtypeStruct((segs, 3, length, HD), jnp.float32),
            jax.ShapeDtypeStruct((segs, 2, count, HD), jnp.float32),
        ),
        in_specs=[smem] * 2 + [vmem] * len(terms),
        out_specs=(vmem,) * 3,
        cost_estimate=pl.CostEstimate(
            flops=20 * DEPTH * segs * length * length,
            bytes_accessed=4 * DEPTH * segs * length * length,
            transcendentals=length * length,
        ),
        compiler_params=SMALL,
        name="prepare",
    )(parents, lengths, *terms)


def advantage_kernel(columns_ref, weights_ref, *refs):
    term_refs, (row_ref, adv_ref) = refs[:-2], refs[-2:]
    segs, _, length, _ = columns_ref.shape
    count = weights_ref.shape[2]
    if len(term_refs) == 1:
        firsts = read_terms(term_refs[0])[1]
    else:
        own = lax.axis_index("seg")
        part, pair, pairs = lax.rem(own, segs), own // segs, count // segs
        seg_id = lax.broadcasted_iota(jnp.int32, (count, length), 0)
        firsts = jnp.zeros((count, length), jnp.float32)
        for index, ref in enumerate(term_refs):
            step, side = divmod(index, segs)
            place = lax.rem(ring_place(pair) - step + pairs, pairs)
            seg = ring_place(place) * segs + lax.rem(part + side, segs)
            firsts = jnp.where(seg_id == seg, read_terms(ref)[1], firsts)
    for i in range(segs):
        later_value = jnp.sum(weights_ref[i, 0] * firsts, axis=(0, 1), keepdims=True)
        later_head = jnp.sum(weights_ref[i, 1] * firsts, axis=(0, 1), keepdims=True)
        advantage = (
            columns_ref[i, 0] + columns_ref[i, 1] * later_value + columns_ref[i, 2] * later_head
        )
        adv_ref[i] = advantage
        if i == 0:
            row_id = lax.broadcasted_iota(jnp.int32, advantage.shape, 0)
            col_id = lax.broadcasted_iota(jnp.int32, advantage.shape, 1)
            row_ref[...] = jnp.sum(
                jnp.where(row_id == col_id, advantage, 0.0), axis=0, keepdims=True
            )


def advantages_of(columns, weights, terms):
    vmem = pl.BlockSpec(memory_space=pltpu.VMEM)
    segs, _, length, _ = columns.shape
    return pl.pallas_call(
        advantage_kernel,
        out_shape=(
            jax.ShapeDtypeStruct((1, length), jnp.float32),
            jax.ShapeDtypeStruct((segs, length, HD), jnp.float32),
        ),
        in_specs=[vmem] * (2 + len(terms)),
        out_specs=(vmem,) * 2,
        cost_estimate=pl.CostEstimate(
            flops=10 * segs * length * HD, bytes_accessed=16 * segs * length * HD, transcendentals=0
        ),
        compiler_params=SMALL,
        name="advantages",
    )(columns, weights, *terms)


def attend_kernel(depth, chunk, segs, sources, group_size, *refs):
    parents_s, adv_ref, bias_ref = refs[:3]
    query_refs, kv_refs = refs[3 : 3 + segs], refs[3 + segs : 3 + segs + sources]
    kv_scr, p_scr, ds_scr, acc_scr = refs[-4:]
    refs = refs[3 + segs + sources : -4]
    steps = sources // segs
    dkv_ref, dq_refs = refs[-1], refs[:segs]

    length = query_refs[0].shape[2]
    own = lax.axis_index("seg")
    for source in range(sources):
        for plane in range(2):
            rows = slice((2 * chunk + plane) * length, (2 * chunk + plane + 1) * length)
            kv_scr[source, plane] = kv_refs[source][rows, :]
    acc_scr[...] = jnp.zeros_like(acc_scr)

    scale = HD**-0.5
    contract_last = (((1,), (1,)), ((), ()))
    contract_first = (((0,), (0,)), ((), ()))
    for i in range(segs):
        ancestor = segment_of(own, segs, i)
        part = lax.rem(own, segs)
        chosen = []
        for slot in range(depth):
            if slot > 0:
                ancestor = parent_of(ancestor, parents_s)
            if segs == 1:
                chosen.append(slot)
            else:
                known = jnp.maximum(ancestor, 0)
                step = ring_place((own - part) // segs) - ring_place(known // segs)
                step = lax.rem(step + sources // segs, sources // segs)
                turn = lax.rem(lax.rem(known, segs) - part + segs, segs)
                chosen.append(jnp.where(ancestor >= 0, step * segs + turn, 0))
        q_list = [query_refs[i][0, j] for j in range(group_size)]
        dir_list = [query_refs[i][1, j] for j in range(group_size)]
        do_list = [(adv_ref[i] * d.astype(jnp.float32)).astype(jnp.bfloat16) for d in dir_list]
        k_all = jnp.concatenate([kv_scr[s, 0] for s in chosen], axis=0)
        v_all = jnp.concatenate([kv_scr[s, 1] for s in chosen], axis=0)
        q_all = jnp.concatenate(q_list, axis=0)
        do_all = jnp.concatenate(do_list, axis=0)
        all_scores = lax.dot_general(
            k_all, q_all, contract_last, preferred_element_type=jnp.float32
        )
        all_dprob = lax.dot_general(
            v_all, do_all, contract_last, preferred_element_type=jnp.float32
        )
        for j in range(group_size):
            columns = slice(j * length, (j + 1) * length)
            scores = all_scores[:, columns] * (scale * LOG2E) + bias_ref[i]
            top = jnp.max(scores, axis=0, keepdims=True)
            unnorm = jnp.exp2(scores - top)
            prob = unnorm * (1.0 / jnp.sum(unnorm, axis=0, keepdims=True))
            prob_low = prob.astype(jnp.bfloat16)
            dprob = all_dprob[:, columns]
            row_dot = jnp.sum(prob_low.astype(jnp.float32) * dprob, axis=0, keepdims=True)
            dscore = (prob * (dprob - row_dot)).astype(jnp.bfloat16)
            p_scr[:, columns] = prob_low
            ds_scr[:, columns] = dscore
        dscore_all = ds_scr[...]
        dq_t = lax.dot_general(
            k_all, dscore_all, contract_first, preferred_element_type=jnp.float32
        )
        for j in range(group_size):
            dq = jnp.transpose(dq_t[:, j * length : (j + 1) * length]) * scale
            dq_refs[i][:, j * HD : (j + 1) * HD] = dq.astype(jnp.bfloat16)
        dk_all = jnp.dot(dscore_all, q_all, preferred_element_type=jnp.float32) * scale
        dv_all = jnp.dot(p_scr[...], do_all, preferred_element_type=jnp.float32)
        for slot, s in enumerate(chosen):
            rows = slice(slot * length, (slot + 1) * length)
            acc_scr[s, 0] += dk_all[rows]
            acc_scr[s, 1] += dv_all[rows]
    for step in range(steps):
        target = step
        if segs > 1:
            place = ring_place(own // segs) - step + steps
            target = ring_place(lax.rem(place, steps))
        for i in range(segs):
            dkv_ref[target, i] = acc_scr[step * segs + i].astype(jnp.bfloat16)


def attend(parents, advantages, bias, query_list, kv_list, chunk):
    segs, length = advantages.shape[:2]
    sources = len(kv_list)
    steps = sources // segs
    group_size = query_list[0].shape[1]
    width = group_size * HD
    keys = DEPTH * length
    smem = pl.BlockSpec(memory_space=pltpu.SMEM)
    vmem = pl.BlockSpec(memory_space=pltpu.VMEM)
    out_shape = [jax.ShapeDtypeStruct((length, width), jnp.bfloat16)] * segs
    out_shape.append(jax.ShapeDtypeStruct((steps, segs, 2, length, HD), jnp.bfloat16))
    outs = pl.pallas_call(
        functools.partial(attend_kernel, DEPTH, chunk, segs, sources, group_size),
        out_shape=out_shape,
        in_specs=[smem] + [vmem] * (2 + segs + sources),
        out_specs=[vmem] * len(out_shape),
        scratch_shapes=[
            pltpu.VMEM((sources, 2, length, HD), jnp.bfloat16),
            pltpu.VMEM((keys, width), jnp.bfloat16),
            pltpu.VMEM((keys, width), jnp.bfloat16),
            pltpu.VMEM((sources, 2, length, HD), jnp.float32),
        ],
        compiler_params=pltpu.CompilerParams(vmem_limit_bytes=16 * 1024 * 1024),
        cost_estimate=pl.CostEstimate(
            flops=5 * 2 * keys * length * width * segs,
            bytes_accessed=8 * 1024 * 1024,
            transcendentals=keys * width * segs,
        ),
        name="tree_attention_backward",
    )(parents, advantages, bias, *query_list, *kv_list)
    return outs[:segs], outs[segs]


def join_queries_kernel(*refs):
    part = lax.rem(lax.axis_index("seg"), 2)
    refs, dq_ref = refs[:-1], refs[-1]
    chunks = len(refs) // 2
    width = refs[0].shape[1]
    for index, ref in enumerate(refs):
        side, chunk = divmod(index, chunks)
        where = part if side == 0 else 1 - part
        column = pl.multiple_of((where * chunks + chunk) * width, HD)
        dq_ref[:, pl.ds(column, width)] = ref[...]


def join_queries(own_list, other_list):
    chunks = len(own_list)
    length, width = own_list[0].shape
    vmem = pl.BlockSpec(memory_space=pltpu.VMEM)
    return pl.pallas_call(
        join_queries_kernel,
        out_shape=jax.ShapeDtypeStruct((length, 2 * chunks * width), jnp.bfloat16),
        in_specs=[vmem] * (2 * chunks),
        out_specs=vmem,
        cost_estimate=pl.CostEstimate(
            flops=0, bytes_accessed=8 * length * width * chunks, transcendentals=0
        ),
        compiler_params=SMALL,
        name="join_queries",
    )(*own_list, *other_list)


def join_keys_kernel(chunks, *refs):
    part = lax.rem(lax.axis_index("seg"), 2)
    other_refs, sum_refs = refs[:chunks], refs[chunks:-2]
    dk_ref, dv_ref = refs[-2:]
    for chunk in range(chunks):
        here = pl.ds(pl.multiple_of((part * chunks + chunk) * HD, HD), HD)
        there = pl.ds(pl.multiple_of(((1 - part) * chunks + chunk) * HD, HD), HD)
        for plane, out_ref in enumerate((dk_ref, dv_ref)):
            blocks = [sum_refs[chunk][pair, 0, plane] for pair in range(sum_refs[chunk].shape[0])]
            total = sum(block.astype(jnp.float32) for block in blocks)
            out_ref[:, here] = total.astype(jnp.bfloat16)
            out_ref[:, there] = other_refs[chunk][plane]


def join_keys(others, summands):
    chunks = len(others)
    length = others[0].shape[1]
    vmem = pl.BlockSpec(memory_space=pltpu.VMEM)
    out = jax.ShapeDtypeStruct((length, 2 * chunks * HD), jnp.bfloat16)
    return pl.pallas_call(
        functools.partial(join_keys_kernel, chunks),
        out_shape=(out, out),
        in_specs=[vmem] * (2 * chunks),
        out_specs=(vmem, vmem),
        cost_estimate=pl.CostEstimate(
            flops=0, bytes_accessed=16 * length * HD * chunks, transcendentals=0
        ),
        compiler_params=SMALL,
        name="join_keys",
    )(*others, *summands)


def permute(array, pairs):
    return lax.ppermute(array, "seg", pairs)


def after(array, *earlier):
    return lax.optimization_barrier((array, *earlier))[0]


def paired_body(queries, direction, key_vectors, value_vectors, token_rows, parents, lengths, log_rate):
    groups = lax.axis_size("seg")
    length = queries.shape[0]
    chunks = key_vectors.shape[1] // HD // 2
    swap = [(i, i ^ 1) for i in range(groups)]
    steps = range(1, groups // 2)
    ring = [0, 1, 3, 2]

    def turn(distance):
        pairs = []
        for place, pair in enumerate(ring):
            target = ring[(place + distance) % len(ring)]
            pairs += [(2 * pair + x, 2 * target + x) for x in range(2)]
        return pairs

    climb = turn(1)

    kept, given = pack(lengths, key_vectors, value_vectors, token_rows, 2, log_rate)
    taken = permute(given, swap)
    chain = [kept, permute(kept, climb)]
    other = [after(taken, chain[1])]
    kept_q, given_q = pack_queries(after(queries, kept), direction, 2, chunks)
    taken_q = [permute(after(given_q[0], *other), swap)]
    bias, columns, weights = prepare(parents, lengths, [kept, other[0]], length, log_rate)
    for step in steps:
        if step + 1 in steps:
            chain.append(permute(chain[-1], climb))
        gate = [bias, taken_q[0]] if step == 1 else []
        other.append(after(permute(other[-1], climb), chain[-1], *gate))
    for block in given_q[1:]:
        taken_q.append(permute(after(block, taken_q[-1]), swap))
    blocks = [block for pair in zip(chain, other) for block in pair]
    row, advantages = advantages_of(columns, weights, blocks)

    dq_own, dq_back, dkv_list = [], [], []
    for chunk in range(chunks):
        query_list = [kept_q[chunk], taken_q[chunk]]
        dq, dkv = attend(parents, advantages, bias, query_list, blocks, chunk)
        dq_own.append(dq[0])
        dq_back.append(dq[1])
        dkv_list.append(dkv)

    last = dq_own[-1]
    columns_of = [list(range(x, groups, 2)) for x in range(2)]
    summands = [
        after(lax.all_to_all(dkv, "seg", 0, 0, axis_index_groups=columns_of, tiled=True), last)
        for dkv in dkv_list
    ]
    dq_back = [permute(after(block, last), swap) for block in dq_back]
    others = []
    for blocks in summands:
        total = sum(blocks[pair, 1].astype(jnp.float32) for pair in range(len(ring)))
        others.append(permute(total.astype(jnp.bfloat16), swap))
    grad_q = join_queries(dq_own, dq_back)
    grad_k, grad_v = join_keys(others, summands)
    return grad_q, grad_k, grad_v, row[0]


def fetch_rows(spread, wanted):
    routed = jnp.take(spread, jnp.maximum(wanted, 0), axis=0)
    return lax.all_to_all(routed, "seg", split_axis=0, concat_axis=2, tiled=True)


def return_rows(grad_rows, wanted, total_segs):
    returned = lax.all_to_all(grad_rows, "seg", split_axis=2, concat_axis=0, tiled=True)
    piece_len = returned.shape[2]
    feature_len = returned.shape[3]
    routed_ids = wanted.reshape(-1)
    targets = jnp.where(routed_ids >= 0, routed_ids, total_segs)
    summed = jax.ops.segment_sum(
        returned.reshape(-1, piece_len * feature_len).astype(jnp.float32),
        targets,
        num_segments=total_segs + 1,
    )[:total_segs]
    return lax.all_to_all(
        summed.reshape(total_segs, piece_len, feature_len),
        "seg",
        split_axis=0,
        concat_axis=1,
        tiled=True,
    )


def routed_body(queries, direction, key_vectors, value_vectors, token_rows, parents, lengths, log_rate):
    total_segs = parents.shape[0]
    length, width = key_vectors.shape
    heads = width // HD
    own = lax.axis_index("seg")
    own_len = lax.dynamic_slice_in_dim(lengths, own, 1)[0]
    terms = jnp.concatenate(token_terms(log_rate, own_len, *token_rows), axis=1)
    bias, columns, weights = prepare(parents, lengths, [terms], length, log_rate)
    terms = lax.all_gather(terms, "seg", axis=0, tiled=True)
    row, advantages = advantages_of(columns, weights, [terms])
    flat = jnp.concatenate([key_vectors, value_vectors], axis=1)[None]
    spread = lax.all_to_all(flat, "seg", split_axis=1, concat_axis=0, tiled=True)
    chains = ancestors(parents, DEPTH - 1)
    arrived = fetch_rows(spread, chains)[0]
    slot_kv = jnp.concatenate([flat, arrived]).reshape(DEPTH, length, 2, heads, HD)
    slot_kv = jnp.transpose(slot_kv, (0, 3, 2, 1, 4)).reshape(DEPTH, -1, HD)
    kv_list = [slot_kv[slot] for slot in range(DEPTH)]
    (kept_q,) = pack_queries(queries, direction, 1, heads)
    dq_list, dkv_list = [], []
    for head in range(heads):
        dq, dkv = attend(parents, advantages, bias, [kept_q[head]], kv_list, head)
        dq_list.append(dq[0])
        dkv_list.append(dkv[:, 0])
    rows = jnp.transpose(jnp.stack(dkv_list), (1, 3, 2, 0, 4)).reshape(1, DEPTH, length, -1)
    summed = return_rows(rows[:, 1:], chains, total_segs)[0] + rows[0, 0].astype(jnp.float32)
    grad_keys = summed[:, :width].astype(jnp.bfloat16)
    grad_values = summed[:, width:].astype(jnp.bfloat16)
    return jnp.concatenate(dq_list, axis=1), grad_keys, grad_values, row[0]


def body(
    queries,
    key_vectors,
    value_vectors,
    direction,
    rewards,
    logprobs,
    ref_logprobs,
    value_est,
    parents,
    seg_lengths,
):
    groups = lax.axis_size("seg")
    assert parents.shape[0] == groups
    log_rate = math.log(LAMBDA_SEG) / rewards.shape[0]
    token_rows = [rewards[None], logprobs[None], ref_logprobs[None], value_est[None]]
    plan = paired_body if groups == PAIRED_GROUPS else routed_body
    return plan(
        queries, direction, key_vectors, value_vectors, token_rows, parents, seg_lengths, log_rate
    )


def solution(mesh):
    in_specs = (
        P(("grp", "seg"), "tp"),
        P(("grp", "seg"), "tp"),
        P(("grp", "seg"), "tp"),
        P(("grp", "seg"), "tp"),
        P(("grp", "seg")),
        P(("grp", "seg")),
        P(("grp", "seg")),
        P(("grp", "seg")),
        P("grp"),
        P("grp"),
    )
    out_specs = (
        P(("grp", "seg"), "tp"),
        P(("grp", "seg"), "tp"),
        P(("grp", "seg"), "tp"),
        P(("grp", "seg")),
    )
    return jax.shard_map(body, mesh=mesh, in_specs=in_specs, out_specs=out_specs, check_vma=False)
```

```python
import functools
import math

import jax
import jax.numpy as jnp
from jax import lax
from jax.experimental import pallas as pl
from jax.experimental.pallas import tpu as pltpu
from jax.sharding import PartitionSpec as P

HD = 128
DEPTH = 5
BETA = 0.1
LAMBDA_SEG = 0.7
PAIRED_GROUPS = 8
TERM_ROWS = 16
LOG2E = math.log2(math.e)
SMALL = pltpu.CompilerParams(vmem_limit_bytes=8 * 1024 * 1024)


def lookup(table_values, lookup_ids):
    matches = lookup_ids[..., None] == jnp.arange(table_values.shape[0], dtype=jnp.int32)
    return jnp.sum(jnp.where(matches, table_values, 0), axis=-1)


def ancestors(parents, count):
    current = jnp.arange(parents.shape[0], dtype=jnp.int32)
    chain_list = []
    for depth_step in range(count):
        parent_ids = lookup(parents, current)
        current = jnp.where(current >= 0, parent_ids, -1)
        chain_list.append(current)
    return jnp.stack(chain_list, axis=1)


def token_terms(log_rate, own_len, rewards, logprobs, ref_logprobs, values):
    positions = lax.broadcasted_iota(jnp.int32, rewards.shape, 1)
    later = jnp.concatenate([values[:, 1:], values[:, :1]], axis=1)
    later = jnp.where(positions + 1 < own_len, later, 0.0)
    deltas = jnp.where(
        positions < own_len, rewards - BETA * (logprobs - ref_logprobs) + later - values, 0.0
    )
    powers = jnp.exp(positions.astype(jnp.float32) * log_rate)
    first_local = jnp.sum(deltas * powers, axis=1, keepdims=True)
    firsts = jnp.where(positions == 0, first_local, jnp.where(positions == 1, values[:, :1], 0.0))
    return deltas, firsts


def split_float(value):
    parts = []
    for _ in range(3):
        part = value.astype(jnp.bfloat16)
        parts.append(part)
        value = value - part.astype(jnp.float32)
    return parts


def pack_kernel(
    log_rate,
    lengths_ref,
    k_ref,
    v_ref,
    rewards_ref,
    logprobs_ref,
    ref_logprobs_ref,
    values_ref,
    *out_refs,
):
    own = lax.axis_index("seg")
    length = k_ref.shape[0]
    parts = len(out_refs)
    heads = k_ref.shape[1] // HD // parts
    terms = token_terms(
        log_rate,
        lengths_ref[own],
        rewards_ref[...],
        logprobs_ref[...],
        ref_logprobs_ref[...],
        values_ref[...],
    )
    tail = [part.astype(jnp.float32) for x in terms for part in split_float(x)]
    tail.append(jnp.zeros((TERM_ROWS - len(tail), HD), jnp.float32))
    tail = jnp.concatenate(tail).astype(jnp.bfloat16)
    for step, out_ref in enumerate(out_refs):
        part = lax.rem(own + step, parts)
        for h in range(heads):
            columns = pl.ds(pl.multiple_of((part * heads + h) * HD, HD), HD)
            for plane, ref in enumerate((k_ref, v_ref)):
                first = (h * 2 + plane) * length
                out_ref[first : first + length, :] = ref[:, columns]
        out_ref[2 * heads * length :, :] = tail


def pack(lengths, k, v, token_rows, parts, log_rate):
    length, width = k.shape
    smem = pl.BlockSpec(memory_space=pltpu.SMEM)
    vmem = pl.BlockSpec(memory_space=pltpu.VMEM)
    heads = width // HD // parts
    assert length == HD
    block = jax.ShapeDtypeStruct((2 * heads * length + TERM_ROWS, HD), k.dtype)
    return pl.pallas_call(
        functools.partial(pack_kernel, log_rate),
        out_shape=(block,) * parts,
        in_specs=[smem] + [vmem] * 6,
        out_specs=(vmem,) * parts,
        cost_estimate=pl.CostEstimate(
            flops=length * 100, bytes_accessed=8 * length * width, transcendentals=length
        ),
        name="pack_keys_values",
    )(lengths, k, v, *token_rows)


def pack_queries_kernel(parts, q_ref, dir_ref, *out_refs):
    own = lax.axis_index("seg")
    chunks = len(out_refs) // parts
    heads = out_refs[0].shape[1]
    for index, out_ref in enumerate(out_refs):
        step, chunk = divmod(index, chunks)
        part = lax.rem(own + step, parts)
        for h in range(heads):
            column = (part * chunks + chunk) * heads + h
            columns = pl.ds(pl.multiple_of(column * HD, HD), HD)
            out_ref[0, h] = q_ref[:, columns]
            out_ref[1, h] = dir_ref[:, columns]


def pack_queries(q, direction, parts, chunks):
    length, width = q.shape
    vmem = pl.BlockSpec(memory_space=pltpu.VMEM)
    block = jax.ShapeDtypeStruct((2, width // HD // parts // chunks, length, HD), q.dtype)
    outs = pl.pallas_call(
        functools.partial(pack_queries_kernel, parts),
        out_shape=(block,) * (parts * chunks),
        in_specs=[vmem, vmem],
        out_specs=(vmem,) * (parts * chunks),
        cost_estimate=pl.CostEstimate(flops=0, bytes_accessed=8 * length * width, transcendentals=0),
        compiler_params=SMALL,
        name="pack_queries",
    )(q, direction)
    return [outs[step * chunks : (step + 1) * chunks] for step in range(parts)]


def parent_of(segment, parents_s):
    known = parents_s[jnp.maximum(segment, 0)]
    return jnp.where(segment >= 0, known, -1).astype(jnp.int32)


def segment_of(own, segs, i):
    part = lax.rem(own, segs)
    return own - part + lax.rem(part + i, segs)


def read_terms(ref):
    if ref.dtype == jnp.float32:
        length = ref.shape[1] // 2
        return ref[:, :length], ref[:, length:]
    tail = ref[ref.shape[0] - TERM_ROWS :, :].astype(jnp.float32)
    return tail[0:1] + tail[1:2] + tail[2:3], tail[3:4] + tail[4:5] + tail[5:6]


def prepare_kernel(log_rate, depth, parents_s, lengths_s, *refs):
    term_refs, (bias_ref, columns_ref, weights_ref) = refs[:-3], refs[-3:]
    segs, _, length = bias_ref.shape
    count = parents_s.shape[0]
    own = lax.axis_index("seg")

    row_id = lax.broadcasted_iota(jnp.int32, (count, count), 0)
    col_id = lax.broadcasted_iota(jnp.int32, (count, count), 1)
    seg_col = lax.broadcasted_iota(jnp.int32, (count, 1), 0)

    def to_col(row):
        return jnp.sum(jnp.where(row_id == col_id, row, 0.0), axis=1, keepdims=True)

    parent_row = jnp.full((1, count), -1, jnp.int32)
    lens_col = jnp.zeros((count, 1), jnp.int32)
    for seg in range(count):
        parent_row = jnp.where(col_id[:1] == seg, parents_s[seg], parent_row)
        lens_col = jnp.where(seg_col == seg, lengths_s[seg], lens_col)
    lens_col = lens_col.astype(jnp.float32)
    children = (parent_row == row_id).astype(jnp.float32)
    tree = children / jnp.maximum(jnp.sum(children, axis=1, keepdims=True), 1.0)
    factor = jnp.exp(lens_col * log_rate)
    last_factor = jnp.exp((lens_col - 1.0) * log_rate)

    u_id = lax.broadcasted_iota(jnp.int32, (length, length), 0)
    t_id = lax.broadcasted_iota(jnp.int32, (length, length), 1)
    offset = (t_id - u_id).astype(jnp.float32)
    discount = jnp.where(offset >= 0, jnp.exp(offset * log_rate), 0.0)
    t_col = lax.broadcasted_iota(jnp.int32, (length, 1), 0)
    lane = lax.broadcasted_iota(jnp.int32, (count, HD), 1)
    for i in range(segs):
        seg = segment_of(own, segs, i)
        seg_len = lengths_s[seg]
        deltas, _ = read_terms(term_refs[i])
        live = t_col < seg_len
        left = (seg_len - t_col).astype(jnp.float32)
        columns = (
            jnp.sum(discount * deltas, axis=1, keepdims=True),
            jnp.exp((left - 1.0) * log_rate),
            jnp.exp(left * log_rate),
        )
        for index, column in enumerate(columns):
            column = jnp.where(live, column, 0.0)
            columns_ref[i, index] = jnp.broadcast_to(column, (length, HD))

        row = jnp.sum(jnp.where(row_id == seg, tree, 0.0), axis=0, keepdims=True)
        value_col = col = total = to_col(row)
        for _ in range(depth):
            col = to_col(jnp.sum(col * factor * tree, axis=0, keepdims=True))
            total = total + col
        through = to_col(jnp.sum(total * last_factor * tree, axis=0, keepdims=True))
        weights_ref[i, 0] = jnp.where(lane == 1, value_col, 0.0)
        weights_ref[i, 1] = jnp.where(lane == 0, total, jnp.where(lane == 1, through, 0.0))

        ancestor = seg
        for slot in range(depth):
            if slot > 0:
                ancestor = parent_of(ancestor, parents_s)
            slot_len = jnp.where(ancestor >= 0, lengths_s[jnp.maximum(ancestor, 0)], 0)
            seen = u_id < slot_len
            if slot == 0:
                seen = jnp.logical_and(seen, u_id <= t_id)
            bias_ref[i, slot * length : (slot + 1) * length, :] = jnp.where(seen, 0.0, -1e30)


def prepare(parents, lengths, terms, length, log_rate):
    smem = pl.BlockSpec(memory_space=pltpu.SMEM)
    vmem = pl.BlockSpec(memory_space=pltpu.VMEM)
    segs, count = len(terms), parents.shape[0]
    return pl.pallas_call(
        functools.partial(prepare_kernel, log_rate, DEPTH),
        out_shape=(
            jax.ShapeDtypeStruct((segs, DEPTH * length, length), jnp.float32),
            jax.ShapeDtypeStruct((segs, 3, length, HD), jnp.float32),
            jax.ShapeDtypeStruct((segs, 2, count, HD), jnp.float32),
        ),
        in_specs=[smem] * 2 + [vmem] * len(terms),
        out_specs=(vmem,) * 3,
        cost_estimate=pl.CostEstimate(
            flops=20 * DEPTH * segs * length * length,
            bytes_accessed=4 * DEPTH * segs * length * length,
            transcendentals=length * length,
        ),
        compiler_params=SMALL,
        name="prepare",
    )(parents, lengths, *terms)


def advantage_kernel(columns_ref, weights_ref, *refs):
    term_refs, (row_ref, adv_ref) = refs[:-2], refs[-2:]
    segs, _, length, _ = columns_ref.shape
    count = weights_ref.shape[2]
    if len(term_refs) == 1:
        firsts = read_terms(term_refs[0])[1]
    else:
        own = lax.axis_index("seg")
        part, pair = lax.rem(own, segs), own // segs
        seg_id = lax.broadcasted_iota(jnp.int32, (count, length), 0)
        firsts = jnp.zeros((count, length), jnp.float32)
        for index, ref in enumerate(term_refs):
            step, side = divmod(index, segs)
            seg = (pair ^ step) * segs + lax.rem(part + side, segs)
            firsts = jnp.where(seg_id == seg, read_terms(ref)[1], firsts)
    for i in range(segs):
        later_value = jnp.sum(weights_ref[i, 0] * firsts, axis=(0, 1), keepdims=True)
        later_head = jnp.sum(weights_ref[i, 1] * firsts, axis=(0, 1), keepdims=True)
        advantage = (
            columns_ref[i, 0] + columns_ref[i, 1] * later_value + columns_ref[i, 2] * later_head
        )
        adv_ref[i] = advantage
        if i == 0:
            row_id = lax.broadcasted_iota(jnp.int32, advantage.shape, 0)
            col_id = lax.broadcasted_iota(jnp.int32, advantage.shape, 1)
            row_ref[...] = jnp.sum(
                jnp.where(row_id == col_id, advantage, 0.0), axis=0, keepdims=True
            )


def advantages_of(columns, weights, terms):
    vmem = pl.BlockSpec(memory_space=pltpu.VMEM)
    segs, _, length, _ = columns.shape
    return pl.pallas_call(
        advantage_kernel,
        out_shape=(
            jax.ShapeDtypeStruct((1, length), jnp.float32),
            jax.ShapeDtypeStruct((segs, length, HD), jnp.float32),
        ),
        in_specs=[vmem] * (2 + len(terms)),
        out_specs=(vmem,) * 2,
        cost_estimate=pl.CostEstimate(
            flops=10 * segs * length * HD, bytes_accessed=16 * segs * length * HD, transcendentals=0
        ),
        compiler_params=SMALL,
        name="advantages",
    )(columns, weights, *terms)


def attend_kernel(depth, chunk, segs, sources, group_size, *refs):
    parents_s, adv_ref, bias_ref = refs[:3]
    query_refs, kv_refs = refs[3 : 3 + segs], refs[3 + segs : 3 + segs + sources]
    kv_scr, p_scr, ds_scr, acc_scr = refs[-4:]
    refs = refs[3 + segs + sources : -4]
    steps = sources // segs
    dkv_refs, dq_refs = refs[-steps:], refs[-steps - segs : -steps]

    length = query_refs[0].shape[2]
    own = lax.axis_index("seg")
    for source in range(sources):
        for plane in range(2):
            rows = slice((2 * chunk + plane) * length, (2 * chunk + plane + 1) * length)
            kv_scr[source, plane] = kv_refs[source][rows, :]
    acc_scr[...] = jnp.zeros_like(acc_scr)

    scale = HD**-0.5
    contract_last = (((1,), (1,)), ((), ()))
    contract_first = (((0,), (0,)), ((), ()))
    for i in range(segs):
        ancestor = segment_of(own, segs, i)
        part = lax.rem(own, segs)
        chosen = []
        for slot in range(depth):
            if slot > 0:
                ancestor = parent_of(ancestor, parents_s)
            if segs == 1:
                chosen.append(slot)
            else:
                known = jnp.maximum(ancestor, 0)
                step = (own // segs) ^ (known // segs)
                turn = lax.rem(lax.rem(known, segs) - part + segs, segs)
                chosen.append(jnp.where(ancestor >= 0, step * segs + turn, 0))
        q_list = [query_refs[i][0, j] for j in range(group_size)]
        dir_list = [query_refs[i][1, j] for j in range(group_size)]
        do_list = [(adv_ref[i] * d.astype(jnp.float32)).astype(jnp.bfloat16) for d in dir_list]
        k_all = jnp.concatenate([kv_scr[s, 0] for s in chosen], axis=0)
        v_all = jnp.concatenate([kv_scr[s, 1] for s in chosen], axis=0)
        q_all = jnp.concatenate(q_list, axis=0)
        do_all = jnp.concatenate(do_list, axis=0)
        all_scores = lax.dot_general(
            k_all, q_all, contract_last, preferred_element_type=jnp.float32
        )
        all_dprob = lax.dot_general(
            v_all, do_all, contract_last, preferred_element_type=jnp.float32
        )
        for j in range(group_size):
            columns = slice(j * length, (j + 1) * length)
            scores = all_scores[:, columns] * (scale * LOG2E) + bias_ref[i]
            top = jnp.max(scores, axis=0, keepdims=True)
            unnorm = jnp.exp2(scores - top)
            prob = unnorm * (1.0 / jnp.sum(unnorm, axis=0, keepdims=True))
            prob_low = prob.astype(jnp.bfloat16)
            dprob = all_dprob[:, columns]
            row_dot = jnp.sum(prob_low.astype(jnp.float32) * dprob, axis=0, keepdims=True)
            dscore = (prob * (dprob - row_dot)).astype(jnp.bfloat16)
            p_scr[:, columns] = prob_low
            ds_scr[:, columns] = dscore
        dscore_all = ds_scr[...]
        dq_t = lax.dot_general(
            k_all, dscore_all, contract_first, preferred_element_type=jnp.float32
        )
        for j in range(group_size):
            dq = jnp.transpose(dq_t[:, j * length : (j + 1) * length]) * scale
            dq_refs[i][:, j * HD : (j + 1) * HD] = dq.astype(jnp.bfloat16)
        dk_all = jnp.dot(dscore_all, q_all, preferred_element_type=jnp.float32) * scale
        dv_all = jnp.dot(p_scr[...], do_all, preferred_element_type=jnp.float32)
        for slot, s in enumerate(chosen):
            rows = slice(slot * length, (slot + 1) * length)
            acc_scr[s, 0] += dk_all[rows]
            acc_scr[s, 1] += dv_all[rows]
    for step in range(steps):
        for i in range(segs):
            dkv_refs[step][i] = acc_scr[step * segs + i].astype(jnp.bfloat16)


def attend(parents, advantages, bias, query_list, kv_list, chunk):
    segs, length = advantages.shape[:2]
    sources = len(kv_list)
    steps = sources // segs
    group_size = query_list[0].shape[1]
    width = group_size * HD
    keys = DEPTH * length
    smem = pl.BlockSpec(memory_space=pltpu.SMEM)
    vmem = pl.BlockSpec(memory_space=pltpu.VMEM)
    out_shape = [jax.ShapeDtypeStruct((length, width), jnp.bfloat16)] * segs
    out_shape += [jax.ShapeDtypeStruct((segs, 2, length, HD), jnp.bfloat16)] * steps
    outs = pl.pallas_call(
        functools.partial(attend_kernel, DEPTH, chunk, segs, sources, group_size),
        out_shape=out_shape,
        in_specs=[smem] + [vmem] * (2 + segs + sources),
        out_specs=[vmem] * len(out_shape),
        scratch_shapes=[
            pltpu.VMEM((sources, 2, length, HD), jnp.bfloat16),
            pltpu.VMEM((keys, width), jnp.bfloat16),
            pltpu.VMEM((keys, width), jnp.bfloat16),
            pltpu.VMEM((sources, 2, length, HD), jnp.float32),
        ],
        compiler_params=pltpu.CompilerParams(vmem_limit_bytes=16 * 1024 * 1024),
        cost_estimate=pl.CostEstimate(
            flops=5 * 2 * keys * length * width * segs,
            bytes_accessed=8 * 1024 * 1024,
            transcendentals=keys * width * segs,
        ),
        name="tree_attention_backward",
    )(parents, advantages, bias, *query_list, *kv_list)
    return outs[:segs], outs[segs:]


def join_queries_kernel(*refs):
    part = lax.rem(lax.axis_index("seg"), 2)
    refs, dq_ref = refs[:-1], refs[-1]
    chunks = len(refs) // 2
    width = refs[0].shape[1]
    for index, ref in enumerate(refs):
        side, chunk = divmod(index, chunks)
        where = part if side == 0 else 1 - part
        column = pl.multiple_of((where * chunks + chunk) * width, HD)
        dq_ref[:, pl.ds(column, width)] = ref[...]


def join_queries(own_list, other_list):
    chunks = len(own_list)
    length, width = own_list[0].shape
    vmem = pl.BlockSpec(memory_space=pltpu.VMEM)
    return pl.pallas_call(
        join_queries_kernel,
        out_shape=jax.ShapeDtypeStruct((length, 2 * chunks * width), jnp.bfloat16),
        in_specs=[vmem] * (2 * chunks),
        out_specs=vmem,
        cost_estimate=pl.CostEstimate(
            flops=0, bytes_accessed=8 * length * width * chunks, transcendentals=0
        ),
        compiler_params=SMALL,
        name="join_queries",
    )(*own_list, *other_list)


def join_keys_kernel(chunks, *refs):
    part = lax.rem(lax.axis_index("seg"), 2)
    other_refs, sum_refs = refs[:chunks], refs[chunks:-2]
    many = len(sum_refs) // chunks
    dk_ref, dv_ref = refs[-2:]
    for chunk in range(chunks):
        here = pl.ds(pl.multiple_of((part * chunks + chunk) * HD, HD), HD)
        there = pl.ds(pl.multiple_of(((1 - part) * chunks + chunk) * HD, HD), HD)
        for plane, out_ref in enumerate((dk_ref, dv_ref)):
            blocks = [ref[0, plane] for ref in sum_refs[chunk * many : (chunk + 1) * many]]
            total = sum(block.astype(jnp.float32) for block in blocks)
            out_ref[:, here] = total.astype(jnp.bfloat16)
            out_ref[:, there] = other_refs[chunk][plane]


def join_keys(others, summands):
    chunks = len(others)
    length = others[0].shape[1]
    vmem = pl.BlockSpec(memory_space=pltpu.VMEM)
    flat = [block for blocks in summands for block in blocks]
    out = jax.ShapeDtypeStruct((length, 2 * chunks * HD), jnp.bfloat16)
    return pl.pallas_call(
        functools.partial(join_keys_kernel, chunks),
        out_shape=(out, out),
        in_specs=[vmem] * (chunks + len(flat)),
        out_specs=(vmem, vmem),
        cost_estimate=pl.CostEstimate(
            flops=0, bytes_accessed=16 * length * HD * chunks, transcendentals=0
        ),
        compiler_params=SMALL,
        name="join_keys",
    )(*others, *flat)


def permute(array, pairs):
    return lax.ppermute(array, "seg", pairs)


def after(array, *earlier):
    return lax.optimization_barrier((array, *earlier))[0]


def paired_body(queries, direction, key_vectors, value_vectors, token_rows, parents, lengths, log_rate):
    groups = lax.axis_size("seg")
    length = queries.shape[0]
    chunks = key_vectors.shape[1] // HD // 2
    swap = [(i, i ^ 1) for i in range(groups)]
    steps = range(1, groups // 2)
    meet = {bits: [(i, i ^ (2 * bits)) for i in range(groups)] for bits in steps}

    kept, given = pack(lengths, key_vectors, value_vectors, token_rows, 2, log_rate)
    taken = permute(given, swap)
    kept_two, kept_one = permute(kept, meet[2]), permute(kept, meet[1])
    kept_q, given_q = pack_queries(after(queries, kept), direction, 2, chunks)
    gated = after(taken, kept_two, kept_one)
    taken_two, taken_one = permute(gated, meet[2]), permute(gated, meet[1])
    kept_three = permute(kept_two, meet[1])
    bias, columns, weights = prepare(parents, lengths, [kept, taken], length, log_rate)
    taken_q = [permute(after(given_q[0], gated), swap)]
    taken_three = permute(after(taken_two, taken_one, kept_three, bias, taken_q[0]), meet[1])
    for block in given_q[1:]:
        taken_q.append(permute(after(block, taken_three), swap))
    chain = [kept, kept_one, kept_two, kept_three]
    other = [taken, taken_one, taken_two, taken_three]
    blocks = [block for pair in zip(chain, other) for block in pair]
    row, advantages = advantages_of(columns, weights, blocks)

    dq_own, dq_back, dkv_list = [], [], []
    for chunk in range(chunks):
        query_list = [kept_q[chunk], taken_q[chunk]]
        dq, dkv = attend(parents, advantages, bias, query_list, blocks, chunk)
        dq_own.append(dq[0])
        dq_back.append(dq[1])
        dkv_list.append(dkv)

    summands = []
    for dkv in dkv_list:
        arrived = [permute(dkv[bits], meet[bits]) for bits in steps[::-1]]
        summands.append([after(dkv[0], dq_own[-1])] + arrived)
    dq_back = [permute(after(block, dq_own[-1]), swap) for block in dq_back]
    others = []
    for blocks in summands:
        total = sum(block[1].astype(jnp.float32) for block in blocks)
        others.append(permute(total.astype(jnp.bfloat16), swap))
    grad_q = join_queries(dq_own, dq_back)
    grad_k, grad_v = join_keys(others, summands)
    return grad_q, grad_k, grad_v, row[0]


def fetch_rows(spread, wanted):
    routed = jnp.take(spread, jnp.maximum(wanted, 0), axis=0)
    return lax.all_to_all(routed, "seg", split_axis=0, concat_axis=2, tiled=True)


def return_rows(grad_rows, wanted, total_segs):
    returned = lax.all_to_all(grad_rows, "seg", split_axis=2, concat_axis=0, tiled=True)
    piece_len = returned.shape[2]
    feature_len = returned.shape[3]
    routed_ids = wanted.reshape(-1)
    targets = jnp.where(routed_ids >= 0, routed_ids, total_segs)
    summed = jax.ops.segment_sum(
        returned.reshape(-1, piece_len * feature_len).astype(jnp.float32),
        targets,
        num_segments=total_segs + 1,
    )[:total_segs]
    return lax.all_to_all(
        summed.reshape(total_segs, piece_len, feature_len),
        "seg",
        split_axis=0,
        concat_axis=1,
        tiled=True,
    )


def routed_body(queries, direction, key_vectors, value_vectors, token_rows, parents, lengths, log_rate):
    total_segs = parents.shape[0]
    length, width = key_vectors.shape
    heads = width // HD
    own = lax.axis_index("seg")
    own_len = lax.dynamic_slice_in_dim(lengths, own, 1)[0]
    terms = jnp.concatenate(token_terms(log_rate, own_len, *token_rows), axis=1)
    bias, columns, weights = prepare(parents, lengths, [terms], length, log_rate)
    terms = lax.all_gather(terms, "seg", axis=0, tiled=True)
    row, advantages = advantages_of(columns, weights, [terms])
    flat = jnp.concatenate([key_vectors, value_vectors], axis=1)[None]
    spread = lax.all_to_all(flat, "seg", split_axis=1, concat_axis=0, tiled=True)
    chains = ancestors(parents, DEPTH - 1)
    arrived = fetch_rows(spread, chains)[0]
    slot_kv = jnp.concatenate([flat, arrived]).reshape(DEPTH, length, 2, heads, HD)
    slot_kv = jnp.transpose(slot_kv, (0, 3, 2, 1, 4)).reshape(DEPTH, -1, HD)
    kv_list = [slot_kv[slot] for slot in range(DEPTH)]
    (kept_q,) = pack_queries(queries, direction, 1, heads)
    dq_list, dkv_list = [], []
    for head in range(heads):
        dq, dkv = attend(parents, advantages, bias, [kept_q[head]], kv_list, head)
        dq_list.append(dq[0])
        dkv_list.append(jnp.concatenate(dkv))
    rows = jnp.transpose(jnp.stack(dkv_list), (1, 3, 2, 0, 4)).reshape(1, DEPTH, length, -1)
    summed = return_rows(rows[:, 1:], chains, total_segs)[0] + rows[0, 0].astype(jnp.float32)
    grad_keys = summed[:, :width].astype(jnp.bfloat16)
    grad_values = summed[:, width:].astype(jnp.bfloat16)
    return jnp.concatenate(dq_list, axis=1), grad_keys, grad_values, row[0]


def body(
    queries,
    key_vectors,
    value_vectors,
    direction,
    rewards,
    logprobs,
    ref_logprobs,
    value_est,
    parents,
    seg_lengths,
):
    groups = lax.axis_size("seg")
    assert parents.shape[0] == groups
    log_rate = math.log(LAMBDA_SEG) / rewards.shape[0]
    token_rows = [rewards[None], logprobs[None], ref_logprobs[None], value_est[None]]
    plan = paired_body if groups == PAIRED_GROUPS else routed_body
    return plan(
        queries, direction, key_vectors, value_vectors, token_rows, parents, seg_lengths, log_rate
    )


def solution(mesh):
    in_specs = (
        P(("grp", "seg"), "tp"),
        P(("grp", "seg"), "tp"),
        P(("grp", "seg"), "tp"),
        P(("grp", "seg"), "tp"),
        P(("grp", "seg")),
        P(("grp", "seg")),
        P(("grp", "seg")),
        P(("grp", "seg")),
        P("grp"),
        P("grp"),
    )
    out_specs = (
        P(("grp", "seg"), "tp"),
        P(("grp", "seg"), "tp"),
        P(("grp", "seg"), "tp"),
        P(("grp", "seg")),
    )
    return jax.shard_map(body, mesh=mesh, in_specs=in_specs, out_specs=out_specs, check_vma=False)
```

```python
import functools
import math

import jax
import jax.numpy as jnp
from jax import lax
from jax.experimental import pallas as pl
from jax.experimental.pallas import tpu as pltpu
from jax.sharding import PartitionSpec as P

HD = 128
DEPTH = 5
BETA = 0.1
LAMBDA_SEG = 0.7
PAIRED_GROUPS = 8
TERM_ROWS = 16
LOG2E = math.log2(math.e)
SMALL = pltpu.CompilerParams(vmem_limit_bytes=8 * 1024 * 1024)


def lookup(table_values, lookup_ids):
    matches = lookup_ids[..., None] == jnp.arange(table_values.shape[0], dtype=jnp.int32)
    return jnp.sum(jnp.where(matches, table_values, 0), axis=-1)


def ancestors(parents, count):
    current = jnp.arange(parents.shape[0], dtype=jnp.int32)
    chain_list = []
    for depth_step in range(count):
        parent_ids = lookup(parents, current)
        current = jnp.where(current >= 0, parent_ids, -1)
        chain_list.append(current)
    return jnp.stack(chain_list, axis=1)


def token_terms(log_rate, own_len, rewards, logprobs, ref_logprobs, values):
    positions = lax.broadcasted_iota(jnp.int32, rewards.shape, 1)
    later = jnp.concatenate([values[:, 1:], values[:, :1]], axis=1)
    later = jnp.where(positions + 1 < own_len, later, 0.0)
    deltas = jnp.where(
        positions < own_len, rewards - BETA * (logprobs - ref_logprobs) + later - values, 0.0
    )
    powers = jnp.exp(positions.astype(jnp.float32) * log_rate)
    first_local = jnp.sum(deltas * powers, axis=1, keepdims=True)
    firsts = jnp.where(positions == 0, first_local, jnp.where(positions == 1, values[:, :1], 0.0))
    return deltas, firsts


def split_float(value):
    parts = []
    for _ in range(3):
        part = value.astype(jnp.bfloat16)
        parts.append(part)
        value = value - part.astype(jnp.float32)
    return parts


def pack_kernel(
    log_rate,
    parts,
    lengths_ref,
    k_ref,
    v_ref,
    rewards_ref,
    logprobs_ref,
    ref_logprobs_ref,
    values_ref,
    *out_refs,
):
    own = lax.axis_index("seg")
    length = k_ref.shape[0]
    heads = len(out_refs) // parts
    terms = token_terms(
        log_rate,
        lengths_ref[own],
        rewards_ref[...],
        logprobs_ref[...],
        ref_logprobs_ref[...],
        values_ref[...],
    )
    tail = [part.astype(jnp.float32) for x in terms for part in split_float(x)]
    tail.append(jnp.zeros((TERM_ROWS - len(tail), HD), jnp.float32))
    tail = jnp.concatenate(tail).astype(jnp.bfloat16)
    for index, out_ref in enumerate(out_refs):
        step, h = divmod(index, heads)
        part = lax.rem(own + step, parts)
        columns = pl.ds(pl.multiple_of((part * heads + h) * HD, HD), HD)
        out_ref[:length, :] = k_ref[:, columns]
        out_ref[length : 2 * length, :] = v_ref[:, columns]
        if h == 0:
            out_ref[2 * length :, :] = tail


def pack(lengths, k, v, token_rows, parts, log_rate):
    length, width = k.shape
    smem = pl.BlockSpec(memory_space=pltpu.SMEM)
    vmem = pl.BlockSpec(memory_space=pltpu.VMEM)
    heads = width // HD // parts
    assert length == HD
    blocks = [
        jax.ShapeDtypeStruct((2 * length + (TERM_ROWS if h == 0 else 0), HD), k.dtype)
        for h in range(heads)
    ]
    outs = pl.pallas_call(
        functools.partial(pack_kernel, log_rate, parts),
        out_shape=blocks * parts,
        in_specs=[smem] + [vmem] * 6,
        out_specs=[vmem] * (heads * parts),
        cost_estimate=pl.CostEstimate(
            flops=length * 100, bytes_accessed=8 * length * width, transcendentals=length
        ),
        name="pack_keys_values",
    )(lengths, k, v, *token_rows)
    return [outs[step * heads : (step + 1) * heads] for step in range(parts)]


def join_blocks_kernel(mine_ref, other_ref, out_ref):
    rows = mine_ref.shape[0]
    out_ref[:rows, :] = mine_ref[...]
    out_ref[rows:, :] = other_ref[...]


def join_blocks(mine, other):
    vmem = pl.BlockSpec(memory_space=pltpu.VMEM)
    return pl.pallas_call(
        join_blocks_kernel,
        out_shape=jax.ShapeDtypeStruct((2 * mine.shape[0], HD), mine.dtype),
        in_specs=[vmem] * 2,
        out_specs=vmem,
        cost_estimate=pl.CostEstimate(flops=0, bytes_accessed=8 * mine.size, transcendentals=0),
        compiler_params=SMALL,
        name="join_blocks",
    )(mine, other)


def pack_queries_kernel(parts, q_ref, dir_ref, *out_refs):
    own = lax.axis_index("seg")
    chunks = len(out_refs) // parts
    heads = out_refs[0].shape[1]
    for index, out_ref in enumerate(out_refs):
        step, chunk = divmod(index, chunks)
        part = lax.rem(own + step, parts)
        for h in range(heads):
            column = (part * chunks + chunk) * heads + h
            columns = pl.ds(pl.multiple_of(column * HD, HD), HD)
            out_ref[0, h] = q_ref[:, columns]
            out_ref[1, h] = dir_ref[:, columns]


def pack_queries(q, direction, parts, chunks):
    length, width = q.shape
    vmem = pl.BlockSpec(memory_space=pltpu.VMEM)
    block = jax.ShapeDtypeStruct((2, width // HD // parts // chunks, length, HD), q.dtype)
    outs = pl.pallas_call(
        functools.partial(pack_queries_kernel, parts),
        out_shape=(block,) * (parts * chunks),
        in_specs=[vmem, vmem],
        out_specs=(vmem,) * (parts * chunks),
        cost_estimate=pl.CostEstimate(flops=0, bytes_accessed=8 * length * width, transcendentals=0),
        compiler_params=SMALL,
        name="pack_queries",
    )(q, direction)
    return [outs[step * chunks : (step + 1) * chunks] for step in range(parts)]


def parent_of(segment, parents_s):
    known = parents_s[jnp.maximum(segment, 0)]
    return jnp.where(segment >= 0, known, -1).astype(jnp.int32)


def segment_of(own, segs, i):
    part = lax.rem(own, segs)
    return own - part + lax.rem(part + i, segs)


def read_terms(ref, end=None):
    if ref.dtype == jnp.float32:
        length = ref.shape[1] // 2
        return ref[:, :length], ref[:, length:]
    tail = ref[end - TERM_ROWS : end, :].astype(jnp.float32)
    return tail[0:1] + tail[1:2] + tail[2:3], tail[3:4] + tail[4:5] + tail[5:6]


def prepare_kernel(log_rate, depth, parents_s, lengths_s, *refs):
    term_refs, (bias_ref, columns_ref, weights_ref) = refs[:-3], refs[-3:]
    segs, _, length = bias_ref.shape
    count = parents_s.shape[0]
    own = lax.axis_index("seg")

    row_id = lax.broadcasted_iota(jnp.int32, (count, count), 0)
    col_id = lax.broadcasted_iota(jnp.int32, (count, count), 1)
    seg_col = lax.broadcasted_iota(jnp.int32, (count, 1), 0)

    def to_col(row):
        return jnp.sum(jnp.where(row_id == col_id, row, 0.0), axis=1, keepdims=True)

    parent_row = jnp.full((1, count), -1, jnp.int32)
    lens_col = jnp.zeros((count, 1), jnp.int32)
    for seg in range(count):
        parent_row = jnp.where(col_id[:1] == seg, parents_s[seg], parent_row)
        lens_col = jnp.where(seg_col == seg, lengths_s[seg], lens_col)
    lens_col = lens_col.astype(jnp.float32)
    children = (parent_row == row_id).astype(jnp.float32)
    tree = children / jnp.maximum(jnp.sum(children, axis=1, keepdims=True), 1.0)
    factor = jnp.exp(lens_col * log_rate)
    last_factor = jnp.exp((lens_col - 1.0) * log_rate)

    u_id = lax.broadcasted_iota(jnp.int32, (length, length), 0)
    t_id = lax.broadcasted_iota(jnp.int32, (length, length), 1)
    offset = (t_id - u_id).astype(jnp.float32)
    discount = jnp.where(offset >= 0, jnp.exp(offset * log_rate), 0.0)
    t_col = lax.broadcasted_iota(jnp.int32, (length, 1), 0)
    lane = lax.broadcasted_iota(jnp.int32, (count, HD), 1)
    for i in range(segs):
        seg = segment_of(own, segs, i)
        seg_len = lengths_s[seg]
        deltas, _ = read_terms(term_refs[i], term_refs[i].shape[0])
        live = t_col < seg_len
        left = (seg_len - t_col).astype(jnp.float32)
        columns = (
            jnp.sum(discount * deltas, axis=1, keepdims=True),
            jnp.exp((left - 1.0) * log_rate),
            jnp.exp(left * log_rate),
        )
        for index, column in enumerate(columns):
            column = jnp.where(live, column, 0.0)
            columns_ref[i, index] = jnp.broadcast_to(column, (length, HD))

        row = jnp.sum(jnp.where(row_id == seg, tree, 0.0), axis=0, keepdims=True)
        value_col = col = total = to_col(row)
        for _ in range(depth):
            col = to_col(jnp.sum(col * factor * tree, axis=0, keepdims=True))
            total = total + col
        through = to_col(jnp.sum(total * last_factor * tree, axis=0, keepdims=True))
        weights_ref[i, 0] = jnp.where(lane == 1, value_col, 0.0)
        weights_ref[i, 1] = jnp.where(lane == 0, total, jnp.where(lane == 1, through, 0.0))

        ancestor = seg
        for slot in range(depth):
            if slot > 0:
                ancestor = parent_of(ancestor, parents_s)
            slot_len = jnp.where(ancestor >= 0, lengths_s[jnp.maximum(ancestor, 0)], 0)
            seen = u_id < slot_len
            if slot == 0:
                seen = jnp.logical_and(seen, u_id <= t_id)
            bias_ref[i, slot * length : (slot + 1) * length, :] = jnp.where(seen, 0.0, -1e30)


def prepare(parents, lengths, terms, length, log_rate):
    smem = pl.BlockSpec(memory_space=pltpu.SMEM)
    vmem = pl.BlockSpec(memory_space=pltpu.VMEM)
    segs, count = len(terms), parents.shape[0]
    return pl.pallas_call(
        functools.partial(prepare_kernel, log_rate, DEPTH),
        out_shape=(
            jax.ShapeDtypeStruct((segs, DEPTH * length, length), jnp.float32),
            jax.ShapeDtypeStruct((segs, 3, length, HD), jnp.float32),
            jax.ShapeDtypeStruct((segs, 2, count, HD), jnp.float32),
        ),
        in_specs=[smem] * 2 + [vmem] * len(terms),
        out_specs=(vmem,) * 3,
        cost_estimate=pl.CostEstimate(
            flops=20 * DEPTH * segs * length * length,
            bytes_accessed=4 * DEPTH * segs * length * length,
            transcendentals=length * length,
        ),
        compiler_params=SMALL,
        name="prepare",
    )(parents, lengths, *terms)


def advantage_kernel(columns_ref, weights_ref, *refs):
    term_refs, (row_ref, adv_ref) = refs[:-2], refs[-2:]
    segs, _, length, _ = columns_ref.shape
    count = weights_ref.shape[2]
    if len(term_refs) == 1:
        firsts = read_terms(term_refs[0])[1]
    else:
        own = lax.axis_index("seg")
        part, pair = lax.rem(own, segs), own // segs
        seg_id = lax.broadcasted_iota(jnp.int32, (count, length), 0)
        firsts = jnp.zeros((count, length), jnp.float32)
        for step, ref in enumerate(term_refs):
            for side in range(segs):
                seg = (pair ^ step) * segs + lax.rem(part + side, segs)
                end = (side + 1) * (ref.shape[0] // segs)
                firsts = jnp.where(seg_id == seg, read_terms(ref, end)[1], firsts)
    for i in range(segs):
        later_value = jnp.sum(weights_ref[i, 0] * firsts, axis=(0, 1), keepdims=True)
        later_head = jnp.sum(weights_ref[i, 1] * firsts, axis=(0, 1), keepdims=True)
        advantage = (
            columns_ref[i, 0] + columns_ref[i, 1] * later_value + columns_ref[i, 2] * later_head
        )
        adv_ref[i] = advantage
        if i == 0:
            row_id = lax.broadcasted_iota(jnp.int32, advantage.shape, 0)
            col_id = lax.broadcasted_iota(jnp.int32, advantage.shape, 1)
            row_ref[...] = jnp.sum(
                jnp.where(row_id == col_id, advantage, 0.0), axis=0, keepdims=True
            )


def advantages_of(columns, weights, terms):
    vmem = pl.BlockSpec(memory_space=pltpu.VMEM)
    segs, _, length, _ = columns.shape
    return pl.pallas_call(
        advantage_kernel,
        out_shape=(
            jax.ShapeDtypeStruct((1, length), jnp.float32),
            jax.ShapeDtypeStruct((segs, length, HD), jnp.float32),
        ),
        in_specs=[vmem] * (2 + len(terms)),
        out_specs=(vmem,) * 2,
        cost_estimate=pl.CostEstimate(
            flops=10 * segs * length * HD, bytes_accessed=16 * segs * length * HD, transcendentals=0
        ),
        compiler_params=SMALL,
        name="advantages",
    )(columns, weights, *terms)


def attend_kernel(depth, segs, steps, group_size, *refs):
    parents_s, adv_ref, bias_ref = refs[:3]
    query_refs, kv_refs = refs[3 : 3 + segs], refs[3 + segs : 3 + segs + steps]
    kv_scr, p_scr, ds_scr, acc_scr = refs[-4:]
    refs = refs[3 + segs + steps : -4]
    dkv_refs, dq_refs = refs[-steps:], refs[-steps - segs : -steps]

    length = query_refs[0].shape[2]
    own = lax.axis_index("seg")
    for source in range(steps * segs):
        step, side = divmod(source, segs)
        for plane in range(2):
            first = side * (kv_refs[step].shape[0] // segs) + plane * length
            kv_scr[source, plane] = kv_refs[step][first : first + length, :]
    acc_scr[...] = jnp.zeros_like(acc_scr)

    scale = HD**-0.5
    contract_last = (((1,), (1,)), ((), ()))
    contract_first = (((0,), (0,)), ((), ()))
    for i in range(segs):
        ancestor = segment_of(own, segs, i)
        part = lax.rem(own, segs)
        chosen = []
        for slot in range(depth):
            if slot > 0:
                ancestor = parent_of(ancestor, parents_s)
            if segs == 1:
                chosen.append(slot)
            else:
                known = jnp.maximum(ancestor, 0)
                step = (own // segs) ^ (known // segs)
                turn = lax.rem(lax.rem(known, segs) - part + segs, segs)
                chosen.append(jnp.where(ancestor >= 0, step * segs + turn, 0))
        q_list = [query_refs[i][0, j] for j in range(group_size)]
        dir_list = [query_refs[i][1, j] for j in range(group_size)]
        do_list = [(adv_ref[i] * d.astype(jnp.float32)).astype(jnp.bfloat16) for d in dir_list]
        k_all = jnp.concatenate([kv_scr[s, 0] for s in chosen], axis=0)
        v_all = jnp.concatenate([kv_scr[s, 1] for s in chosen], axis=0)
        q_all = jnp.concatenate(q_list, axis=0)
        do_all = jnp.concatenate(do_list, axis=0)
        all_scores = lax.dot_general(
            k_all, q_all, contract_last, preferred_element_type=jnp.float32
        )
        all_dprob = lax.dot_general(
            v_all, do_all, contract_last, preferred_element_type=jnp.float32
        )
        for j in range(group_size):
            columns = slice(j * length, (j + 1) * length)
            scores = all_scores[:, columns] * (scale * LOG2E) + bias_ref[i]
            top = jnp.max(scores, axis=0, keepdims=True)
            unnorm = jnp.exp2(scores - top)
            prob = unnorm * (1.0 / jnp.sum(unnorm, axis=0, keepdims=True))
            prob_low = prob.astype(jnp.bfloat16)
            dprob = all_dprob[:, columns]
            row_dot = jnp.sum(prob_low.astype(jnp.float32) * dprob, axis=0, keepdims=True)
            dscore = (prob * (dprob - row_dot)).astype(jnp.bfloat16)
            p_scr[:, columns] = prob_low
            ds_scr[:, columns] = dscore
        dscore_all = ds_scr[...]
        dq_t = lax.dot_general(
            k_all, dscore_all, contract_first, preferred_element_type=jnp.float32
        )
        for j in range(group_size):
            dq = jnp.transpose(dq_t[:, j * length : (j + 1) * length]) * scale
            dq_refs[i][:, j * HD : (j + 1) * HD] = dq.astype(jnp.bfloat16)
        dk_all = jnp.dot(dscore_all, q_all, preferred_element_type=jnp.float32) * scale
        dv_all = jnp.dot(p_scr[...], do_all, preferred_element_type=jnp.float32)
        for slot, s in enumerate(chosen):
            rows = slice(slot * length, (slot + 1) * length)
            acc_scr[s, 0] += dk_all[rows]
            acc_scr[s, 1] += dv_all[rows]
    for step in range(steps):
        for i in range(segs):
            dkv_refs[step][i] = acc_scr[step * segs + i].astype(jnp.bfloat16)


def attend(parents, advantages, bias, query_list, kv_list):
    segs, length = advantages.shape[:2]
    steps = len(kv_list)
    sources = steps * segs
    group_size = query_list[0].shape[1]
    width = group_size * HD
    keys = DEPTH * length
    smem = pl.BlockSpec(memory_space=pltpu.SMEM)
    vmem = pl.BlockSpec(memory_space=pltpu.VMEM)
    out_shape = [jax.ShapeDtypeStruct((length, width), jnp.bfloat16)] * segs
    out_shape += [jax.ShapeDtypeStruct((segs, 2, length, HD), jnp.bfloat16)] * steps
    outs = pl.pallas_call(
        functools.partial(attend_kernel, DEPTH, segs, steps, group_size),
        out_shape=out_shape,
        in_specs=[smem] + [vmem] * (2 + segs + steps),
        out_specs=[vmem] * len(out_shape),
        scratch_shapes=[
            pltpu.VMEM((sources, 2, length, HD), jnp.bfloat16),
            pltpu.VMEM((keys, width), jnp.bfloat16),
            pltpu.VMEM((keys, width), jnp.bfloat16),
            pltpu.VMEM((sources, 2, length, HD), jnp.float32),
        ],
        compiler_params=pltpu.CompilerParams(vmem_limit_bytes=16 * 1024 * 1024),
        cost_estimate=pl.CostEstimate(
            flops=5 * 2 * keys * length * width * segs,
            bytes_accessed=8 * 1024 * 1024,
            transcendentals=keys * width * segs,
        ),
        name="tree_attention_backward",
    )(parents, advantages, bias, *query_list, *kv_list)
    return outs[:segs], outs[segs:]


def join_queries_kernel(*refs):
    part = lax.rem(lax.axis_index("seg"), 2)
    refs, dq_ref = refs[:-1], refs[-1]
    chunks = len(refs) // 2
    width = refs[0].shape[1]
    for index, ref in enumerate(refs):
        side, chunk = divmod(index, chunks)
        where = part if side == 0 else 1 - part
        column = pl.multiple_of((where * chunks + chunk) * width, HD)
        dq_ref[:, pl.ds(column, width)] = ref[...]


def join_queries(own_list, other_list):
    chunks = len(own_list)
    length, width = own_list[0].shape
    vmem = pl.BlockSpec(memory_space=pltpu.VMEM)
    return pl.pallas_call(
        join_queries_kernel,
        out_shape=jax.ShapeDtypeStruct((length, 2 * chunks * width), jnp.bfloat16),
        in_specs=[vmem] * (2 * chunks),
        out_specs=vmem,
        cost_estimate=pl.CostEstimate(
            flops=0, bytes_accessed=8 * length * width * chunks, transcendentals=0
        ),
        compiler_params=SMALL,
        name="join_queries",
    )(*own_list, *other_list)


def join_keys_kernel(chunks, *refs):
    part = lax.rem(lax.axis_index("seg"), 2)
    other_refs, sum_refs = refs[:chunks], refs[chunks:-2]
    many = len(sum_refs) // chunks
    dk_ref, dv_ref = refs[-2:]
    for chunk in range(chunks):
        here = pl.ds(pl.multiple_of((part * chunks + chunk) * HD, HD), HD)
        there = pl.ds(pl.multiple_of(((1 - part) * chunks + chunk) * HD, HD), HD)
        for plane, out_ref in enumerate((dk_ref, dv_ref)):
            blocks = [ref[0, plane] for ref in sum_refs[chunk * many : (chunk + 1) * many]]
            total = sum(block.astype(jnp.float32) for block in blocks)
            out_ref[:, here] = total.astype(jnp.bfloat16)
            out_ref[:, there] = other_refs[chunk][plane]


def join_keys(others, summands):
    chunks = len(others)
    length = others[0].shape[1]
    vmem = pl.BlockSpec(memory_space=pltpu.VMEM)
    flat = [block for blocks in summands for block in blocks]
    out = jax.ShapeDtypeStruct((length, 2 * chunks * HD), jnp.bfloat16)
    return pl.pallas_call(
        functools.partial(join_keys_kernel, chunks),
        out_shape=(out, out),
        in_specs=[vmem] * (chunks + len(flat)),
        out_specs=(vmem, vmem),
        cost_estimate=pl.CostEstimate(
            flops=0, bytes_accessed=16 * length * HD * chunks, transcendentals=0
        ),
        compiler_params=SMALL,
        name="join_keys",
    )(*others, *flat)


def permute(array, pairs):
    return lax.ppermute(array, "seg", pairs)


def after(array, *earlier):
    return lax.optimization_barrier((array, *earlier))[0]


def paired_body(queries, direction, key_vectors, value_vectors, token_rows, parents, lengths, log_rate):
    groups = lax.axis_size("seg")
    length = queries.shape[0]
    chunks = key_vectors.shape[1] // HD // 2
    swap = [(i, i ^ 1) for i in range(groups)]
    steps = range(1, groups // 2)
    meet = {bits: [(i, i ^ (2 * bits)) for i in range(groups)] for bits in steps}

    kept, given = pack(lengths, key_vectors, value_vectors, token_rows, 2, log_rate)
    taken = [permute(block, swap) for block in given]
    kept_q, given_q = pack_queries(after(queries, kept[0]), direction, 2, chunks)
    bias, columns, weights = prepare(parents, lengths, [kept[0], taken[0]], length, log_rate)
    near = [join_blocks(kept[0], after(taken[0], *kept_q)), join_blocks(kept[1], taken[1])]
    two, one = permute(near[0], meet[2]), permute(near[0], meet[1])
    three = permute(after(two, one, near[1], bias), meet[1])
    chains = [[near[0], one, two, three]]
    taken_q = [permute(after(given_q[0], near[0], near[1]), swap)]
    block = after(near[1], two, one, taken_q[0])
    two, one = permute(block, meet[2]), permute(block, meet[1])
    taken_q.append(permute(after(given_q[1], three), swap))
    row, advantages = advantages_of(columns, weights, chains[0])

    dq_own, dq_back, dkv_list = [], [], []
    for chunk in range(chunks):
        query_list = [kept_q[chunk], taken_q[chunk]]
        dq, dkv = attend(parents, advantages, bias, query_list, chains[chunk])
        if chunk == 0:
            three = permute(after(two, dq[0]), meet[1])
            chains.append([block, one, two, three])
        dq_own.append(dq[0])
        dq_back.append(dq[1])
        dkv_list.append(dkv)

    summands = []
    for dkv in dkv_list:
        arrived = [permute(dkv[bits], meet[bits]) for bits in steps[::-1]]
        summands.append([after(dkv[0], dq_own[-1])] + arrived)
    dq_back = [permute(after(block, dq_own[-1]), swap) for block in dq_back]
    others = []
    for blocks in summands:
        total = sum(block[1].astype(jnp.float32) for block in blocks)
        others.append(permute(total.astype(jnp.bfloat16), swap))
    grad_q = join_queries(dq_own, dq_back)
    grad_k, grad_v = join_keys(others, summands)
    return grad_q, grad_k, grad_v, row[0]


def fetch_rows(spread, wanted):
    routed = jnp.take(spread, jnp.maximum(wanted, 0), axis=0)
    return lax.all_to_all(routed, "seg", split_axis=0, concat_axis=2, tiled=True)


def return_rows(grad_rows, wanted, total_segs):
    returned = lax.all_to_all(grad_rows, "seg", split_axis=2, concat_axis=0, tiled=True)
    piece_len = returned.shape[2]
    feature_len = returned.shape[3]
    routed_ids = wanted.reshape(-1)
    targets = jnp.where(routed_ids >= 0, routed_ids, total_segs)
    summed = jax.ops.segment_sum(
        returned.reshape(-1, piece_len * feature_len).astype(jnp.float32),
        targets,
        num_segments=total_segs + 1,
    )[:total_segs]
    return lax.all_to_all(
        summed.reshape(total_segs, piece_len, feature_len),
        "seg",
        split_axis=0,
        concat_axis=1,
        tiled=True,
    )


def routed_body(queries, direction, key_vectors, value_vectors, token_rows, parents, lengths, log_rate):
    total_segs = parents.shape[0]
    length, width = key_vectors.shape
    heads = width // HD
    own = lax.axis_index("seg")
    own_len = lax.dynamic_slice_in_dim(lengths, own, 1)[0]
    terms = jnp.concatenate(token_terms(log_rate, own_len, *token_rows), axis=1)
    bias, columns, weights = prepare(parents, lengths, [terms], length, log_rate)
    terms = lax.all_gather(terms, "seg", axis=0, tiled=True)
    row, advantages = advantages_of(columns, weights, [terms])
    flat = jnp.concatenate([key_vectors, value_vectors], axis=1)[None]
    spread = lax.all_to_all(flat, "seg", split_axis=1, concat_axis=0, tiled=True)
    chains = ancestors(parents, DEPTH - 1)
    arrived = fetch_rows(spread, chains)[0]
    slot_kv = jnp.concatenate([flat, arrived]).reshape(DEPTH, length, 2, heads, HD)
    slot_kv = jnp.transpose(slot_kv, (0, 3, 2, 1, 4)).reshape(DEPTH, heads, 2 * length, HD)
    (kept_q,) = pack_queries(queries, direction, 1, heads)
    dq_list, dkv_list = [], []
    for head in range(heads):
        kv_list = [slot_kv[slot, head] for slot in range(DEPTH)]
        dq, dkv = attend(parents, advantages, bias, [kept_q[head]], kv_list)
        dq_list.append(dq[0])
        dkv_list.append(jnp.concatenate(dkv))
    rows = jnp.transpose(jnp.stack(dkv_list), (1, 3, 2, 0, 4)).reshape(1, DEPTH, length, -1)
    summed = return_rows(rows[:, 1:], chains, total_segs)[0] + rows[0, 0].astype(jnp.float32)
    grad_keys = summed[:, :width].astype(jnp.bfloat16)
    grad_values = summed[:, width:].astype(jnp.bfloat16)
    return jnp.concatenate(dq_list, axis=1), grad_keys, grad_values, row[0]


def body(
    queries,
    key_vectors,
    value_vectors,
    direction,
    rewards,
    logprobs,
    ref_logprobs,
    value_est,
    parents,
    seg_lengths,
):
    groups = lax.axis_size("seg")
    assert parents.shape[0] == groups
    log_rate = math.log(LAMBDA_SEG) / rewards.shape[0]
    token_rows = [rewards[None], logprobs[None], ref_logprobs[None], value_est[None]]
    plan = paired_body if groups == PAIRED_GROUPS else routed_body
    return plan(
        queries, direction, key_vectors, value_vectors, token_rows, parents, seg_lengths, log_rate
    )


def solution(mesh):
    in_specs = (
        P(("grp", "seg"), "tp"),
        P(("grp", "seg"), "tp"),
        P(("grp", "seg"), "tp"),
        P(("grp", "seg"), "tp"),
        P(("grp", "seg")),
        P(("grp", "seg")),
        P(("grp", "seg")),
        P(("grp", "seg")),
        P("grp"),
        P("grp"),
    )
    out_specs = (
        P(("grp", "seg"), "tp"),
        P(("grp", "seg"), "tp"),
        P(("grp", "seg"), "tp"),
        P(("grp", "seg")),
    )
    return jax.shard_map(body, mesh=mesh, in_specs=in_specs, out_specs=out_specs, check_vma=False)
```

```python
import functools
import math

import jax
import jax.numpy as jnp
from jax import lax
from jax.experimental import pallas as pl
from jax.experimental.pallas import tpu as pltpu
from jax.sharding import PartitionSpec as P

HD = 128
DEPTH = 5
BETA = 0.1
LAMBDA_SEG = 0.7
PAIRED_GROUPS = 8
TERM_ROWS = 16
LOG2E = math.log2(math.e)
SMALL = pltpu.CompilerParams(vmem_limit_bytes=8 * 1024 * 1024)


def lookup(table_values, lookup_ids):
    matches = lookup_ids[..., None] == jnp.arange(table_values.shape[0], dtype=jnp.int32)
    return jnp.sum(jnp.where(matches, table_values, 0), axis=-1)


def ancestors(parents, count):
    current = jnp.arange(parents.shape[0], dtype=jnp.int32)
    chain_list = []
    for depth_step in range(count):
        parent_ids = lookup(parents, current)
        current = jnp.where(current >= 0, parent_ids, -1)
        chain_list.append(current)
    return jnp.stack(chain_list, axis=1)


def token_terms(log_rate, own_len, rewards, logprobs, ref_logprobs, values):
    positions = lax.broadcasted_iota(jnp.int32, rewards.shape, 1)
    later = jnp.concatenate([values[:, 1:], values[:, :1]], axis=1)
    later = jnp.where(positions + 1 < own_len, later, 0.0)
    deltas = jnp.where(
        positions < own_len, rewards - BETA * (logprobs - ref_logprobs) + later - values, 0.0
    )
    powers = jnp.exp(positions.astype(jnp.float32) * log_rate)
    first_local = jnp.sum(deltas * powers, axis=1, keepdims=True)
    firsts = jnp.where(positions == 0, first_local, jnp.where(positions == 1, values[:, :1], 0.0))
    return deltas, firsts


def split_float(value):
    parts = []
    for _ in range(3):
        part = value.astype(jnp.bfloat16)
        parts.append(part)
        value = value - part.astype(jnp.float32)
    return parts


def pack_kernel(
    log_rate,
    parts,
    lengths_ref,
    k_ref,
    v_ref,
    rewards_ref,
    logprobs_ref,
    ref_logprobs_ref,
    values_ref,
    *out_refs,
):
    own = lax.axis_index("seg")
    length = k_ref.shape[0]
    heads = len(out_refs) // parts
    terms = token_terms(
        log_rate,
        lengths_ref[own],
        rewards_ref[...],
        logprobs_ref[...],
        ref_logprobs_ref[...],
        values_ref[...],
    )
    tail = [part.astype(jnp.float32) for x in terms for part in split_float(x)]
    tail.append(jnp.zeros((TERM_ROWS - len(tail), HD), jnp.float32))
    tail = jnp.concatenate(tail).astype(jnp.bfloat16)
    for index, out_ref in enumerate(out_refs):
        step, h = divmod(index, heads)
        part = lax.rem(own + step, parts)
        columns = pl.ds(pl.multiple_of((part * heads + h) * HD, HD), HD)
        out_ref[:length, :] = k_ref[:, columns]
        out_ref[length : 2 * length, :] = v_ref[:, columns]
        if h == 0:
            out_ref[2 * length :, :] = tail


def pack(lengths, k, v, token_rows, parts, log_rate):
    length, width = k.shape
    smem = pl.BlockSpec(memory_space=pltpu.SMEM)
    vmem = pl.BlockSpec(memory_space=pltpu.VMEM)
    heads = width // HD // parts
    assert length == HD
    blocks = [
        jax.ShapeDtypeStruct((2 * length + (TERM_ROWS if h == 0 else 0), HD), k.dtype)
        for h in range(heads)
    ]
    outs = pl.pallas_call(
        functools.partial(pack_kernel, log_rate, parts),
        out_shape=blocks * parts,
        in_specs=[smem] + [vmem] * 6,
        out_specs=[vmem] * (heads * parts),
        cost_estimate=pl.CostEstimate(
            flops=length * 100, bytes_accessed=8 * length * width, transcendentals=length
        ),
        name="pack_keys_values",
    )(lengths, k, v, *token_rows)
    return [outs[step * heads : (step + 1) * heads] for step in range(parts)]


def join_blocks_kernel(mine_ref, other_ref, out_ref):
    rows = mine_ref.shape[0]
    out_ref[:rows, :] = mine_ref[...]
    out_ref[rows:, :] = other_ref[...]


def join_blocks(mine, other):
    vmem = pl.BlockSpec(memory_space=pltpu.VMEM)
    return pl.pallas_call(
        join_blocks_kernel,
        out_shape=jax.ShapeDtypeStruct((2 * mine.shape[0], HD), mine.dtype),
        in_specs=[vmem] * 2,
        out_specs=vmem,
        cost_estimate=pl.CostEstimate(flops=0, bytes_accessed=8 * mine.size, transcendentals=0),
        compiler_params=SMALL,
        name="join_blocks",
    )(mine, other)


def pack_queries_kernel(parts, q_ref, dir_ref, *out_refs):
    own = lax.axis_index("seg")
    chunks = len(out_refs) // parts
    heads = out_refs[0].shape[1]
    for index, out_ref in enumerate(out_refs):
        step, chunk = divmod(index, chunks)
        part = lax.rem(own + step, parts)
        for h in range(heads):
            column = (part * chunks + chunk) * heads + h
            columns = pl.ds(pl.multiple_of(column * HD, HD), HD)
            out_ref[0, h] = q_ref[:, columns]
            out_ref[1, h] = dir_ref[:, columns]


def pack_queries(q, direction, parts, chunks):
    length, width = q.shape
    vmem = pl.BlockSpec(memory_space=pltpu.VMEM)
    block = jax.ShapeDtypeStruct((2, width // HD // parts // chunks, length, HD), q.dtype)
    outs = pl.pallas_call(
        functools.partial(pack_queries_kernel, parts),
        out_shape=(block,) * (parts * chunks),
        in_specs=[vmem, vmem],
        out_specs=(vmem,) * (parts * chunks),
        cost_estimate=pl.CostEstimate(flops=0, bytes_accessed=8 * length * width, transcendentals=0),
        compiler_params=SMALL,
        name="pack_queries",
    )(q, direction)
    return [outs[step * chunks : (step + 1) * chunks] for step in range(parts)]


def parent_of(segment, parents_s):
    known = parents_s[jnp.maximum(segment, 0)]
    return jnp.where(segment >= 0, known, -1).astype(jnp.int32)


def segment_of(own, segs, i):
    part = lax.rem(own, segs)
    return own - part + lax.rem(part + i, segs)


def read_terms(ref, end=None):
    if ref.dtype == jnp.float32:
        length = ref.shape[1] // 2
        return ref[:, :length], ref[:, length:]
    tail = ref[end - TERM_ROWS : end, :].astype(jnp.float32)
    return tail[0:1] + tail[1:2] + tail[2:3], tail[3:4] + tail[4:5] + tail[5:6]


def prepare_kernel(log_rate, depth, parents_s, lengths_s, *refs):
    term_refs, (bias_ref, columns_ref, weights_ref) = refs[:-3], refs[-3:]
    segs, _, length = bias_ref.shape
    count = parents_s.shape[0]
    own = lax.axis_index("seg")

    row_id = lax.broadcasted_iota(jnp.int32, (count, count), 0)
    col_id = lax.broadcasted_iota(jnp.int32, (count, count), 1)
    seg_col = lax.broadcasted_iota(jnp.int32, (count, 1), 0)

    def to_col(row):
        return jnp.sum(jnp.where(row_id == col_id, row, 0.0), axis=1, keepdims=True)

    parent_row = jnp.full((1, count), -1, jnp.int32)
    lens_col = jnp.zeros((count, 1), jnp.int32)
    for seg in range(count):
        parent_row = jnp.where(col_id[:1] == seg, parents_s[seg], parent_row)
        lens_col = jnp.where(seg_col == seg, lengths_s[seg], lens_col)
    lens_col = lens_col.astype(jnp.float32)
    children = (parent_row == row_id).astype(jnp.float32)
    tree = children / jnp.maximum(jnp.sum(children, axis=1, keepdims=True), 1.0)
    factor = jnp.exp(lens_col * log_rate)
    last_factor = jnp.exp((lens_col - 1.0) * log_rate)

    u_id = lax.broadcasted_iota(jnp.int32, (length, length), 0)
    t_id = lax.broadcasted_iota(jnp.int32, (length, length), 1)
    offset = (t_id - u_id).astype(jnp.float32)
    discount = jnp.where(offset >= 0, jnp.exp(offset * log_rate), 0.0)
    t_col = lax.broadcasted_iota(jnp.int32, (length, 1), 0)
    lane = lax.broadcasted_iota(jnp.int32, (count, HD), 1)
    for i in range(segs):
        seg = segment_of(own, segs, i)
        seg_len = lengths_s[seg]
        deltas, _ = read_terms(term_refs[i], term_refs[i].shape[0])
        live = t_col < seg_len
        left = (seg_len - t_col).astype(jnp.float32)
        columns = (
            jnp.sum(discount * deltas, axis=1, keepdims=True),
            jnp.exp((left - 1.0) * log_rate),
            jnp.exp(left * log_rate),
        )
        for index, column in enumerate(columns):
            column = jnp.where(live, column, 0.0)
            columns_ref[i, index] = jnp.broadcast_to(column, (length, HD))

        row = jnp.sum(jnp.where(row_id == seg, tree, 0.0), axis=0, keepdims=True)
        value_col = col = total = to_col(row)
        for _ in range(depth):
            col = to_col(jnp.sum(col * factor * tree, axis=0, keepdims=True))
            total = total + col
        through = to_col(jnp.sum(total * last_factor * tree, axis=0, keepdims=True))
        weights_ref[i, 0] = jnp.where(lane == 1, value_col, 0.0)
        weights_ref[i, 1] = jnp.where(lane == 0, total, jnp.where(lane == 1, through, 0.0))

        ancestor = seg
        for slot in range(depth):
            if slot > 0:
                ancestor = parent_of(ancestor, parents_s)
            slot_len = jnp.where(ancestor >= 0, lengths_s[jnp.maximum(ancestor, 0)], 0)
            seen = u_id < slot_len
            if slot == 0:
                seen = jnp.logical_and(seen, u_id <= t_id)
            bias_ref[i, slot * length : (slot + 1) * length, :] = jnp.where(seen, 0.0, -1e30)


def prepare(parents, lengths, terms, length, log_rate):
    smem = pl.BlockSpec(memory_space=pltpu.SMEM)
    vmem = pl.BlockSpec(memory_space=pltpu.VMEM)
    segs, count = len(terms), parents.shape[0]
    return pl.pallas_call(
        functools.partial(prepare_kernel, log_rate, DEPTH),
        out_shape=(
            jax.ShapeDtypeStruct((segs, DEPTH * length, length), jnp.float32),
            jax.ShapeDtypeStruct((segs, 3, length, HD), jnp.float32),
            jax.ShapeDtypeStruct((segs, 2, count, HD), jnp.float32),
        ),
        in_specs=[smem] * 2 + [vmem] * len(terms),
        out_specs=(vmem,) * 3,
        cost_estimate=pl.CostEstimate(
            flops=20 * DEPTH * segs * length * length,
            bytes_accessed=4 * DEPTH * segs * length * length,
            transcendentals=length * length,
        ),
        compiler_params=SMALL,
        name="prepare",
    )(parents, lengths, *terms)


def advantage_kernel(columns_ref, weights_ref, *refs):
    term_refs, (row_ref, adv_ref) = refs[:-2], refs[-2:]
    segs, _, length, _ = columns_ref.shape
    count = weights_ref.shape[2]
    if len(term_refs) == 1:
        firsts = read_terms(term_refs[0])[1]
    else:
        own = lax.axis_index("seg")
        part, pair = lax.rem(own, segs), own // segs
        seg_id = lax.broadcasted_iota(jnp.int32, (count, length), 0)
        firsts = jnp.zeros((count, length), jnp.float32)
        for step, ref in enumerate(term_refs):
            for side in range(segs):
                seg = (pair ^ step) * segs + lax.rem(part + side, segs)
                end = (side + 1) * (ref.shape[0] // segs)
                firsts = jnp.where(seg_id == seg, read_terms(ref, end)[1], firsts)
    for i in range(segs):
        later_value = jnp.sum(weights_ref[i, 0] * firsts, axis=(0, 1), keepdims=True)
        later_head = jnp.sum(weights_ref[i, 1] * firsts, axis=(0, 1), keepdims=True)
        advantage = (
            columns_ref[i, 0] + columns_ref[i, 1] * later_value + columns_ref[i, 2] * later_head
        )
        adv_ref[i] = advantage
        if i == 0:
            row_id = lax.broadcasted_iota(jnp.int32, advantage.shape, 0)
            col_id = lax.broadcasted_iota(jnp.int32, advantage.shape, 1)
            row_ref[...] = jnp.sum(
                jnp.where(row_id == col_id, advantage, 0.0), axis=0, keepdims=True
            )


def advantages_of(columns, weights, terms):
    vmem = pl.BlockSpec(memory_space=pltpu.VMEM)
    segs, _, length, _ = columns.shape
    return pl.pallas_call(
        advantage_kernel,
        out_shape=(
            jax.ShapeDtypeStruct((1, length), jnp.float32),
            jax.ShapeDtypeStruct((segs, length, HD), jnp.float32),
        ),
        in_specs=[vmem] * (2 + len(terms)),
        out_specs=(vmem,) * 2,
        cost_estimate=pl.CostEstimate(
            flops=10 * segs * length * HD, bytes_accessed=16 * segs * length * HD, transcendentals=0
        ),
        compiler_params=SMALL,
        name="advantages",
    )(columns, weights, *terms)


def attend_kernel(depth, segs, steps, group_size, *refs):
    parents_s, adv_ref, bias_ref = refs[:3]
    query_refs, kv_refs = refs[3 : 3 + segs], refs[3 + segs : 3 + segs + steps]
    kv_scr, p_scr, ds_scr, acc_scr = refs[-4:]
    refs = refs[3 + segs + steps : -4]
    dkv_refs, dq_refs = refs[-steps:], refs[-steps - segs : -steps]

    length = query_refs[0].shape[2]
    own = lax.axis_index("seg")
    for source in range(steps * segs):
        step, side = divmod(source, segs)
        for plane in range(2):
            first = side * (kv_refs[step].shape[0] // segs) + plane * length
            kv_scr[source, plane] = kv_refs[step][first : first + length, :]
    acc_scr[...] = jnp.zeros_like(acc_scr)

    scale = HD**-0.5
    contract_last = (((1,), (1,)), ((), ()))
    contract_first = (((0,), (0,)), ((), ()))
    for i in range(segs):
        ancestor = segment_of(own, segs, i)
        part = lax.rem(own, segs)
        chosen = []
        for slot in range(depth):
            if slot > 0:
                ancestor = parent_of(ancestor, parents_s)
            if segs == 1:
                chosen.append(slot)
            else:
                known = jnp.maximum(ancestor, 0)
                step = (own // segs) ^ (known // segs)
                turn = lax.rem(lax.rem(known, segs) - part + segs, segs)
                chosen.append(jnp.where(ancestor >= 0, step * segs + turn, 0))
        q_list = [query_refs[i][0, j] for j in range(group_size)]
        dir_list = [query_refs[i][1, j] for j in range(group_size)]
        do_list = [(adv_ref[i] * d.astype(jnp.float32)).astype(jnp.bfloat16) for d in dir_list]
        k_all = jnp.concatenate([kv_scr[s, 0] for s in chosen], axis=0)
        v_all = jnp.concatenate([kv_scr[s, 1] for s in chosen], axis=0)
        q_all = jnp.concatenate(q_list, axis=0)
        do_all = jnp.concatenate(do_list, axis=0)
        all_scores = lax.dot_general(
            k_all, q_all, contract_last, preferred_element_type=jnp.float32
        )
        all_dprob = lax.dot_general(
            v_all, do_all, contract_last, preferred_element_type=jnp.float32
        )
        for j in range(group_size):
            columns = slice(j * length, (j + 1) * length)
            scores = all_scores[:, columns] * (scale * LOG2E) + bias_ref[i]
            top = jnp.max(scores, axis=0, keepdims=True)
            unnorm = jnp.exp2(scores - top)
            prob = unnorm * (1.0 / jnp.sum(unnorm, axis=0, keepdims=True))
            prob_low = prob.astype(jnp.bfloat16)
            dprob = all_dprob[:, columns]
            row_dot = jnp.sum(prob_low.astype(jnp.float32) * dprob, axis=0, keepdims=True)
            dscore = (prob * (dprob - row_dot)).astype(jnp.bfloat16)
            p_scr[:, columns] = prob_low
            ds_scr[:, columns] = dscore
        dscore_all = ds_scr[...]
        dq_t = lax.dot_general(
            k_all, dscore_all, contract_first, preferred_element_type=jnp.float32
        )
        for j in range(group_size):
            dq = jnp.transpose(dq_t[:, j * length : (j + 1) * length]) * scale
            dq_refs[i][:, j * HD : (j + 1) * HD] = dq.astype(jnp.bfloat16)
        dk_all = jnp.dot(dscore_all, q_all, preferred_element_type=jnp.float32) * scale
        dv_all = jnp.dot(p_scr[...], do_all, preferred_element_type=jnp.float32)
        for slot, s in enumerate(chosen):
            rows = slice(slot * length, (slot + 1) * length)
            acc_scr[s, 0] += dk_all[rows]
            acc_scr[s, 1] += dv_all[rows]
    for step in range(steps):
        for i in range(segs):
            dkv_refs[step][i] = acc_scr[step * segs + i].astype(jnp.bfloat16)


def attend(parents, advantages, bias, query_list, kv_list):
    segs, length = advantages.shape[:2]
    steps = len(kv_list)
    sources = steps * segs
    group_size = query_list[0].shape[1]
    width = group_size * HD
    keys = DEPTH * length
    smem = pl.BlockSpec(memory_space=pltpu.SMEM)
    vmem = pl.BlockSpec(memory_space=pltpu.VMEM)
    out_shape = [jax.ShapeDtypeStruct((length, width), jnp.bfloat16)] * segs
    out_shape += [jax.ShapeDtypeStruct((segs, 2, length, HD), jnp.bfloat16)] * steps
    outs = pl.pallas_call(
        functools.partial(attend_kernel, DEPTH, segs, steps, group_size),
        out_shape=out_shape,
        in_specs=[smem] + [vmem] * (2 + segs + steps),
        out_specs=[vmem] * len(out_shape),
        scratch_shapes=[
            pltpu.VMEM((sources, 2, length, HD), jnp.bfloat16),
            pltpu.VMEM((keys, width), jnp.bfloat16),
            pltpu.VMEM((keys, width), jnp.bfloat16),
            pltpu.VMEM((sources, 2, length, HD), jnp.float32),
        ],
        compiler_params=pltpu.CompilerParams(vmem_limit_bytes=16 * 1024 * 1024),
        cost_estimate=pl.CostEstimate(
            flops=5 * 2 * keys * length * width * segs,
            bytes_accessed=8 * 1024 * 1024,
            transcendentals=keys * width * segs,
        ),
        name="tree_attention_backward",
    )(parents, advantages, bias, *query_list, *kv_list)
    return outs[:segs], outs[segs:]


def join_queries_kernel(*refs):
    part = lax.rem(lax.axis_index("seg"), 2)
    refs, dq_ref = refs[:-1], refs[-1]
    chunks = len(refs) // 2
    width = refs[0].shape[1]
    for index, ref in enumerate(refs):
        side, chunk = divmod(index, chunks)
        where = part if side == 0 else 1 - part
        column = pl.multiple_of((where * chunks + chunk) * width, HD)
        dq_ref[:, pl.ds(column, width)] = ref[...]


def join_queries(own_list, other_list):
    chunks = len(own_list)
    length, width = own_list[0].shape
    vmem = pl.BlockSpec(memory_space=pltpu.VMEM)
    return pl.pallas_call(
        join_queries_kernel,
        out_shape=jax.ShapeDtypeStruct((length, 2 * chunks * width), jnp.bfloat16),
        in_specs=[vmem] * (2 * chunks),
        out_specs=vmem,
        cost_estimate=pl.CostEstimate(
            flops=0, bytes_accessed=8 * length * width * chunks, transcendentals=0
        ),
        compiler_params=SMALL,
        name="join_queries",
    )(*own_list, *other_list)


def join_keys_kernel(chunks, *refs):
    part = lax.rem(lax.axis_index("seg"), 2)
    other_refs, sum_refs = refs[:chunks], refs[chunks:-2]
    many = len(sum_refs) // chunks
    dk_ref, dv_ref = refs[-2:]
    for chunk in range(chunks):
        here = pl.ds(pl.multiple_of((part * chunks + chunk) * HD, HD), HD)
        there = pl.ds(pl.multiple_of(((1 - part) * chunks + chunk) * HD, HD), HD)
        for plane, out_ref in enumerate((dk_ref, dv_ref)):
            blocks = [ref[0, plane] for ref in sum_refs[chunk * many : (chunk + 1) * many]]
            total = sum(block.astype(jnp.float32) for block in blocks)
            out_ref[:, here] = total.astype(jnp.bfloat16)
            out_ref[:, there] = other_refs[chunk][plane]


def join_keys(others, summands):
    chunks = len(others)
    length = others[0].shape[1]
    vmem = pl.BlockSpec(memory_space=pltpu.VMEM)
    flat = [block for blocks in summands for block in blocks]
    out = jax.ShapeDtypeStruct((length, 2 * chunks * HD), jnp.bfloat16)
    return pl.pallas_call(
        functools.partial(join_keys_kernel, chunks),
        out_shape=(out, out),
        in_specs=[vmem] * (chunks + len(flat)),
        out_specs=(vmem, vmem),
        cost_estimate=pl.CostEstimate(
            flops=0, bytes_accessed=16 * length * HD * chunks, transcendentals=0
        ),
        compiler_params=SMALL,
        name="join_keys",
    )(*others, *flat)


def permute(array, pairs):
    return lax.ppermute(array, "seg", pairs)


def after(array, *earlier):
    return lax.optimization_barrier((array, *earlier))[0]


def paired_body(queries, direction, key_vectors, value_vectors, token_rows, parents, lengths, log_rate):
    groups = lax.axis_size("seg")
    length = queries.shape[0]
    chunks = key_vectors.shape[1] // HD // 2
    swap = [(i, i ^ 1) for i in range(groups)]
    steps = range(1, groups // 2)
    meet = {bits: [(i, i ^ (2 * bits)) for i in range(groups)] for bits in steps}

    kept, given = pack(lengths, key_vectors, value_vectors, token_rows, 2, log_rate)
    taken = [permute(block, swap) for block in given]
    kept_q, given_q = pack_queries(after(queries, kept[0]), direction, 2, chunks)
    bias, columns, weights = prepare(parents, lengths, [kept[0], taken[0]], length, log_rate)
    near = [join_blocks(kept[0], after(taken[0], *kept_q)), join_blocks(kept[1], taken[1])]
    two, one = permute(near[0], meet[2]), permute(near[0], meet[1])
    three = permute(after(two, one, near[1], bias), meet[1])
    chains = [[near[0], one, two, three]]
    taken_q = [permute(after(given_q[0], near[0], near[1]), swap)]
    block = after(near[1], two, one)
    two, one = permute(block, meet[2]), permute(block, meet[1])
    taken_q.append(permute(after(given_q[1], taken_q[0]), swap))
    row, advantages = advantages_of(columns, weights, chains[0])

    dq_own, dq_back, dkv_list = [], [], []
    for chunk in range(chunks):
        query_list = [kept_q[chunk], taken_q[chunk]]
        dq, dkv = attend(parents, advantages, bias, query_list, chains[chunk])
        if chunk == 0:
            three = permute(after(two, dq[0]), meet[1])
            chains.append([block, one, two, three])
        dq_own.append(dq[0])
        dq_back.append(dq[1])
        dkv_list.append(dkv)

    summands = []
    for dkv in dkv_list:
        arrived = [permute(dkv[bits], meet[bits]) for bits in steps[::-1]]
        summands.append([after(dkv[0], dq_own[-1])] + arrived)
    dq_back = [permute(block, swap) for block in dq_back]
    others = []
    for blocks in summands:
        total = sum(block[1].astype(jnp.float32) for block in blocks)
        others.append(permute(total.astype(jnp.bfloat16), swap))
    grad_q = join_queries(dq_own, dq_back)
    grad_k, grad_v = join_keys(others, summands)
    return grad_q, grad_k, grad_v, row[0]


def fetch_rows(spread, wanted):
    routed = jnp.take(spread, jnp.maximum(wanted, 0), axis=0)
    return lax.all_to_all(routed, "seg", split_axis=0, concat_axis=2, tiled=True)


def return_rows(grad_rows, wanted, total_segs):
    returned = lax.all_to_all(grad_rows, "seg", split_axis=2, concat_axis=0, tiled=True)
    piece_len = returned.shape[2]
    feature_len = returned.shape[3]
    routed_ids = wanted.reshape(-1)
    targets = jnp.where(routed_ids >= 0, routed_ids, total_segs)
    summed = jax.ops.segment_sum(
        returned.reshape(-1, piece_len * feature_len).astype(jnp.float32),
        targets,
        num_segments=total_segs + 1,
    )[:total_segs]
    return lax.all_to_all(
        summed.reshape(total_segs, piece_len, feature_len),
        "seg",
        split_axis=0,
        concat_axis=1,
        tiled=True,
    )


def routed_body(queries, direction, key_vectors, value_vectors, token_rows, parents, lengths, log_rate):
    total_segs = parents.shape[0]
    length, width = key_vectors.shape
    heads = width // HD
    own = lax.axis_index("seg")
    own_len = lax.dynamic_slice_in_dim(lengths, own, 1)[0]
    terms = jnp.concatenate(token_terms(log_rate, own_len, *token_rows), axis=1)
    bias, columns, weights = prepare(parents, lengths, [terms], length, log_rate)
    terms = lax.all_gather(terms, "seg", axis=0, tiled=True)
    row, advantages = advantages_of(columns, weights, [terms])
    flat = jnp.concatenate([key_vectors, value_vectors], axis=1)[None]
    spread = lax.all_to_all(flat, "seg", split_axis=1, concat_axis=0, tiled=True)
    chains = ancestors(parents, DEPTH - 1)
    arrived = fetch_rows(spread, chains)[0]
    slot_kv = jnp.concatenate([flat, arrived]).reshape(DEPTH, length, 2, heads, HD)
    slot_kv = jnp.transpose(slot_kv, (0, 3, 2, 1, 4)).reshape(DEPTH, heads, 2 * length, HD)
    (kept_q,) = pack_queries(queries, direction, 1, heads)
    dq_list, dkv_list = [], []
    for head in range(heads):
        kv_list = [slot_kv[slot, head] for slot in range(DEPTH)]
        dq, dkv = attend(parents, advantages, bias, [kept_q[head]], kv_list)
        dq_list.append(dq[0])
        dkv_list.append(jnp.concatenate(dkv))
    rows = jnp.transpose(jnp.stack(dkv_list), (1, 3, 2, 0, 4)).reshape(1, DEPTH, length, -1)
    summed = return_rows(rows[:, 1:], chains, total_segs)[0] + rows[0, 0].astype(jnp.float32)
    grad_keys = summed[:, :width].astype(jnp.bfloat16)
    grad_values = summed[:, width:].astype(jnp.bfloat16)
    return jnp.concatenate(dq_list, axis=1), grad_keys, grad_values, row[0]


def body(
    queries,
    key_vectors,
    value_vectors,
    direction,
    rewards,
    logprobs,
    ref_logprobs,
    value_est,
    parents,
    seg_lengths,
):
    groups = lax.axis_size("seg")
    assert parents.shape[0] == groups
    log_rate = math.log(LAMBDA_SEG) / rewards.shape[0]
    token_rows = [rewards[None], logprobs[None], ref_logprobs[None], value_est[None]]
    plan = paired_body if groups == PAIRED_GROUPS else routed_body
    return plan(
        queries, direction, key_vectors, value_vectors, token_rows, parents, seg_lengths, log_rate
    )


def solution(mesh):
    in_specs = (
        P(("grp", "seg"), "tp"),
        P(("grp", "seg"), "tp"),
        P(("grp", "seg"), "tp"),
        P(("grp", "seg"), "tp"),
        P(("grp", "seg")),
        P(("grp", "seg")),
        P(("grp", "seg")),
        P(("grp", "seg")),
        P("grp"),
        P("grp"),
    )
    out_specs = (
        P(("grp", "seg"), "tp"),
        P(("grp", "seg"), "tp"),
        P(("grp", "seg"), "tp"),
        P(("grp", "seg")),
    )
    return jax.shard_map(body, mesh=mesh, in_specs=in_specs, out_specs=out_specs, check_vma=False)
```

```python
import functools
import math

import jax
import jax.numpy as jnp
from jax import lax
from jax.experimental import pallas as pl
from jax.experimental.pallas import tpu as pltpu
from jax.sharding import PartitionSpec as P

HD = 128
DEPTH = 5
BETA = 0.1
LAMBDA_SEG = 0.7
PAIRED_GROUPS = 8
TERM_ROWS = 16
LOG2E = math.log2(math.e)
SMALL = pltpu.CompilerParams(vmem_limit_bytes=8 * 1024 * 1024)


def lookup(table_values, lookup_ids):
    matches = lookup_ids[..., None] == jnp.arange(table_values.shape[0], dtype=jnp.int32)
    return jnp.sum(jnp.where(matches, table_values, 0), axis=-1)


def ancestors(parents, count):
    current = jnp.arange(parents.shape[0], dtype=jnp.int32)
    chain_list = []
    for depth_step in range(count):
        parent_ids = lookup(parents, current)
        current = jnp.where(current >= 0, parent_ids, -1)
        chain_list.append(current)
    return jnp.stack(chain_list, axis=1)


def token_terms(log_rate, own_len, rewards, logprobs, ref_logprobs, values):
    positions = lax.broadcasted_iota(jnp.int32, rewards.shape, 1)
    later = jnp.concatenate([values[:, 1:], values[:, :1]], axis=1)
    later = jnp.where(positions + 1 < own_len, later, 0.0)
    deltas = jnp.where(
        positions < own_len, rewards - BETA * (logprobs - ref_logprobs) + later - values, 0.0
    )
    powers = jnp.exp(positions.astype(jnp.float32) * log_rate)
    first_local = jnp.sum(deltas * powers, axis=1, keepdims=True)
    firsts = jnp.where(positions == 0, first_local, jnp.where(positions == 1, values[:, :1], 0.0))
    return deltas, firsts


def split_float(value):
    parts = []
    for _ in range(3):
        part = value.astype(jnp.bfloat16)
        parts.append(part)
        value = value - part.astype(jnp.float32)
    return parts


def pack_kernel(
    log_rate,
    parts,
    lengths_ref,
    k_ref,
    v_ref,
    rewards_ref,
    logprobs_ref,
    ref_logprobs_ref,
    values_ref,
    *out_refs,
):
    own = lax.axis_index("seg")
    length = k_ref.shape[0]
    heads = len(out_refs) // parts
    terms = token_terms(
        log_rate,
        lengths_ref[own],
        rewards_ref[...],
        logprobs_ref[...],
        ref_logprobs_ref[...],
        values_ref[...],
    )
    tail = [part.astype(jnp.float32) for x in terms for part in split_float(x)]
    tail.append(jnp.zeros((TERM_ROWS - len(tail), HD), jnp.float32))
    tail = jnp.concatenate(tail).astype(jnp.bfloat16)
    for index, out_ref in enumerate(out_refs):
        step, h = divmod(index, heads)
        part = lax.rem(own + step, parts)
        columns = pl.ds(pl.multiple_of((part * heads + h) * HD, HD), HD)
        out_ref[:length, :] = k_ref[:, columns]
        out_ref[length : 2 * length, :] = v_ref[:, columns]
        if h == 0:
            out_ref[2 * length :, :] = tail


def pack(lengths, k, v, token_rows, parts, log_rate):
    length, width = k.shape
    smem = pl.BlockSpec(memory_space=pltpu.SMEM)
    vmem = pl.BlockSpec(memory_space=pltpu.VMEM)
    heads = width // HD // parts
    assert length == HD
    blocks = [
        jax.ShapeDtypeStruct((2 * length + (TERM_ROWS if h == 0 else 0), HD), k.dtype)
        for h in range(heads)
    ]
    outs = pl.pallas_call(
        functools.partial(pack_kernel, log_rate, parts),
        out_shape=blocks * parts,
        in_specs=[smem] + [vmem] * 6,
        out_specs=[vmem] * (heads * parts),
        cost_estimate=pl.CostEstimate(
            flops=length * 100, bytes_accessed=8 * length * width, transcendentals=length
        ),
        name="pack_keys_values",
    )(lengths, k, v, *token_rows)
    return [outs[step * heads : (step + 1) * heads] for step in range(parts)]


def join_blocks_kernel(mine_ref, other_ref, out_ref):
    rows = mine_ref.shape[0]
    out_ref[:rows, :] = mine_ref[...]
    out_ref[rows:, :] = other_ref[...]


def join_blocks(mine, other):
    vmem = pl.BlockSpec(memory_space=pltpu.VMEM)
    return pl.pallas_call(
        join_blocks_kernel,
        out_shape=jax.ShapeDtypeStruct((2 * mine.shape[0], HD), mine.dtype),
        in_specs=[vmem] * 2,
        out_specs=vmem,
        cost_estimate=pl.CostEstimate(flops=0, bytes_accessed=8 * mine.size, transcendentals=0),
        compiler_params=SMALL,
        name="join_blocks",
    )(mine, other)


def pack_queries_kernel(parts, q_ref, dir_ref, *out_refs):
    own = lax.axis_index("seg")
    chunks = len(out_refs) // parts
    heads = out_refs[0].shape[1]
    for index, out_ref in enumerate(out_refs):
        step, chunk = divmod(index, chunks)
        part = lax.rem(own + step, parts)
        for h in range(heads):
            column = (part * chunks + chunk) * heads + h
            columns = pl.ds(pl.multiple_of(column * HD, HD), HD)
            out_ref[0, h] = q_ref[:, columns]
            out_ref[1, h] = dir_ref[:, columns]


def pack_queries(q, direction, parts, chunks):
    length, width = q.shape
    vmem = pl.BlockSpec(memory_space=pltpu.VMEM)
    block = jax.ShapeDtypeStruct((2, width // HD // parts // chunks, length, HD), q.dtype)
    outs = pl.pallas_call(
        functools.partial(pack_queries_kernel, parts),
        out_shape=(block,) * (parts * chunks),
        in_specs=[vmem, vmem],
        out_specs=(vmem,) * (parts * chunks),
        cost_estimate=pl.CostEstimate(flops=0, bytes_accessed=8 * length * width, transcendentals=0),
        compiler_params=SMALL,
        name="pack_queries",
    )(q, direction)
    return [outs[step * chunks : (step + 1) * chunks] for step in range(parts)]


def parent_of(segment, parents_s):
    known = parents_s[jnp.maximum(segment, 0)]
    return jnp.where(segment >= 0, known, -1).astype(jnp.int32)


def segment_of(own, segs, i):
    part = lax.rem(own, segs)
    return own - part + lax.rem(part + i, segs)


def read_terms(ref, end=None):
    if ref.dtype == jnp.float32:
        length = ref.shape[1] // 2
        return ref[:, :length], ref[:, length:]
    tail = ref[end - TERM_ROWS : end, :].astype(jnp.float32)
    return tail[0:1] + tail[1:2] + tail[2:3], tail[3:4] + tail[4:5] + tail[5:6]


def prepare_kernel(log_rate, depth, parents_s, lengths_s, *refs):
    term_refs, (bias_ref, columns_ref, weights_ref) = refs[:-3], refs[-3:]
    segs, _, length = bias_ref.shape
    count = parents_s.shape[0]
    own = lax.axis_index("seg")

    row_id = lax.broadcasted_iota(jnp.int32, (count, count), 0)
    col_id = lax.broadcasted_iota(jnp.int32, (count, count), 1)
    seg_col = lax.broadcasted_iota(jnp.int32, (count, 1), 0)

    def to_col(row):
        return jnp.sum(jnp.where(row_id == col_id, row, 0.0), axis=1, keepdims=True)

    parent_row = jnp.full((1, count), -1, jnp.int32)
    lens_col = jnp.zeros((count, 1), jnp.int32)
    for seg in range(count):
        parent_row = jnp.where(col_id[:1] == seg, parents_s[seg], parent_row)
        lens_col = jnp.where(seg_col == seg, lengths_s[seg], lens_col)
    lens_col = lens_col.astype(jnp.float32)
    children = (parent_row == row_id).astype(jnp.float32)
    tree = children / jnp.maximum(jnp.sum(children, axis=1, keepdims=True), 1.0)
    factor = jnp.exp(lens_col * log_rate)
    last_factor = jnp.exp((lens_col - 1.0) * log_rate)

    u_id = lax.broadcasted_iota(jnp.int32, (length, length), 0)
    t_id = lax.broadcasted_iota(jnp.int32, (length, length), 1)
    offset = (t_id - u_id).astype(jnp.float32)
    discount = jnp.where(offset >= 0, jnp.exp(offset * log_rate), 0.0)
    t_col = lax.broadcasted_iota(jnp.int32, (length, 1), 0)
    lane = lax.broadcasted_iota(jnp.int32, (count, HD), 1)
    for i in range(segs):
        seg = segment_of(own, segs, i)
        seg_len = lengths_s[seg]
        deltas, _ = read_terms(term_refs[i], term_refs[i].shape[0])
        live = t_col < seg_len
        left = (seg_len - t_col).astype(jnp.float32)
        columns = (
            jnp.sum(discount * deltas, axis=1, keepdims=True),
            jnp.exp((left - 1.0) * log_rate),
            jnp.exp(left * log_rate),
        )
        for index, column in enumerate(columns):
            column = jnp.where(live, column, 0.0)
            columns_ref[i, index] = jnp.broadcast_to(column, (length, HD))

        row = jnp.sum(jnp.where(row_id == seg, tree, 0.0), axis=0, keepdims=True)
        value_col = col = total = to_col(row)
        for _ in range(depth):
            col = to_col(jnp.sum(col * factor * tree, axis=0, keepdims=True))
            total = total + col
        through = to_col(jnp.sum(total * last_factor * tree, axis=0, keepdims=True))
        weights_ref[i, 0] = jnp.where(lane == 1, value_col, 0.0)
        weights_ref[i, 1] = jnp.where(lane == 0, total, jnp.where(lane == 1, through, 0.0))

        ancestor = seg
        for slot in range(depth):
            if slot > 0:
                ancestor = parent_of(ancestor, parents_s)
            slot_len = jnp.where(ancestor >= 0, lengths_s[jnp.maximum(ancestor, 0)], 0)
            hidden = jnp.logical_and(t_id == 0, u_id >= slot_len)
            if slot == 0:
                hidden = jnp.logical_or(hidden, jnp.logical_and(t_id > 0, t_id == u_id))
            bias_ref[i, slot * length : (slot + 1) * length, :] = jnp.where(
                hidden, 1.0, 0.0
            ).astype(jnp.bfloat16)


def prepare(parents, lengths, terms, length, log_rate):
    smem = pl.BlockSpec(memory_space=pltpu.SMEM)
    vmem = pl.BlockSpec(memory_space=pltpu.VMEM)
    segs, count = len(terms), parents.shape[0]
    return pl.pallas_call(
        functools.partial(prepare_kernel, log_rate, DEPTH),
        out_shape=(
            jax.ShapeDtypeStruct((segs, DEPTH * length, length), jnp.bfloat16),
            jax.ShapeDtypeStruct((segs, 3, length, HD), jnp.float32),
            jax.ShapeDtypeStruct((segs, 2, count, HD), jnp.float32),
        ),
        in_specs=[smem] * 2 + [vmem] * len(terms),
        out_specs=(vmem,) * 3,
        cost_estimate=pl.CostEstimate(
            flops=20 * DEPTH * segs * length * length,
            bytes_accessed=4 * DEPTH * segs * length * length,
            transcendentals=length * length,
        ),
        compiler_params=SMALL,
        name="prepare",
    )(parents, lengths, *terms)


def advantage_kernel(columns_ref, weights_ref, *refs):
    term_refs, (row_ref, adv_ref) = refs[:-2], refs[-2:]
    segs, _, length, _ = columns_ref.shape
    count = weights_ref.shape[2]
    if len(term_refs) == 1:
        firsts = read_terms(term_refs[0])[1]
    else:
        own = lax.axis_index("seg")
        part, pair = lax.rem(own, segs), own // segs
        seg_id = lax.broadcasted_iota(jnp.int32, (count, length), 0)
        firsts = jnp.zeros((count, length), jnp.float32)
        for step, ref in enumerate(term_refs):
            for side in range(segs):
                seg = (pair ^ step) * segs + lax.rem(part + side, segs)
                end = (side + 1) * (ref.shape[0] // segs)
                firsts = jnp.where(seg_id == seg, read_terms(ref, end)[1], firsts)
    for i in range(segs):
        later_value = jnp.sum(weights_ref[i, 0] * firsts, axis=(0, 1), keepdims=True)
        later_head = jnp.sum(weights_ref[i, 1] * firsts, axis=(0, 1), keepdims=True)
        advantage = (
            columns_ref[i, 0] + columns_ref[i, 1] * later_value + columns_ref[i, 2] * later_head
        )
        adv_ref[i] = advantage
        if i == 0:
            row_id = lax.broadcasted_iota(jnp.int32, advantage.shape, 0)
            col_id = lax.broadcasted_iota(jnp.int32, advantage.shape, 1)
            row_ref[...] = jnp.sum(
                jnp.where(row_id == col_id, advantage, 0.0), axis=0, keepdims=True
            )


def advantages_of(columns, weights, terms):
    vmem = pl.BlockSpec(memory_space=pltpu.VMEM)
    segs, _, length, _ = columns.shape
    return pl.pallas_call(
        advantage_kernel,
        out_shape=(
            jax.ShapeDtypeStruct((1, length), jnp.float32),
            jax.ShapeDtypeStruct((segs, length, HD), jnp.float32),
        ),
        in_specs=[vmem] * (2 + len(terms)),
        out_specs=(vmem,) * 2,
        cost_estimate=pl.CostEstimate(
            flops=10 * segs * length * HD, bytes_accessed=16 * segs * length * HD, transcendentals=0
        ),
        compiler_params=SMALL,
        name="advantages",
    )(columns, weights, *terms)


def attend_kernel(depth, segs, steps, group_size, folded, *refs):
    parents_s, adv_ref, bias_ref = refs[:3]
    query_refs, kv_refs = refs[3 : 3 + segs], refs[3 + segs : 3 + segs + steps]
    kv_scr, p_scr, ds_scr, acc_scr = refs[-4:]
    refs = refs[3 + segs + steps : -4]
    dq_refs, dkv_refs = refs[:segs], refs[segs:]

    length = query_refs[0].shape[2]
    own = lax.axis_index("seg")
    for source in range(steps * segs):
        step, side = divmod(source, segs)
        for plane in range(2):
            first = side * (kv_refs[step].shape[0] // segs) + plane * length
            kv_scr[source, plane] = kv_refs[step][first : first + length, :]
    acc_scr[...] = jnp.zeros_like(acc_scr)

    query_id = lax.broadcasted_iota(jnp.int32, (length, length), 0)
    key_id = lax.broadcasted_iota(jnp.int32, (length, length), 1)
    hides = jnp.logical_or(key_id == 0, key_id > query_id)
    hides = jnp.where(hides, -1e30, 0.0).astype(jnp.bfloat16)
    scale = HD**-0.5
    contract_last = (((1,), (1,)), ((), ()))
    contract_first = (((0,), (0,)), ((), ()))
    for i in range(segs):
        ancestor = segment_of(own, segs, i)
        part = lax.rem(own, segs)
        chosen = []
        for slot in range(depth):
            if slot > 0:
                ancestor = parent_of(ancestor, parents_s)
            if segs == 1:
                chosen.append(slot)
            else:
                known = jnp.maximum(ancestor, 0)
                step = (own // segs) ^ (known // segs)
                turn = lax.rem(lax.rem(known, segs) - part + segs, segs)
                chosen.append(jnp.where(ancestor >= 0, step * segs + turn, 0))
        q_list = [query_refs[i][0, j] for j in range(group_size)]
        dir_list = [query_refs[i][1, j] for j in range(group_size)]
        do_list = [(adv_ref[i] * d.astype(jnp.float32)).astype(jnp.bfloat16) for d in dir_list]
        k_all = jnp.concatenate([kv_scr[s, 0] for s in chosen], axis=0)
        v_all = jnp.concatenate([kv_scr[s, 1] for s in chosen], axis=0)
        q_all = jnp.concatenate(q_list, axis=0)
        do_all = jnp.concatenate(do_list, axis=0)
        all_scores = lax.dot_general(
            jnp.concatenate([k_all, bias_ref[i]], axis=1),
            jnp.concatenate([q_all, jnp.concatenate([hides] * group_size, axis=0)], axis=1),
            contract_last,
            preferred_element_type=jnp.float32,
        )
        all_dprob = lax.dot_general(
            v_all, do_all, contract_last, preferred_element_type=jnp.float32
        )
        for j in range(group_size):
            columns = slice(j * length, (j + 1) * length)
            scores = all_scores[:, columns]
            dprob = all_dprob[:, columns]
            top = jnp.max(scores, axis=0, keepdims=True)
            unnorm = jnp.exp2((scores - top) * (scale * LOG2E))
            inverse = 1.0 / jnp.sum(unnorm, axis=0, keepdims=True)
            row_dot = jnp.sum(unnorm * dprob, axis=0, keepdims=True) * inverse
            prob = unnorm * inverse
            p_scr[:, columns] = prob.astype(jnp.bfloat16)
            ds_scr[:, columns] = (prob * (dprob - row_dot)).astype(jnp.bfloat16)
        dscore_all = ds_scr[...]
        dq_t = lax.dot_general(
            k_all, dscore_all, contract_first, preferred_element_type=jnp.float32
        )
        for j in range(group_size):
            dq = jnp.transpose(dq_t[:, j * length : (j + 1) * length]) * scale
            dq_refs[i][:, j * HD : (j + 1) * HD] = dq.astype(jnp.bfloat16)
        dk_all = jnp.dot(dscore_all, q_all, preferred_element_type=jnp.float32) * scale
        dv_all = jnp.dot(p_scr[...], do_all, preferred_element_type=jnp.float32)
        for slot, s in enumerate(chosen):
            rows = slice(slot * length, (slot + 1) * length)
            acc_scr[s, 0] += dk_all[rows]
            acc_scr[s, 1] += dv_all[rows]
    for step in range(steps):
        ref, first = dkv_refs[step % len(dkv_refs)], 0
        if folded:
            ref, first = dkv_refs[(0, 2, 1, 2)[step]], (0, 0, 0, segs)[step]
        for i in range(segs):
            ref[first + i] = acc_scr[step * segs + i].astype(jnp.bfloat16)


def attend(parents, advantages, bias, query_list, kv_list, folded=False):
    segs, length = advantages.shape[:2]
    steps = len(kv_list)
    sources = steps * segs
    group_size = query_list[0].shape[1]
    width = group_size * HD
    keys = DEPTH * length
    smem = pl.BlockSpec(memory_space=pltpu.SMEM)
    vmem = pl.BlockSpec(memory_space=pltpu.VMEM)
    out_shape = [jax.ShapeDtypeStruct((length, width), jnp.bfloat16)] * segs
    counts = [1, 1, 2] if folded else [1] * steps
    out_shape += [
        jax.ShapeDtypeStruct((many * segs, 2, length, HD), jnp.bfloat16) for many in counts
    ]
    outs = pl.pallas_call(
        functools.partial(attend_kernel, DEPTH, segs, steps, group_size, folded),
        out_shape=out_shape,
        in_specs=[smem] + [vmem] * (2 + segs + steps),
        out_specs=[vmem] * len(out_shape),
        scratch_shapes=[
            pltpu.VMEM((sources, 2, length, HD), jnp.bfloat16),
            pltpu.VMEM((keys, width), jnp.bfloat16),
            pltpu.VMEM((keys, width), jnp.bfloat16),
            pltpu.VMEM((sources, 2, length, HD), jnp.float32),
        ],
        compiler_params=pltpu.CompilerParams(vmem_limit_bytes=16 * 1024 * 1024),
        cost_estimate=pl.CostEstimate(
            flops=5 * 2 * keys * length * width * segs,
            bytes_accessed=8 * 1024 * 1024,
            transcendentals=keys * width * segs,
        ),
        name="tree_attention_backward",
    )(parents, advantages, bias, *query_list, *kv_list)
    return outs[:segs], outs[segs:]


def join_queries_kernel(*refs):
    part = lax.rem(lax.axis_index("seg"), 2)
    refs, dq_ref = refs[:-1], refs[-1]
    chunks = len(refs) // 2
    width = refs[0].shape[1]
    for index, ref in enumerate(refs):
        side, chunk = divmod(index, chunks)
        where = part if side == 0 else 1 - part
        column = pl.multiple_of((where * chunks + chunk) * width, HD)
        dq_ref[:, pl.ds(column, width)] = ref[...]


def join_queries(own_list, other_list):
    chunks = len(own_list)
    length, width = own_list[0].shape
    vmem = pl.BlockSpec(memory_space=pltpu.VMEM)
    return pl.pallas_call(
        join_queries_kernel,
        out_shape=jax.ShapeDtypeStruct((length, 2 * chunks * width), jnp.bfloat16),
        in_specs=[vmem] * (2 * chunks),
        out_specs=vmem,
        cost_estimate=pl.CostEstimate(
            flops=0, bytes_accessed=8 * length * width * chunks, transcendentals=0
        ),
        compiler_params=SMALL,
        name="join_queries",
    )(*own_list, *other_list)


def join_keys_kernel(chunks, ends, *refs):
    part = lax.rem(lax.axis_index("seg"), 2)
    other_refs, sum_refs = refs[:chunks], refs[chunks:-2]
    dk_ref, dv_ref = refs[-2:]
    for chunk in range(chunks):
        here = pl.ds(pl.multiple_of((part * chunks + chunk) * HD, HD), HD)
        there = pl.ds(pl.multiple_of(((1 - part) * chunks + chunk) * HD, HD), HD)
        for plane, out_ref in enumerate((dk_ref, dv_ref)):
            blocks = [ref[0, plane] for ref in sum_refs[ends[chunk] : ends[chunk + 1]]]
            total = sum(block.astype(jnp.float32) for block in blocks)
            out_ref[:, here] = total.astype(jnp.bfloat16)
            out_ref[:, there] = other_refs[chunk][plane]


def join_keys(others, summands):
    chunks = len(others)
    length = others[0].shape[1]
    vmem = pl.BlockSpec(memory_space=pltpu.VMEM)
    flat = [block for blocks in summands for block in blocks]
    ends = [sum(len(blocks) for blocks in summands[:chunk]) for chunk in range(chunks + 1)]
    out = jax.ShapeDtypeStruct((length, 2 * chunks * HD), jnp.bfloat16)
    return pl.pallas_call(
        functools.partial(join_keys_kernel, chunks, ends),
        out_shape=(out, out),
        in_specs=[vmem] * (chunks + len(flat)),
        out_specs=(vmem, vmem),
        cost_estimate=pl.CostEstimate(
            flops=0, bytes_accessed=16 * length * HD * chunks, transcendentals=0
        ),
        compiler_params=SMALL,
        name="join_keys",
    )(*others, *flat)


def permute(array, pairs):
    return lax.ppermute(array, "seg", pairs)


def after(array, *earlier):
    return lax.optimization_barrier((array, *earlier))[0]


def paired_body(queries, direction, key_vectors, value_vectors, token_rows, parents, lengths, log_rate):
    groups = lax.axis_size("seg")
    length = queries.shape[0]
    chunks = key_vectors.shape[1] // HD // 2
    swap = [(i, i ^ 1) for i in range(groups)]
    steps = range(1, groups // 2)
    meet = {bits: [(i, i ^ (2 * bits)) for i in range(groups)] for bits in steps}

    kept, given = pack(lengths, key_vectors, value_vectors, token_rows, 2, log_rate)
    taken = [permute(block, swap) for block in given]
    kept_q, given_q = pack_queries(after(queries, kept[0]), direction, 2, chunks)
    bias, columns, weights = prepare(parents, lengths, [kept[0], taken[0]], length, log_rate)
    near = [join_blocks(kept[0], after(taken[0], *kept_q)), join_blocks(kept[1], taken[1])]
    two, one = permute(near[0], meet[2]), permute(near[0], meet[1])
    three = permute(after(two, one, near[1], bias), meet[1])
    chains = [[near[0], one, two, three]]
    taken_q = [permute(after(given_q[0], near[0], near[1]), swap)]
    block = after(near[1], two, one)
    two, one = permute(block, meet[2]), permute(block, meet[1])
    taken_q.append(permute(after(given_q[1], taken_q[0]), swap))
    row, advantages = advantages_of(columns, weights, chains[0])

    dq_own, dq_back, dkv_list = [], [], []
    for chunk in range(chunks):
        query_list = [kept_q[chunk], taken_q[chunk]]
        dq, dkv = attend(parents, advantages, bias, query_list, chains[chunk], folded=chunk == 0)
        if chunk == 0:
            three = permute(after(two, one, dq[0]), meet[1])
            chains.append([block, one, two, three])
        dq_own.append(dq[0])
        dq_back.append(dq[1])
        dkv_list.append(dkv)

    mine, further, folded = dkv_list[0]
    met = after(permute(after(folded, chains[1][3]), meet[1]), dq_own[-1])
    further = (further.astype(jnp.float32) + met[2:].astype(jnp.float32)).astype(jnp.bfloat16)
    summands = [[mine, met, permute(further, meet[2])]]
    last = lax.optimization_barrier((*dkv_list[1], further))[:-1]
    summands.append([last[0]] + [permute(last[bits], meet[bits]) for bits in steps[::-1]])
    dq_back = [permute(block, swap) for block in dq_back]
    others = []
    for blocks in summands:
        total = sum(block[1].astype(jnp.float32) for block in blocks)
        others.append(permute(total.astype(jnp.bfloat16), swap))
    grad_q = join_queries(dq_own, dq_back)
    grad_k, grad_v = join_keys(others, summands)
    return grad_q, grad_k, grad_v, row[0]


def fetch_rows(spread, wanted):
    routed = jnp.take(spread, jnp.maximum(wanted, 0), axis=0)
    return lax.all_to_all(routed, "seg", split_axis=0, concat_axis=2, tiled=True)


def return_rows(grad_rows, wanted, total_segs):
    returned = lax.all_to_all(grad_rows, "seg", split_axis=2, concat_axis=0, tiled=True)
    piece_len = returned.shape[2]
    feature_len = returned.shape[3]
    routed_ids = wanted.reshape(-1)
    targets = jnp.where(routed_ids >= 0, routed_ids, total_segs)
    summed = jax.ops.segment_sum(
        returned.reshape(-1, piece_len * feature_len).astype(jnp.float32),
        targets,
        num_segments=total_segs + 1,
    )[:total_segs]
    return lax.all_to_all(
        summed.reshape(total_segs, piece_len, feature_len),
        "seg",
        split_axis=0,
        concat_axis=1,
        tiled=True,
    )


def routed_body(queries, direction, key_vectors, value_vectors, token_rows, parents, lengths, log_rate):
    total_segs = parents.shape[0]
    length, width = key_vectors.shape
    heads = width // HD
    own = lax.axis_index("seg")
    own_len = lax.dynamic_slice_in_dim(lengths, own, 1)[0]
    terms = jnp.concatenate(token_terms(log_rate, own_len, *token_rows), axis=1)
    bias, columns, weights = prepare(parents, lengths, [terms], length, log_rate)
    terms = lax.all_gather(terms, "seg", axis=0, tiled=True)
    row, advantages = advantages_of(columns, weights, [terms])
    flat = jnp.concatenate([key_vectors, value_vectors], axis=1)[None]
    spread = lax.all_to_all(flat, "seg", split_axis=1, concat_axis=0, tiled=True)
    chains = ancestors(parents, DEPTH - 1)
    arrived = fetch_rows(spread, chains)[0]
    slot_kv = jnp.concatenate([flat, arrived]).reshape(DEPTH, length, 2, heads, HD)
    slot_kv = jnp.transpose(slot_kv, (0, 3, 2, 1, 4)).reshape(DEPTH, heads, 2 * length, HD)
    (kept_q,) = pack_queries(queries, direction, 1, heads)
    dq_list, dkv_list = [], []
    for head in range(heads):
        kv_list = [slot_kv[slot, head] for slot in range(DEPTH)]
        dq, dkv = attend(parents, advantages, bias, [kept_q[head]], kv_list)
        dq_list.append(dq[0])
        dkv_list.append(jnp.concatenate(dkv))
    rows = jnp.transpose(jnp.stack(dkv_list), (1, 3, 2, 0, 4)).reshape(1, DEPTH, length, -1)
    summed = return_rows(rows[:, 1:], chains, total_segs)[0] + rows[0, 0].astype(jnp.float32)
    grad_keys = summed[:, :width].astype(jnp.bfloat16)
    grad_values = summed[:, width:].astype(jnp.bfloat16)
    return jnp.concatenate(dq_list, axis=1), grad_keys, grad_values, row[0]


def body(
    queries,
    key_vectors,
    value_vectors,
    direction,
    rewards,
    logprobs,
    ref_logprobs,
    value_est,
    parents,
    seg_lengths,
):
    groups = lax.axis_size("seg")
    assert parents.shape[0] == groups
    log_rate = math.log(LAMBDA_SEG) / rewards.shape[0]
    token_rows = [rewards[None], logprobs[None], ref_logprobs[None], value_est[None]]
    plan = paired_body if groups == PAIRED_GROUPS else routed_body
    return plan(
        queries, direction, key_vectors, value_vectors, token_rows, parents, seg_lengths, log_rate
    )


def solution(mesh):
    in_specs = (
        P(("grp", "seg"), "tp"),
        P(("grp", "seg"), "tp"),
        P(("grp", "seg"), "tp"),
        P(("grp", "seg"), "tp"),
        P(("grp", "seg")),
        P(("grp", "seg")),
        P(("grp", "seg")),
        P(("grp", "seg")),
        P("grp"),
        P("grp"),
    )
    out_specs = (
        P(("grp", "seg"), "tp"),
        P(("grp", "seg"), "tp"),
        P(("grp", "seg"), "tp"),
        P(("grp", "seg")),
    )
    return jax.shard_map(body, mesh=mesh, in_specs=in_specs, out_specs=out_specs, check_vma=False)
```

```python
import functools
import math

import jax
import jax.numpy as jnp
from jax import lax
from jax.experimental import pallas as pl
from jax.experimental.pallas import tpu as pltpu
from jax.sharding import PartitionSpec as P

HD = 128
DEPTH = 5
BETA = 0.1
LAMBDA_SEG = 0.7
PAIRED_GROUPS = 8
TERM_ROWS = 16
LOG2E = math.log2(math.e)
SMALL = pltpu.CompilerParams(vmem_limit_bytes=8 * 1024 * 1024)


def lookup(table_values, lookup_ids):
    matches = lookup_ids[..., None] == jnp.arange(table_values.shape[0], dtype=jnp.int32)
    return jnp.sum(jnp.where(matches, table_values, 0), axis=-1)


def ancestors(parents, count):
    current = jnp.arange(parents.shape[0], dtype=jnp.int32)
    chain_list = []
    for depth_step in range(count):
        parent_ids = lookup(parents, current)
        current = jnp.where(current >= 0, parent_ids, -1)
        chain_list.append(current)
    return jnp.stack(chain_list, axis=1)


def token_terms(log_rate, own_len, rewards, logprobs, ref_logprobs, values):
    positions = lax.broadcasted_iota(jnp.int32, rewards.shape, 1)
    later = jnp.concatenate([values[:, 1:], values[:, :1]], axis=1)
    later = jnp.where(positions + 1 < own_len, later, 0.0)
    deltas = jnp.where(
        positions < own_len, rewards - BETA * (logprobs - ref_logprobs) + later - values, 0.0
    )
    powers = jnp.exp(positions.astype(jnp.float32) * log_rate)
    first_local = jnp.sum(deltas * powers, axis=1, keepdims=True)
    firsts = jnp.where(positions == 0, first_local, jnp.where(positions == 1, values[:, :1], 0.0))
    return deltas, firsts


def split_float(value):
    parts = []
    for _ in range(3):
        part = value.astype(jnp.bfloat16)
        parts.append(part)
        value = value - part.astype(jnp.float32)
    return parts


def pack_kernel(
    log_rate,
    parts,
    lengths_ref,
    k_ref,
    v_ref,
    rewards_ref,
    logprobs_ref,
    ref_logprobs_ref,
    values_ref,
    *out_refs,
):
    own = lax.axis_index("seg")
    length = k_ref.shape[0]
    heads = len(out_refs) // parts
    terms = token_terms(
        log_rate,
        lengths_ref[own],
        rewards_ref[...],
        logprobs_ref[...],
        ref_logprobs_ref[...],
        values_ref[...],
    )
    tail = [part.astype(jnp.float32) for x in terms for part in split_float(x)]
    tail.append(jnp.zeros((TERM_ROWS - len(tail), HD), jnp.float32))
    tail = jnp.concatenate(tail).astype(jnp.bfloat16)
    for index, out_ref in enumerate(out_refs):
        step, h = divmod(index, heads)
        part = lax.rem(own + step, parts)
        columns = pl.ds(pl.multiple_of((part * heads + h) * HD, HD), HD)
        out_ref[:length, :] = k_ref[:, columns]
        out_ref[length : 2 * length, :] = v_ref[:, columns]
        if h == 0:
            out_ref[2 * length :, :] = tail


def pack(lengths, k, v, token_rows, parts, log_rate):
    length, width = k.shape
    smem = pl.BlockSpec(memory_space=pltpu.SMEM)
    vmem = pl.BlockSpec(memory_space=pltpu.VMEM)
    heads = width // HD // parts
    assert length == HD
    blocks = [
        jax.ShapeDtypeStruct((2 * length + (TERM_ROWS if h == 0 else 0), HD), k.dtype)
        for h in range(heads)
    ]
    outs = pl.pallas_call(
        functools.partial(pack_kernel, log_rate, parts),
        out_shape=blocks * parts,
        in_specs=[smem] + [vmem] * 6,
        out_specs=[vmem] * (heads * parts),
        cost_estimate=pl.CostEstimate(
            flops=length * 100, bytes_accessed=8 * length * width, transcendentals=length
        ),
        name="pack_keys_values",
    )(lengths, k, v, *token_rows)
    return [outs[step * heads : (step + 1) * heads] for step in range(parts)]


def join_blocks_kernel(mine_ref, other_ref, out_ref):
    rows = mine_ref.shape[0]
    out_ref[:rows, :] = mine_ref[...]
    out_ref[rows:, :] = other_ref[...]


def join_blocks(mine, other):
    vmem = pl.BlockSpec(memory_space=pltpu.VMEM)
    return pl.pallas_call(
        join_blocks_kernel,
        out_shape=jax.ShapeDtypeStruct((2 * mine.shape[0], HD), mine.dtype),
        in_specs=[vmem] * 2,
        out_specs=vmem,
        cost_estimate=pl.CostEstimate(flops=0, bytes_accessed=8 * mine.size, transcendentals=0),
        compiler_params=SMALL,
        name="join_blocks",
    )(mine, other)


def pack_queries_kernel(parts, q_ref, dir_ref, *out_refs):
    own = lax.axis_index("seg")
    chunks = len(out_refs) // parts
    heads = out_refs[0].shape[1]
    for index, out_ref in enumerate(out_refs):
        step, chunk = divmod(index, chunks)
        part = lax.rem(own + step, parts)
        for h in range(heads):
            column = (part * chunks + chunk) * heads + h
            columns = pl.ds(pl.multiple_of(column * HD, HD), HD)
            out_ref[0, h] = q_ref[:, columns]
            out_ref[1, h] = dir_ref[:, columns]


def pack_queries(q, direction, parts, chunks):
    length, width = q.shape
    vmem = pl.BlockSpec(memory_space=pltpu.VMEM)
    block = jax.ShapeDtypeStruct((2, width // HD // parts // chunks, length, HD), q.dtype)
    outs = pl.pallas_call(
        functools.partial(pack_queries_kernel, parts),
        out_shape=(block,) * (parts * chunks),
        in_specs=[vmem, vmem],
        out_specs=(vmem,) * (parts * chunks),
        cost_estimate=pl.CostEstimate(flops=0, bytes_accessed=8 * length * width, transcendentals=0),
        compiler_params=SMALL,
        name="pack_queries",
    )(q, direction)
    return [outs[step * chunks : (step + 1) * chunks] for step in range(parts)]


def parent_of(segment, parents_s):
    known = parents_s[jnp.maximum(segment, 0)]
    return jnp.where(segment >= 0, known, -1).astype(jnp.int32)


def segment_of(own, segs, i):
    part = lax.rem(own, segs)
    return own - part + lax.rem(part + i, segs)


def read_terms(ref, end=None):
    if ref.dtype == jnp.float32:
        length = ref.shape[1] // 2
        return ref[:, :length], ref[:, length:]
    tail = ref[end - TERM_ROWS : end, :].astype(jnp.float32)
    return tail[0:1] + tail[1:2] + tail[2:3], tail[3:4] + tail[4:5] + tail[5:6]


def prepare_kernel(log_rate, depth, parents_s, lengths_s, *refs):
    term_refs, (bias_ref, columns_ref, weights_ref) = refs[:-3], refs[-3:]
    segs, _, length = bias_ref.shape
    count = parents_s.shape[0]
    own = lax.axis_index("seg")

    row_id = lax.broadcasted_iota(jnp.int32, (count, count), 0)
    col_id = lax.broadcasted_iota(jnp.int32, (count, count), 1)
    seg_col = lax.broadcasted_iota(jnp.int32, (count, 1), 0)

    def to_col(row):
        return jnp.sum(jnp.where(row_id == col_id, row, 0.0), axis=1, keepdims=True)

    parent_row = jnp.full((1, count), -1, jnp.int32)
    lens_col = jnp.zeros((count, 1), jnp.int32)
    for seg in range(count):
        parent_row = jnp.where(col_id[:1] == seg, parents_s[seg], parent_row)
        lens_col = jnp.where(seg_col == seg, lengths_s[seg], lens_col)
    lens_col = lens_col.astype(jnp.float32)
    children = (parent_row == row_id).astype(jnp.float32)
    tree = children / jnp.maximum(jnp.sum(children, axis=1, keepdims=True), 1.0)
    factor = jnp.exp(lens_col * log_rate)
    last_factor = jnp.exp((lens_col - 1.0) * log_rate)

    u_id = lax.broadcasted_iota(jnp.int32, (length, length), 0)
    t_id = lax.broadcasted_iota(jnp.int32, (length, length), 1)
    offset = (t_id - u_id).astype(jnp.float32)
    discount = jnp.where(offset >= 0, jnp.exp(offset * log_rate), 0.0)
    t_col = lax.broadcasted_iota(jnp.int32, (length, 1), 0)
    lane = lax.broadcasted_iota(jnp.int32, (count, HD), 1)
    for i in range(segs):
        seg = segment_of(own, segs, i)
        seg_len = lengths_s[seg]
        deltas, _ = read_terms(term_refs[i], term_refs[i].shape[0])
        live = t_col < seg_len
        left = (seg_len - t_col).astype(jnp.float32)
        columns = (
            jnp.sum(discount * deltas, axis=1, keepdims=True),
            jnp.exp((left - 1.0) * log_rate),
            jnp.exp(left * log_rate),
        )
        for index, column in enumerate(columns):
            column = jnp.where(live, column, 0.0)
            columns_ref[i, index] = jnp.broadcast_to(column, (length, HD))

        row = jnp.sum(jnp.where(row_id == seg, tree, 0.0), axis=0, keepdims=True)
        value_col = col = total = to_col(row)
        for _ in range(depth):
            col = to_col(jnp.sum(col * factor * tree, axis=0, keepdims=True))
            total = total + col
        through = to_col(jnp.sum(total * last_factor * tree, axis=0, keepdims=True))
        weights_ref[i, 0] = jnp.where(lane == 1, value_col, 0.0)
        weights_ref[i, 1] = jnp.where(lane == 0, total, jnp.where(lane == 1, through, 0.0))

        ancestor = seg
        for slot in range(depth):
            if slot > 0:
                ancestor = parent_of(ancestor, parents_s)
            slot_len = jnp.where(ancestor >= 0, lengths_s[jnp.maximum(ancestor, 0)], 0)
            seen = u_id < slot_len
            if slot == 0:
                seen = jnp.logical_and(seen, u_id <= t_id)
            bias_ref[i, slot * length : (slot + 1) * length, :] = jnp.where(seen, 0.0, -1e30)


def prepare(parents, lengths, terms, length, log_rate):
    smem = pl.BlockSpec(memory_space=pltpu.SMEM)
    vmem = pl.BlockSpec(memory_space=pltpu.VMEM)
    segs, count = len(terms), parents.shape[0]
    return pl.pallas_call(
        functools.partial(prepare_kernel, log_rate, DEPTH),
        out_shape=(
            jax.ShapeDtypeStruct((segs, DEPTH * length, length), jnp.float32),
            jax.ShapeDtypeStruct((segs, 3, length, HD), jnp.float32),
            jax.ShapeDtypeStruct((segs, 2, count, HD), jnp.float32),
        ),
        in_specs=[smem] * 2 + [vmem] * len(terms),
        out_specs=(vmem,) * 3,
        cost_estimate=pl.CostEstimate(
            flops=20 * DEPTH * segs * length * length,
            bytes_accessed=4 * DEPTH * segs * length * length,
            transcendentals=length * length,
        ),
        compiler_params=SMALL,
        name="prepare",
    )(parents, lengths, *terms)


def advantage_kernel(columns_ref, weights_ref, *refs):
    term_refs, (row_ref, adv_ref) = refs[:-2], refs[-2:]
    segs, _, length, _ = columns_ref.shape
    count = weights_ref.shape[2]
    if len(term_refs) == 1:
        firsts = read_terms(term_refs[0])[1]
    else:
        own = lax.axis_index("seg")
        part, pair = lax.rem(own, segs), own // segs
        seg_id = lax.broadcasted_iota(jnp.int32, (count, length), 0)
        firsts = jnp.zeros((count, length), jnp.float32)
        for step, ref in enumerate(term_refs):
            for side in range(segs):
                seg = (pair ^ step) * segs + lax.rem(part + side, segs)
                end = (side + 1) * (ref.shape[0] // segs)
                firsts = jnp.where(seg_id == seg, read_terms(ref, end)[1], firsts)
    for i in range(segs):
        later_value = jnp.sum(weights_ref[i, 0] * firsts, axis=(0, 1), keepdims=True)
        later_head = jnp.sum(weights_ref[i, 1] * firsts, axis=(0, 1), keepdims=True)
        advantage = (
            columns_ref[i, 0] + columns_ref[i, 1] * later_value + columns_ref[i, 2] * later_head
        )
        adv_ref[i] = advantage
        if i == 0:
            row_id = lax.broadcasted_iota(jnp.int32, advantage.shape, 0)
            col_id = lax.broadcasted_iota(jnp.int32, advantage.shape, 1)
            row_ref[...] = jnp.sum(
                jnp.where(row_id == col_id, advantage, 0.0), axis=0, keepdims=True
            )


def advantages_of(columns, weights, terms):
    vmem = pl.BlockSpec(memory_space=pltpu.VMEM)
    segs, _, length, _ = columns.shape
    return pl.pallas_call(
        advantage_kernel,
        out_shape=(
            jax.ShapeDtypeStruct((1, length), jnp.float32),
            jax.ShapeDtypeStruct((segs, length, HD), jnp.float32),
        ),
        in_specs=[vmem] * (2 + len(terms)),
        out_specs=(vmem,) * 2,
        cost_estimate=pl.CostEstimate(
            flops=10 * segs * length * HD, bytes_accessed=16 * segs * length * HD, transcendentals=0
        ),
        compiler_params=SMALL,
        name="advantages",
    )(columns, weights, *terms)


def attend_kernel(depth, segs, steps, group_size, *refs):
    parents_s, adv_ref, bias_ref = refs[:3]
    query_refs, kv_refs = refs[3 : 3 + segs], refs[3 + segs : 3 + segs + steps]
    kv_scr, both_scr, acc_scr = refs[-3:]
    refs = refs[3 + segs + steps : -3]
    dkv_refs, dq_refs = refs[-steps:], refs[-steps - segs : -steps]

    length = query_refs[0].shape[2]
    own = lax.axis_index("seg")
    for source in range(steps * segs):
        step, side = divmod(source, segs)
        for plane in range(2):
            first = side * (kv_refs[step].shape[0] // segs) + plane * length
            kv_scr[source, plane] = kv_refs[step][first : first + length, :]
    acc_scr[...] = jnp.zeros_like(acc_scr)

    scale = HD**-0.5
    half = group_size * length
    contract_last = (((1,), (1,)), ((), ()))
    contract_first = (((0,), (0,)), ((), ()))
    for i in range(segs):
        ancestor = segment_of(own, segs, i)
        part = lax.rem(own, segs)
        chosen = []
        for slot in range(depth):
            if slot > 0:
                ancestor = parent_of(ancestor, parents_s)
            if segs == 1:
                chosen.append(slot)
            else:
                known = jnp.maximum(ancestor, 0)
                step = (own // segs) ^ (known // segs)
                turn = lax.rem(lax.rem(known, segs) - part + segs, segs)
                chosen.append(jnp.where(ancestor >= 0, step * segs + turn, 0))
        q_list = [query_refs[i][0, j] for j in range(group_size)]
        dir_list = [query_refs[i][1, j] for j in range(group_size)]
        do_list = [(adv_ref[i] * d.astype(jnp.float32)).astype(jnp.bfloat16) for d in dir_list]
        k_all = jnp.concatenate([kv_scr[s, 0] for s in chosen], axis=0)
        v_all = jnp.concatenate([kv_scr[s, 1] for s in chosen], axis=0)
        zeros = jnp.zeros((length, HD), jnp.bfloat16)
        right = []
        for q, grad_out in zip(q_list, do_list):
            right.append(jnp.concatenate([q, zeros], axis=1))
            right.append(jnp.concatenate([zeros, grad_out], axis=1))
        products = lax.dot_general(
            jnp.concatenate([k_all, v_all], axis=1),
            jnp.concatenate(right, axis=0),
            contract_last,
            preferred_element_type=jnp.float32,
        )
        for j in range(group_size):
            columns = slice(j * length, (j + 1) * length)
            first = 2 * j * length
            scores = products[:, first : first + length] * (scale * LOG2E) + bias_ref[i]
            top = jnp.max(scores, axis=0, keepdims=True)
            unnorm = jnp.exp2(scores - top)
            prob = unnorm * (1.0 / jnp.sum(unnorm, axis=0, keepdims=True))
            prob_low = prob.astype(jnp.bfloat16)
            dprob = products[:, first + length : first + 2 * length]
            row_dot = jnp.sum(prob_low.astype(jnp.float32) * dprob, axis=0, keepdims=True)
            dscore = (prob * (dprob - row_dot)).astype(jnp.bfloat16)
            both_scr[:, columns] = prob_low
            both_scr[:, slice(columns.start + half, columns.stop + half)] = dscore
        dscore_all = both_scr[:, half:]
        dq_t = lax.dot_general(
            k_all, dscore_all, contract_first, preferred_element_type=jnp.float32
        )
        for j in range(group_size):
            dq = jnp.transpose(dq_t[:, j * length : (j + 1) * length]) * scale
            dq_refs[i][:, j * HD : (j + 1) * HD] = dq.astype(jnp.bfloat16)
        left = jnp.concatenate(do_list + [jnp.zeros((half, HD), jnp.bfloat16)], axis=0)
        other = jnp.concatenate([jnp.zeros((half, HD), jnp.bfloat16)] + q_list, axis=0)
        grads = jnp.dot(
            both_scr[...],
            jnp.concatenate([left, other], axis=1),
            preferred_element_type=jnp.float32,
        )
        dv_all, dk_all = grads[:, :HD], grads[:, HD:] * scale
        for slot, s in enumerate(chosen):
            rows = slice(slot * length, (slot + 1) * length)
            acc_scr[s, 0] += dk_all[rows]
            acc_scr[s, 1] += dv_all[rows]
    for step in range(steps):
        for i in range(segs):
            dkv_refs[step][i] = acc_scr[step * segs + i].astype(jnp.bfloat16)


def attend(parents, advantages, bias, query_list, kv_list):
    segs, length = advantages.shape[:2]
    steps = len(kv_list)
    sources = steps * segs
    group_size = query_list[0].shape[1]
    width = group_size * HD
    keys = DEPTH * length
    smem = pl.BlockSpec(memory_space=pltpu.SMEM)
    vmem = pl.BlockSpec(memory_space=pltpu.VMEM)
    out_shape = [jax.ShapeDtypeStruct((length, width), jnp.bfloat16)] * segs
    out_shape += [jax.ShapeDtypeStruct((segs, 2, length, HD), jnp.bfloat16)] * steps
    outs = pl.pallas_call(
        functools.partial(attend_kernel, DEPTH, segs, steps, group_size),
        out_shape=out_shape,
        in_specs=[smem] + [vmem] * (2 + segs + steps),
        out_specs=[vmem] * len(out_shape),
        scratch_shapes=[
            pltpu.VMEM((sources, 2, length, HD), jnp.bfloat16),
            pltpu.VMEM((keys, 2 * group_size * length), jnp.bfloat16),
            pltpu.VMEM((sources, 2, length, HD), jnp.float32),
        ],
        compiler_params=pltpu.CompilerParams(vmem_limit_bytes=16 * 1024 * 1024),
        cost_estimate=pl.CostEstimate(
            flops=5 * 2 * keys * length * width * segs,
            bytes_accessed=8 * 1024 * 1024,
            transcendentals=keys * width * segs,
        ),
        name="tree_attention_backward",
    )(parents, advantages, bias, *query_list, *kv_list)
    return outs[:segs], outs[segs:]


def join_queries_kernel(*refs):
    part = lax.rem(lax.axis_index("seg"), 2)
    refs, dq_ref = refs[:-1], refs[-1]
    chunks = len(refs) // 2
    width = refs[0].shape[1]
    for index, ref in enumerate(refs):
        side, chunk = divmod(index, chunks)
        where = part if side == 0 else 1 - part
        column = pl.multiple_of((where * chunks + chunk) * width, HD)
        dq_ref[:, pl.ds(column, width)] = ref[...]


def join_queries(own_list, other_list):
    chunks = len(own_list)
    length, width = own_list[0].shape
    vmem = pl.BlockSpec(memory_space=pltpu.VMEM)
    return pl.pallas_call(
        join_queries_kernel,
        out_shape=jax.ShapeDtypeStruct((length, 2 * chunks * width), jnp.bfloat16),
        in_specs=[vmem] * (2 * chunks),
        out_specs=vmem,
        cost_estimate=pl.CostEstimate(
            flops=0, bytes_accessed=8 * length * width * chunks, transcendentals=0
        ),
        compiler_params=SMALL,
        name="join_queries",
    )(*own_list, *other_list)


def join_keys_kernel(chunks, *refs):
    part = lax.rem(lax.axis_index("seg"), 2)
    other_refs, sum_refs = refs[:chunks], refs[chunks:-2]
    many = len(sum_refs) // chunks
    dk_ref, dv_ref = refs[-2:]
    for chunk in range(chunks):
        here = pl.ds(pl.multiple_of((part * chunks + chunk) * HD, HD), HD)
        there = pl.ds(pl.multiple_of(((1 - part) * chunks + chunk) * HD, HD), HD)
        for plane, out_ref in enumerate((dk_ref, dv_ref)):
            blocks = [ref[0, plane] for ref in sum_refs[chunk * many : (chunk + 1) * many]]
            total = sum(block.astype(jnp.float32) for block in blocks)
            out_ref[:, here] = total.astype(jnp.bfloat16)
            out_ref[:, there] = other_refs[chunk][plane]


def join_keys(others, summands):
    chunks = len(others)
    length = others[0].shape[1]
    vmem = pl.BlockSpec(memory_space=pltpu.VMEM)
    flat = [block for blocks in summands for block in blocks]
    out = jax.ShapeDtypeStruct((length, 2 * chunks * HD), jnp.bfloat16)
    return pl.pallas_call(
        functools.partial(join_keys_kernel, chunks),
        out_shape=(out, out),
        in_specs=[vmem] * (chunks + len(flat)),
        out_specs=(vmem, vmem),
        cost_estimate=pl.CostEstimate(
            flops=0, bytes_accessed=16 * length * HD * chunks, transcendentals=0
        ),
        compiler_params=SMALL,
        name="join_keys",
    )(*others, *flat)


def permute(array, pairs):
    return lax.ppermute(array, "seg", pairs)


def after(array, *earlier):
    return lax.optimization_barrier((array, *earlier))[0]


def paired_body(queries, direction, key_vectors, value_vectors, token_rows, parents, lengths, log_rate):
    groups = lax.axis_size("seg")
    length = queries.shape[0]
    chunks = key_vectors.shape[1] // HD // 2
    swap = [(i, i ^ 1) for i in range(groups)]
    steps = range(1, groups // 2)
    meet = {bits: [(i, i ^ (2 * bits)) for i in range(groups)] for bits in steps}

    kept, given = pack(lengths, key_vectors, value_vectors, token_rows, 2, log_rate)
    taken = [permute(block, swap) for block in given]
    kept_q, given_q = pack_queries(after(queries, kept[0]), direction, 2, chunks)
    bias, columns, weights = prepare(parents, lengths, [kept[0], taken[0]], length, log_rate)
    near = [join_blocks(kept[0], after(taken[0], *kept_q)), join_blocks(kept[1], taken[1])]
    two, one = permute(near[0], meet[2]), permute(near[0], meet[1])
    three = permute(after(two, one, near[1], bias), meet[1])
    chains = [[near[0], one, two, three]]
    taken_q = [permute(after(given_q[0], near[0], near[1]), swap)]
    block = after(near[1], two, one)
    two, one = permute(block, meet[2]), permute(block, meet[1])
    taken_q.append(permute(after(given_q[1], taken_q[0]), swap))
    row, advantages = advantages_of(columns, weights, chains[0])

    dq_own, dq_back, dkv_list = [], [], []
    for chunk in range(chunks):
        query_list = [kept_q[chunk], taken_q[chunk]]
        dq, dkv = attend(parents, advantages, bias, query_list, chains[chunk])
        if chunk == 0:
            three = permute(after(two, dq[0]), meet[1])
            chains.append([block, one, two, three])
        dq_own.append(dq[0])
        dq_back.append(dq[1])
        dkv_list.append(dkv)

    summands = []
    for dkv in dkv_list:
        arrived = [permute(dkv[bits], meet[bits]) for bits in steps[::-1]]
        summands.append([after(dkv[0], dq_own[-1])] + arrived)
    dq_back = [permute(block, swap) for block in dq_back]
    others = []
    for blocks in summands:
        total = sum(block[1].astype(jnp.float32) for block in blocks)
        others.append(permute(total.astype(jnp.bfloat16), swap))
    grad_q = join_queries(dq_own, dq_back)
    grad_k, grad_v = join_keys(others, summands)
    return grad_q, grad_k, grad_v, row[0]


def fetch_rows(spread, wanted):
    routed = jnp.take(spread, jnp.maximum(wanted, 0), axis=0)
    return lax.all_to_all(routed, "seg", split_axis=0, concat_axis=2, tiled=True)


def return_rows(grad_rows, wanted, total_segs):
    returned = lax.all_to_all(grad_rows, "seg", split_axis=2, concat_axis=0, tiled=True)
    piece_len = returned.shape[2]
    feature_len = returned.shape[3]
    routed_ids = wanted.reshape(-1)
    targets = jnp.where(routed_ids >= 0, routed_ids, total_segs)
    summed = jax.ops.segment_sum(
        returned.reshape(-1, piece_len * feature_len).astype(jnp.float32),
        targets,
        num_segments=total_segs + 1,
    )[:total_segs]
    return lax.all_to_all(
        summed.reshape(total_segs, piece_len, feature_len),
        "seg",
        split_axis=0,
        concat_axis=1,
        tiled=True,
    )


def routed_body(queries, direction, key_vectors, value_vectors, token_rows, parents, lengths, log_rate):
    total_segs = parents.shape[0]
    length, width = key_vectors.shape
    heads = width // HD
    own = lax.axis_index("seg")
    own_len = lax.dynamic_slice_in_dim(lengths, own, 1)[0]
    terms = jnp.concatenate(token_terms(log_rate, own_len, *token_rows), axis=1)
    bias, columns, weights = prepare(parents, lengths, [terms], length, log_rate)
    terms = lax.all_gather(terms, "seg", axis=0, tiled=True)
    row, advantages = advantages_of(columns, weights, [terms])
    flat = jnp.concatenate([key_vectors, value_vectors], axis=1)[None]
    spread = lax.all_to_all(flat, "seg", split_axis=1, concat_axis=0, tiled=True)
    chains = ancestors(parents, DEPTH - 1)
    arrived = fetch_rows(spread, chains)[0]
    slot_kv = jnp.concatenate([flat, arrived]).reshape(DEPTH, length, 2, heads, HD)
    slot_kv = jnp.transpose(slot_kv, (0, 3, 2, 1, 4)).reshape(DEPTH, heads, 2 * length, HD)
    (kept_q,) = pack_queries(queries, direction, 1, heads)
    dq_list, dkv_list = [], []
    for head in range(heads):
        kv_list = [slot_kv[slot, head] for slot in range(DEPTH)]
        dq, dkv = attend(parents, advantages, bias, [kept_q[head]], kv_list)
        dq_list.append(dq[0])
        dkv_list.append(jnp.concatenate(dkv))
    rows = jnp.transpose(jnp.stack(dkv_list), (1, 3, 2, 0, 4)).reshape(1, DEPTH, length, -1)
    summed = return_rows(rows[:, 1:], chains, total_segs)[0] + rows[0, 0].astype(jnp.float32)
    grad_keys = summed[:, :width].astype(jnp.bfloat16)
    grad_values = summed[:, width:].astype(jnp.bfloat16)
    return jnp.concatenate(dq_list, axis=1), grad_keys, grad_values, row[0]


def body(
    queries,
    key_vectors,
    value_vectors,
    direction,
    rewards,
    logprobs,
    ref_logprobs,
    value_est,
    parents,
    seg_lengths,
):
    groups = lax.axis_size("seg")
    assert parents.shape[0] == groups
    log_rate = math.log(LAMBDA_SEG) / rewards.shape[0]
    token_rows = [rewards[None], logprobs[None], ref_logprobs[None], value_est[None]]
    plan = paired_body if groups == PAIRED_GROUPS else routed_body
    return plan(
        queries, direction, key_vectors, value_vectors, token_rows, parents, seg_lengths, log_rate
    )


def solution(mesh):
    in_specs = (
        P(("grp", "seg"), "tp"),
        P(("grp", "seg"), "tp"),
        P(("grp", "seg"), "tp"),
        P(("grp", "seg"), "tp"),
        P(("grp", "seg")),
        P(("grp", "seg")),
        P(("grp", "seg")),
        P(("grp", "seg")),
        P("grp"),
        P("grp"),
    )
    out_specs = (
        P(("grp", "seg"), "tp"),
        P(("grp", "seg"), "tp"),
        P(("grp", "seg"), "tp"),
        P(("grp", "seg")),
    )
    return jax.shard_map(body, mesh=mesh, in_specs=in_specs, out_specs=out_specs, check_vma=False)
```

```python
import functools
import math

import jax
import jax.numpy as jnp
from jax import lax
from jax.experimental import pallas as pl
from jax.experimental.pallas import tpu as pltpu
from jax.sharding import PartitionSpec as P

HD = 128
DEPTH = 5
BETA = 0.1
LAMBDA_SEG = 0.7
PAIRED_GROUPS = 8
TERM_ROWS = 16
LOG2E = math.log2(math.e)
SMALL = pltpu.CompilerParams(vmem_limit_bytes=8 * 1024 * 1024)


def lookup(table_values, lookup_ids):
    matches = lookup_ids[..., None] == jnp.arange(table_values.shape[0], dtype=jnp.int32)
    return jnp.sum(jnp.where(matches, table_values, 0), axis=-1)


def ancestors(parents, count):
    current = jnp.arange(parents.shape[0], dtype=jnp.int32)
    chain_list = []
    for depth_step in range(count):
        parent_ids = lookup(parents, current)
        current = jnp.where(current >= 0, parent_ids, -1)
        chain_list.append(current)
    return jnp.stack(chain_list, axis=1)


def token_terms(log_rate, own_len, rewards, logprobs, ref_logprobs, values):
    positions = lax.broadcasted_iota(jnp.int32, rewards.shape, 1)
    later = jnp.concatenate([values[:, 1:], values[:, :1]], axis=1)
    later = jnp.where(positions + 1 < own_len, later, 0.0)
    deltas = jnp.where(
        positions < own_len, rewards - BETA * (logprobs - ref_logprobs) + later - values, 0.0
    )
    powers = jnp.exp(positions.astype(jnp.float32) * log_rate)
    first_local = jnp.sum(deltas * powers, axis=1, keepdims=True)
    firsts = jnp.where(positions == 0, first_local, jnp.where(positions == 1, values[:, :1], 0.0))
    return deltas, firsts


def split_float(value):
    parts = []
    for _ in range(3):
        part = value.astype(jnp.bfloat16)
        parts.append(part)
        value = value - part.astype(jnp.float32)
    return parts


def pack_kernel(
    log_rate,
    parts,
    lengths_ref,
    k_ref,
    v_ref,
    rewards_ref,
    logprobs_ref,
    ref_logprobs_ref,
    values_ref,
    *out_refs,
):
    own = lax.axis_index("seg")
    length = k_ref.shape[0]
    heads = len(out_refs) // parts
    terms = token_terms(
        log_rate,
        lengths_ref[own],
        rewards_ref[...],
        logprobs_ref[...],
        ref_logprobs_ref[...],
        values_ref[...],
    )
    tail = [part.astype(jnp.float32) for x in terms for part in split_float(x)]
    tail.append(jnp.zeros((TERM_ROWS - len(tail), HD), jnp.float32))
    tail = jnp.concatenate(tail).astype(jnp.bfloat16)
    for index, out_ref in enumerate(out_refs):
        step, h = divmod(index, heads)
        part = lax.rem(own + step, parts)
        columns = pl.ds(pl.multiple_of((part * heads + h) * HD, HD), HD)
        out_ref[:length, :] = k_ref[:, columns]
        out_ref[length : 2 * length, :] = v_ref[:, columns]
        if h == 0:
            out_ref[2 * length :, :] = tail


def pack(lengths, k, v, token_rows, parts, log_rate):
    length, width = k.shape
    smem = pl.BlockSpec(memory_space=pltpu.SMEM)
    vmem = pl.BlockSpec(memory_space=pltpu.VMEM)
    heads = width // HD // parts
    assert length == HD
    blocks = [
        jax.ShapeDtypeStruct((2 * length + (TERM_ROWS if h == 0 else 0), HD), k.dtype)
        for h in range(heads)
    ]
    outs = pl.pallas_call(
        functools.partial(pack_kernel, log_rate, parts),
        out_shape=blocks * parts,
        in_specs=[smem] + [vmem] * 6,
        out_specs=[vmem] * (heads * parts),
        cost_estimate=pl.CostEstimate(
            flops=length * 100, bytes_accessed=8 * length * width, transcendentals=length
        ),
        name="pack_keys_values",
    )(lengths, k, v, *token_rows)
    return [outs[step * heads : (step + 1) * heads] for step in range(parts)]


def join_blocks_kernel(mine_ref, other_ref, out_ref):
    rows = mine_ref.shape[0]
    out_ref[:rows, :] = mine_ref[...]
    out_ref[rows:, :] = other_ref[...]


def join_blocks(mine, other):
    vmem = pl.BlockSpec(memory_space=pltpu.VMEM)
    return pl.pallas_call(
        join_blocks_kernel,
        out_shape=jax.ShapeDtypeStruct((2 * mine.shape[0], HD), mine.dtype),
        in_specs=[vmem] * 2,
        out_specs=vmem,
        cost_estimate=pl.CostEstimate(flops=0, bytes_accessed=8 * mine.size, transcendentals=0),
        compiler_params=SMALL,
        name="join_blocks",
    )(mine, other)


def pack_queries_kernel(parts, q_ref, dir_ref, *out_refs):
    own = lax.axis_index("seg")
    chunks = len(out_refs) // parts
    heads = out_refs[0].shape[1]
    for index, out_ref in enumerate(out_refs):
        step, chunk = divmod(index, chunks)
        part = lax.rem(own + step, parts)
        for h in range(heads):
            column = (part * chunks + chunk) * heads + h
            columns = pl.ds(pl.multiple_of(column * HD, HD), HD)
            out_ref[0, h] = q_ref[:, columns]
            out_ref[1, h] = dir_ref[:, columns]


def pack_queries(q, direction, parts, chunks):
    length, width = q.shape
    vmem = pl.BlockSpec(memory_space=pltpu.VMEM)
    block = jax.ShapeDtypeStruct((2, width // HD // parts // chunks, length, HD), q.dtype)
    outs = pl.pallas_call(
        functools.partial(pack_queries_kernel, parts),
        out_shape=(block,) * (parts * chunks),
        in_specs=[vmem, vmem],
        out_specs=(vmem,) * (parts * chunks),
        cost_estimate=pl.CostEstimate(flops=0, bytes_accessed=8 * length * width, transcendentals=0),
        compiler_params=SMALL,
        name="pack_queries",
    )(q, direction)
    return [outs[step * chunks : (step + 1) * chunks] for step in range(parts)]


def parent_of(segment, parents_s):
    known = parents_s[jnp.maximum(segment, 0)]
    return jnp.where(segment >= 0, known, -1).astype(jnp.int32)


def segment_of(own, segs, i):
    part = lax.rem(own, segs)
    return own - part + lax.rem(part + i, segs)


def read_terms(ref, end=None):
    if ref.dtype == jnp.float32:
        length = ref.shape[1] // 2
        return ref[:, :length], ref[:, length:]
    tail = ref[end - TERM_ROWS : end, :].astype(jnp.float32)
    return tail[0:1] + tail[1:2] + tail[2:3], tail[3:4] + tail[4:5] + tail[5:6]


def prepare_kernel(log_rate, depth, parents_s, lengths_s, *refs):
    term_refs, (bias_ref, columns_ref, weights_ref) = refs[:-3], refs[-3:]
    segs, _, length = bias_ref.shape
    count = parents_s.shape[0]
    own = lax.axis_index("seg")

    row_id = lax.broadcasted_iota(jnp.int32, (count, count), 0)
    col_id = lax.broadcasted_iota(jnp.int32, (count, count), 1)
    seg_col = lax.broadcasted_iota(jnp.int32, (count, 1), 0)

    def to_col(row):
        return jnp.sum(jnp.where(row_id == col_id, row, 0.0), axis=1, keepdims=True)

    parent_row = jnp.full((1, count), -1, jnp.int32)
    lens_col = jnp.zeros((count, 1), jnp.int32)
    for seg in range(count):
        parent_row = jnp.where(col_id[:1] == seg, parents_s[seg], parent_row)
        lens_col = jnp.where(seg_col == seg, lengths_s[seg], lens_col)
    lens_col = lens_col.astype(jnp.float32)
    children = (parent_row == row_id).astype(jnp.float32)
    tree = children / jnp.maximum(jnp.sum(children, axis=1, keepdims=True), 1.0)
    factor = jnp.exp(lens_col * log_rate)
    last_factor = jnp.exp((lens_col - 1.0) * log_rate)

    u_id = lax.broadcasted_iota(jnp.int32, (length, length), 0)
    t_id = lax.broadcasted_iota(jnp.int32, (length, length), 1)
    offset = (t_id - u_id).astype(jnp.float32)
    discount = jnp.where(offset >= 0, jnp.exp(offset * log_rate), 0.0)
    t_col = lax.broadcasted_iota(jnp.int32, (length, 1), 0)
    lane = lax.broadcasted_iota(jnp.int32, (count, HD), 1)
    for i in range(segs):
        seg = segment_of(own, segs, i)
        seg_len = lengths_s[seg]
        deltas, _ = read_terms(term_refs[i], term_refs[i].shape[0])
        live = t_col < seg_len
        left = (seg_len - t_col).astype(jnp.float32)
        columns = (
            jnp.sum(discount * deltas, axis=1, keepdims=True),
            jnp.exp((left - 1.0) * log_rate),
            jnp.exp(left * log_rate),
        )
        for index, column in enumerate(columns):
            column = jnp.where(live, column, 0.0)
            columns_ref[i, index] = jnp.broadcast_to(column, (length, HD))

        row = jnp.sum(jnp.where(row_id == seg, tree, 0.0), axis=0, keepdims=True)
        value_col = col = total = to_col(row)
        for _ in range(depth):
            col = to_col(jnp.sum(col * factor * tree, axis=0, keepdims=True))
            total = total + col
        through = to_col(jnp.sum(total * last_factor * tree, axis=0, keepdims=True))
        weights_ref[i, 0] = jnp.where(lane == 1, value_col, 0.0)
        weights_ref[i, 1] = jnp.where(lane == 0, total, jnp.where(lane == 1, through, 0.0))

        ancestor = seg
        for slot in range(depth):
            if slot > 0:
                ancestor = parent_of(ancestor, parents_s)
            slot_len = jnp.where(ancestor >= 0, lengths_s[jnp.maximum(ancestor, 0)], 0)
            seen = u_id < slot_len
            if slot == 0:
                seen = jnp.logical_and(seen, u_id <= t_id)
            bias_ref[i, slot * length : (slot + 1) * length, :] = jnp.where(seen, 0.0, -1e30)


def prepare(parents, lengths, terms, length, log_rate):
    smem = pl.BlockSpec(memory_space=pltpu.SMEM)
    vmem = pl.BlockSpec(memory_space=pltpu.VMEM)
    segs, count = len(terms), parents.shape[0]
    return pl.pallas_call(
        functools.partial(prepare_kernel, log_rate, DEPTH),
        out_shape=(
            jax.ShapeDtypeStruct((segs, DEPTH * length, length), jnp.float32),
            jax.ShapeDtypeStruct((segs, 3, length, HD), jnp.float32),
            jax.ShapeDtypeStruct((segs, 2, count, HD), jnp.float32),
        ),
        in_specs=[smem] * 2 + [vmem] * len(terms),
        out_specs=(vmem,) * 3,
        cost_estimate=pl.CostEstimate(
            flops=20 * DEPTH * segs * length * length,
            bytes_accessed=4 * DEPTH * segs * length * length,
            transcendentals=length * length,
        ),
        compiler_params=SMALL,
        name="prepare",
    )(parents, lengths, *terms)


def advantage_kernel(columns_ref, weights_ref, *refs):
    term_refs, (row_ref, adv_ref) = refs[:-2], refs[-2:]
    segs, _, length, _ = columns_ref.shape
    count = weights_ref.shape[2]
    if len(term_refs) == 1:
        firsts = read_terms(term_refs[0])[1]
    else:
        own = lax.axis_index("seg")
        part, pair = lax.rem(own, segs), own // segs
        seg_id = lax.broadcasted_iota(jnp.int32, (count, length), 0)
        firsts = jnp.zeros((count, length), jnp.float32)
        for step, ref in enumerate(term_refs):
            for side in range(segs):
                seg = (pair ^ step) * segs + lax.rem(part + side, segs)
                end = (side + 1) * (ref.shape[0] // segs)
                firsts = jnp.where(seg_id == seg, read_terms(ref, end)[1], firsts)
    for i in range(segs):
        later_value = jnp.sum(weights_ref[i, 0] * firsts, axis=(0, 1), keepdims=True)
        later_head = jnp.sum(weights_ref[i, 1] * firsts, axis=(0, 1), keepdims=True)
        advantage = (
            columns_ref[i, 0] + columns_ref[i, 1] * later_value + columns_ref[i, 2] * later_head
        )
        adv_ref[i] = advantage
        if i == 0:
            row_id = lax.broadcasted_iota(jnp.int32, advantage.shape, 0)
            col_id = lax.broadcasted_iota(jnp.int32, advantage.shape, 1)
            row_ref[...] = jnp.sum(
                jnp.where(row_id == col_id, advantage, 0.0), axis=0, keepdims=True
            )


def advantages_of(columns, weights, terms):
    vmem = pl.BlockSpec(memory_space=pltpu.VMEM)
    segs, _, length, _ = columns.shape
    return pl.pallas_call(
        advantage_kernel,
        out_shape=(
            jax.ShapeDtypeStruct((1, length), jnp.float32),
            jax.ShapeDtypeStruct((segs, length, HD), jnp.float32),
        ),
        in_specs=[vmem] * (2 + len(terms)),
        out_specs=(vmem,) * 2,
        cost_estimate=pl.CostEstimate(
            flops=10 * segs * length * HD, bytes_accessed=16 * segs * length * HD, transcendentals=0
        ),
        compiler_params=SMALL,
        name="advantages",
    )(columns, weights, *terms)


def attend_kernel(depth, segs, steps, group_size, *refs):
    parents_s, adv_ref, bias_ref = refs[:3]
    query_refs, kv_refs = refs[3 : 3 + segs], refs[3 + segs : 3 + segs + steps]
    kv_scr, p_scr, ds_scr, acc_scr = refs[-4:]
    refs = refs[3 + segs + steps : -4]
    dkv_refs, dq_refs = refs[-steps:], refs[-steps - segs : -steps]

    length = query_refs[0].shape[2]
    own = lax.axis_index("seg")
    for source in range(steps * segs):
        step, side = divmod(source, segs)
        for plane in range(2):
            first = side * (kv_refs[step].shape[0] // segs) + plane * length
            kv_scr[source, plane] = kv_refs[step][first : first + length, :]
    acc_scr[...] = jnp.zeros_like(acc_scr)

    scale = HD**-0.5
    contract_last = (((1,), (1,)), ((), ()))
    contract_first = (((0,), (0,)), ((), ()))
    for i in range(segs):
        ancestor = segment_of(own, segs, i)
        part = lax.rem(own, segs)
        chosen = []
        for slot in range(depth):
            if slot > 0:
                ancestor = parent_of(ancestor, parents_s)
            if segs == 1:
                chosen.append(slot)
            else:
                known = jnp.maximum(ancestor, 0)
                step = (own // segs) ^ (known // segs)
                turn = lax.rem(lax.rem(known, segs) - part + segs, segs)
                chosen.append(jnp.where(ancestor >= 0, step * segs + turn, 0))
        q_list = [query_refs[i][0, j] for j in range(group_size)]
        dir_list = [query_refs[i][1, j] for j in range(group_size)]
        do_list = [(adv_ref[i] * d.astype(jnp.float32)).astype(jnp.bfloat16) for d in dir_list]
        k_all = jnp.concatenate([kv_scr[s, 0] for s in chosen], axis=0)
        v_all = jnp.concatenate([kv_scr[s, 1] for s in chosen], axis=0)
        q_all = jnp.concatenate(q_list, axis=0)
        do_all = jnp.concatenate(do_list, axis=0)
        all_scores = lax.dot_general(
            k_all, q_all, contract_last, preferred_element_type=jnp.float32
        )
        all_dprob = lax.dot_general(
            v_all, do_all, contract_last, preferred_element_type=jnp.float32
        )
        for j in range(group_size):
            columns = slice(j * length, (j + 1) * length)
            scores = all_scores[:, columns] * (scale * LOG2E) + bias_ref[i]
            top = jnp.max(scores, axis=0, keepdims=True)
            unnorm = jnp.exp2(scores - top)
            prob = unnorm * (1.0 / jnp.sum(unnorm, axis=0, keepdims=True))
            prob_low = prob.astype(jnp.bfloat16)
            dprob = all_dprob[:, columns]
            row_dot = jnp.sum(prob_low.astype(jnp.float32) * dprob, axis=0, keepdims=True)
            dscore = (prob * (dprob - row_dot)).astype(jnp.bfloat16)
            p_scr[:, columns] = prob_low
            ds_scr[:, columns] = dscore
        dscore_all = ds_scr[...]
        dq_t = lax.dot_general(
            k_all, dscore_all, contract_first, preferred_element_type=jnp.float32
        )
        for j in range(group_size):
            dq = jnp.transpose(dq_t[:, j * length : (j + 1) * length]) * scale
            dq_refs[i][:, j * HD : (j + 1) * HD] = dq.astype(jnp.bfloat16)
        dk_all = jnp.dot(dscore_all, q_all, preferred_element_type=jnp.float32) * scale
        dv_all = jnp.dot(p_scr[...], do_all, preferred_element_type=jnp.float32)
        for slot, s in enumerate(chosen):
            rows = slice(slot * length, (slot + 1) * length)
            acc_scr[s, 0] += dk_all[rows]
            acc_scr[s, 1] += dv_all[rows]
    for step in range(steps):
        for i in range(segs):
            dkv_refs[step][i] = acc_scr[step * segs + i].astype(jnp.bfloat16)


def attend(parents, advantages, bias, query_list, kv_list):
    segs, length = advantages.shape[:2]
    steps = len(kv_list)
    sources = steps * segs
    group_size = query_list[0].shape[1]
    width = group_size * HD
    keys = DEPTH * length
    smem = pl.BlockSpec(memory_space=pltpu.SMEM)
    vmem = pl.BlockSpec(memory_space=pltpu.VMEM)
    out_shape = [jax.ShapeDtypeStruct((length, width), jnp.bfloat16)] * segs
    out_shape += [jax.ShapeDtypeStruct((segs, 2, length, HD), jnp.bfloat16)] * steps
    outs = pl.pallas_call(
        functools.partial(attend_kernel, DEPTH, segs, steps, group_size),
        out_shape=out_shape,
        in_specs=[smem] + [vmem] * (2 + segs + steps),
        out_specs=[vmem] * len(out_shape),
        scratch_shapes=[
            pltpu.VMEM((sources, 2, length, HD), jnp.bfloat16),
            pltpu.VMEM((keys, width), jnp.bfloat16),
            pltpu.VMEM((keys, width), jnp.bfloat16),
            pltpu.VMEM((sources, 2, length, HD), jnp.float32),
        ],
        compiler_params=pltpu.CompilerParams(vmem_limit_bytes=16 * 1024 * 1024),
        cost_estimate=pl.CostEstimate(
            flops=5 * 2 * keys * length * width * segs,
            bytes_accessed=8 * 1024 * 1024,
            transcendentals=keys * width * segs,
        ),
        name="tree_attention_backward",
    )(parents, advantages, bias, *query_list, *kv_list)
    return outs[:segs], outs[segs:]


def join_queries_kernel(*refs):
    part = lax.rem(lax.axis_index("seg"), 2)
    refs, dq_ref = refs[:-1], refs[-1]
    chunks = len(refs) // 2
    width = refs[0].shape[1]
    for index, ref in enumerate(refs):
        side, chunk = divmod(index, chunks)
        where = part if side == 0 else 1 - part
        column = pl.multiple_of((where * chunks + chunk) * width, HD)
        dq_ref[:, pl.ds(column, width)] = ref[...]


def join_queries(own_list, other_list):
    chunks = len(own_list)
    length, width = own_list[0].shape
    vmem = pl.BlockSpec(memory_space=pltpu.VMEM)
    return pl.pallas_call(
        join_queries_kernel,
        out_shape=jax.ShapeDtypeStruct((length, 2 * chunks * width), jnp.bfloat16),
        in_specs=[vmem] * (2 * chunks),
        out_specs=vmem,
        cost_estimate=pl.CostEstimate(
            flops=0, bytes_accessed=8 * length * width * chunks, transcendentals=0
        ),
        compiler_params=SMALL,
        name="join_queries",
    )(*own_list, *other_list)


def join_keys_kernel(chunks, *refs):
    part = lax.rem(lax.axis_index("seg"), 2)
    other_refs, sum_refs = refs[:chunks], refs[chunks:-2]
    many = len(sum_refs) // chunks
    dk_ref, dv_ref = refs[-2:]
    for chunk in range(chunks):
        here = pl.ds(pl.multiple_of((part * chunks + chunk) * HD, HD), HD)
        there = pl.ds(pl.multiple_of(((1 - part) * chunks + chunk) * HD, HD), HD)
        for plane, out_ref in enumerate((dk_ref, dv_ref)):
            blocks = [ref[0, plane] for ref in sum_refs[chunk * many : (chunk + 1) * many]]
            total = sum(block.astype(jnp.float32) for block in blocks)
            out_ref[:, here] = total.astype(jnp.bfloat16)
            out_ref[:, there] = other_refs[chunk][plane]


def join_keys(others, summands):
    chunks = len(others)
    length = others[0].shape[1]
    vmem = pl.BlockSpec(memory_space=pltpu.VMEM)
    flat = [block for blocks in summands for block in blocks]
    out = jax.ShapeDtypeStruct((length, 2 * chunks * HD), jnp.bfloat16)
    return pl.pallas_call(
        functools.partial(join_keys_kernel, chunks),
        out_shape=(out, out),
        in_specs=[vmem] * (chunks + len(flat)),
        out_specs=(vmem, vmem),
        cost_estimate=pl.CostEstimate(
            flops=0, bytes_accessed=16 * length * HD * chunks, transcendentals=0
        ),
        compiler_params=SMALL,
        name="join_keys",
    )(*others, *flat)


def permute(array, pairs):
    return lax.ppermute(array, "seg", pairs)


def after(array, *earlier):
    return lax.optimization_barrier((array, *earlier))[0]


def paired_body(queries, direction, key_vectors, value_vectors, token_rows, parents, lengths, log_rate):
    groups = lax.axis_size("seg")
    length = queries.shape[0]
    chunks = key_vectors.shape[1] // HD // 2
    swap = [(i, i ^ 1) for i in range(groups)]
    steps = range(1, groups // 2)
    meet = {bits: [(i, i ^ (2 * bits)) for i in range(groups)] for bits in steps}
    home = {bits: [(i, j) for i, j in meet[bits] if j < i] for bits in steps}

    kept, given = pack(lengths, key_vectors, value_vectors, token_rows, 2, log_rate)
    taken = [permute(block, swap) for block in given]
    kept_q, given_q = pack_queries(after(queries, kept[0]), direction, 2, chunks)
    bias, columns, weights = prepare(parents, lengths, [kept[0], taken[0]], length, log_rate)
    near = [join_blocks(kept[0], after(taken[0], *kept_q)), join_blocks(kept[1], taken[1])]
    two, one = permute(near[0], meet[2]), permute(near[0], meet[1])
    three = permute(after(two, one, near[1], bias), meet[1])
    chains = [[near[0], one, two, three]]
    taken_q = [permute(after(given_q[0], near[0], near[1]), swap)]
    block = after(near[1], two, one)
    two, one = permute(block, meet[2]), permute(block, meet[1])
    taken_q.append(permute(after(given_q[1], taken_q[0]), swap))
    row, advantages = advantages_of(columns, weights, chains[0])

    dq_own, dq_back, dkv_list = [], [], []
    for chunk in range(chunks):
        query_list = [kept_q[chunk], taken_q[chunk]]
        dq, dkv = attend(parents, advantages, bias, query_list, chains[chunk])
        if chunk == 0:
            three = permute(after(two, dq[0]), meet[1])
            chains.append([block, one, two, three])
        dq_own.append(dq[0])
        dq_back.append(dq[1])
        dkv_list.append(dkv)

    summands = []
    for dkv in dkv_list:
        arrived = [permute(dkv[bits], home[bits]) for bits in steps[::-1]]
        summands.append([after(dkv[0], dq_own[-1])] + arrived)
    dq_back = [permute(block, swap) for block in dq_back]
    others = []
    for blocks in summands:
        total = sum(block[1].astype(jnp.float32) for block in blocks)
        others.append(permute(total.astype(jnp.bfloat16), swap))
    grad_q = join_queries(dq_own, dq_back)
    grad_k, grad_v = join_keys(others, summands)
    return grad_q, grad_k, grad_v, row[0]


def fetch_rows(spread, wanted):
    routed = jnp.take(spread, jnp.maximum(wanted, 0), axis=0)
    return lax.all_to_all(routed, "seg", split_axis=0, concat_axis=2, tiled=True)


def return_rows(grad_rows, wanted, total_segs):
    returned = lax.all_to_all(grad_rows, "seg", split_axis=2, concat_axis=0, tiled=True)
    piece_len = returned.shape[2]
    feature_len = returned.shape[3]
    routed_ids = wanted.reshape(-1)
    targets = jnp.where(routed_ids >= 0, routed_ids, total_segs)
    summed = jax.ops.segment_sum(
        returned.reshape(-1, piece_len * feature_len).astype(jnp.float32),
        targets,
        num_segments=total_segs + 1,
    )[:total_segs]
    return lax.all_to_all(
        summed.reshape(total_segs, piece_len, feature_len),
        "seg",
        split_axis=0,
        concat_axis=1,
        tiled=True,
    )


def routed_body(queries, direction, key_vectors, value_vectors, token_rows, parents, lengths, log_rate):
    total_segs = parents.shape[0]
    length, width = key_vectors.shape
    heads = width // HD
    own = lax.axis_index("seg")
    own_len = lax.dynamic_slice_in_dim(lengths, own, 1)[0]
    terms = jnp.concatenate(token_terms(log_rate, own_len, *token_rows), axis=1)
    bias, columns, weights = prepare(parents, lengths, [terms], length, log_rate)
    terms = lax.all_gather(terms, "seg", axis=0, tiled=True)
    row, advantages = advantages_of(columns, weights, [terms])
    flat = jnp.concatenate([key_vectors, value_vectors], axis=1)[None]
    spread = lax.all_to_all(flat, "seg", split_axis=1, concat_axis=0, tiled=True)
    chains = ancestors(parents, DEPTH - 1)
    arrived = fetch_rows(spread, chains)[0]
    slot_kv = jnp.concatenate([flat, arrived]).reshape(DEPTH, length, 2, heads, HD)
    slot_kv = jnp.transpose(slot_kv, (0, 3, 2, 1, 4)).reshape(DEPTH, heads, 2 * length, HD)
    (kept_q,) = pack_queries(queries, direction, 1, heads)
    dq_list, dkv_list = [], []
    for head in range(heads):
        kv_list = [slot_kv[slot, head] for slot in range(DEPTH)]
        dq, dkv = attend(parents, advantages, bias, [kept_q[head]], kv_list)
        dq_list.append(dq[0])
        dkv_list.append(jnp.concatenate(dkv))
    rows = jnp.transpose(jnp.stack(dkv_list), (1, 3, 2, 0, 4)).reshape(1, DEPTH, length, -1)
    summed = return_rows(rows[:, 1:], chains, total_segs)[0] + rows[0, 0].astype(jnp.float32)
    grad_keys = summed[:, :width].astype(jnp.bfloat16)
    grad_values = summed[:, width:].astype(jnp.bfloat16)
    return jnp.concatenate(dq_list, axis=1), grad_keys, grad_values, row[0]


def body(
    queries,
    key_vectors,
    value_vectors,
    direction,
    rewards,
    logprobs,
    ref_logprobs,
    value_est,
    parents,
    seg_lengths,
):
    groups = lax.axis_size("seg")
    assert parents.shape[0] == groups
    log_rate = math.log(LAMBDA_SEG) / rewards.shape[0]
    token_rows = [rewards[None], logprobs[None], ref_logprobs[None], value_est[None]]
    plan = paired_body if groups == PAIRED_GROUPS else routed_body
    return plan(
        queries, direction, key_vectors, value_vectors, token_rows, parents, seg_lengths, log_rate
    )


def solution(mesh):
    in_specs = (
        P(("grp", "seg"), "tp"),
        P(("grp", "seg"), "tp"),
        P(("grp", "seg"), "tp"),
        P(("grp", "seg"), "tp"),
        P(("grp", "seg")),
        P(("grp", "seg")),
        P(("grp", "seg")),
        P(("grp", "seg")),
        P("grp"),
        P("grp"),
    )
    out_specs = (
        P(("grp", "seg"), "tp"),
        P(("grp", "seg"), "tp"),
        P(("grp", "seg"), "tp"),
        P(("grp", "seg")),
    )
    return jax.shard_map(body, mesh=mesh, in_specs=in_specs, out_specs=out_specs, check_vma=False)
```

```python
import functools
import math

import jax
import jax.numpy as jnp
from jax import lax
from jax.experimental import pallas as pl
from jax.experimental.pallas import tpu as pltpu
from jax.sharding import PartitionSpec as P

HD = 128
DEPTH = 5
BETA = 0.1
LAMBDA_SEG = 0.7
PAIRED_GROUPS = 8
TERM_ROWS = 16
LOG2E = math.log2(math.e)
SMALL = pltpu.CompilerParams(vmem_limit_bytes=8 * 1024 * 1024)


def lookup(table_values, lookup_ids):
    matches = lookup_ids[..., None] == jnp.arange(table_values.shape[0], dtype=jnp.int32)
    return jnp.sum(jnp.where(matches, table_values, 0), axis=-1)


def ancestors(parents, count):
    current = jnp.arange(parents.shape[0], dtype=jnp.int32)
    chain_list = []
    for depth_step in range(count):
        parent_ids = lookup(parents, current)
        current = jnp.where(current >= 0, parent_ids, -1)
        chain_list.append(current)
    return jnp.stack(chain_list, axis=1)


def token_terms(log_rate, own_len, rewards, logprobs, ref_logprobs, values):
    positions = lax.broadcasted_iota(jnp.int32, rewards.shape, 1)
    later = jnp.concatenate([values[:, 1:], values[:, :1]], axis=1)
    later = jnp.where(positions + 1 < own_len, later, 0.0)
    deltas = jnp.where(
        positions < own_len, rewards - BETA * (logprobs - ref_logprobs) + later - values, 0.0
    )
    powers = jnp.exp(positions.astype(jnp.float32) * log_rate)
    first_local = jnp.sum(deltas * powers, axis=1, keepdims=True)
    firsts = jnp.where(positions == 0, first_local, jnp.where(positions == 1, values[:, :1], 0.0))
    return deltas, firsts


def split_float(value):
    parts = []
    for _ in range(3):
        part = value.astype(jnp.bfloat16)
        parts.append(part)
        value = value - part.astype(jnp.float32)
    return parts


def pack_kernel(
    log_rate,
    parts,
    lengths_ref,
    k_ref,
    v_ref,
    rewards_ref,
    logprobs_ref,
    ref_logprobs_ref,
    values_ref,
    *out_refs,
):
    own = lax.axis_index("seg")
    length = k_ref.shape[0]
    heads = len(out_refs) // parts
    terms = token_terms(
        log_rate,
        lengths_ref[own],
        rewards_ref[...],
        logprobs_ref[...],
        ref_logprobs_ref[...],
        values_ref[...],
    )
    tail = [part.astype(jnp.float32) for x in terms for part in split_float(x)]
    tail.append(jnp.zeros((TERM_ROWS - len(tail), HD), jnp.float32))
    tail = jnp.concatenate(tail).astype(jnp.bfloat16)
    for index, out_ref in enumerate(out_refs):
        step, h = divmod(index, heads)
        part = lax.rem(own + step, parts)
        columns = pl.ds(pl.multiple_of((part * heads + h) * HD, HD), HD)
        out_ref[:length, :] = k_ref[:, columns]
        out_ref[length : 2 * length, :] = v_ref[:, columns]
        if h == 0:
            out_ref[2 * length :, :] = tail


def pack(lengths, k, v, token_rows, parts, log_rate):
    length, width = k.shape
    smem = pl.BlockSpec(memory_space=pltpu.SMEM)
    vmem = pl.BlockSpec(memory_space=pltpu.VMEM)
    heads = width // HD // parts
    assert length == HD
    blocks = [
        jax.ShapeDtypeStruct((2 * length + (TERM_ROWS if h == 0 else 0), HD), k.dtype)
        for h in range(heads)
    ]
    outs = pl.pallas_call(
        functools.partial(pack_kernel, log_rate, parts),
        out_shape=blocks * parts,
        in_specs=[smem] + [vmem] * 6,
        out_specs=[vmem] * (heads * parts),
        cost_estimate=pl.CostEstimate(
            flops=length * 100, bytes_accessed=8 * length * width, transcendentals=length
        ),
        name="pack_keys_values",
    )(lengths, k, v, *token_rows)
    return [outs[step * heads : (step + 1) * heads] for step in range(parts)]


def join_blocks_kernel(mine_ref, other_ref, out_ref):
    rows = mine_ref.shape[0]
    out_ref[:rows, :] = mine_ref[...]
    out_ref[rows:, :] = other_ref[...]


def join_blocks(mine, other):
    vmem = pl.BlockSpec(memory_space=pltpu.VMEM)
    return pl.pallas_call(
        join_blocks_kernel,
        out_shape=jax.ShapeDtypeStruct((2 * mine.shape[0], HD), mine.dtype),
        in_specs=[vmem] * 2,
        out_specs=vmem,
        cost_estimate=pl.CostEstimate(flops=0, bytes_accessed=8 * mine.size, transcendentals=0),
        compiler_params=SMALL,
        name="join_blocks",
    )(mine, other)


def pack_queries_kernel(parts, q_ref, dir_ref, *out_refs):
    own = lax.axis_index("seg")
    chunks = len(out_refs) // parts
    heads = out_refs[0].shape[1]
    for index, out_ref in enumerate(out_refs):
        step, chunk = divmod(index, chunks)
        part = lax.rem(own + step, parts)
        for h in range(heads):
            column = (part * chunks + chunk) * heads + h
            columns = pl.ds(pl.multiple_of(column * HD, HD), HD)
            out_ref[0, h] = q_ref[:, columns]
            out_ref[1, h] = dir_ref[:, columns]


def pack_queries(q, direction, parts, chunks):
    length, width = q.shape
    vmem = pl.BlockSpec(memory_space=pltpu.VMEM)
    block = jax.ShapeDtypeStruct((2, width // HD // parts // chunks, length, HD), q.dtype)
    outs = pl.pallas_call(
        functools.partial(pack_queries_kernel, parts),
        out_shape=(block,) * (parts * chunks),
        in_specs=[vmem, vmem],
        out_specs=(vmem,) * (parts * chunks),
        cost_estimate=pl.CostEstimate(flops=0, bytes_accessed=8 * length * width, transcendentals=0),
        compiler_params=SMALL,
        name="pack_queries",
    )(q, direction)
    return [outs[step * chunks : (step + 1) * chunks] for step in range(parts)]


def parent_of(segment, parents_s):
    known = parents_s[jnp.maximum(segment, 0)]
    return jnp.where(segment >= 0, known, -1).astype(jnp.int32)


def segment_of(own, segs, i):
    part = lax.rem(own, segs)
    return own - part + lax.rem(part + i, segs)


def read_terms(ref, end=None):
    if ref.dtype == jnp.float32:
        length = ref.shape[1] // 2
        return ref[:, :length], ref[:, length:]
    tail = ref[end - TERM_ROWS : end, :].astype(jnp.float32)
    return tail[0:1] + tail[1:2] + tail[2:3], tail[3:4] + tail[4:5] + tail[5:6]


def prepare_kernel(log_rate, depth, parents_s, lengths_s, *refs):
    term_refs, (bias_ref, columns_ref, weights_ref) = refs[:-3], refs[-3:]
    segs, _, length = bias_ref.shape
    count = parents_s.shape[0]
    own = lax.axis_index("seg")

    row_id = lax.broadcasted_iota(jnp.int32, (count, count), 0)
    col_id = lax.broadcasted_iota(jnp.int32, (count, count), 1)
    seg_col = lax.broadcasted_iota(jnp.int32, (count, 1), 0)

    def to_col(row):
        return jnp.sum(jnp.where(row_id == col_id, row, 0.0), axis=1, keepdims=True)

    parent_row = jnp.full((1, count), -1, jnp.int32)
    lens_col = jnp.zeros((count, 1), jnp.int32)
    for seg in range(count):
        parent_row = jnp.where(col_id[:1] == seg, parents_s[seg], parent_row)
        lens_col = jnp.where(seg_col == seg, lengths_s[seg], lens_col)
    lens_col = lens_col.astype(jnp.float32)
    children = (parent_row == row_id).astype(jnp.float32)
    tree = children / jnp.maximum(jnp.sum(children, axis=1, keepdims=True), 1.0)
    factor = jnp.exp(lens_col * log_rate)
    last_factor = jnp.exp((lens_col - 1.0) * log_rate)

    u_id = lax.broadcasted_iota(jnp.int32, (length, length), 0)
    t_id = lax.broadcasted_iota(jnp.int32, (length, length), 1)
    offset = (t_id - u_id).astype(jnp.float32)
    discount = jnp.where(offset >= 0, jnp.exp(offset * log_rate), 0.0)
    t_col = lax.broadcasted_iota(jnp.int32, (length, 1), 0)
    lane = lax.broadcasted_iota(jnp.int32, (count, HD), 1)
    for i in range(segs):
        seg = segment_of(own, segs, i)
        seg_len = lengths_s[seg]
        deltas, _ = read_terms(term_refs[i], term_refs[i].shape[0])
        live = t_col < seg_len
        left = (seg_len - t_col).astype(jnp.float32)
        columns = (
            jnp.sum(discount * deltas, axis=1, keepdims=True),
            jnp.exp((left - 1.0) * log_rate),
            jnp.exp(left * log_rate),
        )
        for index, column in enumerate(columns):
            column = jnp.where(live, column, 0.0)
            columns_ref[i, index] = jnp.broadcast_to(column, (length, HD))

        row = jnp.sum(jnp.where(row_id == seg, tree, 0.0), axis=0, keepdims=True)
        value_col = col = total = to_col(row)
        for _ in range(depth):
            col = to_col(jnp.sum(col * factor * tree, axis=0, keepdims=True))
            total = total + col
        through = to_col(jnp.sum(total * last_factor * tree, axis=0, keepdims=True))
        weights_ref[i, 0] = jnp.where(lane == 1, value_col, 0.0)
        weights_ref[i, 1] = jnp.where(lane == 0, total, jnp.where(lane == 1, through, 0.0))

        ancestor = seg
        for slot in range(depth):
            if slot > 0:
                ancestor = parent_of(ancestor, parents_s)
            slot_len = jnp.where(ancestor >= 0, lengths_s[jnp.maximum(ancestor, 0)], 0)
            seen = u_id < slot_len
            if slot == 0:
                seen = jnp.logical_and(seen, u_id <= t_id)
            bias_ref[i, slot * length : (slot + 1) * length, :] = jnp.where(seen, 0.0, -1e30)


def prepare(parents, lengths, terms, length, log_rate):
    smem = pl.BlockSpec(memory_space=pltpu.SMEM)
    vmem = pl.BlockSpec(memory_space=pltpu.VMEM)
    segs, count = len(terms), parents.shape[0]
    return pl.pallas_call(
        functools.partial(prepare_kernel, log_rate, DEPTH),
        out_shape=(
            jax.ShapeDtypeStruct((segs, DEPTH * length, length), jnp.float32),
            jax.ShapeDtypeStruct((segs, 3, length, HD), jnp.float32),
            jax.ShapeDtypeStruct((segs, 2, count, HD), jnp.float32),
        ),
        in_specs=[smem] * 2 + [vmem] * len(terms),
        out_specs=(vmem,) * 3,
        cost_estimate=pl.CostEstimate(
            flops=20 * DEPTH * segs * length * length,
            bytes_accessed=4 * DEPTH * segs * length * length,
            transcendentals=length * length,
        ),
        compiler_params=SMALL,
        name="prepare",
    )(parents, lengths, *terms)


def advantage_kernel(columns_ref, weights_ref, *refs):
    term_refs, (row_ref, adv_ref) = refs[:-2], refs[-2:]
    segs, _, length, _ = columns_ref.shape
    count = weights_ref.shape[2]
    if len(term_refs) == 1:
        firsts = read_terms(term_refs[0])[1]
    else:
        own = lax.axis_index("seg")
        part, pair = lax.rem(own, segs), own // segs
        seg_id = lax.broadcasted_iota(jnp.int32, (count, length), 0)
        firsts = jnp.zeros((count, length), jnp.float32)
        for step, ref in enumerate(term_refs):
            for side in range(segs):
                seg = (pair ^ step) * segs + lax.rem(part + side, segs)
                end = (side + 1) * (ref.shape[0] // segs)
                firsts = jnp.where(seg_id == seg, read_terms(ref, end)[1], firsts)
    for i in range(segs):
        later_value = jnp.sum(weights_ref[i, 0] * firsts, axis=(0, 1), keepdims=True)
        later_head = jnp.sum(weights_ref[i, 1] * firsts, axis=(0, 1), keepdims=True)
        advantage = (
            columns_ref[i, 0] + columns_ref[i, 1] * later_value + columns_ref[i, 2] * later_head
        )
        adv_ref[i] = advantage
        if i == 0:
            row_id = lax.broadcasted_iota(jnp.int32, advantage.shape, 0)
            col_id = lax.broadcasted_iota(jnp.int32, advantage.shape, 1)
            row_ref[...] = jnp.sum(
                jnp.where(row_id == col_id, advantage, 0.0), axis=0, keepdims=True
            )


def advantages_of(columns, weights, terms):
    vmem = pl.BlockSpec(memory_space=pltpu.VMEM)
    segs, _, length, _ = columns.shape
    return pl.pallas_call(
        advantage_kernel,
        out_shape=(
            jax.ShapeDtypeStruct((1, length), jnp.float32),
            jax.ShapeDtypeStruct((segs, length, HD), jnp.float32),
        ),
        in_specs=[vmem] * (2 + len(terms)),
        out_specs=(vmem,) * 2,
        cost_estimate=pl.CostEstimate(
            flops=10 * segs * length * HD, bytes_accessed=16 * segs * length * HD, transcendentals=0
        ),
        compiler_params=SMALL,
        name="advantages",
    )(columns, weights, *terms)


def attend_kernel(depth, segs, steps, group_size, *refs):
    parents_s, adv_ref, bias_ref = refs[:3]
    query_refs, kv_refs = refs[3 : 3 + segs], refs[3 + segs : 3 + segs + steps]
    kv_scr, p_scr, ds_scr, acc_scr = refs[-4:]
    refs = refs[3 + segs + steps : -4]
    dkv_refs, dq_refs = refs[-steps:], refs[-steps - segs : -steps]

    length = query_refs[0].shape[2]
    own = lax.axis_index("seg")
    for source in range(steps * segs):
        step, side = divmod(source, segs)
        for plane in range(2):
            first = side * (kv_refs[step].shape[0] // segs) + plane * length
            kv_scr[source, plane] = kv_refs[step][first : first + length, :]
    acc_scr[...] = jnp.zeros_like(acc_scr)

    scale = HD**-0.5
    contract_last = (((1,), (1,)), ((), ()))
    contract_first = (((0,), (0,)), ((), ()))
    for i in range(segs):
        ancestor = segment_of(own, segs, i)
        part = lax.rem(own, segs)
        chosen = []
        for slot in range(depth):
            if slot > 0:
                ancestor = parent_of(ancestor, parents_s)
            if segs == 1:
                chosen.append(slot)
            else:
                known = jnp.maximum(ancestor, 0)
                step = (own // segs) ^ (known // segs)
                turn = lax.rem(lax.rem(known, segs) - part + segs, segs)
                chosen.append(jnp.where(ancestor >= 0, step * segs + turn, 0))
        q_list = [query_refs[i][0, j] for j in range(group_size)]
        dir_list = [query_refs[i][1, j] for j in range(group_size)]
        do_list = [(adv_ref[i] * d.astype(jnp.float32)).astype(jnp.bfloat16) for d in dir_list]
        k_all = jnp.concatenate([kv_scr[s, 0] for s in chosen], axis=0)
        v_all = jnp.concatenate([kv_scr[s, 1] for s in chosen], axis=0)
        q_all = jnp.concatenate(q_list, axis=0)
        do_all = jnp.concatenate(do_list, axis=0)
        all_scores = lax.dot_general(
            k_all, q_all, contract_last, preferred_element_type=jnp.float32
        )
        all_dprob = lax.dot_general(
            v_all, do_all, contract_last, preferred_element_type=jnp.float32
        )
        for j in range(group_size):
            columns = slice(j * length, (j + 1) * length)
            scores = all_scores[:, columns] * (scale * LOG2E) + bias_ref[i]
            top = jnp.max(scores, axis=0, keepdims=True)
            unnorm = jnp.exp2(scores - top)
            prob = unnorm * (1.0 / jnp.sum(unnorm, axis=0, keepdims=True))
            prob_low = prob.astype(jnp.bfloat16)
            dprob = all_dprob[:, columns]
            row_dot = jnp.sum(prob_low.astype(jnp.float32) * dprob, axis=0, keepdims=True)
            dscore = (prob * (dprob - row_dot)).astype(jnp.bfloat16)
            p_scr[:, columns] = prob_low
            ds_scr[:, columns] = dscore
        dscore_all = ds_scr[...]
        dq_t = lax.dot_general(
            k_all, dscore_all, contract_first, preferred_element_type=jnp.float32
        )
        for j in range(group_size):
            dq = jnp.transpose(dq_t[:, j * length : (j + 1) * length]) * scale
            dq_refs[i][:, j * HD : (j + 1) * HD] = dq.astype(jnp.bfloat16)
        dk_all = jnp.dot(dscore_all, q_all, preferred_element_type=jnp.float32) * scale
        dv_all = jnp.dot(p_scr[...], do_all, preferred_element_type=jnp.float32)
        for slot, s in enumerate(chosen):
            rows = slice(slot * length, (slot + 1) * length)
            acc_scr[s, 0] += dk_all[rows]
            acc_scr[s, 1] += dv_all[rows]
    for step in range(steps):
        for i in range(segs):
            dkv_refs[step][i] = acc_scr[step * segs + i].astype(jnp.bfloat16)


def attend(parents, advantages, bias, query_list, kv_list):
    segs, length = advantages.shape[:2]
    steps = len(kv_list)
    sources = steps * segs
    group_size = query_list[0].shape[1]
    width = group_size * HD
    keys = DEPTH * length
    smem = pl.BlockSpec(memory_space=pltpu.SMEM)
    vmem = pl.BlockSpec(memory_space=pltpu.VMEM)
    out_shape = [jax.ShapeDtypeStruct((length, width), jnp.bfloat16)] * segs
    out_shape += [jax.ShapeDtypeStruct((segs, 2, length, HD), jnp.bfloat16)] * steps
    outs = pl.pallas_call(
        functools.partial(attend_kernel, DEPTH, segs, steps, group_size),
        out_shape=out_shape,
        in_specs=[smem] + [vmem] * (2 + segs + steps),
        out_specs=[vmem] * len(out_shape),
        scratch_shapes=[
            pltpu.VMEM((sources, 2, length, HD), jnp.bfloat16),
            pltpu.VMEM((keys, width), jnp.bfloat16),
            pltpu.VMEM((keys, width), jnp.bfloat16),
            pltpu.VMEM((sources, 2, length, HD), jnp.float32),
        ],
        compiler_params=pltpu.CompilerParams(vmem_limit_bytes=16 * 1024 * 1024),
        cost_estimate=pl.CostEstimate(
            flops=5 * 2 * keys * length * width * segs,
            bytes_accessed=8 * 1024 * 1024,
            transcendentals=keys * width * segs,
        ),
        name="tree_attention_backward",
    )(parents, advantages, bias, *query_list, *kv_list)
    return outs[:segs], outs[segs:]


def join_queries_kernel(*refs):
    part = lax.rem(lax.axis_index("seg"), 2)
    refs, dq_ref = refs[:-1], refs[-1]
    chunks = len(refs) // 2
    width = refs[0].shape[1]
    for index, ref in enumerate(refs):
        side, chunk = divmod(index, chunks)
        where = part if side == 0 else 1 - part
        column = pl.multiple_of((where * chunks + chunk) * width, HD)
        dq_ref[:, pl.ds(column, width)] = ref[...]


def join_queries(own_list, other_list):
    chunks = len(own_list)
    length, width = own_list[0].shape
    vmem = pl.BlockSpec(memory_space=pltpu.VMEM)
    return pl.pallas_call(
        join_queries_kernel,
        out_shape=jax.ShapeDtypeStruct((length, 2 * chunks * width), jnp.bfloat16),
        in_specs=[vmem] * (2 * chunks),
        out_specs=vmem,
        cost_estimate=pl.CostEstimate(
            flops=0, bytes_accessed=8 * length * width * chunks, transcendentals=0
        ),
        compiler_params=SMALL,
        name="join_queries",
    )(*own_list, *other_list)


def join_keys_kernel(chunks, *refs):
    part = lax.rem(lax.axis_index("seg"), 2)
    other_refs, sum_refs = refs[:chunks], refs[chunks:-2]
    many = len(sum_refs) // chunks
    dk_ref, dv_ref = refs[-2:]
    for chunk in range(chunks):
        here = pl.ds(pl.multiple_of((part * chunks + chunk) * HD, HD), HD)
        there = pl.ds(pl.multiple_of(((1 - part) * chunks + chunk) * HD, HD), HD)
        for plane, out_ref in enumerate((dk_ref, dv_ref)):
            blocks = [ref[0, plane] for ref in sum_refs[chunk * many : (chunk + 1) * many]]
            total = sum(block.astype(jnp.float32) for block in blocks)
            out_ref[:, here] = total.astype(jnp.bfloat16)
            out_ref[:, there] = other_refs[chunk][plane]


def join_keys(others, summands):
    chunks = len(others)
    length = others[0].shape[1]
    vmem = pl.BlockSpec(memory_space=pltpu.VMEM)
    flat = [block for blocks in summands for block in blocks]
    out = jax.ShapeDtypeStruct((length, 2 * chunks * HD), jnp.bfloat16)
    return pl.pallas_call(
        functools.partial(join_keys_kernel, chunks),
        out_shape=(out, out),
        in_specs=[vmem] * (chunks + len(flat)),
        out_specs=(vmem, vmem),
        cost_estimate=pl.CostEstimate(
            flops=0, bytes_accessed=16 * length * HD * chunks, transcendentals=0
        ),
        compiler_params=SMALL,
        name="join_keys",
    )(*others, *flat)


def permute(array, pairs):
    return lax.ppermute(array, "seg", pairs)


def after(array, *earlier):
    return lax.optimization_barrier((array, *earlier))[0]


def paired_body(queries, direction, key_vectors, value_vectors, token_rows, parents, lengths, log_rate):
    groups = lax.axis_size("seg")
    length = queries.shape[0]
    chunks = key_vectors.shape[1] // HD // 2
    swap = [(i, i ^ 1) for i in range(groups)]
    steps = range(1, groups // 2)
    meet = {bits: [(i, i ^ (2 * bits)) for i in range(groups)] for bits in steps}

    kept, given = pack(lengths, key_vectors, value_vectors, token_rows, 2, log_rate)
    taken = [permute(block, swap) for block in given]
    kept_q, given_q = pack_queries(after(queries, kept[0]), direction, 2, chunks)
    bias, columns, weights = prepare(parents, lengths, [kept[0], taken[0]], length, log_rate)
    near = [join_blocks(kept[0], after(taken[0], *kept_q)), join_blocks(kept[1], taken[1])]
    two, one = permute(near[0], meet[2]), permute(near[0], meet[1])
    three = permute(after(two, one, near[1], bias), meet[1])
    chains = [[near[0], one, two, three]]
    taken_q = [permute(after(given_q[0], near[0], near[1]), swap)]
    block = after(near[1], two, one, taken_q[0])
    two, one = permute(block, meet[2]), permute(block, meet[1])
    taken_q.append(permute(after(given_q[1], three), swap))
    row, advantages = advantages_of(columns, weights, chains[0])

    dq_own, dq_back, dkv_list = [], [], []
    for chunk in range(chunks):
        query_list = [kept_q[chunk], taken_q[chunk]]
        dq, dkv = attend(parents, advantages, bias, query_list, chains[chunk])
        if chunk == 0:
            three = permute(after(two, dq[0]), meet[1])
            chains.append([block, one, two, three])
        dq_own.append(dq[0])
        dq_back.append(dq[1])
        dkv_list.append(dkv)

    summands = []
    for dkv in dkv_list:
        arrived = [permute(dkv[bits], meet[bits]) for bits in steps[::-1]]
        summands.append([after(dkv[0], dq_own[-1])] + arrived)
    dq_back = [permute(block, swap) for block in dq_back]
    others = []
    for blocks in summands:
        total = sum(block[1].astype(jnp.float32) for block in blocks)
        others.append(permute(total.astype(jnp.bfloat16), swap))
    grad_q = join_queries(dq_own, dq_back)
    grad_k, grad_v = join_keys(others, summands)
    return grad_q, grad_k, grad_v, row[0]


def fetch_rows(spread, wanted):
    routed = jnp.take(spread, jnp.maximum(wanted, 0), axis=0)
    return lax.all_to_all(routed, "seg", split_axis=0, concat_axis=2, tiled=True)


def return_rows(grad_rows, wanted, total_segs):
    returned = lax.all_to_all(grad_rows, "seg", split_axis=2, concat_axis=0, tiled=True)
    piece_len = returned.shape[2]
    feature_len = returned.shape[3]
    routed_ids = wanted.reshape(-1)
    targets = jnp.where(routed_ids >= 0, routed_ids, total_segs)
    summed = jax.ops.segment_sum(
        returned.reshape(-1, piece_len * feature_len).astype(jnp.float32),
        targets,
        num_segments=total_segs + 1,
    )[:total_segs]
    return lax.all_to_all(
        summed.reshape(total_segs, piece_len, feature_len),
        "seg",
        split_axis=0,
        concat_axis=1,
        tiled=True,
    )


def routed_body(queries, direction, key_vectors, value_vectors, token_rows, parents, lengths, log_rate):
    total_segs = parents.shape[0]
    length, width = key_vectors.shape
    heads = width // HD
    own = lax.axis_index("seg")
    own_len = lax.dynamic_slice_in_dim(lengths, own, 1)[0]
    terms = jnp.concatenate(token_terms(log_rate, own_len, *token_rows), axis=1)
    bias, columns, weights = prepare(parents, lengths, [terms], length, log_rate)
    terms = lax.all_gather(terms, "seg", axis=0, tiled=True)
    row, advantages = advantages_of(columns, weights, [terms])
    flat = jnp.concatenate([key_vectors, value_vectors], axis=1)[None]
    spread = lax.all_to_all(flat, "seg", split_axis=1, concat_axis=0, tiled=True)
    chains = ancestors(parents, DEPTH - 1)
    arrived = fetch_rows(spread, chains)[0]
    slot_kv = jnp.concatenate([flat, arrived]).reshape(DEPTH, length, 2, heads, HD)
    slot_kv = jnp.transpose(slot_kv, (0, 3, 2, 1, 4)).reshape(DEPTH, heads, 2 * length, HD)
    (kept_q,) = pack_queries(queries, direction, 1, heads)
    dq_list, dkv_list = [], []
    for head in range(heads):
        kv_list = [slot_kv[slot, head] for slot in range(DEPTH)]
        dq, dkv = attend(parents, advantages, bias, [kept_q[head]], kv_list)
        dq_list.append(dq[0])
        dkv_list.append(jnp.concatenate(dkv))
    rows = jnp.transpose(jnp.stack(dkv_list), (1, 3, 2, 0, 4)).reshape(1, DEPTH, length, -1)
    summed = return_rows(rows[:, 1:], chains, total_segs)[0] + rows[0, 0].astype(jnp.float32)
    grad_keys = summed[:, :width].astype(jnp.bfloat16)
    grad_values = summed[:, width:].astype(jnp.bfloat16)
    return jnp.concatenate(dq_list, axis=1), grad_keys, grad_values, row[0]


def body(
    queries,
    key_vectors,
    value_vectors,
    direction,
    rewards,
    logprobs,
    ref_logprobs,
    value_est,
    parents,
    seg_lengths,
):
    groups = lax.axis_size("seg")
    assert parents.shape[0] == groups
    log_rate = math.log(LAMBDA_SEG) / rewards.shape[0]
    token_rows = [rewards[None], logprobs[None], ref_logprobs[None], value_est[None]]
    plan = paired_body if groups == PAIRED_GROUPS else routed_body
    return plan(
        queries, direction, key_vectors, value_vectors, token_rows, parents, seg_lengths, log_rate
    )


def solution(mesh):
    in_specs = (
        P(("grp", "seg"), "tp"),
        P(("grp", "seg"), "tp"),
        P(("grp", "seg"), "tp"),
        P(("grp", "seg"), "tp"),
        P(("grp", "seg")),
        P(("grp", "seg")),
        P(("grp", "seg")),
        P(("grp", "seg")),
        P("grp"),
        P("grp"),
    )
    out_specs = (
        P(("grp", "seg"), "tp"),
        P(("grp", "seg"), "tp"),
        P(("grp", "seg"), "tp"),
        P(("grp", "seg")),
    )
    return jax.shard_map(body, mesh=mesh, in_specs=in_specs, out_specs=out_specs, check_vma=False)
```

```python
import functools
import math

import jax
import jax.numpy as jnp
from jax import lax
from jax.experimental import pallas as pl
from jax.experimental.pallas import tpu as pltpu
from jax.sharding import PartitionSpec as P

HD = 128
DEPTH = 5
BETA = 0.1
LAMBDA_SEG = 0.7
PAIRED_GROUPS = 8
TERM_ROWS = 16
LOG2E = math.log2(math.e)
SMALL = pltpu.CompilerParams(vmem_limit_bytes=8 * 1024 * 1024)


def lookup(table_values, lookup_ids):
    matches = lookup_ids[..., None] == jnp.arange(table_values.shape[0], dtype=jnp.int32)
    return jnp.sum(jnp.where(matches, table_values, 0), axis=-1)


def ancestors(parents, count):
    current = jnp.arange(parents.shape[0], dtype=jnp.int32)
    chain_list = []
    for depth_step in range(count):
        parent_ids = lookup(parents, current)
        current = jnp.where(current >= 0, parent_ids, -1)
        chain_list.append(current)
    return jnp.stack(chain_list, axis=1)


def token_terms(log_rate, own_len, rewards, logprobs, ref_logprobs, values):
    positions = lax.broadcasted_iota(jnp.int32, rewards.shape, 1)
    later = jnp.concatenate([values[:, 1:], values[:, :1]], axis=1)
    later = jnp.where(positions + 1 < own_len, later, 0.0)
    deltas = jnp.where(
        positions < own_len, rewards - BETA * (logprobs - ref_logprobs) + later - values, 0.0
    )
    powers = jnp.exp(positions.astype(jnp.float32) * log_rate)
    first_local = jnp.sum(deltas * powers, axis=1, keepdims=True)
    firsts = jnp.where(positions == 0, first_local, jnp.where(positions == 1, values[:, :1], 0.0))
    return deltas, firsts


def split_float(value):
    parts = []
    for _ in range(3):
        part = value.astype(jnp.bfloat16)
        parts.append(part)
        value = value - part.astype(jnp.float32)
    return parts


def pack_kernel(
    log_rate,
    parts,
    lengths_ref,
    k_ref,
    v_ref,
    rewards_ref,
    logprobs_ref,
    ref_logprobs_ref,
    values_ref,
    *out_refs,
):
    own = lax.axis_index("seg")
    length = k_ref.shape[0]
    heads = len(out_refs) // parts
    terms = token_terms(
        log_rate,
        lengths_ref[own],
        rewards_ref[...],
        logprobs_ref[...],
        ref_logprobs_ref[...],
        values_ref[...],
    )
    tail = [part.astype(jnp.float32) for x in terms for part in split_float(x)]
    tail.append(jnp.zeros((TERM_ROWS - len(tail), HD), jnp.float32))
    tail = jnp.concatenate(tail).astype(jnp.bfloat16)
    for index, out_ref in enumerate(out_refs):
        step, h = divmod(index, heads)
        part = lax.rem(own + step, parts)
        columns = pl.ds(pl.multiple_of((part * heads + h) * HD, HD), HD)
        out_ref[:length, :] = k_ref[:, columns]
        out_ref[length : 2 * length, :] = v_ref[:, columns]
        if h == 0:
            out_ref[2 * length :, :] = tail


def pack(lengths, k, v, token_rows, parts, log_rate):
    length, width = k.shape
    smem = pl.BlockSpec(memory_space=pltpu.SMEM)
    vmem = pl.BlockSpec(memory_space=pltpu.VMEM)
    heads = width // HD // parts
    assert length == HD
    blocks = [
        jax.ShapeDtypeStruct((2 * length + (TERM_ROWS if h == 0 else 0), HD), k.dtype)
        for h in range(heads)
    ]
    outs = pl.pallas_call(
        functools.partial(pack_kernel, log_rate, parts),
        out_shape=blocks * parts,
        in_specs=[smem] + [vmem] * 6,
        out_specs=[vmem] * (heads * parts),
        cost_estimate=pl.CostEstimate(
            flops=length * 100, bytes_accessed=8 * length * width, transcendentals=length
        ),
        name="pack_keys_values",
    )(lengths, k, v, *token_rows)
    return [outs[step * heads : (step + 1) * heads] for step in range(parts)]


def join_blocks_kernel(mine_ref, other_ref, out_ref):
    rows = mine_ref.shape[0]
    out_ref[:rows, :] = mine_ref[...]
    out_ref[rows:, :] = other_ref[...]


def join_blocks(mine, other):
    vmem = pl.BlockSpec(memory_space=pltpu.VMEM)
    return pl.pallas_call(
        join_blocks_kernel,
        out_shape=jax.ShapeDtypeStruct((2 * mine.shape[0], HD), mine.dtype),
        in_specs=[vmem] * 2,
        out_specs=vmem,
        cost_estimate=pl.CostEstimate(flops=0, bytes_accessed=8 * mine.size, transcendentals=0),
        compiler_params=SMALL,
        name="join_blocks",
    )(mine, other)


def pack_queries_kernel(parts, q_ref, dir_ref, *out_refs):
    own = lax.axis_index("seg")
    chunks = len(out_refs) // parts
    heads = out_refs[0].shape[1]
    for index, out_ref in enumerate(out_refs):
        step, chunk = divmod(index, chunks)
        part = lax.rem(own + step, parts)
        for h in range(heads):
            column = (part * chunks + chunk) * heads + h
            columns = pl.ds(pl.multiple_of(column * HD, HD), HD)
            out_ref[0, h] = q_ref[:, columns]
            out_ref[1, h] = dir_ref[:, columns]


def pack_queries(q, direction, parts, chunks):
    length, width = q.shape
    vmem = pl.BlockSpec(memory_space=pltpu.VMEM)
    block = jax.ShapeDtypeStruct((2, width // HD // parts // chunks, length, HD), q.dtype)
    outs = pl.pallas_call(
        functools.partial(pack_queries_kernel, parts),
        out_shape=(block,) * (parts * chunks),
        in_specs=[vmem, vmem],
        out_specs=(vmem,) * (parts * chunks),
        cost_estimate=pl.CostEstimate(flops=0, bytes_accessed=8 * length * width, transcendentals=0),
        compiler_params=SMALL,
        name="pack_queries",
    )(q, direction)
    return [outs[step * chunks : (step + 1) * chunks] for step in range(parts)]


def parent_of(segment, parents_s):
    known = parents_s[jnp.maximum(segment, 0)]
    return jnp.where(segment >= 0, known, -1).astype(jnp.int32)


def segment_of(own, segs, i):
    part = lax.rem(own, segs)
    return own - part + lax.rem(part + i, segs)


def read_terms(ref, end=None):
    if ref.dtype == jnp.float32:
        length = ref.shape[1] // 2
        return ref[:, :length], ref[:, length:]
    tail = ref[end - TERM_ROWS : end, :].astype(jnp.float32)
    return tail[0:1] + tail[1:2] + tail[2:3], tail[3:4] + tail[4:5] + tail[5:6]


def prepare_kernel(log_rate, depth, parents_s, lengths_s, *refs):
    term_refs, (bias_ref, columns_ref, weights_ref) = refs[:-3], refs[-3:]
    segs, _, length = bias_ref.shape
    count = parents_s.shape[0]
    own = lax.axis_index("seg")

    row_id = lax.broadcasted_iota(jnp.int32, (count, count), 0)
    col_id = lax.broadcasted_iota(jnp.int32, (count, count), 1)
    seg_col = lax.broadcasted_iota(jnp.int32, (count, 1), 0)

    def to_col(row):
        return jnp.sum(jnp.where(row_id == col_id, row, 0.0), axis=1, keepdims=True)

    parent_row = jnp.full((1, count), -1, jnp.int32)
    lens_col = jnp.zeros((count, 1), jnp.int32)
    for seg in range(count):
        parent_row = jnp.where(col_id[:1] == seg, parents_s[seg], parent_row)
        lens_col = jnp.where(seg_col == seg, lengths_s[seg], lens_col)
    lens_col = lens_col.astype(jnp.float32)
    children = (parent_row == row_id).astype(jnp.float32)
    tree = children / jnp.maximum(jnp.sum(children, axis=1, keepdims=True), 1.0)
    factor = jnp.exp(lens_col * log_rate)
    last_factor = jnp.exp((lens_col - 1.0) * log_rate)

    u_id = lax.broadcasted_iota(jnp.int32, (length, length), 0)
    t_id = lax.broadcasted_iota(jnp.int32, (length, length), 1)
    offset = (t_id - u_id).astype(jnp.float32)
    discount = jnp.where(offset >= 0, jnp.exp(offset * log_rate), 0.0)
    t_col = lax.broadcasted_iota(jnp.int32, (length, 1), 0)
    lane = lax.broadcasted_iota(jnp.int32, (count, HD), 1)
    for i in range(segs):
        seg = segment_of(own, segs, i)
        seg_len = lengths_s[seg]
        deltas, _ = read_terms(term_refs[i], term_refs[i].shape[0])
        live = t_col < seg_len
        left = (seg_len - t_col).astype(jnp.float32)
        columns = (
            jnp.sum(discount * deltas, axis=1, keepdims=True),
            jnp.exp((left - 1.0) * log_rate),
            jnp.exp(left * log_rate),
        )
        for index, column in enumerate(columns):
            column = jnp.where(live, column, 0.0)
            columns_ref[i, index] = jnp.broadcast_to(column, (length, HD))

        row = jnp.sum(jnp.where(row_id == seg, tree, 0.0), axis=0, keepdims=True)
        value_col = col = total = to_col(row)
        for _ in range(depth):
            col = to_col(jnp.sum(col * factor * tree, axis=0, keepdims=True))
            total = total + col
        through = to_col(jnp.sum(total * last_factor * tree, axis=0, keepdims=True))
        weights_ref[i, 0] = jnp.where(lane == 1, value_col, 0.0)
        weights_ref[i, 1] = jnp.where(lane == 0, total, jnp.where(lane == 1, through, 0.0))

        ancestor = seg
        for slot in range(depth):
            if slot > 0:
                ancestor = parent_of(ancestor, parents_s)
            slot_len = jnp.where(ancestor >= 0, lengths_s[jnp.maximum(ancestor, 0)], 0)
            seen = u_id < slot_len
            if slot == 0:
                seen = jnp.logical_and(seen, u_id <= t_id)
            bias_ref[i, slot * length : (slot + 1) * length, :] = jnp.where(seen, 0.0, -1e30)


def prepare(parents, lengths, terms, length, log_rate):
    smem = pl.BlockSpec(memory_space=pltpu.SMEM)
    vmem = pl.BlockSpec(memory_space=pltpu.VMEM)
    segs, count = len(terms), parents.shape[0]
    return pl.pallas_call(
        functools.partial(prepare_kernel, log_rate, DEPTH),
        out_shape=(
            jax.ShapeDtypeStruct((segs, DEPTH * length, length), jnp.float32),
            jax.ShapeDtypeStruct((segs, 3, length, HD), jnp.float32),
            jax.ShapeDtypeStruct((segs, 2, count, HD), jnp.float32),
        ),
        in_specs=[smem] * 2 + [vmem] * len(terms),
        out_specs=(vmem,) * 3,
        cost_estimate=pl.CostEstimate(
            flops=20 * DEPTH * segs * length * length,
            bytes_accessed=4 * DEPTH * segs * length * length,
            transcendentals=length * length,
        ),
        compiler_params=SMALL,
        name="prepare",
    )(parents, lengths, *terms)


def advantage_kernel(columns_ref, weights_ref, *refs):
    term_refs, (row_ref, adv_ref) = refs[:-2], refs[-2:]
    segs, _, length, _ = columns_ref.shape
    count = weights_ref.shape[2]
    if len(term_refs) == 1:
        firsts = read_terms(term_refs[0])[1]
    else:
        own = lax.axis_index("seg")
        part, pair = lax.rem(own, segs), own // segs
        seg_id = lax.broadcasted_iota(jnp.int32, (count, length), 0)
        firsts = jnp.zeros((count, length), jnp.float32)
        for step, ref in enumerate(term_refs):
            for side in range(segs):
                seg = (pair ^ step) * segs + lax.rem(part + side, segs)
                end = (side + 1) * (ref.shape[0] // segs)
                firsts = jnp.where(seg_id == seg, read_terms(ref, end)[1], firsts)
    for i in range(segs):
        later_value = jnp.sum(weights_ref[i, 0] * firsts, axis=(0, 1), keepdims=True)
        later_head = jnp.sum(weights_ref[i, 1] * firsts, axis=(0, 1), keepdims=True)
        advantage = (
            columns_ref[i, 0] + columns_ref[i, 1] * later_value + columns_ref[i, 2] * later_head
        )
        adv_ref[i] = advantage
        if i == 0:
            row_id = lax.broadcasted_iota(jnp.int32, advantage.shape, 0)
            col_id = lax.broadcasted_iota(jnp.int32, advantage.shape, 1)
            row_ref[...] = jnp.sum(
                jnp.where(row_id == col_id, advantage, 0.0), axis=0, keepdims=True
            )


def advantages_of(columns, weights, terms):
    vmem = pl.BlockSpec(memory_space=pltpu.VMEM)
    segs, _, length, _ = columns.shape
    return pl.pallas_call(
        advantage_kernel,
        out_shape=(
            jax.ShapeDtypeStruct((1, length), jnp.float32),
            jax.ShapeDtypeStruct((segs, length, HD), jnp.float32),
        ),
        in_specs=[vmem] * (2 + len(terms)),
        out_specs=(vmem,) * 2,
        cost_estimate=pl.CostEstimate(
            flops=10 * segs * length * HD, bytes_accessed=16 * segs * length * HD, transcendentals=0
        ),
        compiler_params=SMALL,
        name="advantages",
    )(columns, weights, *terms)


def attend_kernel(depth, segs, steps, group_size, *refs):
    parents_s, adv_ref, bias_ref = refs[:3]
    query_refs, kv_refs = refs[3 : 3 + segs], refs[3 + segs : 3 + segs + steps]
    kv_scr, p_scr, ds_scr, acc_scr = refs[-4:]
    refs = refs[3 + segs + steps : -4]
    dkv_refs, dq_refs = refs[-steps:], refs[-steps - segs : -steps]

    length = query_refs[0].shape[2]
    own = lax.axis_index("seg")
    for source in range(steps * segs):
        step, side = divmod(source, segs)
        for plane in range(2):
            first = side * (kv_refs[step].shape[0] // segs) + plane * length
            kv_scr[source, plane] = kv_refs[step][first : first + length, :]
    acc_scr[...] = jnp.zeros_like(acc_scr)

    scale = HD**-0.5
    contract_last = (((1,), (1,)), ((), ()))
    contract_first = (((0,), (0,)), ((), ()))
    for i in range(segs):
        ancestor = segment_of(own, segs, i)
        part = lax.rem(own, segs)
        chosen = []
        for slot in range(depth):
            if slot > 0:
                ancestor = parent_of(ancestor, parents_s)
            if segs == 1:
                chosen.append(slot)
            else:
                known = jnp.maximum(ancestor, 0)
                step = (own // segs) ^ (known // segs)
                turn = lax.rem(lax.rem(known, segs) - part + segs, segs)
                chosen.append(jnp.where(ancestor >= 0, step * segs + turn, 0))
        q_list = [query_refs[i][0, j] for j in range(group_size)]
        dir_list = [query_refs[i][1, j] for j in range(group_size)]
        do_list = [(adv_ref[i] * d.astype(jnp.float32)).astype(jnp.bfloat16) for d in dir_list]
        k_all = jnp.concatenate([kv_scr[s, 0] for s in chosen], axis=0)
        v_all = jnp.concatenate([kv_scr[s, 1] for s in chosen], axis=0)
        q_all = jnp.concatenate(q_list, axis=0)
        do_all = jnp.concatenate(do_list, axis=0)
        all_scores = lax.dot_general(
            k_all, q_all, contract_last, preferred_element_type=jnp.float32
        )
        all_dprob = lax.dot_general(
            v_all, do_all, contract_last, preferred_element_type=jnp.float32
        )
        for j in range(group_size):
            columns = slice(j * length, (j + 1) * length)
            scores = all_scores[:, columns] * (scale * LOG2E) + bias_ref[i]
            top = jnp.max(scores, axis=0, keepdims=True)
            unnorm = jnp.exp2(scores - top)
            prob = unnorm * (1.0 / jnp.sum(unnorm, axis=0, keepdims=True))
            prob_low = prob.astype(jnp.bfloat16)
            dprob = all_dprob[:, columns]
            row_dot = jnp.sum(prob_low.astype(jnp.float32) * dprob, axis=0, keepdims=True)
            dscore = (prob * (dprob - row_dot)).astype(jnp.bfloat16)
            p_scr[:, columns] = prob_low
            ds_scr[:, columns] = dscore
        dscore_all = ds_scr[...]
        dq_t = lax.dot_general(
            k_all, dscore_all, contract_first, preferred_element_type=jnp.float32
        )
        for j in range(group_size):
            dq = jnp.transpose(dq_t[:, j * length : (j + 1) * length]) * scale
            dq_refs[i][:, j * HD : (j + 1) * HD] = dq.astype(jnp.bfloat16)
        dk_all = jnp.dot(dscore_all, q_all, preferred_element_type=jnp.float32) * scale
        dv_all = jnp.dot(p_scr[...], do_all, preferred_element_type=jnp.float32)
        for slot, s in enumerate(chosen):
            rows = slice(slot * length, (slot + 1) * length)
            acc_scr[s, 0] += dk_all[rows]
            acc_scr[s, 1] += dv_all[rows]
    for step in range(steps):
        for i in range(segs):
            dkv_refs[step][i] = acc_scr[step * segs + i].astype(jnp.bfloat16)


def attend(parents, advantages, bias, query_list, kv_list):
    segs, length = advantages.shape[:2]
    steps = len(kv_list)
    sources = steps * segs
    group_size = query_list[0].shape[1]
    width = group_size * HD
    keys = DEPTH * length
    smem = pl.BlockSpec(memory_space=pltpu.SMEM)
    vmem = pl.BlockSpec(memory_space=pltpu.VMEM)
    out_shape = [jax.ShapeDtypeStruct((length, width), jnp.bfloat16)] * segs
    out_shape += [jax.ShapeDtypeStruct((segs, 2, length, HD), jnp.bfloat16)] * steps
    outs = pl.pallas_call(
        functools.partial(attend_kernel, DEPTH, segs, steps, group_size),
        out_shape=out_shape,
        in_specs=[smem] + [vmem] * (2 + segs + steps),
        out_specs=[vmem] * len(out_shape),
        scratch_shapes=[
            pltpu.VMEM((sources, 2, length, HD), jnp.bfloat16),
            pltpu.VMEM((keys, width), jnp.bfloat16),
            pltpu.VMEM((keys, width), jnp.bfloat16),
            pltpu.VMEM((sources, 2, length, HD), jnp.float32),
        ],
        compiler_params=pltpu.CompilerParams(vmem_limit_bytes=16 * 1024 * 1024),
        cost_estimate=pl.CostEstimate(
            flops=5 * 2 * keys * length * width * segs,
            bytes_accessed=8 * 1024 * 1024,
            transcendentals=keys * width * segs,
        ),
        name="tree_attention_backward",
    )(parents, advantages, bias, *query_list, *kv_list)
    return outs[:segs], outs[segs:]


def join_queries_kernel(*refs):
    part = lax.rem(lax.axis_index("seg"), 2)
    refs, dq_ref = refs[:-1], refs[-1]
    chunks = len(refs) // 2
    width = refs[0].shape[1]
    for index, ref in enumerate(refs):
        side, chunk = divmod(index, chunks)
        where = part if side == 0 else 1 - part
        column = pl.multiple_of((where * chunks + chunk) * width, HD)
        dq_ref[:, pl.ds(column, width)] = ref[...]


def join_queries(own_list, other_list):
    chunks = len(own_list)
    length, width = own_list[0].shape
    vmem = pl.BlockSpec(memory_space=pltpu.VMEM)
    return pl.pallas_call(
        join_queries_kernel,
        out_shape=jax.ShapeDtypeStruct((length, 2 * chunks * width), jnp.bfloat16),
        in_specs=[vmem] * (2 * chunks),
        out_specs=vmem,
        cost_estimate=pl.CostEstimate(
            flops=0, bytes_accessed=8 * length * width * chunks, transcendentals=0
        ),
        compiler_params=SMALL,
        name="join_queries",
    )(*own_list, *other_list)


def join_keys_kernel(chunks, *refs):
    part = lax.rem(lax.axis_index("seg"), 2)
    other_refs, sum_refs = refs[:chunks], refs[chunks:-2]
    many = len(sum_refs) // chunks
    dk_ref, dv_ref = refs[-2:]
    for chunk in range(chunks):
        here = pl.ds(pl.multiple_of((part * chunks + chunk) * HD, HD), HD)
        there = pl.ds(pl.multiple_of(((1 - part) * chunks + chunk) * HD, HD), HD)
        for plane, out_ref in enumerate((dk_ref, dv_ref)):
            blocks = [ref[0, plane] for ref in sum_refs[chunk * many : (chunk + 1) * many]]
            total = sum(block.astype(jnp.float32) for block in blocks)
            out_ref[:, here] = total.astype(jnp.bfloat16)
            out_ref[:, there] = other_refs[chunk][plane]


def join_keys(others, summands):
    chunks = len(others)
    length = others[0].shape[1]
    vmem = pl.BlockSpec(memory_space=pltpu.VMEM)
    flat = [block for blocks in summands for block in blocks]
    out = jax.ShapeDtypeStruct((length, 2 * chunks * HD), jnp.bfloat16)
    return pl.pallas_call(
        functools.partial(join_keys_kernel, chunks),
        out_shape=(out, out),
        in_specs=[vmem] * (chunks + len(flat)),
        out_specs=(vmem, vmem),
        cost_estimate=pl.CostEstimate(
            flops=0, bytes_accessed=16 * length * HD * chunks, transcendentals=0
        ),
        compiler_params=SMALL,
        name="join_keys",
    )(*others, *flat)


def permute(array, pairs):
    return lax.ppermute(array, "seg", pairs)


def after(array, *earlier):
    return lax.optimization_barrier((array, *earlier))[0]


def paired_body(queries, direction, key_vectors, value_vectors, token_rows, parents, lengths, log_rate):
    groups = lax.axis_size("seg")
    length = queries.shape[0]
    chunks = key_vectors.shape[1] // HD // 2
    swap = [(i, i ^ 1) for i in range(groups)]
    steps = range(1, groups // 2)
    meet = {bits: [(i, i ^ (2 * bits)) for i in range(groups)] for bits in steps}

    kept, given = pack(lengths, key_vectors, value_vectors, token_rows, 2, log_rate)
    taken = [permute(block, swap) for block in given]
    kept_q, given_q = pack_queries(after(queries, kept[0]), direction, 2, chunks)
    bias, columns, weights = prepare(parents, lengths, [kept[0], taken[0]], length, log_rate)
    near = [join_blocks(kept[0], after(taken[0], *kept_q)), join_blocks(kept[1], taken[1])]
    two, one = permute(near[0], meet[2]), permute(near[0], meet[1])
    three = permute(after(two, one, near[1], bias), meet[1])
    chains = [[near[0], one, two, three]]
    taken_q = [permute(after(given_q[0], near[0], near[1]), swap)]
    block = after(near[1], two, one)
    two, one = permute(block, meet[2]), permute(block, meet[1])
    taken_q.append(permute(after(given_q[1], taken_q[0]), swap))
    row, advantages = advantages_of(columns, weights, chains[0])

    dq_own, dq_back, dkv_list = [], [], []
    for chunk in range(chunks):
        query_list = [kept_q[chunk], taken_q[chunk]]
        dq, dkv = attend(parents, advantages, bias, query_list, chains[chunk])
        if chunk == 0:
            three = permute(after(two, dq[0]), meet[1])
            chains.append([block, one, two, three])
        dq_own.append(dq[0])
        dq_back.append(dq[1])
        dkv_list.append(dkv)

    summands = []
    for dkv in dkv_list:
        arrived = [permute(dkv[bits], meet[bits]) for bits in steps[::-1]]
        summands.append([after(dkv[0], dq_own[-1])] + arrived)
    dq_back = [permute(after(block, dq_own[-1]), swap) for block in dq_back]
    others = []
    for blocks in summands:
        total = sum(block[1].astype(jnp.float32) for block in blocks)
        others.append(permute(total.astype(jnp.bfloat16), swap))
    grad_q = join_queries(dq_own, dq_back)
    grad_k, grad_v = join_keys(others, summands)
    return grad_q, grad_k, grad_v, row[0]


def fetch_rows(spread, wanted):
    routed = jnp.take(spread, jnp.maximum(wanted, 0), axis=0)
    return lax.all_to_all(routed, "seg", split_axis=0, concat_axis=2, tiled=True)


def return_rows(grad_rows, wanted, total_segs):
    returned = lax.all_to_all(grad_rows, "seg", split_axis=2, concat_axis=0, tiled=True)
    piece_len = returned.shape[2]
    feature_len = returned.shape[3]
    routed_ids = wanted.reshape(-1)
    targets = jnp.where(routed_ids >= 0, routed_ids, total_segs)
    summed = jax.ops.segment_sum(
        returned.reshape(-1, piece_len * feature_len).astype(jnp.float32),
        targets,
        num_segments=total_segs + 1,
    )[:total_segs]
    return lax.all_to_all(
        summed.reshape(total_segs, piece_len, feature_len),
        "seg",
        split_axis=0,
        concat_axis=1,
        tiled=True,
    )


def routed_body(queries, direction, key_vectors, value_vectors, token_rows, parents, lengths, log_rate):
    total_segs = parents.shape[0]
    length, width = key_vectors.shape
    heads = width // HD
    own = lax.axis_index("seg")
    own_len = lax.dynamic_slice_in_dim(lengths, own, 1)[0]
    terms = jnp.concatenate(token_terms(log_rate, own_len, *token_rows), axis=1)
    bias, columns, weights = prepare(parents, lengths, [terms], length, log_rate)
    terms = lax.all_gather(terms, "seg", axis=0, tiled=True)
    row, advantages = advantages_of(columns, weights, [terms])
    flat = jnp.concatenate([key_vectors, value_vectors], axis=1)[None]
    spread = lax.all_to_all(flat, "seg", split_axis=1, concat_axis=0, tiled=True)
    chains = ancestors(parents, DEPTH - 1)
    arrived = fetch_rows(spread, chains)[0]
    slot_kv = jnp.concatenate([flat, arrived]).reshape(DEPTH, length, 2, heads, HD)
    slot_kv = jnp.transpose(slot_kv, (0, 3, 2, 1, 4)).reshape(DEPTH, heads, 2 * length, HD)
    (kept_q,) = pack_queries(queries, direction, 1, heads)
    dq_list, dkv_list = [], []
    for head in range(heads):
        kv_list = [slot_kv[slot, head] for slot in range(DEPTH)]
        dq, dkv = attend(parents, advantages, bias, [kept_q[head]], kv_list)
        dq_list.append(dq[0])
        dkv_list.append(jnp.concatenate(dkv))
    rows = jnp.transpose(jnp.stack(dkv_list), (1, 3, 2, 0, 4)).reshape(1, DEPTH, length, -1)
    summed = return_rows(rows[:, 1:], chains, total_segs)[0] + rows[0, 0].astype(jnp.float32)
    grad_keys = summed[:, :width].astype(jnp.bfloat16)
    grad_values = summed[:, width:].astype(jnp.bfloat16)
    return jnp.concatenate(dq_list, axis=1), grad_keys, grad_values, row[0]


def body(
    queries,
    key_vectors,
    value_vectors,
    direction,
    rewards,
    logprobs,
    ref_logprobs,
    value_est,
    parents,
    seg_lengths,
):
    groups = lax.axis_size("seg")
    assert parents.shape[0] == groups
    log_rate = math.log(LAMBDA_SEG) / rewards.shape[0]
    token_rows = [rewards[None], logprobs[None], ref_logprobs[None], value_est[None]]
    plan = paired_body if groups == PAIRED_GROUPS else routed_body
    return plan(
        queries, direction, key_vectors, value_vectors, token_rows, parents, seg_lengths, log_rate
    )


def solution(mesh):
    in_specs = (
        P(("grp", "seg"), "tp"),
        P(("grp", "seg"), "tp"),
        P(("grp", "seg"), "tp"),
        P(("grp", "seg"), "tp"),
        P(("grp", "seg")),
        P(("grp", "seg")),
        P(("grp", "seg")),
        P(("grp", "seg")),
        P("grp"),
        P("grp"),
    )
    out_specs = (
        P(("grp", "seg"), "tp"),
        P(("grp", "seg"), "tp"),
        P(("grp", "seg"), "tp"),
        P(("grp", "seg")),
    )
    return jax.shard_map(body, mesh=mesh, in_specs=in_specs, out_specs=out_specs, check_vma=False)
```
